32 devices in a mesh: seq: 4 (over y, x), grp: 8 (over z, core).
Axes of the slice: x: 2, y: 2, z: 4, core: 2. Of those that a mesh axis runs over, the one named last changes fastest.
Arguments:
- layer_in: bfloat16 [8, 768, 2048], P('seq', 'grp'), may hold values from -6 to 6
- gain_one: bfloat16 [2048], P(('seq', 'grp')), may hold values from 0.5 to 1.5
- w_branch: bfloat16 [2048, 2816], P('seq', 'grp'), may hold values from -0.125 to 0.125
- w_rec: bfloat16 [2048, 2816], P('seq', 'grp'), may hold values from -0.125 to 0.125
- conv_w: bfloat16 [16, 4, 176], P('grp', None, 'seq'), may hold values from -3 to 3
- conv_b: bfloat16 [16, 176], P('grp', 'seq'), may hold values from -3 to 3
- gate_a_w: bfloat16 [16, 176, 176], P('grp', 'seq'), may hold values from -0.4375 to 0.4375
- gate_a_b: bfloat16 [16, 176], P('grp', 'seq'), may hold values from -4 to 4
- gate_x_w: bfloat16 [16, 176, 176], P('grp', 'seq'), may hold values from -0.4375 to 0.4375
- gate_x_b: bfloat16 [16, 176], P('grp', 'seq'), may hold values from -4 to 4
- decay_logit: bfloat16 [16, 176], P('grp', 'seq'), may hold values from 5 to 12
- w_out: bfloat16 [2816, 2048], P('grp', 'seq'), may hold values from -0.3125 to 0.3125
- gain_two: bfloat16 [2048], P(('seq', 'grp')), may hold values from 0.5 to 1.5
- mlp_gate: bfloat16 [2048, 6144], P('seq', 'grp'), may hold values from -0.125 to 0.125
- mlp_up: bfloat16 [2048, 6144], P('seq', 'grp'), may hold values from -0.125 to 0.125
- mlp_down: bfloat16 [6144, 2048], P('grp', 'seq'), may hold values from -0.15625 to 0.15625
- out_grad: bfloat16 [8, 768, 2048], P('seq', 'grp'), may hold values from -6 to 6
Outputs:
- layer_out: bfloat16 [8, 768, 2048], P('seq', 'grp')
- grad_x: float32 [8, 768, 2048], P('seq', 'grp')
- grad_gain_one: float32 [2048], P(('seq', 'grp'))
- grad_w_branch: float32 [2048, 2816], P('seq', 'grp')
- grad_w_rec: float32 [2048, 2816], P('seq', 'grp')
- grad_conv_w: float32 [16, 4, 176], P('grp', None, 'seq')
- grad_conv_b: float32 [16, 176], P('grp', 'seq')
- grad_gate_a_w: float32 [16, 176, 176], P('grp', 'seq')
- grad_gate_a_b: float32 [16, 176], P('grp', 'seq')
- grad_gate_x_w: float32 [16, 176, 176], P('grp', 'seq')
- grad_gate_x_b: float32 [16, 176], P('grp', 'seq')
- grad_decay_logit: float32 [16, 176], P('grp', 'seq')
- grad_w_out: float32 [2816, 2048], P('grp', 'seq')
- grad_gain_two: float32 [2048], P(('seq', 'grp'))
- grad_mlp_gate: float32 [2048, 6144], P('seq', 'grp')
- grad_mlp_up: float32 [2048, 6144], P('seq', 'grp')
- grad_mlp_down: float32 [6144, 2048], P('grp', 'seq')
The draws below stay inside these ranges and needn't reach their ends.
All inputs are finite; a program needn't handle non-finite values.
Results may differ from the reference program's by a relative error of at most 0.013.
Values may be sent and summed in bfloat16 or wider, within the bound.
A program may use at most 512 MiB of HBM per device.

```python
import jax
import jax.numpy as jnp
from jax import lax

D = 2048
R = 2816
H = 16
HD = 176
FF = 6144
KCONV = 4
SEQUENCES = 8
SEQ_LEN = 768


def levels(key, extent, cuts, low, top_value):
    level = 1.0
    for dim, blocks in cuts:
        heights = jax.random.uniform(jax.random.fold_in(jax.random.fold_in(key, 6), dim), (blocks,), jnp.float32, low / len(cuts), top_value / len(cuts))
        level = level * jnp.repeat(jnp.exp(heights), extent[dim] // blocks).reshape((-1,) + (1,) * (len(extent) - 1 - dim))
    return level


def centred(own_key, shape, spread, reach, split=(), kind=jnp.bfloat16):
    factor_of = levels(own_key, shape, split, -0.22, 0.18) if split else 1.0
    array = jax.random.normal(own_key, shape, jnp.float32) * spread * factor_of
    return jnp.minimum(jnp.maximum(array, -reach), reach).astype(kind)


def setup_inputs(seed: int = 0) -> dict:
    key_of = jax.random.split(jax.random.key(seed), 18)
    layer_in = centred(key_of[0], (SEQUENCES, SEQ_LEN, D), 1.0, 6.0, ((0, 4), (1, 8)))
    gain_one = jnp.clip(1.0 + 0.1 * jax.random.normal(key_of[1], (D,), jnp.float32), 0.5, 1.5).astype(jnp.bfloat16)
    w_branch = centred(key_of[2], (D, R), D ** -0.5, 0.125, ((0, 4), (1, 8)))
    w_rec = centred(key_of[3], (D, R), D ** -0.5, 0.125, ((0, 4), (1, 8)))
    conv_w = centred(key_of[4], (H, KCONV, HD), 0.5, 3.0, ((0, 8), (2, 4)))
    conv_b = centred(key_of[5], (H, HD), 0.5, 3.0, ((0, 8), (1, 4)))
    gate_a_w = centred(key_of[6], (H, HD, HD), HD ** -0.5, 0.4375, ((0, 8), (1, 4)))
    gate_a_b = centred(key_of[7], (H, HD), 1.0, 4.0, ((0, 8), (1, 4)))
    gate_x_w = centred(key_of[8], (H, HD, HD), HD ** -0.5, 0.4375, ((0, 8), (1, 4)))
    gate_x_b = centred(key_of[9], (H, HD), 1.0, 4.0, ((0, 8), (1, 4)))
    decay_logit = jnp.clip(5.0 + 7.0 * jax.random.uniform(key_of[10], (H, HD), jnp.float32) ** levels(key_of[10], (H, HD), ((0, 8), (1, 4)), -0.2, 0.2), 5.0, 12.0).astype(jnp.bfloat16)
    w_out = centred(key_of[11], (R, D), (R // 8) ** -0.5, 0.3125, ((0, 8), (1, 4)))
    gain_two = jnp.clip(1.0 + 0.1 * jax.random.normal(key_of[12], (D,), jnp.float32), 0.5, 1.5).astype(jnp.bfloat16)
    mlp_gate = centred(key_of[13], (D, FF), D ** -0.5, 0.125, ((0, 4), (1, 8)))
    mlp_up = centred(key_of[14], (D, FF), D ** -0.5, 0.125, ((0, 4), (1, 8)))
    mlp_down = centred(key_of[15], (FF, D), (FF // 4) ** -0.5, 0.15625, ((0, 8), (1, 4)))
    out_grad = centred(key_of[16], (SEQUENCES, SEQ_LEN, D), 1.0, 6.0, ((0, 4), (1, 8)))
    return {"layer_in": layer_in, "gain_one": gain_one, "w_branch": w_branch, "w_rec": w_rec, "conv_w": conv_w, "conv_b": conv_b, "gate_a_w": gate_a_w, "gate_a_b": gate_a_b, "gate_x_w": gate_x_w, "gate_x_b": gate_x_b, "decay_logit": decay_logit, "w_out": w_out, "gain_two": gain_two, "mlp_gate": mlp_gate, "mlp_up": mlp_up, "mlp_down": mlp_down, "out_grad": out_grad}


epsilon = 1e-06

@jax.custom_vjp
def low(v):
    return lax.optimization_barrier(v.astype(jnp.bfloat16)).astype(jnp.float32)

@jax.custom_vjp
def low_back(v):
    return v

def low_keep(v):
    return (low(v), None)

def low_pass(kept, grad):
    return (grad,)

def back_keep(v):
    return (v, None)

def back_low(kept, grad):
    return (low(grad),)
low.defvjp(low_keep, low_pass)
low_back.defvjp(back_keep, back_low)

def product(left, right):
    return jnp.dot(left, right, precision=lax.Precision.HIGHEST, preferred_element_type=jnp.float32)

def rms_norm(values, gain):
    return values * lax.rsqrt(lax.optimization_barrier(jnp.mean(values * values, axis=-1, keepdims=True)) + epsilon) * gain

def combine(earlier, latter):
    return (earlier[0] * latter[0], latter[0] * earlier[1] + latter[1])

def one_sequence(weights, sequence):
    gain_one, w_branch, w_rec, conv_w, conv_b, gate_a_w, gate_a_b, gate_x_w, gate_x_b, decay_logit, w_out, gain_two, mlp_gate, mlp_up, mlp_down = weights
    seq_len = sequence.shape[0]
    head_count, tap_count, head_dim = conv_w.shape
    channels = head_count * head_dim
    normed_one = low(rms_norm(sequence, gain_one))
    branch_pre = low_back(product(normed_one, w_branch))
    gelu_branch = jax.nn.gelu(branch_pre)
    feed = low_back(low(product(normed_one, w_rec)))
    kernel = jnp.transpose(conv_w, (1, 0, 2)).reshape(tap_count, channels)
    padded = jnp.concatenate([jnp.zeros((tap_count - 1, channels), jnp.float32), feed], axis=0)
    conv_sum = jnp.zeros((seq_len, channels), jnp.float32) + conv_b.reshape(channels)
    for offset in range(tap_count):
        start = tap_count - 1 - offset
        conv_sum = conv_sum + kernel[offset] * padded[start:start + seq_len]
    conv_low = low(conv_sum)
    conv_heads = conv_low.reshape(seq_len, head_count, head_dim)
    pre_a = low_back(jnp.einsum('lhi,hij->lhj', conv_heads, gate_a_w, precision=lax.Precision.HIGHEST)).reshape(seq_len, channels) + gate_a_b.reshape(channels)
    pre_x = low_back(jnp.einsum('lhi,hij->lhj', conv_heads, gate_x_w, precision=lax.Precision.HIGHEST)).reshape(seq_len, channels) + gate_x_b.reshape(channels)
    rate_gate = jax.nn.sigmoid(pre_a)
    input_gate = jax.nn.sigmoid(pre_x)
    log_decay = -8.0 * rate_gate * jax.nn.softplus(-decay_logit.reshape(channels))
    decay_rate = jnp.exp(log_decay)
    input_scale = jnp.sqrt(-jnp.expm1(2.0 * log_decay))
    drive_term = input_scale * input_gate * conv_low
    states = lax.associative_scan(combine, (decay_rate, drive_term), axis=0)[1]
    state_low = low_back(low(states))
    mixed = low(gelu_branch * state_low)
    residual = sequence + low_back(product(mixed, w_out))
    normed_two = low(rms_norm(residual, gain_two))
    gate_pre = low_back(product(normed_two, mlp_gate))
    up_proj = low_back(product(normed_two, mlp_up))
    hidden = low(jax.nn.gelu(gate_pre) * up_proj)
    return residual + low_back(product(hidden, mlp_down))

def reference(layer_in, gain_one, w_branch, w_rec, conv_w, conv_b, gate_a_w, gate_a_b, gate_x_w, gate_x_b, decay_logit, w_out, gain_two, mlp_gate, mlp_up, mlp_down, out_grad):
    weights = tuple((param.astype(jnp.float32) for param in (gain_one, w_branch, w_rec, conv_w, conv_b, gate_a_w, gate_a_b, gate_x_w, gate_x_b, decay_logit, w_out, gain_two, mlp_gate, mlp_up, mlp_down)))
    inputs = layer_in.astype(jnp.float32)

    def forward(params, sequences):

        def per_sequence(sequence):
            return one_sequence(params, sequence)
        return lax.map(jax.checkpoint(per_sequence), sequences)
    layer_out, pullback = jax.vjp(forward, weights, inputs)
    grad_weights, grad_inputs = pullback(out_grad.astype(jnp.float32))
    return (layer_out.astype(jnp.bfloat16), grad_inputs, grad_weights[0], grad_weights[1], grad_weights[2], grad_weights[3], grad_weights[4], grad_weights[5], grad_weights[6], grad_weights[7], grad_weights[8], grad_weights[9], grad_weights[10], grad_weights[11], grad_weights[12], grad_weights[13], grad_weights[14])
```

```python
import jax
import jax.numpy as jnp
from jax import lax
from jax.sharding import PartitionSpec as P

epsilon = 1e-06


def matmul(left, right):
    return jnp.dot(left, right, preferred_element_type=jnp.float32)


def matmul_tn(left, right):
    return lax.dot_general(
        left, right, (((0,), (0,)), ((), ())), preferred_element_type=jnp.float32
    )


def matmul_nt(left, right):
    return lax.dot_general(
        left, right, (((1,), (1,)), ((), ())), preferred_element_type=jnp.float32
    )


def combine(earlier, latter):
    return (earlier[0] * latter[0], latter[0] * earlier[1] + latter[1])


def run_scan(decay_rate, drive_term):
    return lax.associative_scan(combine, (decay_rate, drive_term), axis=1)[1]


def norm_back(grad_normed, normal_part, inverse, gain):
    scaled = grad_normed * gain
    return inverse * (scaled - normal_part * jnp.mean(scaled * normal_part, axis=-1, keepdims=True))


def gather_rows(weights):
    return (
        lax.all_gather(weights[0], "seq", axis=0, tiled=True),
        lax.all_gather(weights[1], "seq", axis=0, tiled=True),
        lax.all_gather(weights[2], "seq", axis=1, tiled=True),
    )


def gather_tokens(values):
    return jnp.stack(
        [lax.all_gather(values[s], "grp", axis=0, tiled=True) for s in range(values.shape[0])]
    ).reshape(-1, values.shape[-1])


def scatter_tokens(values, seqs_here):
    parts = values.astype(jnp.bfloat16).reshape(seqs_here, -1, values.shape[-1])
    return jnp.concatenate(
        [
            lax.psum_scatter(parts[s], "grp", scatter_dimension=0, tiled=True)
            for s in range(seqs_here)
        ]
    ).astype(jnp.float32)


def sum_rows(grads):
    low = [grad.astype(jnp.bfloat16) for grad in grads]
    return (
        lax.psum_scatter(low[0], "seq", scatter_dimension=0, tiled=True).astype(jnp.float32),
        lax.psum_scatter(low[1], "seq", scatter_dimension=0, tiled=True).astype(jnp.float32),
        lax.psum_scatter(low[2], "seq", scatter_dimension=1, tiled=True).astype(jnp.float32),
    )


def per_device(
    layer_in,
    gain_one,
    w_branch,
    w_rec,
    conv_w,
    conv_b,
    gate_a_w,
    gate_a_b,
    gate_x_w,
    gate_x_b,
    decay_logit,
    w_out,
    gain_two,
    mlp_gate,
    mlp_up,
    mlp_down,
    out_grad,
):
    seqs_here, positions, model_width = layer_in.shape
    tokens_here = seqs_here * positions
    gains = (
        lax.all_gather(gain_one, ("seq", "grp"), axis=0, tiled=True),
        lax.all_gather(gain_two, ("seq", "grp"), axis=0, tiled=True),
    )
    gain_first = gains[0].astype(jnp.float32)
    gain_second = gains[1].astype(jnp.float32)
    mixer_set = gather_rows((w_branch, w_rec, w_out))
    mlp_set = gather_rows((mlp_gate, mlp_up, mlp_down))
    branch_w, rec_w, out_w = mixer_set
    gate_w, up_w, down_w = mlp_set
    rec_params = (
        lax.all_gather(conv_w, "seq", axis=2, tiled=True),
        lax.all_gather(conv_b, "seq", axis=1, tiled=True),
        lax.all_gather(gate_a_w, "seq", axis=1, tiled=True),
        lax.all_gather(gate_a_b, "seq", axis=1, tiled=True),
        lax.all_gather(gate_x_w, "seq", axis=1, tiled=True),
        lax.all_gather(gate_x_b, "seq", axis=1, tiled=True),
        lax.all_gather(decay_logit, "seq", axis=1, tiled=True),
    )
    taps_full, taps_bias, weight_a, bias_a, weight_x, bias_x, logit_full = rec_params
    heads_here, tap_count, head_dim = taps_full.shape
    channels = heads_here * head_dim
    inputs = layer_in.reshape(tokens_here, model_width).astype(jnp.float32)
    inverse_one = lax.rsqrt(jnp.mean(inputs * inputs, axis=-1, keepdims=True) + epsilon)
    normal_one = inputs * inverse_one
    normed_own = (normal_one * gain_first).astype(jnp.bfloat16)
    normed_one = gather_tokens(normed_own.reshape(layer_in.shape))
    gelu_branch, branch_pull = jax.vjp(jax.nn.gelu, matmul(normed_one, branch_w))
    channel_feed = matmul(normed_one, rec_w).astype(jnp.bfloat16).reshape(seqs_here, -1, channels)
    seq_len = channel_feed.shape[1]
    feed_float = channel_feed.astype(jnp.float32)
    kernel = jnp.transpose(taps_full, (1, 0, 2)).reshape(tap_count, channels).astype(jnp.float32)
    padded = jnp.pad(feed_float, ((0, 0), (tap_count - 1, 0), (0, 0)))
    conv_sum = jnp.zeros((seqs_here, seq_len, channels), jnp.float32) + taps_bias.reshape(
        channels
    ).astype(jnp.float32)
    for offset in range(tap_count):
        start = tap_count - 1 - offset
        conv_sum = conv_sum + kernel[offset] * padded[:, start : start + seq_len]
    conv_low = conv_sum.astype(jnp.bfloat16)
    conv_heads = conv_low.reshape(seqs_here, seq_len, heads_here, head_dim)
    pre_a = jnp.einsum(
        "slhi,hij->slhj", conv_heads, weight_a, preferred_element_type=jnp.float32
    ).reshape(seqs_here, seq_len, channels)
    pre_x = jnp.einsum(
        "slhi,hij->slhj", conv_heads, weight_x, preferred_element_type=jnp.float32
    ).reshape(seqs_here, seq_len, channels)
    rate_gate = jax.nn.sigmoid(pre_a + bias_a.reshape(channels).astype(jnp.float32))
    input_gate = jax.nn.sigmoid(pre_x + bias_x.reshape(channels).astype(jnp.float32))
    logit_float = logit_full.reshape(channels).astype(jnp.float32)
    softness = jax.nn.softplus(-logit_float)
    log_decay = -8.0 * rate_gate * softness
    decay_rate = jnp.exp(log_decay)
    input_scale = jnp.sqrt(-jnp.expm1(2.0 * log_decay))
    conv_float = conv_low.astype(jnp.float32)
    states = run_scan(decay_rate, input_scale * input_gate * conv_float)
    state_low = states.astype(jnp.bfloat16)
    state_float = state_low.reshape(-1, channels).astype(jnp.float32)
    mixed_low = (gelu_branch * state_float).astype(jnp.bfloat16)
    residual = inputs + scatter_tokens(matmul(mixed_low, out_w), seqs_here)
    inverse_two = lax.rsqrt(jnp.mean(residual * residual, axis=-1, keepdims=True) + epsilon)
    normal_two = residual * inverse_two
    normed_two_own = (normal_two * gain_second).astype(jnp.bfloat16)
    normed_two = gather_tokens(normed_two_own.reshape(layer_in.shape))
    up_proj = matmul(normed_two, up_w)
    gate_act, gate_pull = jax.vjp(jax.nn.gelu, matmul(normed_two, gate_w))
    hidden_low = (gate_act * up_proj).astype(jnp.bfloat16)
    down_term = scatter_tokens(matmul(hidden_low, down_w), seqs_here)
    layer_sum = residual + down_term
    layer_out = layer_sum.astype(jnp.bfloat16).reshape(layer_in.shape)
    grad_output = gather_tokens(out_grad)
    grad_down = matmul_tn(hidden_low, grad_output)
    grad_hidden = matmul_nt(grad_output, down_w)
    grad_gate = gate_pull(grad_hidden * up_proj)[0].astype(jnp.bfloat16)
    grad_up = (grad_hidden * gate_act).astype(jnp.bfloat16)
    normed_two_term = scatter_tokens(
        matmul_nt(grad_gate, gate_w) + matmul_nt(grad_up, up_w), seqs_here
    )
    mlp_grads = (matmul_tn(normed_two, grad_gate), matmul_tn(normed_two, grad_up), grad_down)
    mlp_grads = sum_rows(mlp_grads)
    gain_two_local = jnp.sum(normed_two_term * normal_two, axis=0)
    grad_own = out_grad.reshape(tokens_here, model_width).astype(jnp.float32)
    grad_residual = grad_own + norm_back(
        normed_two_term, normal_two, inverse_two, gain_second
    )
    residual_own = grad_residual.astype(jnp.bfloat16)
    residual_low = gather_tokens(residual_own.reshape(layer_in.shape))
    out_weight_grad = matmul_tn(mixed_low, residual_low)
    grad_mixed = matmul_nt(residual_low, out_w)
    grad_state = (grad_mixed * gelu_branch).astype(jnp.bfloat16)
    grad_branch = branch_pull(grad_mixed * state_float)[0].astype(jnp.bfloat16)
    channel_grad = grad_state.reshape(seqs_here, seq_len, channels).astype(jnp.float32)
    next_decay = jnp.concatenate([decay_rate[:, 1:], jnp.zeros_like(decay_rate[:, :1])], axis=1)
    carried = jnp.flip(run_scan(jnp.flip(next_decay, 1), jnp.flip(channel_grad, 1)), 1)
    previous = jnp.concatenate([jnp.zeros_like(states[:, :1]), states[:, :-1]], axis=1)
    grad_scale = carried * input_gate * conv_float
    grad_log = carried * previous * decay_rate - grad_scale * decay_rate * decay_rate / input_scale
    grad_logit = 8.0 * jax.nn.sigmoid(-logit_float) * jnp.sum(grad_log * rate_gate, axis=(0, 1))
    grad_pre_a = -8.0 * softness * grad_log * rate_gate * (1.0 - rate_gate)
    grad_pre_x = carried * input_scale * conv_float * input_gate * (1.0 - input_gate)
    low_a = grad_pre_a.astype(jnp.bfloat16).reshape(seqs_here, seq_len, heads_here, head_dim)
    low_x = grad_pre_x.astype(jnp.bfloat16).reshape(seqs_here, seq_len, heads_here, head_dim)
    grad_weight_a = jnp.einsum(
        "slhi,slhj->hij", conv_heads, low_a, preferred_element_type=jnp.float32
    )
    grad_weight_x = jnp.einsum(
        "slhi,slhj->hij", conv_heads, low_x, preferred_element_type=jnp.float32
    )
    back_gates = jnp.einsum(
        "slhj,hij->slhi", low_a, weight_a, preferred_element_type=jnp.float32
    ) + jnp.einsum("slhj,hij->slhi", low_x, weight_x, preferred_element_type=jnp.float32)
    grad_conv = carried * input_scale * input_gate + back_gates.reshape(
        seqs_here, seq_len, channels
    )
    tap_grads = []
    for offset in range(tap_count):
        start = tap_count - 1 - offset
        tap_grads.append(jnp.sum(grad_conv * padded[:, start : start + seq_len], axis=(0, 1)))
    grad_taps = jnp.transpose(
        jnp.stack(tap_grads, axis=0).reshape(tap_count, heads_here, head_dim), (1, 0, 2)
    )
    grad_padded = jnp.pad(grad_conv, ((0, 0), (0, tap_count - 1), (0, 0)))
    grad_feed = jnp.zeros((seqs_here, seq_len, channels), jnp.float32)
    for offset in range(tap_count):
        grad_feed = grad_feed + kernel[offset] * grad_padded[:, offset : offset + seq_len]
    feed_grad_low = grad_feed.astype(jnp.bfloat16)
    rec_parts = (
        lax.psum_scatter(grad_taps, "seq", scatter_dimension=2, tiled=True),
        lax.psum_scatter(
            jnp.sum(grad_conv, axis=(0, 1)).reshape(heads_here, head_dim),
            "seq",
            scatter_dimension=1,
            tiled=True,
        ),
        lax.psum_scatter(grad_weight_a, "seq", scatter_dimension=1, tiled=True),
        lax.psum_scatter(
            jnp.sum(grad_pre_a, axis=(0, 1)).reshape(heads_here, head_dim),
            "seq",
            scatter_dimension=1,
            tiled=True,
        ),
        lax.psum_scatter(grad_weight_x, "seq", scatter_dimension=1, tiled=True),
        lax.psum_scatter(
            jnp.sum(grad_pre_x, axis=(0, 1)).reshape(heads_here, head_dim),
            "seq",
            scatter_dimension=1,
            tiled=True,
        ),
        lax.psum_scatter(
            grad_logit.reshape(heads_here, head_dim), "seq", scatter_dimension=1, tiled=True
        ),
    )
    feed_rows = feed_grad_low.reshape(-1, channels)
    normed_one_term = scatter_tokens(
        matmul_nt(grad_branch, branch_w) + matmul_nt(feed_rows, rec_w), seqs_here
    )
    mixer_grads = (
        matmul_tn(normed_one, grad_branch),
        matmul_tn(normed_one, feed_rows),
        out_weight_grad,
    )
    mixer_grads = sum_rows(mixer_grads)
    gain_one_local = jnp.sum(normed_one_term * normal_one, axis=0)
    grad_input = grad_residual + norm_back(normed_one_term, normal_one, inverse_one, gain_first)
    gain_parts = (
        lax.psum_scatter(gain_one_local, ("seq", "grp"), scatter_dimension=0, tiled=True),
        lax.psum_scatter(gain_two_local, ("seq", "grp"), scatter_dimension=0, tiled=True),
    )
    return (
        layer_out,
        grad_input.reshape(layer_in.shape),
        gain_parts[0],
        mixer_grads[0],
        mixer_grads[1],
        rec_parts[0],
        rec_parts[1],
        rec_parts[2],
        rec_parts[3],
        rec_parts[4],
        rec_parts[5],
        rec_parts[6],
        mixer_grads[2],
        gain_parts[1],
        mlp_grads[0],
        mlp_grads[1],
        mlp_grads[2],
    )


def solution(mesh):
    placed = (
        P("seq", "grp", None),
        P(("seq", "grp")),
        P("seq", "grp"),
        P("seq", "grp"),
        P("grp", None, "seq"),
        P("grp", "seq"),
        P("grp", "seq", None),
        P("grp", "seq"),
        P("grp", "seq", None),
        P("grp", "seq"),
        P("grp", "seq"),
        P("grp", "seq"),
        P(("seq", "grp")),
        P("seq", "grp"),
        P("seq", "grp"),
        P("grp", "seq"),
        P("seq", "grp", None),
    )
    return jax.shard_map(
        per_device,
        mesh=mesh,
        in_specs=placed,
        out_specs=(
            P("seq", "grp", None),
            P("seq", "grp", None),
            P(("seq", "grp")),
            P("seq", "grp"),
            P("seq", "grp"),
            P("grp", None, "seq"),
            P("grp", "seq"),
            P("grp", "seq", None),
            P("grp", "seq"),
            P("grp", "seq", None),
            P("grp", "seq"),
            P("grp", "seq"),
            P("grp", "seq"),
            P(("seq", "grp")),
            P("seq", "grp"),
            P("seq", "grp"),
            P("grp", "seq"),
        ),
        check_vma=False,
    )
```

```python
import math

import jax
import jax.numpy as jnp
from jax import lax
from jax.experimental import pallas as pl
from jax.experimental.pallas import tpu as pltpu
from jax.sharding import PartitionSpec as P

epsilon = 1e-06
gelu_slope = math.sqrt(2.0 / math.pi)
gelu_cubic = 0.044715


def matmul(left, right):
    return jnp.dot(left, right, preferred_element_type=jnp.float32)


def matmul_tn(left, right):
    return lax.dot_general(
        left, right, (((0,), (0,)), ((), ())), preferred_element_type=jnp.float32
    )


def matmul_nt(left, right):
    return lax.dot_general(
        left, right, (((1,), (1,)), ((), ())), preferred_element_type=jnp.float32
    )


def norm_back(grad_normed, normal_part, inverse, gain):
    scaled = grad_normed * gain
    return inverse * (scaled - normal_part * jnp.mean(scaled * normal_part, axis=-1, keepdims=True))


def gather_rows(weights):
    return (
        lax.all_gather(weights[0], "seq", axis=0, tiled=True),
        lax.all_gather(weights[1], "seq", axis=0, tiled=True),
        lax.all_gather(weights[2], "seq", axis=1, tiled=True),
    )


def gather_tokens(values):
    return jnp.stack(
        [lax.all_gather(values[s], "grp", axis=0, tiled=True) for s in range(values.shape[0])]
    ).reshape(-1, values.shape[-1])


def scatter_tokens(values, seqs_here):
    parts = values.astype(jnp.bfloat16).reshape(seqs_here, -1, values.shape[-1])
    return jnp.concatenate(
        [
            lax.psum_scatter(parts[s], "grp", scatter_dimension=0, tiled=True)
            for s in range(seqs_here)
        ]
    ).astype(jnp.float32)


def sum_rows(grads):
    low = [grad.astype(jnp.bfloat16) for grad in grads]
    return (
        lax.psum_scatter(low[0], "seq", scatter_dimension=0, tiled=True).astype(jnp.float32),
        lax.psum_scatter(low[1], "seq", scatter_dimension=0, tiled=True).astype(jnp.float32),
        lax.psum_scatter(low[2], "seq", scatter_dimension=1, tiled=True).astype(jnp.float32),
    )


def head_diagonal(blocks):
    heads, head_dim, _ = blocks.shape
    rows = []
    for h in range(heads):
        row = [jnp.zeros((head_dim, head_dim), blocks.dtype)] * heads
        row[h] = blocks[h]
        rows.append(jnp.concatenate(row, axis=1))
    return jnp.concatenate(rows, axis=0)


def diagonal_heads(square, heads):
    head_dim = square.shape[0] // heads
    return jnp.stack(
        [
            square[h * head_dim : (h + 1) * head_dim, h * head_dim : (h + 1) * head_dim]
            for h in range(heads)
        ]
    )


def pick_rows(seq_len):
    for rows in (128, 96, 64, 32, 16):
        if seq_len % rows == 0:
            return rows
    return seq_len


def gelu_parts(x):
    cubic = gelu_slope * (x + gelu_cubic * x * x * x)
    bend = jnp.tanh(cubic)
    gate = 0.5 * (1.0 + bend)
    slope = gate + 0.5 * x * (1.0 - bend * bend) * gelu_slope * (1.0 + 3.0 * gelu_cubic * x * x)
    return x * gate, slope


def minus_expm1(x):
    series = 1.0 + x * (1.0 / 9.0)
    for k in (8, 7, 6, 5, 4, 3, 2):
        series = 1.0 + x * (1.0 / k) * series
    return jnp.where(x > -0.4, -x * series, 1.0 - jnp.exp(x))


def shift_down(values, by, fill):
    rows = values.shape[0]
    if by % 8 == 0:
        return jnp.concatenate([jnp.full((by, values.shape[1]), fill), values[: rows - by]], axis=0)
    index = lax.broadcasted_iota(jnp.int32, values.shape, 0)
    return jnp.where(index >= by, pltpu.roll(values, by, 0), fill)


def shift_up(values, by, fill):
    rows = values.shape[0]
    if by % 8 == 0:
        return jnp.concatenate([values[by:], jnp.full((by, values.shape[1]), fill)], axis=0)
    index = lax.broadcasted_iota(jnp.int32, values.shape, 0)
    return jnp.where(index < rows - by, pltpu.roll(values, rows - by, 0), fill)


def scan_block(decay, drive, shift):
    by = 1
    while by < decay.shape[0]:
        drive = drive + decay * shift(drive, by, 0.0)
        decay = decay * shift(decay, by, 1.0)
        by *= 2
    return decay, drive


def decay_parts(rate, softness):
    log_decay = -8.0 * rate * softness
    return jnp.exp(log_decay), jnp.sqrt(minus_expm1(2.0 * log_decay))


def rec_forward_body(
    feed_ref, branch_ref, vectors_ref, softness_ref, gate_a_ref, gate_x_ref,
    conv_ref, rate_ref, input_ref, state_ref, mixed_ref, window, carry,
):
    seqs, rows, _ = feed_ref.shape

    @pl.when(pl.program_id(0) == 0)
    def _():
        window[...] = jnp.zeros_like(window)
        carry[...] = jnp.zeros_like(carry)

    softness = softness_ref[...]
    for s in range(seqs):
        window[s, pl.ds(8, rows), :] = feed_ref[s].astype(jnp.float32)
        conv = vectors_ref[4:5, :] + vectors_ref[0:1, :] * window[s, pl.ds(8, rows), :]
        for k in range(1, 4):
            conv = conv + vectors_ref[k : k + 1, :] * window[s, pl.ds(8 - k, rows), :]
        window[s, pl.ds(0, 8), :] = window[s, pl.ds(rows, 8), :]
        conv_low = conv.astype(jnp.bfloat16)
        conv_ref[s] = conv_low
        rate = jax.nn.sigmoid(matmul(conv_low, gate_a_ref[...]) + vectors_ref[5:6, :])
        gate = jax.nn.sigmoid(matmul(conv_low, gate_x_ref[...]) + vectors_ref[6:7, :])
        rate_ref[s] = rate
        input_ref[s] = gate
        decay, scale = decay_parts(rate, softness)
        total, state = scan_block(decay, scale * gate * conv_low.astype(jnp.float32), shift_down)
        state = state + total * carry[s, 0:1, :]
        carry[s, 0:1, :] = state[rows - 1 : rows, :]
        state_ref[s] = state
        gelu_branch = gelu_parts(branch_ref[s])[0]
        mixed_ref[s] = (gelu_branch * state.astype(jnp.bfloat16).astype(jnp.float32)).astype(
            jnp.bfloat16
        )


def rec_backward_body(
    grad_mixed_ref, branch_ref, feed_ref, feed_before_ref, conv_ref, rate_ref, input_ref,
    state_ref, state_before_ref, vectors_ref, softness_ref, gate_a_ref, gate_x_ref,
    grad_branch_ref, grad_feed_ref, grad_a_ref, grad_x_ref, sums_ref, window, later, carry,
):
    seqs, rows, channels = feed_ref.shape
    step = pl.program_id(0)
    first_block = step == pl.num_programs(0) - 1
    before = feed_before_ref.shape[1]

    @pl.when(step == 0)
    def _():
        later[...] = jnp.zeros_like(later)
        carry[...] = jnp.zeros_like(carry)
        grad_a_ref[...] = jnp.zeros_like(grad_a_ref)
        grad_x_ref[...] = jnp.zeros_like(grad_x_ref)
        sums_ref[...] = jnp.zeros_like(sums_ref)

    softness = softness_ref[...]
    keep = jnp.where(first_block, 0.0, 1.0)
    for s in range(seqs):
        gelu_branch, slope = gelu_parts(branch_ref[s])
        grad_mixed = grad_mixed_ref[s]
        state = state_ref[s]
        state_low = state.astype(jnp.bfloat16).astype(jnp.float32)
        grad_state = (grad_mixed * gelu_branch).astype(jnp.bfloat16).astype(jnp.float32)
        grad_branch_ref[s] = (slope * grad_mixed * state_low).astype(jnp.bfloat16)
        rate = rate_ref[s]
        gate = input_ref[s]
        decay, scale = decay_parts(rate, softness)
        total, carried = scan_block(shift_up(decay, 1, 1.0), grad_state, shift_up)
        carried = carried + total * carry[s, 0:1, :]
        carry[s, 0:1, :] = decay[0:1, :] * carried[0:1, :]
        index = lax.broadcasted_iota(jnp.int32, state.shape, 0)
        last = state_before_ref[s][7:8, :] * keep
        previous = jnp.where(index >= 1, pltpu.roll(state, 1, 0), last)
        conv_low = conv_ref[s]
        conv = conv_low.astype(jnp.float32)
        grad_log = carried * previous * decay - carried * gate * conv * decay * decay / scale
        log_rate = grad_log * rate
        pre_a = -8.0 * softness * log_rate * (1.0 - rate)
        pre_x = carried * scale * conv * gate * (1.0 - gate)
        low_a = pre_a.astype(jnp.bfloat16)
        low_x = pre_x.astype(jnp.bfloat16)
        grad_a_ref[...] += matmul_tn(conv_low, low_a)
        grad_x_ref[...] += matmul_tn(conv_low, low_x)
        grad_conv = (
            carried * scale * gate
            + matmul_nt(low_a, gate_a_ref[...])
            + matmul_nt(low_x, gate_x_ref[...])
        )
        window[s, pl.ds(0, 8), :] = feed_before_ref[s].astype(jnp.float32)[before - 8 :, :] * keep
        window[s, pl.ds(8, rows), :] = feed_ref[s].astype(jnp.float32)
        later[s, pl.ds(rows, 8), :] = later[s, pl.ds(0, 8), :]
        later[s, pl.ds(0, rows), :] = grad_conv
        grad_feed = vectors_ref[0:1, :] * grad_conv
        sums_ref[0:1, :] += jnp.sum(grad_conv * window[s, pl.ds(8, rows), :], axis=0, keepdims=True)
        for k in range(1, 4):
            grad_feed = grad_feed + vectors_ref[k : k + 1, :] * later[s, pl.ds(k, rows), :]
            sums_ref[k : k + 1, :] += jnp.sum(
                grad_conv * window[s, pl.ds(8 - k, rows), :], axis=0, keepdims=True
            )
        grad_feed_ref[s] = grad_feed.astype(jnp.bfloat16)
        sums_ref[4:5, :] += jnp.sum(grad_conv, axis=0, keepdims=True)
        sums_ref[5:6, :] += jnp.sum(pre_a, axis=0, keepdims=True)
        sums_ref[6:7, :] += jnp.sum(pre_x, axis=0, keepdims=True)
        sums_ref[7:8, :] += jnp.sum(log_rate, axis=0, keepdims=True)


def whole(shape):
    return pl.BlockSpec(shape, lambda i: (0,) * len(shape))


def rec_forward(feed, branch, vectors, softness, gate_a, gate_x):
    seqs, seq_len, channels = feed.shape
    rows = pick_rows(seq_len)
    block = pl.BlockSpec((seqs, rows, channels), lambda i: (0, i, 0))
    full = jax.ShapeDtypeStruct(feed.shape, jnp.float32)
    low = jax.ShapeDtypeStruct(feed.shape, jnp.bfloat16)
    return pl.pallas_call(
        rec_forward_body,
        grid=(seq_len // rows,),
        in_specs=[block, block]
        + [whole(v.shape) for v in (vectors, softness, gate_a, gate_x)],
        out_specs=[block] * 5,
        out_shape=[low, full, full, full, low],
        scratch_shapes=[
            pltpu.VMEM((seqs, rows + 8, channels), jnp.float32),
            pltpu.VMEM((seqs, 8, channels), jnp.float32),
        ],
        compiler_params=pltpu.CompilerParams(vmem_limit_bytes=40 << 20),
        name="rec_forward",
    )(feed, branch, vectors, softness, gate_a, gate_x)


def rec_backward(grad_mixed, branch, feed, conv, rate, gate, state, vectors, softness, gate_a, gate_x):
    seqs, seq_len, channels = feed.shape
    rows = pick_rows(seq_len)
    blocks = seq_len // rows
    block = pl.BlockSpec((seqs, rows, channels), lambda i: (0, blocks - 1 - i, 0))

    def ahead(by):
        return pl.BlockSpec(
            (seqs, by, channels),
            lambda i: (0, jnp.maximum((blocks - 1 - i) * (rows // by) - 1, 0), 0),
        )

    low = jax.ShapeDtypeStruct(feed.shape, jnp.bfloat16)
    square = jax.ShapeDtypeStruct((channels, channels), jnp.float32)
    return pl.pallas_call(
        rec_backward_body,
        grid=(blocks,),
        in_specs=[block, block, block, ahead(16), block, block, block, block, ahead(8)]
        + [whole(v.shape) for v in (vectors, softness, gate_a, gate_x)],
        out_specs=[block, block, whole((channels, channels)), whole((channels, channels)), whole((8, channels))],
        out_shape=[low, low, square, square, jax.ShapeDtypeStruct((8, channels), jnp.float32)],
        scratch_shapes=[
            pltpu.VMEM((seqs, rows + 8, channels), jnp.float32),
            pltpu.VMEM((seqs, rows + 8, channels), jnp.float32),
            pltpu.VMEM((seqs, 8, channels), jnp.float32),
        ],
        compiler_params=pltpu.CompilerParams(vmem_limit_bytes=40 << 20),
        name="rec_backward",
    )(grad_mixed, branch, feed, feed, conv, rate, gate, state, state, vectors, softness, gate_a, gate_x)


def per_device(
    layer_in, gain_one, w_branch, w_rec, conv_w, conv_b, gate_a_w, gate_a_b, gate_x_w, gate_x_b,
    decay_logit, w_out, gain_two, mlp_gate, mlp_up, mlp_down, out_grad,
):
    seqs_here, positions, model_width = layer_in.shape
    tokens_here = seqs_here * positions
    heads_here, tap_count, part_dim = conv_w.shape
    seq_devices = lax.axis_size("seq")
    head_dim = part_dim * seq_devices
    channels = heads_here * head_dim
    f32 = jnp.float32

    own_gains = lax.all_gather(jnp.stack([gain_one, gain_two]), "grp", axis=1, tiled=True)
    own_params = jnp.concatenate(
        [jnp.transpose(conv_w, (0, 2, 1))]
        + [v[:, :, None] for v in (conv_b, gate_a_b, gate_x_b, decay_logit)]
        + [gate_a_w, gate_x_w],
        axis=2,
    )
    packed = jnp.concatenate([own_gains.reshape(-1), own_params.reshape(-1)])
    packed = lax.all_gather(packed, "seq", axis=0).reshape(seq_devices, -1)
    gains = packed[:, : own_gains.size].reshape(seq_devices, 2, -1)
    gains = jnp.transpose(gains, (1, 0, 2)).reshape(2, model_width).astype(f32)
    params = packed[:, own_gains.size :].reshape(seq_devices, heads_here, part_dim, -1)
    params = jnp.transpose(params, (1, 0, 2, 3)).reshape(heads_here, head_dim, -1)
    vectors = params[:, :, : tap_count + 4].reshape(channels, -1).T.astype(f32)
    diag_a = head_diagonal(params[:, :, tap_count + 4 : tap_count + 4 + head_dim])
    diag_x = head_diagonal(params[:, :, tap_count + 4 + head_dim :])
    logit = vectors[tap_count + 3 :]
    softness = jax.nn.softplus(-logit)

    branch_w, rec_w, out_w = gather_rows((w_branch, w_rec, w_out))
    gate_w, up_w, down_w = gather_rows((mlp_gate, mlp_up, mlp_down))

    inputs = layer_in.reshape(tokens_here, model_width).astype(f32)
    inverse_one = lax.rsqrt(jnp.mean(inputs * inputs, axis=-1, keepdims=True) + epsilon)
    normal_one = inputs * inverse_one
    normed_own = (normal_one * gains[0]).astype(jnp.bfloat16)
    normed_one = gather_tokens(normed_own.reshape(layer_in.shape))
    branch_pre = matmul(normed_one, branch_w).reshape(seqs_here, -1, channels)
    feed = matmul(normed_one, rec_w).astype(jnp.bfloat16).reshape(seqs_here, -1, channels)
    conv, rate, gate, state, mixed = rec_forward(feed, branch_pre, vectors, softness, diag_a, diag_x)
    mixed = mixed.reshape(-1, channels)
    residual = inputs + scatter_tokens(matmul(mixed, out_w), seqs_here)
    inverse_two = lax.rsqrt(jnp.mean(residual * residual, axis=-1, keepdims=True) + epsilon)
    normal_two = residual * inverse_two
    normed_two_own = (normal_two * gains[1]).astype(jnp.bfloat16)
    normed_two = gather_tokens(normed_two_own.reshape(layer_in.shape))
    up_proj = matmul(normed_two, up_w)
    gate_act, gate_pull = jax.vjp(jax.nn.gelu, matmul(normed_two, gate_w))
    hidden = (gate_act * up_proj).astype(jnp.bfloat16)
    layer_sum = residual + scatter_tokens(matmul(hidden, down_w), seqs_here)
    layer_out = layer_sum.astype(jnp.bfloat16).reshape(layer_in.shape)

    grad_output = gather_tokens(out_grad)
    grad_down = matmul_tn(hidden, grad_output)
    grad_hidden = matmul_nt(grad_output, down_w)
    grad_gate = gate_pull(grad_hidden * up_proj)[0].astype(jnp.bfloat16)
    grad_up = (grad_hidden * gate_act).astype(jnp.bfloat16)
    normed_two_term = scatter_tokens(
        matmul_nt(grad_gate, gate_w) + matmul_nt(grad_up, up_w), seqs_here
    )
    mlp_grads = sum_rows((matmul_tn(normed_two, grad_gate), matmul_tn(normed_two, grad_up), grad_down))
    gain_two_local = jnp.sum(normed_two_term * normal_two, axis=0)
    grad_residual = out_grad.reshape(tokens_here, model_width).astype(f32) + norm_back(
        normed_two_term, normal_two, inverse_two, gains[1]
    )
    residual_low = gather_tokens(grad_residual.astype(jnp.bfloat16).reshape(layer_in.shape))
    out_weight_grad = matmul_tn(mixed, residual_low)
    grad_mixed = matmul_nt(residual_low, out_w).reshape(seqs_here, -1, channels)
    grad_branch, grad_feed, square_a, square_x, sums = rec_backward(
        grad_mixed, branch_pre, feed, conv, rate, gate, state, vectors, softness, diag_a, diag_x
    )
    grad_branch = grad_branch.reshape(-1, channels)
    grad_feed = grad_feed.reshape(-1, channels)
    vector_grads = jnp.concatenate(
        [sums[: tap_count + 3], 8.0 * jax.nn.sigmoid(-logit) * sums[tap_count + 3 :]]
    )
    rec_grads = jnp.concatenate(
        [
            vector_grads.T.reshape(heads_here, head_dim, -1),
            diagonal_heads(square_a, heads_here),
            diagonal_heads(square_x, heads_here),
        ],
        axis=2,
    )
    rec_grads = lax.psum_scatter(rec_grads, "seq", scatter_dimension=1, tiled=True)
    normed_one_term = scatter_tokens(
        matmul_nt(grad_branch, branch_w) + matmul_nt(grad_feed, rec_w), seqs_here
    )
    mixer_grads = sum_rows(
        (matmul_tn(normed_one, grad_branch), matmul_tn(normed_one, grad_feed), out_weight_grad)
    )
    gain_one_local = jnp.sum(normed_one_term * normal_one, axis=0)
    grad_input = grad_residual + norm_back(normed_one_term, normal_one, inverse_one, gains[0])
    gain_grads = lax.psum_scatter(
        jnp.stack([gain_one_local, gain_two_local]), "seq", scatter_dimension=1, tiled=True
    )
    gain_grads = lax.psum_scatter(gain_grads, "grp", scatter_dimension=1, tiled=True)
    at = tap_count + 4
    return (
        layer_out,
        grad_input.reshape(layer_in.shape),
        gain_grads[0],
        mixer_grads[0],
        mixer_grads[1],
        jnp.transpose(rec_grads[:, :, :tap_count], (0, 2, 1)),
        rec_grads[:, :, tap_count],
        rec_grads[:, :, at : at + head_dim],
        rec_grads[:, :, tap_count + 1],
        rec_grads[:, :, at + head_dim :],
        rec_grads[:, :, tap_count + 2],
        rec_grads[:, :, tap_count + 3],
        mixer_grads[2],
        gain_grads[1],
        mlp_grads[0],
        mlp_grads[1],
        mlp_grads[2],
    )


def solution(mesh):
    placed = (
        P("seq", "grp", None),
        P(("seq", "grp")),
        P("seq", "grp"),
        P("seq", "grp"),
        P("grp", None, "seq"),
        P("grp", "seq"),
        P("grp", "seq", None),
        P("grp", "seq"),
        P("grp", "seq", None),
        P("grp", "seq"),
        P("grp", "seq"),
        P("grp", "seq"),
        P(("seq", "grp")),
        P("seq", "grp"),
        P("seq", "grp"),
        P("grp", "seq"),
        P("seq", "grp", None),
    )
    return jax.shard_map(
        per_device,
        mesh=mesh,
        in_specs=placed,
        out_specs=(
            P("seq", "grp", None),
            P("seq", "grp", None),
            P(("seq", "grp")),
            P("seq", "grp"),
            P("seq", "grp"),
            P("grp", None, "seq"),
            P("grp", "seq"),
            P("grp", "seq", None),
            P("grp", "seq"),
            P("grp", "seq", None),
            P("grp", "seq"),
            P("grp", "seq"),
            P("grp", "seq"),
            P(("seq", "grp")),
            P("seq", "grp"),
            P("seq", "grp"),
            P("grp", "seq"),
        ),
        check_vma=False,
    )
```

```python
import math

import jax
import jax.numpy as jnp
from jax import lax
from jax.experimental import pallas as pl
from jax.experimental.pallas import tpu as pltpu
from jax.sharding import PartitionSpec as P

epsilon = 1e-06
gelu_slope = math.sqrt(2.0 / math.pi)
gelu_cubic = 0.044715
MESH = pl.DeviceIdType.MESH


def matmul(left, right):
    return jnp.dot(left, right, preferred_element_type=jnp.float32)


def matmul_tn(left, right):
    return lax.dot_general(
        left, right, (((0,), (0,)), ((), ())), preferred_element_type=jnp.float32
    )


def matmul_nt(left, right):
    return lax.dot_general(
        left, right, (((1,), (1,)), ((), ())), preferred_element_type=jnp.float32
    )


def norm_back(grad_normed, normal_part, inverse, gain):
    scaled = grad_normed * gain
    return inverse * (scaled - normal_part * jnp.mean(scaled * normal_part, axis=-1, keepdims=True))


def gather_rows(weights):
    return (
        lax.all_gather(weights[0], "seq", axis=0, tiled=True),
        lax.all_gather(weights[1], "seq", axis=0, tiled=True),
        lax.all_gather(weights[2], "seq", axis=1, tiled=True),
    )


def sum_rows(grads):
    low = [grad.astype(jnp.bfloat16) for grad in grads]
    return (
        lax.psum_scatter(low[0], "seq", scatter_dimension=0, tiled=True).astype(jnp.float32),
        lax.psum_scatter(low[1], "seq", scatter_dimension=0, tiled=True).astype(jnp.float32),
        lax.psum_scatter(low[2], "seq", scatter_dimension=1, tiled=True).astype(jnp.float32),
    )


def padded_rows(values):
    flat = values.reshape(values.shape[0], -1)
    flat = jnp.pad(flat, ((0, 0), (0, -flat.shape[1] % 1024)))
    return flat.reshape(values.shape[0], -1, 128)


def head_diagonal(blocks):
    heads, head_dim, _ = blocks.shape
    rows = []
    for h in range(heads):
        row = [jnp.zeros((head_dim, head_dim), blocks.dtype)] * heads
        row[h] = blocks[h]
        rows.append(jnp.concatenate(row, axis=1))
    return jnp.concatenate(rows, axis=0)


def diagonal_heads(square, heads):
    head_dim = square.shape[0] // heads
    return jnp.stack(
        [
            square[h * head_dim : (h + 1) * head_dim, h * head_dim : (h + 1) * head_dim]
            for h in range(heads)
        ]
    )


def pick_rows(seq_len):
    for rows in (128, 96, 64, 32, 16):
        if seq_len % rows == 0:
            return rows
    return seq_len


def gelu_parts(x):
    cubic = gelu_slope * (x + gelu_cubic * x * x * x)
    bend = jnp.tanh(cubic)
    gate = 0.5 * (1.0 + bend)
    slope = gate + 0.5 * x * (1.0 - bend * bend) * gelu_slope * (1.0 + 3.0 * gelu_cubic * x * x)
    return x * gate, slope


def minus_expm1(x):
    series = 1.0 + x * (1.0 / 9.0)
    for k in (8, 7, 6, 5, 4, 3, 2):
        series = 1.0 + x * (1.0 / k) * series
    return jnp.where(x > -0.4, -x * series, 1.0 - jnp.exp(x))


def shift_down(values, by, fill):
    rows = values.shape[0]
    if by % 8 == 0:
        return jnp.concatenate([jnp.full((by, values.shape[1]), fill), values[: rows - by]], axis=0)
    index = lax.broadcasted_iota(jnp.int32, values.shape, 0)
    return jnp.where(index >= by, pltpu.roll(values, by, 0), fill)


def shift_up(values, by, fill):
    rows = values.shape[0]
    if by % 8 == 0:
        return jnp.concatenate([values[by:], jnp.full((by, values.shape[1]), fill)], axis=0)
    index = lax.broadcasted_iota(jnp.int32, values.shape, 0)
    return jnp.where(index < rows - by, pltpu.roll(values, rows - by, 0), fill)


def scan_block(decay, drive, shift):
    by = 1
    while by < decay.shape[0]:
        drive = drive + decay * shift(drive, by, 0.0)
        decay = decay * shift(decay, by, 1.0)
        by *= 2
    return decay, drive


def decay_parts(rate, softness):
    log_decay = -8.0 * rate * softness
    return jnp.exp(log_decay), jnp.sqrt(minus_expm1(2.0 * log_decay))


def rec_forward_body(
    feed_ref, branch_ref, vectors_ref, softness_ref, gate_a_ref, gate_x_ref,
    conv_ref, rate_ref, input_ref, state_ref, mixed_ref, window, carry,
):
    seqs, rows, _ = feed_ref.shape

    @pl.when(pl.program_id(0) == 0)
    def _():
        window[...] = jnp.zeros_like(window)
        carry[...] = jnp.zeros_like(carry)

    softness = softness_ref[...]
    for s in range(seqs):
        window[s, pl.ds(8, rows), :] = feed_ref[s].astype(jnp.float32)
        conv = vectors_ref[4:5, :] + vectors_ref[0:1, :] * window[s, pl.ds(8, rows), :]
        for k in range(1, 4):
            conv = conv + vectors_ref[k : k + 1, :] * window[s, pl.ds(8 - k, rows), :]
        window[s, pl.ds(0, 8), :] = window[s, pl.ds(rows, 8), :]
        conv_low = conv.astype(jnp.bfloat16)
        conv_ref[s] = conv_low
        rate = jax.nn.sigmoid(matmul(conv_low, gate_a_ref[...]) + vectors_ref[5:6, :])
        gate = jax.nn.sigmoid(matmul(conv_low, gate_x_ref[...]) + vectors_ref[6:7, :])
        rate_ref[s] = rate
        input_ref[s] = gate
        decay, scale = decay_parts(rate, softness)
        total, state = scan_block(decay, scale * gate * conv_low.astype(jnp.float32), shift_down)
        state = state + total * carry[s, 0:1, :]
        carry[s, 0:1, :] = state[rows - 1 : rows, :]
        state_ref[s] = state
        gelu_branch = gelu_parts(branch_ref[s])[0]
        mixed_ref[s] = (gelu_branch * state.astype(jnp.bfloat16).astype(jnp.float32)).astype(
            jnp.bfloat16
        )


def rec_backward_body(
    grad_mixed_ref, branch_ref, feed_ref, feed_before_ref, conv_ref, rate_ref, input_ref,
    state_ref, state_before_ref, vectors_ref, softness_ref, gate_a_ref, gate_x_ref,
    grad_branch_ref, grad_feed_ref, grad_a_ref, grad_x_ref, sums_ref, window, later, carry,
):
    seqs, rows, channels = feed_ref.shape
    step = pl.program_id(0)
    first_block = step == pl.num_programs(0) - 1
    before = feed_before_ref.shape[1]

    @pl.when(step == 0)
    def _():
        later[...] = jnp.zeros_like(later)
        carry[...] = jnp.zeros_like(carry)
        grad_a_ref[...] = jnp.zeros_like(grad_a_ref)
        grad_x_ref[...] = jnp.zeros_like(grad_x_ref)
        sums_ref[...] = jnp.zeros_like(sums_ref)

    softness = softness_ref[...]
    keep = jnp.where(first_block, 0.0, 1.0)
    for s in range(seqs):
        gelu_branch, slope = gelu_parts(branch_ref[s])
        grad_mixed = grad_mixed_ref[s]
        state = state_ref[s]
        state_low = state.astype(jnp.bfloat16).astype(jnp.float32)
        grad_state = (grad_mixed * gelu_branch).astype(jnp.bfloat16).astype(jnp.float32)
        grad_branch_ref[s] = (slope * grad_mixed * state_low).astype(jnp.bfloat16)
        rate = rate_ref[s]
        gate = input_ref[s]
        decay, scale = decay_parts(rate, softness)
        total, carried = scan_block(shift_up(decay, 1, 1.0), grad_state, shift_up)
        carried = carried + total * carry[s, 0:1, :]
        carry[s, 0:1, :] = decay[0:1, :] * carried[0:1, :]
        index = lax.broadcasted_iota(jnp.int32, state.shape, 0)
        last = state_before_ref[s][7:8, :] * keep
        previous = jnp.where(index >= 1, pltpu.roll(state, 1, 0), last)
        conv_low = conv_ref[s]
        conv = conv_low.astype(jnp.float32)
        grad_log = carried * previous * decay - carried * gate * conv * decay * decay / scale
        log_rate = grad_log * rate
        pre_a = -8.0 * softness * log_rate * (1.0 - rate)
        pre_x = carried * scale * conv * gate * (1.0 - gate)
        low_a = pre_a.astype(jnp.bfloat16)
        low_x = pre_x.astype(jnp.bfloat16)
        grad_a_ref[...] += matmul_tn(conv_low, low_a)
        grad_x_ref[...] += matmul_tn(conv_low, low_x)
        grad_conv = (
            carried * scale * gate
            + matmul_nt(low_a, gate_a_ref[...])
            + matmul_nt(low_x, gate_x_ref[...])
        )
        window[s, pl.ds(0, 8), :] = feed_before_ref[s].astype(jnp.float32)[before - 8 :, :] * keep
        window[s, pl.ds(8, rows), :] = feed_ref[s].astype(jnp.float32)
        later[s, pl.ds(rows, 8), :] = later[s, pl.ds(0, 8), :]
        later[s, pl.ds(0, rows), :] = grad_conv
        grad_feed = vectors_ref[0:1, :] * grad_conv
        sums_ref[0:1, :] += jnp.sum(grad_conv * window[s, pl.ds(8, rows), :], axis=0, keepdims=True)
        for k in range(1, 4):
            grad_feed = grad_feed + vectors_ref[k : k + 1, :] * later[s, pl.ds(k, rows), :]
            sums_ref[k : k + 1, :] += jnp.sum(
                grad_conv * window[s, pl.ds(8 - k, rows), :], axis=0, keepdims=True
            )
        grad_feed_ref[s] = grad_feed.astype(jnp.bfloat16)
        sums_ref[4:5, :] += jnp.sum(grad_conv, axis=0, keepdims=True)
        sums_ref[5:6, :] += jnp.sum(pre_a, axis=0, keepdims=True)
        sums_ref[6:7, :] += jnp.sum(pre_x, axis=0, keepdims=True)
        sums_ref[7:8, :] += jnp.sum(log_rate, axis=0, keepdims=True)


def whole(shape):
    return pl.BlockSpec(shape, lambda i: (0,) * len(shape))


def rec_forward(feed, branch, vectors, softness, gate_a, gate_x):
    seqs, seq_len, channels = feed.shape
    rows = pick_rows(seq_len)
    block = pl.BlockSpec((seqs, rows, channels), lambda i: (0, i, 0))
    full = jax.ShapeDtypeStruct(feed.shape, jnp.float32)
    low = jax.ShapeDtypeStruct(feed.shape, jnp.bfloat16)
    return pl.pallas_call(
        rec_forward_body,
        grid=(seq_len // rows,),
        in_specs=[block, block]
        + [whole(v.shape) for v in (vectors, softness, gate_a, gate_x)],
        out_specs=[block] * 5,
        out_shape=[low, full, full, full, low],
        scratch_shapes=[
            pltpu.VMEM((seqs, rows + 8, channels), jnp.float32),
            pltpu.VMEM((seqs, 8, channels), jnp.float32),
        ],
        compiler_params=pltpu.CompilerParams(vmem_limit_bytes=40 << 20),
        name="rec_forward",
    )(feed, branch, vectors, softness, gate_a, gate_x)


def rec_backward(grad_mixed, branch, feed, conv, rate, gate, state, vectors, softness, gate_a, gate_x):
    seqs, seq_len, channels = feed.shape
    rows = pick_rows(seq_len)
    blocks = seq_len // rows
    block = pl.BlockSpec((seqs, rows, channels), lambda i: (0, blocks - 1 - i, 0))

    def ahead(by):
        return pl.BlockSpec(
            (seqs, by, channels),
            lambda i: (0, jnp.maximum((blocks - 1 - i) * (rows // by) - 1, 0), 0),
        )

    low = jax.ShapeDtypeStruct(feed.shape, jnp.bfloat16)
    square = jax.ShapeDtypeStruct((channels, channels), jnp.float32)
    return pl.pallas_call(
        rec_backward_body,
        grid=(blocks,),
        in_specs=[block, block, block, ahead(16), block, block, block, block, ahead(8)]
        + [whole(v.shape) for v in (vectors, softness, gate_a, gate_x)],
        out_specs=[block, block, whole((channels, channels)), whole((channels, channels)), whole((8, channels))],
        out_shape=[low, low, square, square, jax.ShapeDtypeStruct((8, channels), jnp.float32)],
        scratch_shapes=[
            pltpu.VMEM((seqs, rows + 8, channels), jnp.float32),
            pltpu.VMEM((seqs, rows + 8, channels), jnp.float32),
            pltpu.VMEM((seqs, 8, channels), jnp.float32),
        ],
        compiler_params=pltpu.CompilerParams(vmem_limit_bytes=40 << 20),
        name="rec_backward",
    )(grad_mixed, branch, feed, feed, conv, rate, gate, state, state, vectors, softness, gate_a, gate_x)


def line_place():
    return lax.axis_size("grp") // 2, lax.axis_index("grp") // 2, lax.axis_index("grp") % 2


def greet_line():
    chips, chip, core = line_place()
    barrier = pltpu.get_barrier_semaphore()

    def signal(place):
        pl.semaphore_signal(barrier, inc=1, device_id={"grp": place}, device_id_type=MESH)

    signal(chip * 2 + 1 - core)

    @pl.when(chip > 0)
    def _():
        signal(chip * 2 + core - 2)

    @pl.when(chip < chips - 1)
    def _():
        signal(chip * 2 + core + 2)

    ends = (chip == 0).astype(jnp.int32) + (chip == chips - 1).astype(jnp.int32)
    pl.semaphore_wait(barrier, 3 - ends)


def greet_axes(axes):
    barrier = pltpu.get_barrier_semaphore()
    for axis in axes:
        size = lax.axis_size(axis)
        for k in range(1, size):
            pl.semaphore_signal(
                barrier,
                inc=1,
                device_id={axis: lax.rem(lax.axis_index(axis) + k, size)},
                device_id_type=MESH,
            )
    pl.semaphore_wait(barrier, sum(lax.axis_size(axis) - 1 for axis in axes))


class Gather:
    def __init__(self, sources, outs, rows, send_sem, recv_sem, own_sem):
        self.chips, self.chip, self.core = line_place()
        self.me = self.chip * 2 + self.core
        self.sources, self.outs, self.rows = sources, outs, rows
        self.send_sem, self.recv_sem, self.own_sem = send_sem, recv_sem, own_sem

    def slot(self, p, origin):
        return self.outs[p].at[pl.ds(pl.multiple_of(origin * self.rows, self.rows), self.rows), :]

    def copy(self, p, source, origin, target, way):
        return pltpu.make_async_remote_copy(
            src_ref=source,
            dst_ref=self.slot(p, origin),
            send_sem=self.send_sem.at[way, p, origin],
            recv_sem=self.recv_sem.at[p, origin],
            device_id={"grp": target},
            device_id_type=MESH,
        )

    def to_right(self, p, source, origin):
        return self.copy(p, source, origin, self.me + 2, 0)

    def to_left(self, p, source, origin):
        return self.copy(p, source, origin, self.me - 2, 1)

    def to_partner(self, p, source, origin):
        return self.copy(p, source, origin, self.chip * 2 + 1 - self.core, 2)

    def own(self, p):
        return pltpu.make_async_copy(self.sources[p], self.slot(p, self.me), self.own_sem.at[p])

    def start(self, p):
        source = self.sources[p]

        @pl.when(self.chip < self.chips - 1)
        def _():
            self.to_right(p, source, self.me).start()

        @pl.when(self.chip > 0)
        def _():
            self.to_left(p, source, self.me).start()

        self.to_partner(p, source, self.me).start()
        self.own(p).start()

    def hop(self, p, h):
        left_origin = self.me - 2 - 2 * h
        right_origin = self.me + 2 + 2 * h

        @pl.when(self.chip - 1 - h >= 0)
        def _():
            here = self.slot(p, left_origin)
            self.to_right(p, here, left_origin).wait_recv()

            @pl.when(self.chip < self.chips - 1)
            def _():
                self.to_right(p, here, left_origin).start()

            self.to_partner(p, here, left_origin).start()

        @pl.when(self.chip + 1 + h <= self.chips - 1)
        def _():
            here = self.slot(p, right_origin)
            self.to_left(p, here, right_origin).wait_recv()

            @pl.when(self.chip > 0)
            def _():
                self.to_left(p, here, right_origin).start()

            self.to_partner(p, here, right_origin).start()

    def finish(self, p):
        for c in range(self.chips):
            origin = c * 2 + 1 - self.core
            self.to_partner(p, self.slot(p, origin), origin).wait_recv()
        self.own(p).wait()
        for c in range(self.chips):
            origin = c * 2 + self.core
            here = self.slot(p, origin)
            self.to_partner(p, here, origin).wait_send()

            @pl.when((c <= self.chip) & (self.chip < self.chips - 1))
            def _():
                self.to_right(p, here, origin).wait_send()

            @pl.when((c >= self.chip) & (self.chip > 0))
            def _():
                self.to_left(p, here, origin).wait_send()


def gather_sems(pieces):
    n = lax.axis_size("grp")
    return [
        pltpu.SemaphoreType.DMA((3, pieces, n)),
        pltpu.SemaphoreType.DMA((pieces, n)),
        pltpu.SemaphoreType.DMA((pieces,)),
    ]


class Scatter:
    def __init__(self, rows, part, out, swap_in, line_in, send_sem, recv_sem):
        self.chips, self.chip, self.core = line_place()
        self.me = self.chip * 2 + self.core
        self.rows, self.part, self.out = rows, part, out
        self.swap_in, self.line_in = swap_in, line_in
        self.send_sem, self.recv_sem = send_sem, recv_sem

    def copy(self, dest, place, way, slot, p):
        return pltpu.make_async_remote_copy(
            src_ref=self.out.at[p, slot],
            dst_ref=dest,
            send_sem=self.send_sem.at[way, p, slot],
            recv_sem=self.recv_sem.at[way, p, slot],
            device_id={"grp": place},
            device_id_type=MESH,
        )

    def swap(self, p, c):
        return self.copy(self.swap_in.at[p, c], self.chip * 2 + 1 - self.core, 0, c, p)

    def right(self, p, c):
        return self.copy(self.line_in.at[p, c], self.me + 2, 1, c, p)

    def left(self, p, c):
        slot = jnp.where(c == self.chip - 1, self.chips, c)
        return self.copy(self.line_in.at[p, slot], self.me - 2, 2, c, p)

    def from_right(self, p, c):
        slot = jnp.where(c == self.chip, self.chips, c)
        return self.copy(self.line_in.at[p, slot], self.me + 2, 2, c, p)

    def fill(self, p, s, lefts, rights, transposed, width=512):
        def rows_of(ref, core):
            at = [pl.multiple_of((c * 2 + core) * self.rows, self.rows) for c in range(self.chips)]
            return jnp.concatenate([ref[s, pl.ds(a, self.rows), :] for a in at], axis=0)

        def product(core, store):
            chosen = [rows_of(ref, core) for ref in lefts]

            @pl.loop(0, self.out.shape[-1] // width)
            def _(j):
                columns = pl.ds(pl.multiple_of(j * width, width), width)
                total = None
                for left, right in zip(chosen, rights):
                    term = matmul_nt(left, right[columns, :]) if transposed else matmul(left, right[:, columns])
                    total = term if total is None else total + term
                for c in range(self.chips):
                    store(c, columns, total[c * self.rows : (c + 1) * self.rows])

        def to_out(c, columns, value):
            self.out[p, c, :, columns] = value.astype(jnp.bfloat16)

        def to_part(c, columns, value):
            self.part[p, c, :, columns] = value

        product(1 - self.core, to_out)
        for c in range(self.chips):
            self.swap(p, c).start()
        product(self.core, to_part)

    def own(self, p, c):
        self.swap(p, c).wait_recv()
        return self.part[p, c] + self.swap_in[p, c].astype(jnp.float32)

    def hop(self, p, h):
        c = self.chips - 1 - h

        @pl.when(c > self.chip)
        def _():
            self.swap(p, c).wait_send()

            @pl.when(self.chip == 0)
            def _():
                self.out[p, c] = self.own(p, c).astype(jnp.bfloat16)

            @pl.when(self.chip > 0)
            def _():
                total = self.own(p, c)
                self.right(p, c).wait_recv()
                self.out[p, c] = (total + self.line_in[p, c].astype(jnp.float32)).astype(jnp.bfloat16)

            self.right(p, c).start()

        @pl.when(h < self.chip)
        def _():
            self.swap(p, h).wait_send()

            @pl.when(self.chip == self.chips - 1)
            def _():
                self.out[p, h] = self.own(p, h).astype(jnp.bfloat16)

            @pl.when(self.chip < self.chips - 1)
            def _():
                total = self.own(p, h)
                self.from_right(p, h).wait_recv()
                self.out[p, h] = (total + self.line_in[p, h].astype(jnp.float32)).astype(jnp.bfloat16)

            self.left(p, h).start()

    def result(self, p):
        chip = self.chip
        self.part[p, chip] = self.own(p, chip)

        @pl.when(chip > 0)
        def _():
            self.right(p, chip).wait_recv()
            self.part[p, chip] += self.line_in[p, chip].astype(jnp.float32)

        @pl.when(chip < self.chips - 1)
        def _():
            self.from_right(p, chip).wait_recv()
            self.part[p, chip] += self.line_in[p, self.chips].astype(jnp.float32)

        return self.part.at[p, chip]

    def finish(self, p):
        self.swap(p, self.chip).wait_send()
        for c in range(self.chips):

            @pl.when(c > self.chip)
            def _():
                self.right(p, c).wait_send()

            @pl.when(c < self.chip)
            def _():
                self.left(p, c).wait_send()


def scatter_scratch(pieces, rows, width):
    chips = lax.axis_size("grp") // 2
    return [
        pltpu.VMEM((pieces, chips, rows, width), jnp.float32),
        pltpu.VMEM((pieces, chips, rows, width), jnp.bfloat16),
        pltpu.VMEM((pieces, chips, rows, width), jnp.bfloat16),
        pltpu.VMEM((pieces, chips + 1, rows, width), jnp.bfloat16),
        pltpu.SemaphoreType.DMA((3, pieces, chips)),
        pltpu.SemaphoreType.DMA((3, pieces, chips)),
    ]


in_vmem = pl.BlockSpec(memory_space=pltpu.VMEM)
in_hbm = pl.BlockSpec(memory_space=pl.ANY)


def call(body, name, number, inputs, in_specs, outs, out_specs, scratch, us):
    return pl.pallas_call(
        body,
        in_specs=in_specs,
        out_specs=out_specs,
        out_shape=outs,
        scratch_shapes=scratch,
        name=name,
        cost_estimate=pl.CostEstimate(
            flops=us * 1000000000, bytes_accessed=us * 3000000, transcendentals=0
        ),
        compiler_params=pltpu.CompilerParams(
            collective_id=number, has_side_effects=True, vmem_limit_bytes=60 << 20
        ),
    )(*inputs)


def views(ref):
    return [ref.at[s] for s in range(ref.shape[0])]


def first_body(seqs, x_ref, pack_ref, *refs):
    full_ref, params_ref, gains_ref = refs[:3]
    small_send, small_recv, gain_send, gain_recv = refs[6:]
    greet_axes(("seq", "grp"))
    gather = Gather(views(x_ref), views(full_ref), x_ref.shape[1], *refs[3:6])
    for s in range(seqs):
        gather.start(s)
    size, me = lax.axis_size("seq"), lax.axis_index("seq")

    def small(k, owner):
        return pltpu.make_async_remote_copy(
            src_ref=pack_ref,
            dst_ref=params_ref.at[owner],
            send_sem=small_send.at[k],
            recv_sem=small_recv.at[k],
            device_id={"seq": lax.rem(me + k, size)},
            device_id_type=MESH,
        )

    for k in range(1, size):
        small(k, me).start()
    params_ref[me] = pack_ref[...]
    for k in range(1, size):
        small(k, lax.rem(me - k + size, size)).wait_recv()
    n, place = lax.axis_size("grp"), lax.axis_index("grp")
    for owner in range(size):
        gains_ref[place, owner] = params_ref[owner, pl.ds(pack_ref.shape[0] - 8, 8), :]

    def gain(k, owner):
        return pltpu.make_async_remote_copy(
            src_ref=gains_ref.at[place],
            dst_ref=gains_ref.at[owner],
            send_sem=gain_send.at[k],
            recv_sem=gain_recv.at[k],
            device_id={"grp": lax.rem(place + k, n)},
            device_id_type=MESH,
        )

    for k in range(1, n):
        gain(k, place).start()
    for h in range(gather.chips - 1):
        for s in range(seqs):
            gather.hop(s, h)
    for k in range(1, n):
        gain(k, lax.rem(place - k + n, n)).wait_recv()
    for k in range(1, size):
        small(k, me).wait_send()
    for k in range(1, n):
        gain(k, place).wait_send()
    for s in range(seqs):
        gather.finish(s)


def gather_first(layer_in, pack):
    seqs, rows, width = layer_in.shape
    n, size = lax.axis_size("grp"), lax.axis_size("seq")
    full = jax.ShapeDtypeStruct((seqs, n * rows, width), jnp.bfloat16)
    return call(
        lambda *refs: first_body(seqs, *refs), "gather_first", 1,
        (layer_in, pack), [in_hbm, in_vmem],
        [
            full,
            jax.ShapeDtypeStruct((size,) + pack.shape, jnp.float32),
            jax.ShapeDtypeStruct((n, size, 8, 128), jnp.float32),
        ],
        [in_hbm] + [in_vmem] * 2,
        gather_sems(seqs)
        + [pltpu.SemaphoreType.DMA((size,))] * 2
        + [pltpu.SemaphoreType.DMA((n,))] * 2,
        70,
    )


def mean_of(values):
    return jnp.mean(values, axis=-1, keepdims=True)


def mixer_out_body(seqs, mixed_ref, out_w_ref, x_ref, grad_ref, gain_ref, *refs):
    residual_ref, normed_ref, grads_ref, low_ref = refs[:4]
    greet_line()
    rows = x_ref.shape[1]
    gather = Gather(
        views(low_ref) + views(grad_ref), views(normed_ref) + views(grads_ref), rows, *refs[4:7]
    )
    scatter = Scatter(rows, *refs[7:])
    hops = range(gather.chips - 1)
    for s in range(seqs):
        scatter.fill(s, s, [mixed_ref], [out_w_ref], False)
        if s == 0:
            gather.start(seqs)
    for s in range(seqs):
        for h in hops:
            scatter.hop(s, h)
            if s == 0:
                gather.hop(seqs, h)
            else:
                gather.hop(s - 1, h)
        residual = x_ref[s].astype(jnp.float32) + scatter.result(s)[...]
        residual_ref[s] = residual
        normal = residual * lax.rsqrt(mean_of(residual * residual) + epsilon)
        low_ref[s] = (normal * gain_ref[...]).astype(jnp.bfloat16)
        gather.start(s)
    for s in range(1, seqs):
        gather.start(seqs + s)
    for h in hops:
        gather.hop(seqs - 1, h)
        for s in range(1, seqs):
            gather.hop(seqs + s, h)
    for s in range(seqs):
        scatter.finish(s)
        gather.finish(s)
        gather.finish(seqs + s)


def mixer_out(mixed, out_w, layer_in, out_grad, gain):
    seqs, rows, width = layer_in.shape
    full = jax.ShapeDtypeStruct((seqs, lax.axis_size("grp") * rows, width), jnp.bfloat16)
    return call(
        lambda *refs: mixer_out_body(seqs, *refs), "mixer_out", 2,
        (mixed, out_w, layer_in, out_grad, gain), [in_vmem] * 3 + [in_hbm] + [in_vmem],
        [jax.ShapeDtypeStruct(layer_in.shape, jnp.float32), full, full],
        [in_vmem] + [in_hbm] * 2,
        [pltpu.VMEM(layer_in.shape, jnp.bfloat16)]
        + gather_sems(2 * seqs)
        + scatter_scratch(seqs, rows, width),
        130,
    )


def mlp_back_body(seqs, gate_ref, up_ref, gate_w_ref, up_w_ref, residual_ref, grad_ref, gain_ref, *refs):
    grad_residual_ref, gain_grad_ref, full_ref, low_ref = refs[:4]
    greet_line()
    rows = grad_ref.shape[1]
    gather = Gather(views(low_ref), views(full_ref), rows, *refs[4:7])
    scatter = Scatter(rows, *refs[7:])
    hops = range(gather.chips - 1)
    for s in range(seqs):
        scatter.fill(s, s, [gate_ref, up_ref], [gate_w_ref, up_w_ref], True)
    gain_grad_ref[...] = jnp.zeros_like(gain_grad_ref)
    for s in range(seqs):
        for h in hops:
            scatter.hop(s, h)
            if s:
                gather.hop(s - 1, h)
        term = scatter.result(s)[...]
        residual = residual_ref[s]
        inverse = lax.rsqrt(mean_of(residual * residual) + epsilon)
        normal = residual * inverse
        gain_grad_ref[0:1, :] += jnp.sum(term * normal, axis=0, keepdims=True)
        grad = grad_ref[s].astype(jnp.float32) + norm_back(term, normal, inverse, gain_ref[...])
        grad_residual_ref[s] = grad
        low_ref[s] = grad.astype(jnp.bfloat16)
        gather.start(s)
    for h in hops:
        gather.hop(seqs - 1, h)
    for s in range(seqs):
        scatter.finish(s)
        gather.finish(s)


def mlp_back(grad_gate, grad_up, gate_w, up_w, residual, out_grad, gain):
    seqs, rows, width = residual.shape
    full = jax.ShapeDtypeStruct((seqs, lax.axis_size("grp") * rows, width), jnp.bfloat16)
    return call(
        lambda *refs: mlp_back_body(seqs, *refs), "mlp_back", 3,
        (grad_gate, grad_up, gate_w, up_w, residual, out_grad, gain), [in_vmem] * 7,
        [
            jax.ShapeDtypeStruct(residual.shape, jnp.float32),
            jax.ShapeDtypeStruct((8, width), jnp.float32),
            full,
        ],
        [in_vmem] * 2 + [in_hbm],
        [pltpu.VMEM(residual.shape, jnp.bfloat16)] + gather_sems(seqs) + scatter_scratch(seqs, rows, width),
        110,
    )


class Exchange:
    def __init__(self, axis, source, slots, send_sem, recv_sem):
        self.axis, self.source, self.slots = axis, source, slots
        self.size, self.me = lax.axis_size(axis), lax.axis_index(axis)
        self.send_sem, self.recv_sem = send_sem, recv_sem

    def copy(self, k, owner):
        peer = lax.rem(self.me + k, self.size)
        return pltpu.make_async_remote_copy(
            src_ref=self.source(peer),
            dst_ref=self.slots.at[owner],
            send_sem=self.send_sem.at[k],
            recv_sem=self.recv_sem.at[k],
            device_id={self.axis: peer},
            device_id_type=MESH,
        )

    def start(self):
        for k in range(1, self.size):
            self.copy(k, self.me).start()

    def finish(self):
        for k in range(1, self.size):
            self.copy(k, lax.rem(self.me - k + self.size, self.size)).wait_recv()
        for k in range(1, self.size):
            self.copy(k, self.me).wait_send()

    def total(self):
        total = self.slots[0]
        for k in range(1, self.size):
            total = total + self.slots[k]
        return total


def out_body(seqs, hidden_ref, down_w_ref, residual_ref, layer_out_ref, scatter, first):
    def fill(s):
        scatter.fill(first + s, s, [hidden_ref], [down_w_ref], False)

    def store(s):
        layer_out_ref[s] = (residual_ref[s] + scatter.result(first + s)[...]).astype(jnp.bfloat16)

    return fill, store


def last_body(
    seqs, with_out, branch_ref, feed_ref, branch_w_ref, rec_w_ref, x_ref, grad_ref, gain_ref, gain_two_ref, rec_ref, *refs
):
    if with_out:
        hidden_ref, down_w_ref, residual_ref = refs[:3]
        refs = refs[3:]
    grad_x_ref, rec_sum_ref, gain_sum_ref = refs[:3]
    refs = refs[3:]
    if with_out:
        layer_out_ref = refs[0]
        refs = refs[1:]
    rec_slots, gain_local, gain_part, gain_slots, part_slots = refs[:5]
    rec_sems, gain_sems, part_sems = refs[5:7], refs[7:9], refs[9:11]
    greet_axes(("seq", "grp"))
    rows = x_ref.shape[1]
    scatter = Scatter(rows, *refs[11:])
    rec = Exchange("seq", lambda peer: rec_ref.at[peer], rec_slots, *rec_sems)
    rec.start()
    rec_slots[rec.me] = rec_ref[rec.me]
    fills = [lambda s=s: scatter.fill(s, s, [branch_ref, feed_ref], [branch_w_ref, rec_w_ref], True) for s in range(seqs)]
    stores = []
    if with_out:
        fill, store = out_body(seqs, hidden_ref, down_w_ref, residual_ref, layer_out_ref, scatter, seqs)
        fills += [lambda s=s: fill(s) for s in range(seqs)]
        stores = [lambda s=s: store(s) for s in range(seqs)]
    gain_local[...] = jnp.zeros_like(gain_local)
    gain_local[1:2, :] = gain_two_ref[0:1, :]

    def finish_grad(s):
        term = scatter.result(s)[...]
        inputs = x_ref[s].astype(jnp.float32)
        inverse = lax.rsqrt(mean_of(inputs * inputs) + epsilon)
        normal = inputs * inverse
        gain_local[0:1, :] += jnp.sum(term * normal, axis=0, keepdims=True)
        grad_x_ref[s] = grad_ref[s] + norm_back(term, normal, inverse, gain_ref[...])

    stores = [lambda s=s: finish_grad(s) for s in range(seqs)] + stores
    ahead = seqs
    for p in range(min(ahead, len(fills))):
        fills[p]()
    for p in range(len(fills)):
        for h in range(scatter.chips - 1):
            scatter.hop(p, h)
        if p + ahead < len(fills):
            fills[p + ahead]()
        stores[p]()
        if p == seqs - 1:
            part = gain_part.shape[1]

            def lanes(owner):
                return gain_local.at[:, pl.ds(pl.multiple_of(owner * part, part), part)]

            across = Exchange("seq", lanes, gain_slots, *gain_sems)
            across.start()
            gain_slots[across.me] = lanes(across.me)[...]
    across.finish()
    gain_part[...] = across.total()
    along = Exchange("grp", lambda peer: gain_part, part_slots, *part_sems)
    along.start()
    part_slots[along.me] = gain_part[...]
    rec.finish()
    rec_sum_ref[...] = rec.total()
    along.finish()
    gain_sum_ref[...] = along.total()
    for p in range(len(fills)):
        scatter.finish(p)


def last(grad_branch, grad_feed, branch_w, rec_w, layer_in, grad_residual, gain, gain_two_grad, rec_blocks, out_inputs):
    seqs, rows, width = layer_in.shape
    size, n = lax.axis_size("seq"), lax.axis_size("grp")
    f32 = jnp.float32
    inputs = (grad_branch, grad_feed, branch_w, rec_w, layer_in, grad_residual, gain, gain_two_grad, rec_blocks)
    inputs = inputs + tuple(out_inputs)
    outs = [
        jax.ShapeDtypeStruct(layer_in.shape, f32),
        jax.ShapeDtypeStruct(rec_blocks.shape[1:], f32),
        jax.ShapeDtypeStruct((8, width // size), f32),
    ]
    if out_inputs:
        outs.append(jax.ShapeDtypeStruct(layer_in.shape, jnp.bfloat16))
    return call(
        lambda *refs: last_body(seqs, bool(out_inputs), *refs), "last", 4,
        inputs, [in_vmem] * len(inputs), outs, [in_vmem] * len(outs),
        [
            pltpu.VMEM(rec_blocks.shape, f32),
            pltpu.VMEM((8, width), f32),
            pltpu.VMEM((8, width // size), f32),
            pltpu.VMEM((size, 8, width // size), f32),
            pltpu.VMEM((n, 8, width // size), f32),
        ]
        + [pltpu.SemaphoreType.DMA((size,))] * 4
        + [pltpu.SemaphoreType.DMA((n,))] * 2
        + scatter_scratch(seqs * (2 if out_inputs else 1), rows, width),
        110,
    )


def out_only_body(seqs, hidden_ref, down_w_ref, residual_ref, layer_out_ref, *scratch):
    greet_line()
    scatter = Scatter(residual_ref.shape[1], *scratch)
    fill, store = out_body(seqs, hidden_ref, down_w_ref, residual_ref, layer_out_ref, scatter, 0)
    for s in range(seqs):
        fill(s)
    for s in range(seqs):
        for h in range(scatter.chips - 1):
            scatter.hop(s, h)
        store(s)
    for s in range(seqs):
        scatter.finish(s)


def out_only(hidden, down_w, residual):
    seqs, rows, width = residual.shape
    return call(
        lambda *refs: out_only_body(seqs, *refs), "layer_out", 5,
        (hidden, down_w, residual), [in_vmem] * 3,
        [jax.ShapeDtypeStruct(residual.shape, jnp.bfloat16)], [in_vmem],
        scatter_scratch(seqs, rows, width), 60,
    )[0]


def per_device(
    layer_in, gain_one, w_branch, w_rec, conv_w, conv_b, gate_a_w, gate_a_b, gate_x_w, gate_x_b,
    decay_logit, w_out, gain_two, mlp_gate, mlp_up, mlp_down, out_grad,
):
    seqs_here, positions, model_width = layer_in.shape
    heads_here, tap_count, part_dim = conv_w.shape
    seq_devices, grp_devices = lax.axis_size("seq"), lax.axis_size("grp")
    head_dim = part_dim * seq_devices
    channels = heads_here * head_dim
    f32 = jnp.float32

    own_params = jnp.concatenate(
        [jnp.transpose(conv_w, (0, 2, 1))]
        + [v[:, :, None] for v in (conv_b, gate_a_b, gate_x_b, decay_logit)]
        + [gate_a_w, gate_x_w],
        axis=2,
    ).astype(f32)
    own_gains = jnp.concatenate([gain_one, gain_two]).astype(f32)
    pack = jnp.concatenate(
        [padded_rows(own_params.reshape(1, -1))[0], padded_rows(own_gains.reshape(1, -1))[0]]
    )
    x_full, params, gains = gather_first(layer_in, pack)
    branch_w, rec_w, out_w = gather_rows((w_branch, w_rec, w_out))
    gate_w, up_w, down_w = gather_rows((mlp_gate, mlp_up, mlp_down))

    gains = gains.reshape(grp_devices, seq_devices, -1)[:, :, : own_gains.size]
    gains = jnp.transpose(gains.reshape(grp_devices, seq_devices, 2, -1), (2, 1, 0, 3)).reshape(2, 1, -1)
    params = params.reshape(seq_devices, -1)[:, : own_params.size]
    params = params.reshape((seq_devices,) + own_params.shape)
    params = jnp.transpose(params, (1, 0, 2, 3)).reshape(heads_here, head_dim, -1)
    vectors = params[:, :, : tap_count + 4].reshape(channels, -1).T
    at = tap_count + 4
    diag_a = head_diagonal(params[:, :, at : at + head_dim].astype(jnp.bfloat16))
    diag_x = head_diagonal(params[:, :, at + head_dim :].astype(jnp.bfloat16))
    logit = vectors[tap_count + 3 :]
    softness = jax.nn.softplus(-logit)

    inputs = x_full.astype(f32)
    normal_one = inputs * lax.rsqrt(mean_of(inputs * inputs) + epsilon)
    normed_one = (normal_one * gains[0]).astype(jnp.bfloat16).reshape(-1, model_width)
    branch_pre = matmul(normed_one, branch_w).reshape(seqs_here, -1, channels)
    feed = matmul(normed_one, rec_w).astype(jnp.bfloat16).reshape(seqs_here, -1, channels)
    conv, rate, gate, state, mixed = rec_forward(feed, branch_pre, vectors, softness, diag_a, diag_x)
    residual, normed_two, grad_output = mixer_out(mixed, out_w, layer_in, out_grad, gains[1])
    mixed = mixed.reshape(-1, channels)
    normed_two = normed_two.reshape(-1, model_width)
    grad_output = grad_output.reshape(-1, model_width)
    up_proj = matmul(normed_two, up_w)
    gate_act, gate_pull = jax.vjp(jax.nn.gelu, matmul(normed_two, gate_w))
    hidden = (gate_act * up_proj).astype(jnp.bfloat16)
    grad_down = matmul_tn(hidden, grad_output)
    grad_hidden = matmul_nt(grad_output, down_w)
    grad_gate = gate_pull(grad_hidden * up_proj)[0].astype(jnp.bfloat16)
    grad_up = (grad_hidden * gate_act).astype(jnp.bfloat16)
    mlp_grads = sum_rows((matmul_tn(normed_two, grad_gate), matmul_tn(normed_two, grad_up), grad_down))

    def by_seq(values):
        return values.reshape(seqs_here, -1, values.shape[-1])

    grad_residual, gain_two_grad, residual_low = mlp_back(
        by_seq(grad_gate), by_seq(grad_up), gate_w, up_w, residual, out_grad, gains[1]
    )
    residual_low = residual_low.reshape(-1, model_width)
    out_weight_grad = matmul_tn(mixed, residual_low)
    grad_mixed = by_seq(matmul_nt(residual_low, out_w))
    grad_branch, grad_feed, square_a, square_x, sums = rec_backward(
        grad_mixed, branch_pre, feed, conv, rate, gate, state, vectors, softness, diag_a, diag_x
    )
    vector_grads = jnp.concatenate(
        [sums[: tap_count + 3], 8.0 * jax.nn.sigmoid(-logit) * sums[tap_count + 3 :]]
    )
    rec_grads = jnp.concatenate(
        [
            vector_grads.T.reshape(heads_here, head_dim, -1),
            diagonal_heads(square_a, heads_here),
            diagonal_heads(square_x, heads_here),
        ],
        axis=2,
    )
    rec_grads = rec_grads.reshape(heads_here, seq_devices, part_dim, -1)
    rec_blocks = padded_rows(jnp.transpose(rec_grads, (1, 0, 2, 3)))
    mixer_grads = sum_rows(
        (
            matmul_tn(normed_one, grad_branch.reshape(-1, channels)),
            matmul_tn(normed_one, grad_feed.reshape(-1, channels)),
            out_weight_grad,
        )
    )
    last_inputs = (
        grad_branch, grad_feed, branch_w, rec_w, layer_in, grad_residual, gains[0], gain_two_grad, rec_blocks
    )
    out_inputs = (by_seq(hidden), down_w, residual)
    if grp_devices > 8:
        layer_out = out_only(*out_inputs)
        grad_x, rec_sum, gain_sum = last(*last_inputs, ())
    else:
        grad_x, rec_sum, gain_sum, layer_out = last(*last_inputs, out_inputs)
    rec_sum = rec_sum.reshape(-1)[: own_params.size].reshape(own_params.shape)
    own_part = gain_one.shape[0]
    gain_grads = lax.dynamic_slice_in_dim(gain_sum, lax.axis_index("grp") * own_part, own_part, 1)
    return (
        layer_out,
        grad_x,
        gain_grads[0],
        mixer_grads[0],
        mixer_grads[1],
        jnp.transpose(rec_sum[:, :, :tap_count], (0, 2, 1)),
        rec_sum[:, :, tap_count],
        rec_sum[:, :, at : at + head_dim],
        rec_sum[:, :, tap_count + 1],
        rec_sum[:, :, at + head_dim :],
        rec_sum[:, :, tap_count + 2],
        rec_sum[:, :, tap_count + 3],
        mixer_grads[2],
        gain_grads[1],
        mlp_grads[0],
        mlp_grads[1],
        mlp_grads[2],
    )


def solution(mesh):
    placed = (
        P("seq", "grp", None),
        P(("seq", "grp")),
        P("seq", "grp"),
        P("seq", "grp"),
        P("grp", None, "seq"),
        P("grp", "seq"),
        P("grp", "seq", None),
        P("grp", "seq"),
        P("grp", "seq", None),
        P("grp", "seq"),
        P("grp", "seq"),
        P("grp", "seq"),
        P(("seq", "grp")),
        P("seq", "grp"),
        P("seq", "grp"),
        P("grp", "seq"),
        P("seq", "grp", None),
    )
    return jax.shard_map(
        per_device,
        mesh=mesh,
        in_specs=placed,
        out_specs=(
            P("seq", "grp", None),
            P("seq", "grp", None),
            P(("seq", "grp")),
            P("seq", "grp"),
            P("seq", "grp"),
            P("grp", None, "seq"),
            P("grp", "seq"),
            P("grp", "seq", None),
            P("grp", "seq"),
            P("grp", "seq", None),
            P("grp", "seq"),
            P("grp", "seq"),
            P("grp", "seq"),
            P(("seq", "grp")),
            P("seq", "grp"),
            P("seq", "grp"),
            P("grp", "seq"),
        ),
        check_vma=False,
    )
```

```python
import functools
import math

import jax
import jax.numpy as jnp
from jax import lax
from jax.experimental import pallas as pl
from jax.experimental.pallas import tpu as pltpu
from jax.sharding import PartitionSpec as P

epsilon = 1e-06
gelu_slope = math.sqrt(2.0 / math.pi)
gelu_cubic = 0.044715
MESH = pl.DeviceIdType.MESH


def matmul(left, right):
    return jnp.dot(left, right, preferred_element_type=jnp.float32)


def matmul_tn(left, right):
    return lax.dot_general(
        left, right, (((0,), (0,)), ((), ())), preferred_element_type=jnp.float32
    )


def matmul_nt(left, right):
    return lax.dot_general(
        left, right, (((1,), (1,)), ((), ())), preferred_element_type=jnp.float32
    )


def norm_back(grad_normed, normal_part, inverse, gain):
    scaled = grad_normed * gain
    return inverse * (scaled - normal_part * jnp.mean(scaled * normal_part, axis=-1, keepdims=True))


def low_all(grads):
    return tuple(grad.astype(jnp.bfloat16) for grad in grads)


def sum_slots(grads, slots):
    sums = []
    for grad, slot, axis in zip(grads, slots, weight_axes):
        size = slot.shape[1 + axis]
        own = lax.dynamic_slice_in_dim(grad, lax.axis_index("seq") * size, size, axis)
        for k in range(slot.shape[0]):
            own = own.astype(jnp.float32) + slot[k].astype(jnp.float32)
        sums.append(own)
    return sums


def padded_rows(values):
    flat = values.reshape(values.shape[0], -1)
    flat = jnp.pad(flat, ((0, 0), (0, -flat.shape[1] % 1024)))
    return flat.reshape(values.shape[0], -1, 128)


def head_diagonal(blocks):
    heads, head_dim, _ = blocks.shape
    rows = []
    for h in range(heads):
        row = [jnp.zeros((head_dim, head_dim), blocks.dtype)] * heads
        row[h] = blocks[h]
        rows.append(jnp.concatenate(row, axis=1))
    return jnp.concatenate(rows, axis=0)


def diagonal_heads(square, heads):
    head_dim = square.shape[0] // heads
    return jnp.stack(
        [
            square[h * head_dim : (h + 1) * head_dim, h * head_dim : (h + 1) * head_dim]
            for h in range(heads)
        ]
    )


def pick_rows(seq_len):
    for rows in (128, 96, 64, 32, 16):
        if seq_len % rows == 0:
            return rows
    return seq_len


def gelu_parts(x):
    cubic = gelu_slope * (x + gelu_cubic * x * x * x)
    bend = jnp.tanh(cubic)
    gate = 0.5 * (1.0 + bend)
    slope = gate + 0.5 * x * (1.0 - bend * bend) * gelu_slope * (1.0 + 3.0 * gelu_cubic * x * x)
    return x * gate, slope


def minus_expm1(x):
    series = 1.0 + x * (1.0 / 9.0)
    for k in (8, 7, 6, 5, 4, 3, 2):
        series = 1.0 + x * (1.0 / k) * series
    return jnp.where(x > -0.4, -x * series, 1.0 - jnp.exp(x))


def shift_down(values, by, fill):
    rows = values.shape[0]
    if by % 8 == 0:
        return jnp.concatenate([jnp.full((by, values.shape[1]), fill), values[: rows - by]], axis=0)
    index = lax.broadcasted_iota(jnp.int32, values.shape, 0)
    return jnp.where(index >= by, pltpu.roll(values, by, 0), fill)


def shift_up(values, by, fill):
    rows = values.shape[0]
    if by % 8 == 0:
        return jnp.concatenate([values[by:], jnp.full((by, values.shape[1]), fill)], axis=0)
    index = lax.broadcasted_iota(jnp.int32, values.shape, 0)
    return jnp.where(index < rows - by, pltpu.roll(values, rows - by, 0), fill)


def scan_block(decay, drive, shift):
    by = 1
    while by < decay.shape[0]:
        drive = drive + decay * shift(drive, by, 0.0)
        decay = decay * shift(decay, by, 1.0)
        by *= 2
    return decay, drive


def decay_parts(rate, softness):
    log_decay = -8.0 * rate * softness
    return jnp.exp(log_decay), jnp.sqrt(minus_expm1(2.0 * log_decay))


def rec_forward_body(
    feed_ref, branch_ref, vectors_ref, softness_ref, gate_a_ref, gate_x_ref,
    conv_ref, rate_ref, input_ref, state_ref, mixed_ref, window, carry,
):
    seqs, rows, _ = feed_ref.shape

    @pl.when(pl.program_id(0) == 0)
    def _():
        window[...] = jnp.zeros_like(window)
        carry[...] = jnp.zeros_like(carry)

    softness = softness_ref[...]
    for s in range(seqs):
        window[s, pl.ds(8, rows), :] = feed_ref[s].astype(jnp.float32)
        conv = vectors_ref[4:5, :] + vectors_ref[0:1, :] * window[s, pl.ds(8, rows), :]
        for k in range(1, 4):
            conv = conv + vectors_ref[k : k + 1, :] * window[s, pl.ds(8 - k, rows), :]
        window[s, pl.ds(0, 8), :] = window[s, pl.ds(rows, 8), :]
        conv_low = conv.astype(jnp.bfloat16)
        conv_ref[s] = conv_low
        rate = jax.nn.sigmoid(matmul(conv_low, gate_a_ref[...]) + vectors_ref[5:6, :])
        gate = jax.nn.sigmoid(matmul(conv_low, gate_x_ref[...]) + vectors_ref[6:7, :])
        rate_ref[s] = rate
        input_ref[s] = gate
        decay, scale = decay_parts(rate, softness)
        total, state = scan_block(decay, scale * gate * conv_low.astype(jnp.float32), shift_down)
        state = state + total * carry[s, 0:1, :]
        carry[s, 0:1, :] = state[rows - 1 : rows, :]
        state_ref[s] = state
        gelu_branch = gelu_parts(branch_ref[s])[0]
        mixed_ref[s] = (gelu_branch * state.astype(jnp.bfloat16).astype(jnp.float32)).astype(
            jnp.bfloat16
        )


def rec_backward_body(
    grad_mixed_ref, branch_ref, feed_ref, feed_before_ref, conv_ref, rate_ref, input_ref,
    state_ref, state_before_ref, vectors_ref, softness_ref, gate_a_ref, gate_x_ref,
    grad_branch_ref, grad_feed_ref, grad_a_ref, grad_x_ref, sums_ref, window, later, carry,
):
    seqs, rows, channels = feed_ref.shape
    step = pl.program_id(0)
    first_block = step == pl.num_programs(0) - 1
    before = feed_before_ref.shape[1]

    @pl.when(step == 0)
    def _():
        later[...] = jnp.zeros_like(later)
        carry[...] = jnp.zeros_like(carry)
        grad_a_ref[...] = jnp.zeros_like(grad_a_ref)
        grad_x_ref[...] = jnp.zeros_like(grad_x_ref)
        sums_ref[...] = jnp.zeros_like(sums_ref)

    softness = softness_ref[...]
    keep = jnp.where(first_block, 0.0, 1.0)
    for s in range(seqs):
        gelu_branch, slope = gelu_parts(branch_ref[s])
        grad_mixed = grad_mixed_ref[s]
        state = state_ref[s]
        state_low = state.astype(jnp.bfloat16).astype(jnp.float32)
        grad_state = (grad_mixed * gelu_branch).astype(jnp.bfloat16).astype(jnp.float32)
        grad_branch_ref[s] = (slope * grad_mixed * state_low).astype(jnp.bfloat16)
        rate = rate_ref[s]
        gate = input_ref[s]
        decay, scale = decay_parts(rate, softness)
        total, carried = scan_block(shift_up(decay, 1, 1.0), grad_state, shift_up)
        carried = carried + total * carry[s, 0:1, :]
        carry[s, 0:1, :] = decay[0:1, :] * carried[0:1, :]
        index = lax.broadcasted_iota(jnp.int32, state.shape, 0)
        last = state_before_ref[s][7:8, :] * keep
        previous = jnp.where(index >= 1, pltpu.roll(state, 1, 0), last)
        conv_low = conv_ref[s]
        conv = conv_low.astype(jnp.float32)
        grad_log = carried * previous * decay - carried * gate * conv * decay * decay / scale
        log_rate = grad_log * rate
        pre_a = -8.0 * softness * log_rate * (1.0 - rate)
        pre_x = carried * scale * conv * gate * (1.0 - gate)
        low_a = pre_a.astype(jnp.bfloat16)
        low_x = pre_x.astype(jnp.bfloat16)
        grad_a_ref[...] += matmul_tn(conv_low, low_a)
        grad_x_ref[...] += matmul_tn(conv_low, low_x)
        grad_conv = (
            carried * scale * gate
            + matmul_nt(low_a, gate_a_ref[...])
            + matmul_nt(low_x, gate_x_ref[...])
        )
        window[s, pl.ds(0, 8), :] = feed_before_ref[s].astype(jnp.float32)[before - 8 :, :] * keep
        window[s, pl.ds(8, rows), :] = feed_ref[s].astype(jnp.float32)
        later[s, pl.ds(rows, 8), :] = later[s, pl.ds(0, 8), :]
        later[s, pl.ds(0, rows), :] = grad_conv
        grad_feed = vectors_ref[0:1, :] * grad_conv
        sums_ref[0:1, :] += jnp.sum(grad_conv * window[s, pl.ds(8, rows), :], axis=0, keepdims=True)
        for k in range(1, 4):
            grad_feed = grad_feed + vectors_ref[k : k + 1, :] * later[s, pl.ds(k, rows), :]
            sums_ref[k : k + 1, :] += jnp.sum(
                grad_conv * window[s, pl.ds(8 - k, rows), :], axis=0, keepdims=True
            )
        grad_feed_ref[s] = grad_feed.astype(jnp.bfloat16)
        sums_ref[4:5, :] += jnp.sum(grad_conv, axis=0, keepdims=True)
        sums_ref[5:6, :] += jnp.sum(pre_a, axis=0, keepdims=True)
        sums_ref[6:7, :] += jnp.sum(pre_x, axis=0, keepdims=True)
        sums_ref[7:8, :] += jnp.sum(log_rate, axis=0, keepdims=True)


def whole(shape):
    return pl.BlockSpec(shape, lambda i: (0,) * len(shape))


def rec_forward(feed, branch, vectors, softness, gate_a, gate_x):
    seqs, seq_len, channels = feed.shape
    rows = pick_rows(seq_len)
    block = pl.BlockSpec((seqs, rows, channels), lambda i: (0, i, 0))
    full = jax.ShapeDtypeStruct(feed.shape, jnp.float32)
    low = jax.ShapeDtypeStruct(feed.shape, jnp.bfloat16)
    return pl.pallas_call(
        rec_forward_body,
        grid=(seq_len // rows,),
        in_specs=[block, block]
        + [whole(v.shape) for v in (vectors, softness, gate_a, gate_x)],
        out_specs=[block] * 5,
        out_shape=[low, full, full, full, low],
        scratch_shapes=[
            pltpu.VMEM((seqs, rows + 8, channels), jnp.float32),
            pltpu.VMEM((seqs, 8, channels), jnp.float32),
        ],
        compiler_params=pltpu.CompilerParams(vmem_limit_bytes=40 << 20),
        name="rec_forward",
    )(feed, branch, vectors, softness, gate_a, gate_x)


def rec_backward(grad_mixed, branch, feed, conv, rate, gate, state, vectors, softness, gate_a, gate_x):
    seqs, seq_len, channels = feed.shape
    rows = pick_rows(seq_len)
    blocks = seq_len // rows
    block = pl.BlockSpec((seqs, rows, channels), lambda i: (0, blocks - 1 - i, 0))

    def ahead(by):
        return pl.BlockSpec(
            (seqs, by, channels),
            lambda i: (0, jnp.maximum((blocks - 1 - i) * (rows // by) - 1, 0), 0),
        )

    low = jax.ShapeDtypeStruct(feed.shape, jnp.bfloat16)
    square = jax.ShapeDtypeStruct((channels, channels), jnp.float32)
    return pl.pallas_call(
        rec_backward_body,
        grid=(blocks,),
        in_specs=[block, block, block, ahead(16), block, block, block, block, ahead(8)]
        + [whole(v.shape) for v in (vectors, softness, gate_a, gate_x)],
        out_specs=[block, block, whole((channels, channels)), whole((channels, channels)), whole((8, channels))],
        out_shape=[low, low, square, square, jax.ShapeDtypeStruct((8, channels), jnp.float32)],
        scratch_shapes=[
            pltpu.VMEM((seqs, rows + 8, channels), jnp.float32),
            pltpu.VMEM((seqs, rows + 8, channels), jnp.float32),
            pltpu.VMEM((seqs, 8, channels), jnp.float32),
        ],
        compiler_params=pltpu.CompilerParams(vmem_limit_bytes=40 << 20),
        name="rec_backward",
    )(grad_mixed, branch, feed, feed, conv, rate, gate, state, state, vectors, softness, gate_a, gate_x)


def line_place():
    return lax.axis_size("grp") // 2, lax.axis_index("grp") // 2, lax.axis_index("grp") % 2


def greet_line():
    chips, chip, core = line_place()
    barrier = pltpu.get_barrier_semaphore()

    def signal(place):
        pl.semaphore_signal(barrier, inc=1, device_id={"grp": place}, device_id_type=MESH)

    signal(chip * 2 + 1 - core)

    @pl.when(chip > 0)
    def _():
        signal(chip * 2 + core - 2)

    @pl.when(chip < chips - 1)
    def _():
        signal(chip * 2 + core + 2)

    ends = (chip == 0).astype(jnp.int32) + (chip == chips - 1).astype(jnp.int32)
    pl.semaphore_wait(barrier, 3 - ends)


def greet_axes(axes):
    barrier = pltpu.get_barrier_semaphore()
    for axis in axes:
        size = lax.axis_size(axis)
        for k in range(1, size):
            pl.semaphore_signal(
                barrier,
                inc=1,
                device_id={axis: lax.rem(lax.axis_index(axis) + k, size)},
                device_id_type=MESH,
            )
    pl.semaphore_wait(barrier, sum(lax.axis_size(axis) - 1 for axis in axes))


class Gather:
    def __init__(self, sources, outs, rows, send_sem, recv_sem, own_sem):
        self.chips, self.chip, self.core = line_place()
        self.me = self.chip * 2 + self.core
        self.sources, self.outs, self.rows = sources, outs, rows
        self.send_sem, self.recv_sem, self.own_sem = send_sem, recv_sem, own_sem

    def slot(self, p, origin):
        return self.outs[p].at[pl.ds(pl.multiple_of(origin * self.rows, self.rows), self.rows), :]

    def copy(self, p, source, origin, target, way):
        return pltpu.make_async_remote_copy(
            src_ref=source,
            dst_ref=self.slot(p, origin),
            send_sem=self.send_sem.at[way, p, origin],
            recv_sem=self.recv_sem.at[p, origin],
            device_id={"grp": target},
            device_id_type=MESH,
        )

    def to_right(self, p, source, origin):
        return self.copy(p, source, origin, self.me + 2, 0)

    def to_left(self, p, source, origin):
        return self.copy(p, source, origin, self.me - 2, 1)

    def to_partner(self, p, source, origin):
        return self.copy(p, source, origin, self.chip * 2 + 1 - self.core, 2)

    def own(self, p):
        return pltpu.make_async_copy(self.sources[p], self.slot(p, self.me), self.own_sem.at[p])

    def start(self, p):
        source = self.sources[p]

        @pl.when(self.chip < self.chips - 1)
        def _():
            self.to_right(p, source, self.me).start()

        @pl.when(self.chip > 0)
        def _():
            self.to_left(p, source, self.me).start()

        self.to_partner(p, source, self.me).start()
        self.own(p).start()

    def hop(self, p, h):
        left_origin = self.me - 2 - 2 * h
        right_origin = self.me + 2 + 2 * h

        @pl.when(self.chip - 1 - h >= 0)
        def _():
            here = self.slot(p, left_origin)
            self.to_right(p, here, left_origin).wait_recv()

            @pl.when(self.chip < self.chips - 1)
            def _():
                self.to_right(p, here, left_origin).start()

            self.to_partner(p, here, left_origin).start()

        @pl.when(self.chip + 1 + h <= self.chips - 1)
        def _():
            here = self.slot(p, right_origin)
            self.to_left(p, here, right_origin).wait_recv()

            @pl.when(self.chip > 0)
            def _():
                self.to_left(p, here, right_origin).start()

            self.to_partner(p, here, right_origin).start()

    def finish(self, p):
        for c in range(self.chips):
            origin = c * 2 + 1 - self.core
            self.to_partner(p, self.slot(p, origin), origin).wait_recv()
        self.own(p).wait()
        for c in range(self.chips):
            origin = c * 2 + self.core
            here = self.slot(p, origin)
            self.to_partner(p, here, origin).wait_send()

            @pl.when((c <= self.chip) & (self.chip < self.chips - 1))
            def _():
                self.to_right(p, here, origin).wait_send()

            @pl.when((c >= self.chip) & (self.chip > 0))
            def _():
                self.to_left(p, here, origin).wait_send()


def gather_sems(pieces):
    n = lax.axis_size("grp")
    return [
        pltpu.SemaphoreType.DMA((3, pieces, n)),
        pltpu.SemaphoreType.DMA((pieces, n)),
        pltpu.SemaphoreType.DMA((pieces,)),
    ]


class Scatter:
    def __init__(self, rows, part, out, swap_in, line_in, send_sem, recv_sem):
        self.chips, self.chip, self.core = line_place()
        self.me = self.chip * 2 + self.core
        self.rows, self.part, self.out = rows, part, out
        self.swap_in, self.line_in = swap_in, line_in
        self.send_sem, self.recv_sem = send_sem, recv_sem

    def copy(self, dest, place, way, slot, p):
        return pltpu.make_async_remote_copy(
            src_ref=self.out.at[p, slot],
            dst_ref=dest,
            send_sem=self.send_sem.at[way, p, slot],
            recv_sem=self.recv_sem.at[way, p, slot],
            device_id={"grp": place},
            device_id_type=MESH,
        )

    def swap(self, p, c):
        return self.copy(self.swap_in.at[p, c], self.chip * 2 + 1 - self.core, 0, c, p)

    def right(self, p, c):
        return self.copy(self.line_in.at[p, c], self.me + 2, 1, c, p)

    def left(self, p, c):
        slot = jnp.where(c == self.chip - 1, self.chips, c)
        return self.copy(self.line_in.at[p, slot], self.me - 2, 2, c, p)

    def from_right(self, p, c):
        slot = jnp.where(c == self.chip, self.chips, c)
        return self.copy(self.line_in.at[p, slot], self.me + 2, 2, c, p)

    def fill(self, p, s, lefts, rights, transposed, width=512):
        def rows_of(ref, core):
            at = [pl.multiple_of((c * 2 + core) * self.rows, self.rows) for c in range(self.chips)]
            return jnp.concatenate([ref[s, pl.ds(a, self.rows), :] for a in at], axis=0)

        def product(core, store):
            chosen = [rows_of(ref, core) for ref in lefts]

            @pl.loop(0, self.out.shape[-1] // width)
            def _(j):
                columns = pl.ds(pl.multiple_of(j * width, width), width)
                total = None
                for left, right in zip(chosen, rights):
                    term = matmul_nt(left, right[columns, :]) if transposed else matmul(left, right[:, columns])
                    total = term if total is None else total + term
                for c in range(self.chips):
                    store(c, columns, total[c * self.rows : (c + 1) * self.rows])

        def to_out(c, columns, value):
            self.out[p, c, :, columns] = value.astype(jnp.bfloat16)

        def to_part(c, columns, value):
            self.part[p, c, :, columns] = value

        product(1 - self.core, to_out)
        for c in range(self.chips):
            self.swap(p, c).start()
        product(self.core, to_part)

    def own(self, p, c):
        self.swap(p, c).wait_recv()
        return self.part[p, c] + self.swap_in[p, c].astype(jnp.float32)

    def hop(self, p, t):
        last = self.chips - 1

        def send(c, first, arrival, onward):
            self.swap(p, c).wait_send()
            total = self.own(p, c)

            @pl.when(first)
            def _():
                self.out[p, c] = total.astype(jnp.bfloat16)

            @pl.when(jnp.logical_not(first))
            def _():
                arrival(p, c).wait_recv()
                self.out[p, c] = (total + self.line_in[p, c].astype(jnp.float32)).astype(jnp.bfloat16)

            onward(p, c).start()

        @pl.when(self.chip <= t)
        def _():
            send(last - t + self.chip, self.chip == 0, self.right, self.right)

        @pl.when(last - self.chip <= t)
        def _():
            send(t - last + self.chip, self.chip == last, self.from_right, self.left)

    def result(self, p):
        chip = self.chip
        self.part[p, chip] = self.own(p, chip)

        @pl.when(chip > 0)
        def _():
            self.right(p, chip).wait_recv()
            self.part[p, chip] += self.line_in[p, chip].astype(jnp.float32)

        @pl.when(chip < self.chips - 1)
        def _():
            self.from_right(p, chip).wait_recv()
            self.part[p, chip] += self.line_in[p, self.chips].astype(jnp.float32)

        return self.part.at[p, chip]

    def finish(self, p):
        self.swap(p, self.chip).wait_send()
        for c in range(self.chips):

            @pl.when(c > self.chip)
            def _():
                self.right(p, c).wait_send()

            @pl.when(c < self.chip)
            def _():
                self.left(p, c).wait_send()


def scatter_scratch(pieces, rows, width):
    chips = lax.axis_size("grp") // 2
    return [
        pltpu.VMEM((pieces, chips, rows, width), jnp.float32),
        pltpu.VMEM((pieces, chips, rows, width), jnp.bfloat16),
        pltpu.VMEM((pieces, chips, rows, width), jnp.bfloat16),
        pltpu.VMEM((pieces, chips + 1, rows, width), jnp.bfloat16),
        pltpu.SemaphoreType.DMA((3, pieces, chips)),
        pltpu.SemaphoreType.DMA((3, pieces, chips)),
    ]


in_vmem = pl.BlockSpec(memory_space=pltpu.VMEM)
in_hbm = pl.BlockSpec(memory_space=pl.ANY)


def call(body, name, number, inputs, in_specs, outs, out_specs, scratch, us):
    return pl.pallas_call(
        body,
        in_specs=in_specs,
        out_specs=out_specs,
        out_shape=outs,
        scratch_shapes=scratch,
        name=name,
        cost_estimate=pl.CostEstimate(
            flops=us * 1000000000, bytes_accessed=us * 3000000, transcendentals=0
        ),
        compiler_params=pltpu.CompilerParams(
            collective_id=number, has_side_effects=True, vmem_limit_bytes=60 << 20
        ),
    )(*inputs)


class Exchange:
    def __init__(self, axis, source, slot, send_sem, recv_sem, steps=None):
        self.axis, self.source, self.slot, self.steps = axis, source, slot, steps
        self.size, self.me = lax.axis_size(axis), lax.axis_index(axis)
        self.send_sem, self.recv_sem = send_sem, recv_sem

    def copy(self, k, owner):
        peer = lax.rem(self.me + k, self.size)
        return pltpu.make_async_remote_copy(
            src_ref=self.source(peer),
            dst_ref=self.slot(owner) if self.slot else self.steps.at[k - 1],
            send_sem=self.send_sem.at[k],
            recv_sem=self.recv_sem.at[k],
            device_id={self.axis: peer},
            device_id_type=MESH,
        )

    def own(self):
        return pltpu.make_async_copy(self.source(self.me), self.slot(self.me), self.send_sem.at[0])

    def start(self):
        self.own().start()
        self.start_others()

    def start_others(self):
        for k in range(1, self.size):
            self.copy(k, self.me).start()

    def finish(self):
        self.own().wait()
        self.finish_others()

    def finish_others(self):
        for k in range(1, self.size):
            self.copy(k, lax.rem(self.me - k + self.size, self.size)).wait_recv()
        for k in range(1, self.size):
            self.copy(k, self.me).wait_send()


def sum_of(slots):
    total = slots[0]
    for k in range(1, slots.shape[0]):
        total = total + slots[k]
    return total


def block(ref, axis, parts):
    size = ref.shape[axis] // parts

    def view(k):
        at = pl.ds(pl.multiple_of(k * size, size), size)
        return ref.at[at, :] if axis == 0 else ref.at[:, at]

    return view


def weight_gathers(axes, sources, outs, send_sem, recv_sem):
    parts = lax.axis_size("seq")
    return [
        Exchange(
            "seq", lambda k, ref=source: ref, block(out, axis, parts), send_sem.at[i], recv_sem.at[i]
        )
        for i, (axis, source, out) in enumerate(zip(axes, sources, outs))
    ]


def weight_sums(axes, sources, outs, send_sem, recv_sem):
    parts = lax.axis_size("seq")
    return [
        Exchange(
            "seq", block(source, axis, parts), None, send_sem.at[i], recv_sem.at[i], out
        )
        for i, (axis, source, out) in enumerate(zip(axes, sources, outs))
    ]


def seq_sems(count):
    return [pltpu.SemaphoreType.DMA((count, lax.axis_size("seq")))] * 2


def gathered(block_of, axis):
    shape = list(block_of.shape)
    shape[axis] *= lax.axis_size("seq")
    return jax.ShapeDtypeStruct(shape, block_of.dtype)


def slots_of(matrix, axis):
    shape = list(matrix.shape)
    size = lax.axis_size("seq")
    shape[axis] //= size
    return jax.ShapeDtypeStruct((size - 1, *shape), matrix.dtype)


weight_axes = (0, 0, 1)


def views(ref):
    return [ref.at[s] for s in range(ref.shape[0])]


def first_body(x_ref, grad_ref, pack_ref, w0, w1, w2, later_ref, full_ref, params_ref, gains_ref, o0, o1, o2, *refs):
    small_send, small_recv, gain_send, gain_recv, weight_send, weight_recv = refs[3:]
    greet_axes(("seq", "grp"))
    seqs = x_ref.shape[0]
    gather = Gather(views(x_ref), views(full_ref), x_ref.shape[1], *refs[:3])
    weights = weight_gathers(weight_axes, (w0, w1, w2), (o0, o1, o2), weight_send, weight_recv)
    small = Exchange("seq", lambda k: pack_ref, lambda k: params_ref.at[k], small_send, small_recv)
    small.start()
    for s in range(seqs):
        gather.start(s)
    for weight in weights:
        weight.start()
    later_ref[...] = grad_ref[...]
    small.finish()
    place = lax.axis_index("grp")
    for owner in range(small.size):
        gains_ref[place, owner] = params_ref[owner, pl.ds(pack_ref.shape[0] - 8, 8), :]
    gains = Exchange("grp", lambda k: gains_ref.at[place], lambda k: gains_ref.at[k], gain_send, gain_recv)
    gains.start_others()
    for h in range(gather.chips - 1):
        for s in range(seqs):
            gather.hop(s, h)
    gains.finish_others()
    for weight in weights:
        weight.finish()
    for s in range(seqs):
        gather.finish(s)


def gather_first(layer_in, out_grad, pack, weights):
    seqs, rows, width = layer_in.shape
    n, size = lax.axis_size("grp"), lax.axis_size("seq")
    return call(
        first_body, "gather_first", 1,
        (layer_in, out_grad, pack, *weights), [in_vmem] * 6,
        [
            jax.ShapeDtypeStruct(out_grad.shape, out_grad.dtype),
            jax.ShapeDtypeStruct((seqs, n * rows, width), jnp.bfloat16),
            jax.ShapeDtypeStruct((size,) + pack.shape, jnp.float32),
            jax.ShapeDtypeStruct((n, size, 8, 128), jnp.float32),
        ]
        + [gathered(w, axis) for w, axis in zip(weights, weight_axes)],
        [in_vmem, in_hbm] + [in_vmem] * 2 + [in_hbm] * 3,
        gather_sems(seqs)
        + [pltpu.SemaphoreType.DMA((size,))] * 2
        + [pltpu.SemaphoreType.DMA((n,))] * 2
        + seq_sems(3),
        70,
    )


def mean_of(values):
    return jnp.mean(values, axis=-1, keepdims=True)


def sum_then_gather(scatter, gather, fills, stores):
    hops = range(1, scatter.chips - 1)
    fills[0]()
    scatter.hop(0, 0)
    for p, store in enumerate(stores):
        if p + 1 < len(fills):
            fills[p + 1]()
        for h in hops:
            scatter.hop(p, h)
            if gather and p:
                gather.hop(p - 1, h - 1)
        if p + 1 < len(fills):
            scatter.hop(p + 1, 0)
        store()
        if gather:
            gather.start(p)
            if p:
                gather.hop(p - 1, gather.chips - 2)
    if gather:
        for h in range(gather.chips - 1):
            gather.hop(len(stores) - 1, h)
        for p in range(len(stores)):
            gather.finish(p)
    for p in range(len(fills)):
        scatter.finish(p)


def mixer_out_body(mixed_ref, out_w_ref, x_ref, gain_ref, w0, w1, w2, residual_ref, normed_ref, o0, o1, o2, low_ref, *refs):
    greet_axes(("seq", "grp"))
    seqs, rows, _ = x_ref.shape
    weights = weight_gathers(weight_axes, (w0, w1, w2), (o0, o1, o2), *refs[:2])
    for weight in weights:
        weight.start()
    gather = Gather(views(low_ref), views(normed_ref), rows, *refs[2:5])
    scatter = Scatter(rows, *refs[5:])

    def fill(s):
        scatter.fill(s, s, [mixed_ref], [out_w_ref], False)

    def store(s):
        residual = x_ref[s].astype(jnp.float32) + scatter.result(s)[...]
        residual_ref[s] = residual
        normal = residual * lax.rsqrt(mean_of(residual * residual) + epsilon)
        low_ref[s] = (normal * gain_ref[...]).astype(jnp.bfloat16)

    sum_then_gather(
        scatter, gather, [functools.partial(fill, s) for s in range(seqs)], [functools.partial(store, s) for s in range(seqs)]
    )
    for weight in weights:
        weight.finish()


def mixer_out(mixed, out_w, layer_in, gain, weights):
    seqs, rows, width = layer_in.shape
    full = jax.ShapeDtypeStruct((seqs, lax.axis_size("grp") * rows, width), jnp.bfloat16)
    return call(
        mixer_out_body, "mixer_out", 2,
        (mixed, out_w, layer_in, gain, *weights), [in_vmem] * 7,
        [jax.ShapeDtypeStruct(layer_in.shape, jnp.float32), full]
        + [gathered(w, axis) for w, axis in zip(weights, weight_axes)],
        [in_vmem] + [in_hbm] * 4,
        [pltpu.VMEM(layer_in.shape, jnp.bfloat16)]
        + seq_sems(3)
        + gather_sems(seqs)
        + scatter_scratch(seqs, rows, width),
        100,
    )


def mlp_back_body(
    gate_ref, up_ref, gate_w_ref, up_w_ref, residual_ref, grad_ref, gain_ref, w0, w1, w2,
    grad_residual_ref, gain_grad_ref, full_ref, o0, o1, o2, low_ref, *refs,
):
    greet_axes(("seq", "grp"))
    seqs, rows, _ = grad_ref.shape
    sums = weight_sums(weight_axes, (w0, w1, w2), (o0, o1, o2), *refs[:2])
    for weight in sums:
        weight.start_others()
    gather = Gather(views(low_ref), views(full_ref), rows, *refs[2:5])
    scatter = Scatter(rows, *refs[5:])
    gain_grad_ref[...] = jnp.zeros_like(gain_grad_ref)

    def fill(s):
        scatter.fill(s, s, [gate_ref, up_ref], [gate_w_ref, up_w_ref], True)

    def store(s):
        term = scatter.result(s)[...]
        residual = residual_ref[s]
        inverse = lax.rsqrt(mean_of(residual * residual) + epsilon)
        normal = residual * inverse
        gain_grad_ref[0:1, :] += jnp.sum(term * normal, axis=0, keepdims=True)
        grad = grad_ref[s].astype(jnp.float32) + norm_back(term, normal, inverse, gain_ref[...])
        grad_residual_ref[s] = grad
        low_ref[s] = grad.astype(jnp.bfloat16)

    sum_then_gather(
        scatter, gather, [functools.partial(fill, s) for s in range(seqs)], [functools.partial(store, s) for s in range(seqs)]
    )
    for weight in sums:
        weight.finish_others()


def mlp_back(grad_gate, grad_up, gate_w, up_w, residual, out_grad, gain, grads):
    seqs, rows, width = residual.shape
    return call(
        mlp_back_body, "mlp_back", 3,
        (grad_gate, grad_up, gate_w, up_w, residual, out_grad, gain, *grads), [in_vmem] * 7 + [in_hbm] * 3,
        [
            jax.ShapeDtypeStruct(residual.shape, jnp.float32),
            jax.ShapeDtypeStruct((8, width), jnp.float32),
            jax.ShapeDtypeStruct((seqs, lax.axis_size("grp") * rows, width), jnp.bfloat16),
        ]
        + [slots_of(grad, axis) for grad, axis in zip(grads, weight_axes)],
        [in_vmem] * 2 + [in_hbm] * 4,
        [pltpu.VMEM(residual.shape, jnp.bfloat16)]
        + seq_sems(3)
        + gather_sems(seqs)
        + scatter_scratch(seqs, rows, width),
        110,
    )


def out_body(hidden_ref, down_w_ref, residual_ref, layer_out_ref, scatter, first):
    def fill(s):
        scatter.fill(first + s, s, [hidden_ref], [down_w_ref], False)

    def store(s):
        layer_out_ref[s] = (residual_ref[s] + scatter.result(first + s)[...]).astype(jnp.bfloat16)

    return fill, store


def last_body(
    with_out, branch_ref, feed_ref, branch_w_ref, rec_w_ref, x_ref, grad_ref, gain_ref, gain_two_ref, rec_ref,
    w0, w1, w2, *refs,
):
    if with_out:
        hidden_ref, down_w_ref, residual_ref = refs[:3]
        refs = refs[3:]
    grad_x_ref, rec_sum_ref, gain_sum_ref, o0, o1, o2 = refs[:6]
    refs = refs[6:]
    if with_out:
        layer_out_ref = refs[0]
        refs = refs[1:]
    rec_slots, gain_local, gain_part, gain_slots, part_slots = refs[:5]
    rec_sems, gain_sems, part_sems = refs[5:7], refs[7:9], refs[9:11]
    greet_axes(("seq", "grp"))
    seqs, rows, _ = x_ref.shape
    sums = weight_sums(weight_axes, (w0, w1, w2), (o0, o1, o2), *refs[11:13])
    scatter = Scatter(rows, *refs[13:])
    rec = Exchange("seq", lambda k: rec_ref.at[k], lambda k: rec_slots.at[k], *rec_sems)
    rec.start()
    for weight in sums:
        weight.start_others()
    gain_local[...] = jnp.zeros_like(gain_local)
    gain_local[1:2, :] = gain_two_ref[0:1, :]

    def fill(s):
        scatter.fill(s, s, [branch_ref, feed_ref], [branch_w_ref, rec_w_ref], True)

    across = Exchange(
        "seq", block(gain_local, 1, lax.axis_size("seq")), lambda k: gain_slots.at[k], *gain_sems
    )

    def store(s):
        term = scatter.result(s)[...]
        inputs = x_ref[s].astype(jnp.float32)
        inverse = lax.rsqrt(mean_of(inputs * inputs) + epsilon)
        normal = inputs * inverse
        gain_local[0:1, :] += jnp.sum(term * normal, axis=0, keepdims=True)
        if s == seqs - 1:
            across.start()
        grad_x_ref[s] = grad_ref[s] + norm_back(term, normal, inverse, gain_ref[...])

    fills = [functools.partial(fill, s) for s in range(seqs)]
    stores = [functools.partial(store, s) for s in range(seqs)]
    if with_out:
        fill_out, store_out = out_body(hidden_ref, down_w_ref, residual_ref, layer_out_ref, scatter, seqs)
        fills += [functools.partial(fill_out, s) for s in range(seqs)]
        stores += [functools.partial(store_out, s) for s in range(seqs)]
    sum_then_gather(scatter, None, fills, stores)
    across.finish()
    gain_part[...] = sum_of(gain_slots)
    along = Exchange("grp", lambda k: gain_part, lambda k: part_slots.at[k], *part_sems)
    along.start()
    rec.finish()
    rec_sum_ref[...] = sum_of(rec_slots)
    for weight in sums:
        weight.finish_others()
    along.finish()
    gain_sum_ref[...] = sum_of(part_slots)


def last(grad_branch, grad_feed, branch_w, rec_w, layer_in, grad_residual, gain, gain_two_grad, rec_blocks, grads, out_inputs):
    seqs, rows, width = layer_in.shape
    size, n = lax.axis_size("seq"), lax.axis_size("grp")
    f32 = jnp.float32
    inputs = (grad_branch, grad_feed, branch_w, rec_w, layer_in, grad_residual, gain, gain_two_grad, rec_blocks)
    outs = [
        jax.ShapeDtypeStruct(layer_in.shape, f32),
        jax.ShapeDtypeStruct(rec_blocks.shape[1:], f32),
        jax.ShapeDtypeStruct((8, width // size), f32),
    ]
    outs += [slots_of(grad, axis) for grad, axis in zip(grads, weight_axes)]
    out_specs = [in_vmem] * 3 + [in_hbm] * 3
    if out_inputs:
        outs.append(jax.ShapeDtypeStruct(layer_in.shape, jnp.bfloat16))
        out_specs.append(in_vmem)
    return call(
        functools.partial(last_body, bool(out_inputs)), "last", 4,
        inputs + tuple(grads) + tuple(out_inputs),
        [in_vmem] * len(inputs) + [in_hbm] * 3 + [in_vmem] * len(out_inputs),
        outs, out_specs,
        [
            pltpu.VMEM(rec_blocks.shape, f32),
            pltpu.VMEM((8, width), f32),
            pltpu.VMEM((8, width // size), f32),
            pltpu.VMEM((size, 8, width // size), f32),
            pltpu.VMEM((n, 8, width // size), f32),
        ]
        + [pltpu.SemaphoreType.DMA((size,))] * 4
        + [pltpu.SemaphoreType.DMA((n,))] * 2
        + seq_sems(3)
        + scatter_scratch(seqs * (2 if out_inputs else 1), rows, width),
        110,
    )


def out_only_body(hidden_ref, down_w_ref, residual_ref, layer_out_ref, *scratch):
    greet_line()
    scatter = Scatter(residual_ref.shape[1], *scratch)
    fill, store = out_body(hidden_ref, down_w_ref, residual_ref, layer_out_ref, scatter, 0)
    seqs = range(residual_ref.shape[0])
    sum_then_gather(
        scatter, None, [functools.partial(fill, s) for s in seqs], [functools.partial(store, s) for s in seqs]
    )


def out_only(hidden, down_w, residual):
    seqs, rows, width = residual.shape
    return call(
        out_only_body, "layer_out", 5,
        (hidden, down_w, residual), [in_vmem] * 3,
        [jax.ShapeDtypeStruct(residual.shape, jnp.bfloat16)], [in_vmem],
        scatter_scratch(seqs, rows, width), 60,
    )[0]


def per_device(
    layer_in, gain_one, w_branch, w_rec, conv_w, conv_b, gate_a_w, gate_a_b, gate_x_w, gate_x_b,
    decay_logit, w_out, gain_two, mlp_gate, mlp_up, mlp_down, out_grad,
):
    seqs_here, positions, model_width = layer_in.shape
    heads_here, tap_count, part_dim = conv_w.shape
    seq_devices, grp_devices = lax.axis_size("seq"), lax.axis_size("grp")
    head_dim = part_dim * seq_devices
    channels = heads_here * head_dim
    f32 = jnp.float32

    own_params = jnp.concatenate(
        [jnp.transpose(conv_w, (0, 2, 1))]
        + [v[:, :, None] for v in (conv_b, gate_a_b, gate_x_b, decay_logit)]
        + [gate_a_w, gate_x_w],
        axis=2,
    ).astype(f32)
    own_gains = jnp.concatenate([gain_one, gain_two]).astype(f32)
    pack = jnp.concatenate(
        [padded_rows(own_params.reshape(1, -1))[0], padded_rows(own_gains.reshape(1, -1))[0]]
    )
    late_grad, x_full, params, gains, branch_w, rec_w, out_w = gather_first(
        layer_in, out_grad, pack, (w_branch, w_rec, w_out)
    )
    grad_output = jnp.concatenate(
        [lax.all_gather(late_grad[s], "grp", axis=0, tiled=True) for s in range(seqs_here)]
    )

    gains = gains.reshape(grp_devices, seq_devices, -1)[:, :, : own_gains.size]
    gains = jnp.transpose(gains.reshape(grp_devices, seq_devices, 2, -1), (2, 1, 0, 3)).reshape(2, 1, -1)
    params = params.reshape(seq_devices, -1)[:, : own_params.size]
    params = params.reshape((seq_devices,) + own_params.shape)
    params = jnp.transpose(params, (1, 0, 2, 3)).reshape(heads_here, head_dim, -1)
    vectors = params[:, :, : tap_count + 4].reshape(channels, -1).T
    at = tap_count + 4
    diag_a = head_diagonal(params[:, :, at : at + head_dim].astype(jnp.bfloat16))
    diag_x = head_diagonal(params[:, :, at + head_dim :].astype(jnp.bfloat16))
    logit = vectors[tap_count + 3 :]
    softness = jax.nn.softplus(-logit)

    inputs = x_full.astype(f32)
    normal_one = inputs * lax.rsqrt(mean_of(inputs * inputs) + epsilon)
    normed_one = (normal_one * gains[0]).astype(jnp.bfloat16).reshape(-1, model_width)
    branch_pre = matmul(normed_one, branch_w).reshape(seqs_here, -1, channels)
    feed = matmul(normed_one, rec_w).astype(jnp.bfloat16).reshape(seqs_here, -1, channels)
    conv, rate, gate, state, mixed = rec_forward(feed, branch_pre, vectors, softness, diag_a, diag_x)
    residual, normed_two, gate_w, up_w, down_w = mixer_out(
        mixed, out_w, layer_in, gains[1], (mlp_gate, mlp_up, mlp_down)
    )
    mixed = mixed.reshape(-1, channels)
    normed_two = normed_two.reshape(-1, model_width)
    up_proj = matmul(normed_two, up_w)
    gate_act, gate_pull = jax.vjp(jax.nn.gelu, matmul(normed_two, gate_w))
    hidden = (gate_act * up_proj).astype(jnp.bfloat16)
    grad_hidden = matmul_nt(grad_output, down_w)
    grad_gate = gate_pull(grad_hidden * up_proj)[0].astype(jnp.bfloat16)
    grad_up = (grad_hidden * gate_act).astype(jnp.bfloat16)
    mlp_grads = low_all(
        (matmul_tn(normed_two, grad_gate), matmul_tn(normed_two, grad_up), matmul_tn(hidden, grad_output))
    )

    def by_seq(values):
        return values.reshape(seqs_here, -1, values.shape[-1])

    grad_residual, gain_two_grad, residual_low, *mlp_slots = mlp_back(
        by_seq(grad_gate), by_seq(grad_up), gate_w, up_w, residual, out_grad, gains[1], mlp_grads
    )
    mlp_grads = sum_slots(mlp_grads, mlp_slots)
    residual_low = residual_low.reshape(-1, model_width)
    out_weight_grad = matmul_tn(mixed, residual_low)
    grad_mixed = by_seq(matmul_nt(residual_low, out_w))
    grad_branch, grad_feed, square_a, square_x, sums = rec_backward(
        grad_mixed, branch_pre, feed, conv, rate, gate, state, vectors, softness, diag_a, diag_x
    )
    vector_grads = jnp.concatenate(
        [sums[: tap_count + 3], 8.0 * jax.nn.sigmoid(-logit) * sums[tap_count + 3 :]]
    )
    rec_grads = jnp.concatenate(
        [
            vector_grads.T.reshape(heads_here, head_dim, -1),
            diagonal_heads(square_a, heads_here),
            diagonal_heads(square_x, heads_here),
        ],
        axis=2,
    )
    rec_grads = rec_grads.reshape(heads_here, seq_devices, part_dim, -1)
    rec_blocks = padded_rows(jnp.transpose(rec_grads, (1, 0, 2, 3)))
    mixer_grads = low_all(
        (
            matmul_tn(normed_one, grad_branch.reshape(-1, channels)),
            matmul_tn(normed_one, grad_feed.reshape(-1, channels)),
            out_weight_grad,
        )
    )
    last_inputs = (
        grad_branch, grad_feed, branch_w, rec_w, layer_in, grad_residual, gains[0], gain_two_grad, rec_blocks,
        mixer_grads,
    )
    out_inputs = (by_seq(hidden), down_w, residual)
    if grp_devices > 8:
        layer_out = out_only(*out_inputs)
        grad_x, rec_sum, gain_sum, *mixer_slots = last(*last_inputs, ())
    else:
        grad_x, rec_sum, gain_sum, *mixer_slots, layer_out = last(*last_inputs, out_inputs)
    mixer_grads = sum_slots(mixer_grads, mixer_slots)
    rec_sum = rec_sum.reshape(-1)[: own_params.size].reshape(own_params.shape)
    own_part = gain_one.shape[0]
    gain_grads = lax.dynamic_slice_in_dim(gain_sum, lax.axis_index("grp") * own_part, own_part, 1)
    return (
        layer_out,
        grad_x,
        gain_grads[0],
        mixer_grads[0],
        mixer_grads[1],
        jnp.transpose(rec_sum[:, :, :tap_count], (0, 2, 1)),
        rec_sum[:, :, tap_count],
        rec_sum[:, :, at : at + head_dim],
        rec_sum[:, :, tap_count + 1],
        rec_sum[:, :, at + head_dim :],
        rec_sum[:, :, tap_count + 2],
        rec_sum[:, :, tap_count + 3],
        mixer_grads[2],
        gain_grads[1],
        mlp_grads[0],
        mlp_grads[1],
        mlp_grads[2],
    )


def solution(mesh):
    placed = (
        P("seq", "grp", None),
        P(("seq", "grp")),
        P("seq", "grp"),
        P("seq", "grp"),
        P("grp", None, "seq"),
        P("grp", "seq"),
        P("grp", "seq", None),
        P("grp", "seq"),
        P("grp", "seq", None),
        P("grp", "seq"),
        P("grp", "seq"),
        P("grp", "seq"),
        P(("seq", "grp")),
        P("seq", "grp"),
        P("seq", "grp"),
        P("grp", "seq"),
        P("seq", "grp", None),
    )
    return jax.shard_map(
        per_device,
        mesh=mesh,
        in_specs=placed,
        out_specs=(
            P("seq", "grp", None),
            P("seq", "grp", None),
            P(("seq", "grp")),
            P("seq", "grp"),
            P("seq", "grp"),
            P("grp", None, "seq"),
            P("grp", "seq"),
            P("grp", "seq", None),
            P("grp", "seq"),
            P("grp", "seq", None),
            P("grp", "seq"),
            P("grp", "seq"),
            P("grp", "seq"),
            P(("seq", "grp")),
            P("seq", "grp"),
            P("seq", "grp"),
            P("grp", "seq"),
        ),
        check_vma=False,
    )
```

```python
import functools
import math

import jax
import jax.numpy as jnp
from jax import lax
from jax.experimental import pallas as pl
from jax.experimental.pallas import tpu as pltpu
from jax.sharding import PartitionSpec as P

epsilon = 1e-06
gelu_slope = math.sqrt(2.0 / math.pi)
gelu_cubic = 0.044715
MESH = pl.DeviceIdType.MESH


def matmul(left, right):
    return jnp.dot(left, right, preferred_element_type=jnp.float32)


def matmul_tn(left, right):
    return lax.dot_general(
        left, right, (((0,), (0,)), ((), ())), preferred_element_type=jnp.float32
    )


def matmul_nt(left, right):
    return lax.dot_general(
        left, right, (((1,), (1,)), ((), ())), preferred_element_type=jnp.float32
    )


def norm_back(grad_normed, normal_part, inverse, gain):
    scaled = grad_normed * gain
    return inverse * (scaled - normal_part * jnp.mean(scaled * normal_part, axis=-1, keepdims=True))


def low_all(grads):
    return tuple(grad.astype(jnp.bfloat16) for grad in grads)


def sum_slots(grads, slots):
    sums = []
    for grad, slot, axis in zip(grads, slots, weight_axes):
        size = slot.shape[1 + axis]
        own = lax.dynamic_slice_in_dim(grad, lax.axis_index("seq") * size, size, axis)
        for k in range(slot.shape[0]):
            own = own.astype(jnp.float32) + slot[k].astype(jnp.float32)
        sums.append(own)
    return sums


def padded_rows(values):
    flat = values.reshape(values.shape[0], -1)
    flat = jnp.pad(flat, ((0, 0), (0, -flat.shape[1] % 1024)))
    return flat.reshape(values.shape[0], -1, 128)


def head_diagonal(blocks):
    heads, head_dim, _ = blocks.shape
    rows = []
    for h in range(heads):
        row = [jnp.zeros((head_dim, head_dim), blocks.dtype)] * heads
        row[h] = blocks[h]
        rows.append(jnp.concatenate(row, axis=1))
    return jnp.concatenate(rows, axis=0)


def diagonal_heads(square, heads):
    head_dim = square.shape[0] // heads
    return jnp.stack(
        [
            square[h * head_dim : (h + 1) * head_dim, h * head_dim : (h + 1) * head_dim]
            for h in range(heads)
        ]
    )


def pick_rows(seq_len, choices=(128, 96, 64, 32, 16)):
    for rows in choices:
        if seq_len % rows == 0:
            return rows
    return seq_len


def gelu_parts(x):
    cubic = gelu_slope * (x + gelu_cubic * x * x * x)
    bend = jnp.tanh(cubic)
    gate = 0.5 * (1.0 + bend)
    slope = gate + 0.5 * x * (1.0 - bend * bend) * gelu_slope * (1.0 + 3.0 * gelu_cubic * x * x)
    return x * gate, slope


def minus_expm1(x):
    series = 1.0 + x * (1.0 / 9.0)
    for k in (8, 7, 6, 5, 4, 3, 2):
        series = 1.0 + x * (1.0 / k) * series
    return jnp.where(x > -0.4, -x * series, 1.0 - jnp.exp(x))


def shift_down(values, by, fill):
    rows = values.shape[0]
    if by % 8 == 0:
        return jnp.concatenate([jnp.full((by, values.shape[1]), fill), values[: rows - by]], axis=0)
    index = lax.broadcasted_iota(jnp.int32, values.shape, 0)
    return jnp.where(index >= by, pltpu.roll(values, by, 0), fill)


def shift_up(values, by, fill):
    rows = values.shape[0]
    if by % 8 == 0:
        return jnp.concatenate([values[by:], jnp.full((by, values.shape[1]), fill)], axis=0)
    index = lax.broadcasted_iota(jnp.int32, values.shape, 0)
    return jnp.where(index < rows - by, pltpu.roll(values, rows - by, 0), fill)


def scan_block(decay, drive, shift):
    by = 1
    while by < decay.shape[0]:
        drive = drive + decay * shift(drive, by, 0.0)
        decay = decay * shift(decay, by, 1.0)
        by *= 2
    return decay, drive


def decay_parts(rate, softness):
    log_decay = -8.0 * rate * softness
    return jnp.exp(log_decay), jnp.sqrt(minus_expm1(2.0 * log_decay))


def rec_forward_rows(feed, branch, vectors_ref, softness_ref, gate_a_ref, gate_x_ref, window, carry):
    rows = feed.shape[0]
    window[pl.ds(8, rows), :] = feed.astype(jnp.float32)
    conv = vectors_ref[4:5, :] + vectors_ref[0:1, :] * window[pl.ds(8, rows), :]
    for k in range(1, 4):
        conv = conv + vectors_ref[k : k + 1, :] * window[pl.ds(8 - k, rows), :]
    window[pl.ds(0, 8), :] = window[pl.ds(rows, 8), :]
    conv_low = conv.astype(jnp.bfloat16)
    rate = jax.nn.sigmoid(matmul(conv_low, gate_a_ref[...]) + vectors_ref[5:6, :])
    gate = jax.nn.sigmoid(matmul(conv_low, gate_x_ref[...]) + vectors_ref[6:7, :])
    decay, scale = decay_parts(rate, softness_ref[...])
    total, state = scan_block(decay, scale * gate * conv_low.astype(jnp.float32), shift_down)
    state = state + total * carry[0:1, :]
    carry[0:1, :] = state[rows - 1 : rows, :]
    gelu_branch = gelu_parts(branch)[0]
    mixed = (gelu_branch * state.astype(jnp.bfloat16).astype(jnp.float32)).astype(jnp.bfloat16)
    return conv_low, rate, gate, state, mixed


def rec_forward_body(
    feed_ref, branch_ref, vectors_ref, softness_ref, gate_a_ref, gate_x_ref,
    conv_ref, rate_ref, input_ref, state_ref, mixed_ref, window, carry,
):
    @pl.when(pl.program_id(0) == 0)
    def _():
        window[...] = jnp.zeros_like(window)
        carry[...] = jnp.zeros_like(carry)

    for s in range(feed_ref.shape[0]):
        conv_ref[s], rate_ref[s], input_ref[s], state_ref[s], mixed_ref[s] = rec_forward_rows(
            feed_ref[s], branch_ref[s], vectors_ref, softness_ref, gate_a_ref, gate_x_ref, window.at[s], carry.at[s]
        )


def rec_backward_body(
    grad_mixed_ref, branch_ref, feed_ref, feed_before_ref, conv_ref, rate_ref, input_ref,
    state_ref, state_before_ref, vectors_ref, softness_ref, gate_a_ref, gate_x_ref,
    grad_branch_ref, grad_feed_ref, grad_a_ref, grad_x_ref, sums_ref, window, later, carry,
):
    seqs, rows, channels = feed_ref.shape
    step = pl.program_id(0)
    first_block = step == pl.num_programs(0) - 1
    before = feed_before_ref.shape[1]

    @pl.when(step == 0)
    def _():
        later[...] = jnp.zeros_like(later)
        carry[...] = jnp.zeros_like(carry)
        grad_a_ref[...] = jnp.zeros_like(grad_a_ref)
        grad_x_ref[...] = jnp.zeros_like(grad_x_ref)
        sums_ref[...] = jnp.zeros_like(sums_ref)

    softness = softness_ref[...]
    keep = jnp.where(first_block, 0.0, 1.0)
    for s in range(seqs):
        gelu_branch, slope = gelu_parts(branch_ref[s])
        grad_mixed = grad_mixed_ref[s]
        state = state_ref[s]
        state_low = state.astype(jnp.bfloat16).astype(jnp.float32)
        grad_state = (grad_mixed * gelu_branch).astype(jnp.bfloat16).astype(jnp.float32)
        grad_branch_ref[s] = (slope * grad_mixed * state_low).astype(jnp.bfloat16)
        rate = rate_ref[s]
        gate = input_ref[s]
        decay, scale = decay_parts(rate, softness)
        total, carried = scan_block(shift_up(decay, 1, 1.0), grad_state, shift_up)
        carried = carried + total * carry[s, 0:1, :]
        carry[s, 0:1, :] = decay[0:1, :] * carried[0:1, :]
        index = lax.broadcasted_iota(jnp.int32, state.shape, 0)
        last = state_before_ref[s][7:8, :] * keep
        previous = jnp.where(index >= 1, pltpu.roll(state, 1, 0), last)
        conv_low = conv_ref[s]
        conv = conv_low.astype(jnp.float32)
        grad_log = carried * previous * decay - carried * gate * conv * decay * decay / scale
        log_rate = grad_log * rate
        pre_a = -8.0 * softness * log_rate * (1.0 - rate)
        pre_x = carried * scale * conv * gate * (1.0 - gate)
        low_a = pre_a.astype(jnp.bfloat16)
        low_x = pre_x.astype(jnp.bfloat16)
        grad_a_ref[...] += matmul_tn(conv_low, low_a)
        grad_x_ref[...] += matmul_tn(conv_low, low_x)
        grad_conv = (
            carried * scale * gate
            + matmul_nt(low_a, gate_a_ref[...])
            + matmul_nt(low_x, gate_x_ref[...])
        )
        window[s, pl.ds(0, 8), :] = feed_before_ref[s].astype(jnp.float32)[before - 8 :, :] * keep
        window[s, pl.ds(8, rows), :] = feed_ref[s].astype(jnp.float32)
        later[s, pl.ds(rows, 8), :] = later[s, pl.ds(0, 8), :]
        later[s, pl.ds(0, rows), :] = grad_conv
        grad_feed = vectors_ref[0:1, :] * grad_conv
        sums_ref[0:1, :] += jnp.sum(grad_conv * window[s, pl.ds(8, rows), :], axis=0, keepdims=True)
        for k in range(1, 4):
            grad_feed = grad_feed + vectors_ref[k : k + 1, :] * later[s, pl.ds(k, rows), :]
            sums_ref[k : k + 1, :] += jnp.sum(
                grad_conv * window[s, pl.ds(8 - k, rows), :], axis=0, keepdims=True
            )
        grad_feed_ref[s] = grad_feed.astype(jnp.bfloat16)
        sums_ref[4:5, :] += jnp.sum(grad_conv, axis=0, keepdims=True)
        sums_ref[5:6, :] += jnp.sum(pre_a, axis=0, keepdims=True)
        sums_ref[6:7, :] += jnp.sum(pre_x, axis=0, keepdims=True)
        sums_ref[7:8, :] += jnp.sum(log_rate, axis=0, keepdims=True)


def whole(shape):
    return pl.BlockSpec(shape, lambda i: (0,) * len(shape))


def rec_forward(feed, branch, vectors, softness, gate_a, gate_x):
    seqs, seq_len, channels = feed.shape
    rows = pick_rows(seq_len)
    block = pl.BlockSpec((seqs, rows, channels), lambda i: (0, i, 0))
    full = jax.ShapeDtypeStruct(feed.shape, jnp.float32)
    low = jax.ShapeDtypeStruct(feed.shape, jnp.bfloat16)
    return pl.pallas_call(
        rec_forward_body,
        grid=(seq_len // rows,),
        in_specs=[block, block]
        + [whole(v.shape) for v in (vectors, softness, gate_a, gate_x)],
        out_specs=[block] * 5,
        out_shape=[low, full, full, full, low],
        scratch_shapes=[
            pltpu.VMEM((seqs, rows + 8, channels), jnp.float32),
            pltpu.VMEM((seqs, 8, channels), jnp.float32),
        ],
        compiler_params=pltpu.CompilerParams(vmem_limit_bytes=40 << 20),
        name="rec_forward",
    )(feed, branch, vectors, softness, gate_a, gate_x)


def rec_backward(grad_mixed, branch, feed, conv, rate, gate, state, vectors, softness, gate_a, gate_x):
    seqs, seq_len, channels = feed.shape
    rows = pick_rows(seq_len)
    blocks = seq_len // rows
    block = pl.BlockSpec((seqs, rows, channels), lambda i: (0, blocks - 1 - i, 0))

    def ahead(by):
        return pl.BlockSpec(
            (seqs, by, channels),
            lambda i: (0, jnp.maximum((blocks - 1 - i) * (rows // by) - 1, 0), 0),
        )

    low = jax.ShapeDtypeStruct(feed.shape, jnp.bfloat16)
    square = jax.ShapeDtypeStruct((channels, channels), jnp.float32)
    return pl.pallas_call(
        rec_backward_body,
        grid=(blocks,),
        in_specs=[block, block, block, ahead(16), block, block, block, block, ahead(8)]
        + [whole(v.shape) for v in (vectors, softness, gate_a, gate_x)],
        out_specs=[block, block, whole((channels, channels)), whole((channels, channels)), whole((8, channels))],
        out_shape=[low, low, square, square, jax.ShapeDtypeStruct((8, channels), jnp.float32)],
        scratch_shapes=[
            pltpu.VMEM((seqs, rows + 8, channels), jnp.float32),
            pltpu.VMEM((seqs, rows + 8, channels), jnp.float32),
            pltpu.VMEM((seqs, 8, channels), jnp.float32),
        ],
        compiler_params=pltpu.CompilerParams(vmem_limit_bytes=40 << 20),
        name="rec_backward",
    )(grad_mixed, branch, feed, feed, conv, rate, gate, state, state, vectors, softness, gate_a, gate_x)


def line_place():
    return lax.axis_size("grp") // 2, lax.axis_index("grp") // 2, lax.axis_index("grp") % 2


def greet_line():
    chips, chip, core = line_place()
    barrier = pltpu.get_barrier_semaphore()

    def signal(place):
        pl.semaphore_signal(barrier, inc=1, device_id={"grp": place}, device_id_type=MESH)

    signal(chip * 2 + 1 - core)

    @pl.when(chip > 0)
    def _():
        signal(chip * 2 + core - 2)

    @pl.when(chip < chips - 1)
    def _():
        signal(chip * 2 + core + 2)

    ends = (chip == 0).astype(jnp.int32) + (chip == chips - 1).astype(jnp.int32)
    pl.semaphore_wait(barrier, 3 - ends)


def greet_axes(axes):
    barrier = pltpu.get_barrier_semaphore()
    for axis in axes:
        size = lax.axis_size(axis)
        for k in range(1, size):
            pl.semaphore_signal(
                barrier,
                inc=1,
                device_id={axis: lax.rem(lax.axis_index(axis) + k, size)},
                device_id_type=MESH,
            )
    pl.semaphore_wait(barrier, sum(lax.axis_size(axis) - 1 for axis in axes))


class Gather:
    def __init__(self, sources, outs, rows, send_sem, recv_sem, own_sem):
        self.chips, self.chip, self.core = line_place()
        self.me = self.chip * 2 + self.core
        self.sources, self.outs, self.rows = sources, outs, rows
        self.send_sem, self.recv_sem, self.own_sem = send_sem, recv_sem, own_sem

    def slot(self, p, origin):
        return self.outs[p].at[pl.ds(pl.multiple_of(origin * self.rows, self.rows), self.rows), :]

    def copy(self, p, source, origin, target, way):
        return pltpu.make_async_remote_copy(
            src_ref=source,
            dst_ref=self.slot(p, origin),
            send_sem=self.send_sem.at[way, p, origin],
            recv_sem=self.recv_sem.at[p, origin],
            device_id={"grp": target},
            device_id_type=MESH,
        )

    def to_right(self, p, source, origin):
        return self.copy(p, source, origin, self.me + 2, 0)

    def to_left(self, p, source, origin):
        return self.copy(p, source, origin, self.me - 2, 1)

    def to_partner(self, p, source, origin):
        return self.copy(p, source, origin, self.chip * 2 + 1 - self.core, 2)

    def own(self, p):
        return pltpu.make_async_copy(self.sources[p], self.slot(p, self.me), self.own_sem.at[p])

    def start(self, p):
        source = self.sources[p]

        @pl.when(self.chip < self.chips - 1)
        def _():
            self.to_right(p, source, self.me).start()

        @pl.when(self.chip > 0)
        def _():
            self.to_left(p, source, self.me).start()

        self.to_partner(p, source, self.me).start()
        self.own(p).start()

    def hop(self, p, h):
        left_origin = self.me - 2 - 2 * h
        right_origin = self.me + 2 + 2 * h

        @pl.when(self.chip - 1 - h >= 0)
        def _():
            here = self.slot(p, left_origin)
            self.to_right(p, here, left_origin).wait_recv()

            @pl.when(self.chip < self.chips - 1)
            def _():
                self.to_right(p, here, left_origin).start()

            self.to_partner(p, here, left_origin).start()

        @pl.when(self.chip + 1 + h <= self.chips - 1)
        def _():
            here = self.slot(p, right_origin)
            self.to_left(p, here, right_origin).wait_recv()

            @pl.when(self.chip > 0)
            def _():
                self.to_left(p, here, right_origin).start()

            self.to_partner(p, here, right_origin).start()

    def finish(self, p):
        for c in range(self.chips):
            origin = c * 2 + 1 - self.core
            self.to_partner(p, self.slot(p, origin), origin).wait_recv()
        self.own(p).wait()
        for c in range(self.chips):
            origin = c * 2 + self.core
            here = self.slot(p, origin)
            self.to_partner(p, here, origin).wait_send()

            @pl.when((c <= self.chip) & (self.chip < self.chips - 1))
            def _():
                self.to_right(p, here, origin).wait_send()

            @pl.when((c >= self.chip) & (self.chip > 0))
            def _():
                self.to_left(p, here, origin).wait_send()


def gather_sems(pieces):
    n = lax.axis_size("grp")
    return [
        pltpu.SemaphoreType.DMA((3, pieces, n)),
        pltpu.SemaphoreType.DMA((pieces, n)),
        pltpu.SemaphoreType.DMA((pieces,)),
    ]


class Scatter:
    def __init__(self, rows, part, out, swap_in, line_in, send_sem, recv_sem):
        self.chips, self.chip, self.core = line_place()
        self.me = self.chip * 2 + self.core
        self.rows, self.part, self.out = rows, part, out
        self.swap_in, self.line_in = swap_in, line_in
        self.send_sem, self.recv_sem = send_sem, recv_sem

    def copy(self, dest, place, way, slot, p):
        return pltpu.make_async_remote_copy(
            src_ref=self.out.at[p, slot],
            dst_ref=dest,
            send_sem=self.send_sem.at[way, p, slot],
            recv_sem=self.recv_sem.at[way, p, slot],
            device_id={"grp": place},
            device_id_type=MESH,
        )

    def swap(self, p, c):
        return self.copy(self.swap_in.at[p, c], self.chip * 2 + 1 - self.core, 0, c, p)

    def right(self, p, c):
        return self.copy(self.line_in.at[p, c], self.me + 2, 1, c, p)

    def left(self, p, c):
        slot = jnp.where(c == self.chip - 1, self.chips, c)
        return self.copy(self.line_in.at[p, slot], self.me - 2, 2, c, p)

    def from_right(self, p, c):
        slot = jnp.where(c == self.chip, self.chips, c)
        return self.copy(self.line_in.at[p, slot], self.me + 2, 2, c, p)

    def fill(self, p, s, lefts, rights, transposed, width=512):
        def rows_of(ref, core):
            at = [pl.multiple_of((c * 2 + core) * self.rows, self.rows) for c in range(self.chips)]
            return jnp.concatenate([ref[s, pl.ds(a, self.rows), :] for a in at], axis=0)

        def product(core, store):
            chosen = [rows_of(ref, core) for ref in lefts]

            @pl.loop(0, self.out.shape[-1] // width)
            def _(j):
                columns = pl.ds(pl.multiple_of(j * width, width), width)
                total = None
                for left, right in zip(chosen, rights):
                    term = matmul_nt(left, right[columns, :]) if transposed else matmul(left, right[:, columns])
                    total = term if total is None else total + term
                for c in range(self.chips):
                    store(c, columns, total[c * self.rows : (c + 1) * self.rows])

        def to_out(c, columns, value):
            self.out[p, c, :, columns] = value.astype(jnp.bfloat16)

        def to_part(c, columns, value):
            self.part[p, c, :, columns] = value

        def partners():
            product(1 - self.core, to_out)
            for c in range(self.chips):
                self.swap(p, c).start()

        def own():
            product(self.core, to_part)

        return partners, own

    def own(self, p, c):
        self.swap(p, c).wait_recv()
        return self.part[p, c] + self.swap_in[p, c].astype(jnp.float32)

    def hop(self, p, t):
        last = self.chips - 1

        def send(c, first, arrival, onward):
            self.swap(p, c).wait_send()
            total = self.own(p, c)

            @pl.when(first)
            def _():
                self.out[p, c] = total.astype(jnp.bfloat16)

            @pl.when(jnp.logical_not(first))
            def _():
                arrival(p, c).wait_recv()
                self.out[p, c] = (total + self.line_in[p, c].astype(jnp.float32)).astype(jnp.bfloat16)

            onward(p, c).start()

        @pl.when(self.chip <= t)
        def _():
            send(last - t + self.chip, self.chip == 0, self.right, self.right)

        @pl.when(last - self.chip <= t)
        def _():
            send(t - last + self.chip, self.chip == last, self.from_right, self.left)

    def result(self, p):
        chip = self.chip
        self.part[p, chip] = self.own(p, chip)

        @pl.when(chip > 0)
        def _():
            self.right(p, chip).wait_recv()
            self.part[p, chip] += self.line_in[p, chip].astype(jnp.float32)

        @pl.when(chip < self.chips - 1)
        def _():
            self.from_right(p, chip).wait_recv()
            self.part[p, chip] += self.line_in[p, self.chips].astype(jnp.float32)

        return self.part.at[p, chip]

    def finish(self, p):
        self.swap(p, self.chip).wait_send()
        for c in range(self.chips):

            @pl.when(c > self.chip)
            def _():
                self.right(p, c).wait_send()

            @pl.when(c < self.chip)
            def _():
                self.left(p, c).wait_send()


def scatter_scratch(pieces, rows, width):
    chips = lax.axis_size("grp") // 2
    return [
        pltpu.VMEM((pieces, chips, rows, width), jnp.float32),
        pltpu.VMEM((pieces, chips, rows, width), jnp.bfloat16),
        pltpu.VMEM((pieces, chips, rows, width), jnp.bfloat16),
        pltpu.VMEM((pieces, chips + 1, rows, width), jnp.bfloat16),
        pltpu.SemaphoreType.DMA((3, pieces, chips)),
        pltpu.SemaphoreType.DMA((3, pieces, chips)),
    ]


in_vmem = pl.BlockSpec(memory_space=pltpu.VMEM)
in_hbm = pl.BlockSpec(memory_space=pl.ANY)


def call(body, name, number, inputs, in_specs, outs, out_specs, scratch, us):
    return pl.pallas_call(
        body,
        in_specs=in_specs,
        out_specs=out_specs,
        out_shape=outs,
        scratch_shapes=scratch,
        name=name,
        cost_estimate=pl.CostEstimate(
            flops=us * 1000000000, bytes_accessed=us * 3000000, transcendentals=0
        ),
        compiler_params=pltpu.CompilerParams(
            collective_id=number, has_side_effects=True, vmem_limit_bytes=60 << 20
        ),
    )(*inputs)


class Exchange:
    def __init__(self, axis, source, slot, send_sem, recv_sem, steps=None):
        self.axis, self.source, self.slot, self.steps = axis, source, slot, steps
        self.size, self.me = lax.axis_size(axis), lax.axis_index(axis)
        self.send_sem, self.recv_sem = send_sem, recv_sem

    def copy(self, k, owner):
        peer = lax.rem(self.me + k, self.size)
        return pltpu.make_async_remote_copy(
            src_ref=self.source(peer),
            dst_ref=self.slot(owner) if self.slot else self.steps.at[k - 1],
            send_sem=self.send_sem.at[k],
            recv_sem=self.recv_sem.at[k],
            device_id={self.axis: peer},
            device_id_type=MESH,
        )

    def own(self):
        return pltpu.make_async_copy(self.source(self.me), self.slot(self.me), self.send_sem.at[0])

    def start(self):
        self.own().start()
        self.start_others()

    def start_others(self):
        for k in range(1, self.size):
            self.copy(k, self.me).start()

    def finish(self):
        self.own().wait()
        self.finish_others()

    def finish_others(self):
        for k in range(1, self.size):
            self.copy(k, lax.rem(self.me - k + self.size, self.size)).wait_recv()
        for k in range(1, self.size):
            self.copy(k, self.me).wait_send()


def sum_of(slots):
    total = slots[0]
    for k in range(1, slots.shape[0]):
        total = total + slots[k]
    return total


def block(ref, axis, parts):
    size = ref.shape[axis] // parts

    def view(k):
        at = pl.ds(pl.multiple_of(k * size, size), size)
        return ref.at[at, :] if axis == 0 else ref.at[:, at]

    return view


def weight_gathers(axes, sources, outs, send_sem, recv_sem):
    parts = lax.axis_size("seq")
    return [
        Exchange(
            "seq", lambda k, ref=source: ref, block(out, axis, parts), send_sem.at[i], recv_sem.at[i]
        )
        for i, (axis, source, out) in enumerate(zip(axes, sources, outs))
    ]


def weight_sums(axes, sources, outs, send_sem, recv_sem):
    parts = lax.axis_size("seq")
    return [
        Exchange(
            "seq", block(source, axis, parts), None, send_sem.at[i], recv_sem.at[i], out
        )
        for i, (axis, source, out) in enumerate(zip(axes, sources, outs))
    ]


def seq_sems(count):
    return [pltpu.SemaphoreType.DMA((count, lax.axis_size("seq")))] * 2


def gathered(block_of, axis):
    shape = list(block_of.shape)
    shape[axis] *= lax.axis_size("seq")
    return jax.ShapeDtypeStruct(shape, block_of.dtype)


def slots_of(matrix, axis):
    shape = list(matrix.shape)
    size = lax.axis_size("seq")
    shape[axis] //= size
    return jax.ShapeDtypeStruct((size - 1, *shape), matrix.dtype)


weight_axes = (0, 0, 1)


def views(ref):
    return [ref.at[s] for s in range(ref.shape[0])]


def first_body(x_ref, grad_ref, pack_ref, w0, w1, w2, later_ref, full_ref, params_ref, gains_ref, o0, o1, o2, *refs):
    small_send, small_recv, gain_send, gain_recv, weight_send, weight_recv = refs[3:]
    greet_axes(("seq", "grp"))
    seqs = x_ref.shape[0]
    gather = Gather(views(x_ref), views(full_ref), x_ref.shape[1], *refs[:3])
    weights = weight_gathers(weight_axes, (w0, w1, w2), (o0, o1, o2), weight_send, weight_recv)
    small = Exchange("seq", lambda k: pack_ref, lambda k: params_ref.at[k], small_send, small_recv)
    small.start()
    for s in range(seqs):
        gather.start(s)
    for weight in weights:
        weight.start()
    later_ref[...] = grad_ref[...]
    small.finish()
    place = lax.axis_index("grp")
    for owner in range(small.size):
        gains_ref[place, owner] = params_ref[owner, pl.ds(pack_ref.shape[0] - 8, 8), :]
    gains = Exchange("grp", lambda k: gains_ref.at[place], lambda k: gains_ref.at[k], gain_send, gain_recv)
    gains.start_others()
    for h in range(gather.chips - 1):
        for s in range(seqs):
            gather.hop(s, h)
    gains.finish_others()
    for weight in weights:
        weight.finish()
    for s in range(seqs):
        gather.finish(s)


def gather_first(layer_in, out_grad, pack, weights):
    seqs, rows, width = layer_in.shape
    n, size = lax.axis_size("grp"), lax.axis_size("seq")
    return call(
        first_body, "gather_first", 1,
        (layer_in, out_grad, pack, *weights), [in_vmem] * 6,
        [
            jax.ShapeDtypeStruct(out_grad.shape, out_grad.dtype),
            jax.ShapeDtypeStruct((seqs, n * rows, width), jnp.bfloat16),
            jax.ShapeDtypeStruct((size,) + pack.shape, jnp.float32),
            jax.ShapeDtypeStruct((n, size, 8, 128), jnp.float32),
        ]
        + [gathered(w, axis) for w, axis in zip(weights, weight_axes)],
        [in_vmem, in_hbm] + [in_vmem] * 2 + [in_hbm] * 3,
        gather_sems(seqs)
        + [pltpu.SemaphoreType.DMA((size,))] * 2
        + [pltpu.SemaphoreType.DMA((n,))] * 2
        + seq_sems(3),
        70,
    )


def mean_of(values):
    return jnp.mean(values, axis=-1, keepdims=True)


def sum_then_gather(scatter, gather, fills, stores, count=0):
    hops = range(1, scatter.chips - 1)
    for step in fills[0]:
        step()
    scatter.hop(0, 0)
    for p, store in enumerate(stores):
        ahead = list(fills[p + 1]) if p + 1 < len(fills) else []
        for h in hops:
            if ahead:
                ahead.pop(0)()
            scatter.hop(p, h)
            if 0 < p <= count:
                gather.hop(p - 1, h - 1)
        for step in ahead:
            step()
        if p + 1 < len(fills):
            scatter.hop(p + 1, 0)
        store()
        if p < count:
            gather.start(p)
        if 0 < p <= count:
            gather.hop(p - 1, gather.chips - 2)
    if count == len(stores):
        for h in range(gather.chips - 1):
            gather.hop(count - 1, h)
    for p in range(count):
        gather.finish(p)
    for p in range(len(fills)):
        scatter.finish(p)


def out_body(hidden_ref, down_w_ref, residual_ref, layer_out_ref, scatter, first):
    def fill(s):
        return scatter.fill(first + s, s, [hidden_ref], [down_w_ref], False)

    def store(s):
        layer_out_ref[s] = (residual_ref[s] + scatter.result(first + s)[...]).astype(jnp.bfloat16)

    return fill, store


def mixer_out_body(mixed_ref, out_w_ref, x_ref, gain_ref, w0, w1, w2, residual_ref, normed_ref, o0, o1, o2, low_ref, *refs):
    greet_axes(("seq", "grp"))
    seqs, rows, _ = x_ref.shape
    weights = weight_gathers(weight_axes, (w0, w1, w2), (o0, o1, o2), *refs[:2])
    for weight in weights:
        weight.start()
    gather = Gather(views(low_ref), views(normed_ref), rows, *refs[2:5])
    scatter = Scatter(rows, *refs[5:])

    def fill(s):
        return scatter.fill(s, s, [mixed_ref], [out_w_ref], False)

    def store(s):
        residual = x_ref[s].astype(jnp.float32) + scatter.result(s)[...]
        residual_ref[s] = residual
        normal = residual * lax.rsqrt(mean_of(residual * residual) + epsilon)
        low_ref[s] = (normal * gain_ref[...]).astype(jnp.bfloat16)

    sum_then_gather(
        scatter, gather, [fill(s) for s in range(seqs)], [functools.partial(store, s) for s in range(seqs)], seqs
    )
    for weight in weights:
        weight.finish()


def mixer_out(mixed, out_w, layer_in, gain, weights):
    seqs, rows, width = layer_in.shape
    full = jax.ShapeDtypeStruct((seqs, lax.axis_size("grp") * rows, width), jnp.bfloat16)
    return call(
        mixer_out_body, "mixer_out", 2,
        (mixed, out_w, layer_in, gain, *weights), [in_vmem] * 7,
        [jax.ShapeDtypeStruct(layer_in.shape, jnp.float32), full]
        + [gathered(w, axis) for w, axis in zip(weights, weight_axes)],
        [in_vmem] + [in_hbm] * 4,
        [pltpu.VMEM(layer_in.shape, jnp.bfloat16)]
        + seq_sems(3)
        + gather_sems(seqs)
        + scatter_scratch(seqs, rows, width),
        100,
    )


def mixer_forward_body(
    x_full_ref, gains_ref, branch_w_ref, rec_w_ref, out_w_ref, vectors_ref, softness_ref, gate_a_ref, gate_x_ref,
    grad_ref, w0, w1, w2,
    normed_one_ref, branch_ref, feed_ref, conv_ref, rate_ref, input_ref, state_ref, mixed_ref, residual_ref,
    normed_ref, grads_ref, o0, o1, o2, low_ref, window, carry, *refs,
):
    greet_axes(("seq", "grp"))
    seqs, seq_len, _ = x_full_ref.shape
    rows = grad_ref.shape[1]
    me = lax.axis_index("grp")
    weights = weight_gathers(weight_axes, (w0, w1, w2), (o0, o1, o2), *refs[:2])
    gather = Gather(views(low_ref) + views(grad_ref), views(normed_ref) + views(grads_ref), rows, *refs[2:5])
    scatter = Scatter(rows, *refs[5:])
    for s in range(seqs):
        gather.start(seqs + s)
    for weight in weights:
        weight.start()
    tile = pick_rows(seq_len, (256, 192, 128, 96, 64, 32, 16))
    chunk = window.shape[0] - 8
    window[...] = jnp.zeros_like(window)

    def project(s):
        @pl.loop(0, seq_len // tile)
        def _(i):
            at = pl.ds(pl.multiple_of(i * tile, tile), tile)
            inputs = x_full_ref[s, at, :].astype(jnp.float32)
            normal = inputs * lax.rsqrt(mean_of(inputs * inputs) + epsilon)
            normed = (normal * gains_ref[0]).astype(jnp.bfloat16)
            normed_one_ref[s, at, :] = normed
            branch_ref[s, at, :] = matmul(normed, branch_w_ref[...])
            feed_ref[s, at, :] = matmul(normed, rec_w_ref[...]).astype(jnp.bfloat16)

    def recur(s):
        window[pl.ds(0, 8), :] = jnp.zeros((8, window.shape[1]), jnp.float32)
        carry[...] = jnp.zeros_like(carry)

        @pl.loop(0, seq_len // chunk)
        def _(i):
            at = pl.ds(pl.multiple_of(i * chunk, chunk), chunk)
            conv, rate, gate, state, mixed = rec_forward_rows(
                feed_ref[s, at, :], branch_ref[s, at, :], vectors_ref, softness_ref, gate_a_ref, gate_x_ref, window, carry
            )
            conv_ref[s, at, :] = conv
            rate_ref[s, at, :] = rate
            input_ref[s, at, :] = gate
            state_ref[s, at, :] = state
            mixed_ref[s, at, :] = mixed

    def late_hop(h):
        if h < gather.chips - 1:
            for s in range(seqs):
                gather.hop(seqs + s, h)

    def steps(s):
        partners, own = scatter.fill(s, s, [mixed_ref], [out_w_ref], False)
        late = [functools.partial(late_hop, h) for h in range(gather.chips - 1)]

        def second():
            if s == 0:
                late_hop(0)
            recur(s)

        def third():
            partners()
            if s == 0:
                late_hop(1)

        def fourth():
            own()
            if s == seqs - 1:
                for hop in late[2 if seqs > 1 else 1 :]:
                    hop()

        return [functools.partial(project, s), second, third, fourth]

    def store(s):
        own = x_full_ref[s, pl.ds(pl.multiple_of(me * rows, rows), rows), :]
        residual = own.astype(jnp.float32) + scatter.result(s)[...]
        residual_ref[s] = residual
        normal = residual * lax.rsqrt(mean_of(residual * residual) + epsilon)
        low_ref[s] = (normal * gains_ref[1]).astype(jnp.bfloat16)

    sum_then_gather(
        scatter, gather, [steps(s) for s in range(seqs)], [functools.partial(store, s) for s in range(seqs)], seqs
    )
    for s in range(seqs):
        gather.finish(seqs + s)
    for weight in weights:
        weight.finish()


def mixer_forward(x_full, gains, branch_w, rec_w, out_w, vectors, softness, gate_a, gate_x, out_grad, weights):
    seqs, seq_len, width = x_full.shape
    rows, channels = out_grad.shape[1], vectors.shape[1]
    low = jax.ShapeDtypeStruct((seqs, seq_len, channels), jnp.bfloat16)
    full = jax.ShapeDtypeStruct((seqs, seq_len, channels), jnp.float32)
    outs = [x_full, full, low, low, full, full, full, low]
    outs += [jax.ShapeDtypeStruct(out_grad.shape, jnp.float32), x_full, x_full]
    outs = [jax.ShapeDtypeStruct(out.shape, out.dtype) for out in outs]
    outs += [gathered(w, axis) for w, axis in zip(weights, weight_axes)]
    return call(
        mixer_forward_body, "mixer_forward", 2,
        (x_full, gains, branch_w, rec_w, out_w, vectors, softness, gate_a, gate_x, out_grad, *weights),
        [in_vmem] * 13,
        outs, [in_vmem] * 9 + [in_hbm] * 5,
        [
            pltpu.VMEM(out_grad.shape, jnp.bfloat16),
            pltpu.VMEM((pick_rows(seq_len) + 8, channels), jnp.float32),
            pltpu.VMEM((8, channels), jnp.float32),
        ]
        + seq_sems(3)
        + gather_sems(2 * seqs)
        + scatter_scratch(seqs, rows, width),
        130,
    )


def mlp_back_body(
    with_out, gate_ref, up_ref, gate_w_ref, up_w_ref, residual_ref, grad_ref, gain_ref, w0, w1, w2, *refs
):
    if with_out:
        hidden_ref, down_w_ref = refs[:2]
        refs = refs[2:]
    grad_residual_ref, gain_grad_ref, full_ref, o0, o1, o2 = refs[:6]
    refs = refs[6:]
    if with_out:
        layer_out_ref = refs[0]
        refs = refs[1:]
    low_ref, *refs = refs
    greet_axes(("seq", "grp"))
    seqs, rows, _ = grad_ref.shape
    sums = weight_sums(weight_axes, (w0, w1, w2), (o0, o1, o2), *refs[:2])
    for weight in sums:
        weight.start_others()
    gather = Gather(views(low_ref), views(full_ref), rows, *refs[2:5])
    scatter = Scatter(rows, *refs[5:])
    gain_grad_ref[...] = jnp.zeros_like(gain_grad_ref)

    def fill(s):
        return scatter.fill(s, s, [gate_ref, up_ref], [gate_w_ref, up_w_ref], True)

    def store(s):
        term = scatter.result(s)[...]
        residual = residual_ref[s]
        inverse = lax.rsqrt(mean_of(residual * residual) + epsilon)
        normal = residual * inverse
        gain_grad_ref[0:1, :] += jnp.sum(term * normal, axis=0, keepdims=True)
        grad = grad_ref[s].astype(jnp.float32) + norm_back(term, normal, inverse, gain_ref[...])
        grad_residual_ref[s] = grad
        low_ref[s] = grad.astype(jnp.bfloat16)

    fills = [fill(s) for s in range(seqs)]
    stores = [functools.partial(store, s) for s in range(seqs)]
    if with_out:
        fill_out, store_out = out_body(hidden_ref, down_w_ref, residual_ref, layer_out_ref, scatter, seqs)
        fills += [fill_out(s) for s in range(seqs)]
        stores += [functools.partial(store_out, s) for s in range(seqs)]
    sum_then_gather(scatter, gather, fills, stores, seqs)
    for weight in sums:
        weight.finish_others()


def mlp_back(grad_gate, grad_up, gate_w, up_w, residual, out_grad, gain, grads, out_inputs):
    seqs, rows, width = residual.shape
    outs = [
        jax.ShapeDtypeStruct(residual.shape, jnp.float32),
        jax.ShapeDtypeStruct((8, width), jnp.float32),
        jax.ShapeDtypeStruct((seqs, lax.axis_size("grp") * rows, width), jnp.bfloat16),
    ]
    outs += [slots_of(grad, axis) for grad, axis in zip(grads, weight_axes)]
    out_specs = [in_vmem] * 2 + [in_hbm] * 4
    if out_inputs:
        outs.append(jax.ShapeDtypeStruct(residual.shape, jnp.bfloat16))
        out_specs.append(in_vmem)
    return call(
        functools.partial(mlp_back_body, bool(out_inputs)), "mlp_back", 3,
        (grad_gate, grad_up, gate_w, up_w, residual, out_grad, gain, *grads, *out_inputs),
        [in_vmem] * 7 + [in_hbm] * 3 + [in_vmem] * len(out_inputs),
        outs, out_specs,
        [pltpu.VMEM(residual.shape, jnp.bfloat16)]
        + seq_sems(3)
        + gather_sems(seqs)
        + scatter_scratch(seqs * (2 if out_inputs else 1), rows, width),
        130,
    )


def last_body(
    branch_ref, feed_ref, branch_w_ref, rec_w_ref, x_ref, grad_ref, gain_ref, gain_two_ref, rec_ref,
    w0, w1, w2, *refs,
):
    grad_x_ref, rec_sum_ref, gain_sum_ref, o0, o1, o2 = refs[:6]
    refs = refs[6:]
    rec_slots, gain_local, gain_part, gain_slots, part_slots = refs[:5]
    rec_sems, gain_sems, part_sems = refs[5:7], refs[7:9], refs[9:11]
    greet_axes(("seq", "grp"))
    seqs, rows, _ = x_ref.shape
    sums = weight_sums(weight_axes, (w0, w1, w2), (o0, o1, o2), *refs[11:13])
    scatter = Scatter(rows, *refs[13:])
    rec = Exchange("seq", lambda k: rec_ref.at[k], lambda k: rec_slots.at[k], *rec_sems)
    rec.start()
    for weight in sums:
        weight.start_others()
    gain_local[...] = jnp.zeros_like(gain_local)
    gain_local[1:2, :] = gain_two_ref[0:1, :]

    def fill(s):
        return scatter.fill(s, s, [branch_ref, feed_ref], [branch_w_ref, rec_w_ref], True)

    across = Exchange(
        "seq", block(gain_local, 1, lax.axis_size("seq")), lambda k: gain_slots.at[k], *gain_sems
    )

    def store(s):
        term = scatter.result(s)[...]
        inputs = x_ref[s].astype(jnp.float32)
        inverse = lax.rsqrt(mean_of(inputs * inputs) + epsilon)
        normal = inputs * inverse
        gain_local[0:1, :] += jnp.sum(term * normal, axis=0, keepdims=True)
        if s == seqs - 1:
            across.start()
        grad_x_ref[s] = grad_ref[s] + norm_back(term, normal, inverse, gain_ref[...])

    sum_then_gather(
        scatter, None, [fill(s) for s in range(seqs)], [functools.partial(store, s) for s in range(seqs)]
    )
    across.finish()
    gain_part[...] = sum_of(gain_slots)
    along = Exchange("grp", lambda k: gain_part, lambda k: part_slots.at[k], *part_sems)
    along.start()
    rec.finish()
    rec_sum_ref[...] = sum_of(rec_slots)
    for weight in sums:
        weight.finish_others()
    along.finish()
    gain_sum_ref[...] = sum_of(part_slots)


def last(grad_branch, grad_feed, branch_w, rec_w, layer_in, grad_residual, gain, gain_two_grad, rec_blocks, grads):
    seqs, rows, width = layer_in.shape
    size, n = lax.axis_size("seq"), lax.axis_size("grp")
    f32 = jnp.float32
    inputs = (grad_branch, grad_feed, branch_w, rec_w, layer_in, grad_residual, gain, gain_two_grad, rec_blocks)
    outs = [
        jax.ShapeDtypeStruct(layer_in.shape, f32),
        jax.ShapeDtypeStruct(rec_blocks.shape[1:], f32),
        jax.ShapeDtypeStruct((8, width // size), f32),
    ]
    outs += [slots_of(grad, axis) for grad, axis in zip(grads, weight_axes)]
    out_specs = [in_vmem] * 3 + [in_hbm] * 3
    return call(
        last_body, "last", 4,
        inputs + tuple(grads), [in_vmem] * len(inputs) + [in_hbm] * 3,
        outs, out_specs,
        [
            pltpu.VMEM(rec_blocks.shape, f32),
            pltpu.VMEM((8, width), f32),
            pltpu.VMEM((8, width // size), f32),
            pltpu.VMEM((size, 8, width // size), f32),
            pltpu.VMEM((n, 8, width // size), f32),
        ]
        + [pltpu.SemaphoreType.DMA((size,))] * 4
        + [pltpu.SemaphoreType.DMA((n,))] * 2
        + seq_sems(3)
        + scatter_scratch(seqs, rows, width),
        80,
    )


def out_only_body(hidden_ref, down_w_ref, residual_ref, layer_out_ref, *scratch):
    greet_line()
    scatter = Scatter(residual_ref.shape[1], *scratch)
    fill, store = out_body(hidden_ref, down_w_ref, residual_ref, layer_out_ref, scatter, 0)
    seqs = range(residual_ref.shape[0])
    sum_then_gather(
        scatter, None, [fill(s) for s in seqs], [functools.partial(store, s) for s in seqs]
    )


def out_only(hidden, down_w, residual):
    seqs, rows, width = residual.shape
    return call(
        out_only_body, "layer_out", 5,
        (hidden, down_w, residual), [in_vmem] * 3,
        [jax.ShapeDtypeStruct(residual.shape, jnp.bfloat16)], [in_vmem],
        scatter_scratch(seqs, rows, width), 60,
    )[0]


def per_device(
    layer_in, gain_one, w_branch, w_rec, conv_w, conv_b, gate_a_w, gate_a_b, gate_x_w, gate_x_b,
    decay_logit, w_out, gain_two, mlp_gate, mlp_up, mlp_down, out_grad,
):
    seqs_here, positions, model_width = layer_in.shape
    heads_here, tap_count, part_dim = conv_w.shape
    seq_devices, grp_devices = lax.axis_size("seq"), lax.axis_size("grp")
    head_dim = part_dim * seq_devices
    channels = heads_here * head_dim
    f32 = jnp.float32

    own_params = jnp.concatenate(
        [jnp.transpose(conv_w, (0, 2, 1))]
        + [v[:, :, None] for v in (conv_b, gate_a_b, gate_x_b, decay_logit)]
        + [gate_a_w, gate_x_w],
        axis=2,
    ).astype(f32)
    own_gains = jnp.concatenate([gain_one, gain_two]).astype(f32)
    pack = jnp.concatenate(
        [padded_rows(own_params.reshape(1, -1))[0], padded_rows(own_gains.reshape(1, -1))[0]]
    )
    late_grad, x_full, params, gains, branch_w, rec_w, out_w = gather_first(
        layer_in, out_grad, pack, (w_branch, w_rec, w_out)
    )

    gains = gains.reshape(grp_devices, seq_devices, -1)[:, :, : own_gains.size]
    gains = jnp.transpose(gains.reshape(grp_devices, seq_devices, 2, -1), (2, 1, 0, 3)).reshape(2, 1, -1)
    params = params.reshape(seq_devices, -1)[:, : own_params.size]
    params = params.reshape((seq_devices,) + own_params.shape)
    params = jnp.transpose(params, (1, 0, 2, 3)).reshape(heads_here, head_dim, -1)
    vectors = params[:, :, : tap_count + 4].reshape(channels, -1).T
    at = tap_count + 4
    diag_a = head_diagonal(params[:, :, at : at + head_dim].astype(jnp.bfloat16))
    diag_x = head_diagonal(params[:, :, at + head_dim :].astype(jnp.bfloat16))
    logit = vectors[tap_count + 3 :]
    softness = jax.nn.softplus(-logit)

    short_line = seqs_here * positions * grp_devices <= 2048
    mlp_weights = (mlp_gate, mlp_up, mlp_down)
    if short_line:
        (
            normed_one, branch_pre, feed, conv, rate, gate, state, mixed, residual, normed_two, grad_output,
            gate_w, up_w, down_w,
        ) = mixer_forward(
            x_full, gains, branch_w, rec_w, out_w, vectors, softness, diag_a, diag_x, late_grad, mlp_weights
        )
        normed_one = normed_one.reshape(-1, model_width)
        grad_output = grad_output.reshape(-1, model_width)
    else:
        grad_output = jnp.concatenate(
            [lax.all_gather(late_grad[s], "grp", axis=0, tiled=True) for s in range(seqs_here)]
        )
        inputs = x_full.astype(f32)
        normal_one = inputs * lax.rsqrt(mean_of(inputs * inputs) + epsilon)
        normed_one = (normal_one * gains[0]).astype(jnp.bfloat16).reshape(-1, model_width)
        branch_pre = matmul(normed_one, branch_w).reshape(seqs_here, -1, channels)
        feed = matmul(normed_one, rec_w).astype(jnp.bfloat16).reshape(seqs_here, -1, channels)
        conv, rate, gate, state, mixed = rec_forward(feed, branch_pre, vectors, softness, diag_a, diag_x)
        residual, normed_two, gate_w, up_w, down_w = mixer_out(
            mixed, out_w, layer_in, gains[1], mlp_weights
        )
    mixed = mixed.reshape(-1, channels)
    normed_two = normed_two.reshape(-1, model_width)
    up_proj = matmul(normed_two, up_w)
    gate_act, gate_pull = jax.vjp(jax.nn.gelu, matmul(normed_two, gate_w))
    hidden = (gate_act * up_proj).astype(jnp.bfloat16)
    grad_hidden = matmul_nt(grad_output, down_w)
    grad_gate = gate_pull(grad_hidden * up_proj)[0].astype(jnp.bfloat16)
    grad_up = (grad_hidden * gate_act).astype(jnp.bfloat16)
    mlp_grads = low_all(
        (matmul_tn(normed_two, grad_gate), matmul_tn(normed_two, grad_up), matmul_tn(hidden, grad_output))
    )

    def by_seq(values):
        return values.reshape(seqs_here, -1, values.shape[-1])

    back_inputs = (
        by_seq(grad_gate), by_seq(grad_up), gate_w, up_w, residual, out_grad, gains[1], mlp_grads
    )
    if not short_line:
        layer_out = out_only(by_seq(hidden), down_w, residual)
        grad_residual, gain_two_grad, residual_low, *mlp_slots = mlp_back(*back_inputs, ())
    else:
        grad_residual, gain_two_grad, residual_low, *mlp_slots, layer_out = mlp_back(
            *back_inputs, (by_seq(hidden), down_w)
        )
    mlp_grads = sum_slots(mlp_grads, mlp_slots)
    residual_low = residual_low.reshape(-1, model_width)
    out_weight_grad = matmul_tn(mixed, residual_low)
    grad_mixed = by_seq(matmul_nt(residual_low, out_w))
    grad_branch, grad_feed, square_a, square_x, sums = rec_backward(
        grad_mixed, branch_pre, feed, conv, rate, gate, state, vectors, softness, diag_a, diag_x
    )
    vector_grads = jnp.concatenate(
        [sums[: tap_count + 3], 8.0 * jax.nn.sigmoid(-logit) * sums[tap_count + 3 :]]
    )
    rec_grads = jnp.concatenate(
        [
            vector_grads.T.reshape(heads_here, head_dim, -1),
            diagonal_heads(square_a, heads_here),
            diagonal_heads(square_x, heads_here),
        ],
        axis=2,
    )
    rec_grads = rec_grads.reshape(heads_here, seq_devices, part_dim, -1)
    rec_blocks = padded_rows(jnp.transpose(rec_grads, (1, 0, 2, 3)))
    mixer_grads = low_all(
        (
            matmul_tn(normed_one, grad_branch.reshape(-1, channels)),
            matmul_tn(normed_one, grad_feed.reshape(-1, channels)),
            out_weight_grad,
        )
    )
    grad_x, rec_sum, gain_sum, *mixer_slots = last(
        grad_branch, grad_feed, branch_w, rec_w, layer_in, grad_residual, gains[0], gain_two_grad, rec_blocks,
        mixer_grads,
    )
    mixer_grads = sum_slots(mixer_grads, mixer_slots)
    rec_sum = rec_sum.reshape(-1)[: own_params.size].reshape(own_params.shape)
    own_part = gain_one.shape[0]
    gain_grads = lax.dynamic_slice_in_dim(gain_sum, lax.axis_index("grp") * own_part, own_part, 1)
    return (
        layer_out,
        grad_x,
        gain_grads[0],
        mixer_grads[0],
        mixer_grads[1],
        jnp.transpose(rec_sum[:, :, :tap_count], (0, 2, 1)),
        rec_sum[:, :, tap_count],
        rec_sum[:, :, at : at + head_dim],
        rec_sum[:, :, tap_count + 1],
        rec_sum[:, :, at + head_dim :],
        rec_sum[:, :, tap_count + 2],
        rec_sum[:, :, tap_count + 3],
        mixer_grads[2],
        gain_grads[1],
        mlp_grads[0],
        mlp_grads[1],
        mlp_grads[2],
    )


def solution(mesh):
    placed = (
        P("seq", "grp", None),
        P(("seq", "grp")),
        P("seq", "grp"),
        P("seq", "grp"),
        P("grp", None, "seq"),
        P("grp", "seq"),
        P("grp", "seq", None),
        P("grp", "seq"),
        P("grp", "seq", None),
        P("grp", "seq"),
        P("grp", "seq"),
        P("grp", "seq"),
        P(("seq", "grp")),
        P("seq", "grp"),
        P("seq", "grp"),
        P("grp", "seq"),
        P("seq", "grp", None),
    )
    return jax.shard_map(
        per_device,
        mesh=mesh,
        in_specs=placed,
        out_specs=(
            P("seq", "grp", None),
            P("seq", "grp", None),
            P(("seq", "grp")),
            P("seq", "grp"),
            P("seq", "grp"),
            P("grp", None, "seq"),
            P("grp", "seq"),
            P("grp", "seq", None),
            P("grp", "seq"),
            P("grp", "seq", None),
            P("grp", "seq"),
            P("grp", "seq"),
            P("grp", "seq"),
            P(("seq", "grp")),
            P("seq", "grp"),
            P("seq", "grp"),
            P("grp", "seq"),
        ),
        check_vma=False,
    )
```

```python
import functools
import math

import jax
import jax.numpy as jnp
from jax import lax
from jax.experimental import pallas as pl
from jax.experimental.pallas import tpu as pltpu
from jax.sharding import PartitionSpec as P

epsilon = 1e-06
gelu_slope = math.sqrt(2.0 / math.pi)
gelu_cubic = 0.044715
MESH = pl.DeviceIdType.MESH


def matmul(left, right):
    return jnp.dot(left, right, preferred_element_type=jnp.float32)


def matmul_tn(left, right):
    return lax.dot_general(
        left, right, (((0,), (0,)), ((), ())), preferred_element_type=jnp.float32
    )


def matmul_nt(left, right):
    return lax.dot_general(
        left, right, (((1,), (1,)), ((), ())), preferred_element_type=jnp.float32
    )


def norm_back(grad_normed, normal_part, inverse, gain):
    scaled = grad_normed * gain
    return inverse * (scaled - normal_part * jnp.mean(scaled * normal_part, axis=-1, keepdims=True))


def low_all(grads):
    return tuple(grad.astype(jnp.bfloat16) for grad in grads)


def sum_slots(grads, slots, axes):
    sums = []
    for grad, slot, axis in zip(grads, slots, axes):
        size = slot.shape[1 + axis]
        own = lax.dynamic_slice_in_dim(grad, lax.axis_index("seq") * size, size, axis)
        for k in range(slot.shape[0]):
            own = own.astype(jnp.float32) + slot[k].astype(jnp.float32)
        sums.append(own)
    return sums


def sum_all(slots):
    total = slots[0].astype(jnp.float32)
    for k in range(1, slots.shape[0]):
        total = total + slots[k].astype(jnp.float32)
    return total


def padded_rows(values):
    flat = values.reshape(values.shape[0], -1)
    flat = jnp.pad(flat, ((0, 0), (0, -flat.shape[1] % 1024)))
    return flat.reshape(values.shape[0], -1, 128)


def head_diagonal(blocks):
    heads, head_dim, _ = blocks.shape
    rows = []
    for h in range(heads):
        row = [jnp.zeros((head_dim, head_dim), blocks.dtype)] * heads
        row[h] = blocks[h]
        rows.append(jnp.concatenate(row, axis=1))
    return jnp.concatenate(rows, axis=0)


def diagonal_heads(square, heads):
    head_dim = square.shape[0] // heads
    return jnp.stack(
        [
            square[h * head_dim : (h + 1) * head_dim, h * head_dim : (h + 1) * head_dim]
            for h in range(heads)
        ]
    )


def pick_rows(seq_len, choices=(128, 96, 64, 32, 16)):
    for rows in choices:
        if seq_len % rows == 0:
            return rows
    return seq_len


def gelu_parts(x):
    cubic = gelu_slope * (x + gelu_cubic * x * x * x)
    bend = jnp.tanh(cubic)
    gate = 0.5 * (1.0 + bend)
    slope = gate + 0.5 * x * (1.0 - bend * bend) * gelu_slope * (1.0 + 3.0 * gelu_cubic * x * x)
    return x * gate, slope


def minus_expm1(x):
    series = 1.0 + x * (1.0 / 9.0)
    for k in (8, 7, 6, 5, 4, 3, 2):
        series = 1.0 + x * (1.0 / k) * series
    return jnp.where(x > -0.4, -x * series, 1.0 - jnp.exp(x))


def shift_down(values, by, fill):
    rows = values.shape[0]
    if by % 8 == 0:
        return jnp.concatenate([jnp.full((by, values.shape[1]), fill), values[: rows - by]], axis=0)
    index = lax.broadcasted_iota(jnp.int32, values.shape, 0)
    return jnp.where(index >= by, pltpu.roll(values, by, 0), fill)


def shift_up(values, by, fill):
    rows = values.shape[0]
    if by % 8 == 0:
        return jnp.concatenate([values[by:], jnp.full((by, values.shape[1]), fill)], axis=0)
    index = lax.broadcasted_iota(jnp.int32, values.shape, 0)
    return jnp.where(index < rows - by, pltpu.roll(values, rows - by, 0), fill)


def scan_block(decay, drive, shift):
    by = 1
    while by < decay.shape[0]:
        drive = drive + decay * shift(drive, by, 0.0)
        decay = decay * shift(decay, by, 1.0)
        by *= 2
    return decay, drive


def decay_parts(rate, softness):
    log_decay = -8.0 * rate * softness
    return jnp.exp(log_decay), jnp.sqrt(minus_expm1(2.0 * log_decay))


def rec_forward_rows(feed, branch, vectors_ref, softness_ref, gate_a_ref, gate_x_ref, window, carry):
    rows = feed.shape[0]
    window[pl.ds(8, rows), :] = feed.astype(jnp.float32)
    conv = vectors_ref[4:5, :] + vectors_ref[0:1, :] * window[pl.ds(8, rows), :]
    for k in range(1, 4):
        conv = conv + vectors_ref[k : k + 1, :] * window[pl.ds(8 - k, rows), :]
    window[pl.ds(0, 8), :] = window[pl.ds(rows, 8), :]
    conv_low = conv.astype(jnp.bfloat16)
    rate = jax.nn.sigmoid(matmul(conv_low, gate_a_ref[...]) + vectors_ref[5:6, :])
    gate = jax.nn.sigmoid(matmul(conv_low, gate_x_ref[...]) + vectors_ref[6:7, :])
    decay, scale = decay_parts(rate, softness_ref[...])
    total, state = scan_block(decay, scale * gate * conv_low.astype(jnp.float32), shift_down)
    state = state + total * carry[0:1, :]
    carry[0:1, :] = state[rows - 1 : rows, :]
    gelu_branch = gelu_parts(branch)[0]
    mixed = (gelu_branch * state.astype(jnp.bfloat16).astype(jnp.float32)).astype(jnp.bfloat16)
    return conv_low, rate, gate, state, mixed


def rec_forward_body(
    feed_ref, branch_ref, vectors_ref, softness_ref, gate_a_ref, gate_x_ref,
    conv_ref, rate_ref, input_ref, state_ref, mixed_ref, window, carry,
):
    @pl.when(pl.program_id(0) == 0)
    def _():
        window[...] = jnp.zeros_like(window)
        carry[...] = jnp.zeros_like(carry)

    for s in range(feed_ref.shape[0]):
        conv_ref[s], rate_ref[s], input_ref[s], state_ref[s], mixed_ref[s] = rec_forward_rows(
            feed_ref[s], branch_ref[s], vectors_ref, softness_ref, gate_a_ref, gate_x_ref, window.at[s], carry.at[s]
        )


def rec_backward_rows(
    grad_mixed, branch, feed, feed_before, conv_low, rate, gate, state, state_before,
    vectors_ref, softness_ref, gate_a_ref, gate_x_ref, grad_a_ref, grad_x_ref, sums_ref, window, later, carry,
):
    rows = feed.shape[0]
    softness = softness_ref[...]
    gelu_branch, slope = gelu_parts(branch)
    state_low = state.astype(jnp.bfloat16).astype(jnp.float32)
    grad_state = (grad_mixed * gelu_branch).astype(jnp.bfloat16).astype(jnp.float32)
    grad_branch = (slope * grad_mixed * state_low).astype(jnp.bfloat16)
    decay, scale = decay_parts(rate, softness)
    total, carried = scan_block(shift_up(decay, 1, 1.0), grad_state, shift_up)
    carried = carried + total * carry[0:1, :]
    carry[0:1, :] = decay[0:1, :] * carried[0:1, :]
    index = lax.broadcasted_iota(jnp.int32, state.shape, 0)
    previous = jnp.where(index >= 1, pltpu.roll(state, 1, 0), state_before[7:8, :])
    conv = conv_low.astype(jnp.float32)
    grad_log = carried * previous * decay - carried * gate * conv * decay * decay / scale
    log_rate = grad_log * rate
    pre_a = -8.0 * softness * log_rate * (1.0 - rate)
    pre_x = carried * scale * conv * gate * (1.0 - gate)
    low_a = pre_a.astype(jnp.bfloat16)
    low_x = pre_x.astype(jnp.bfloat16)
    grad_a_ref[...] += matmul_tn(conv_low, low_a)
    grad_x_ref[...] += matmul_tn(conv_low, low_x)
    grad_conv = (
        carried * scale * gate
        + matmul_nt(low_a, gate_a_ref[...])
        + matmul_nt(low_x, gate_x_ref[...])
    )
    window[pl.ds(0, 8), :] = feed_before
    window[pl.ds(8, rows), :] = feed.astype(jnp.float32)
    later[pl.ds(rows, 8), :] = later[pl.ds(0, 8), :]
    later[pl.ds(0, rows), :] = grad_conv
    grad_feed = vectors_ref[0:1, :] * grad_conv
    sums_ref[0:1, :] += jnp.sum(grad_conv * window[pl.ds(8, rows), :], axis=0, keepdims=True)
    for k in range(1, 4):
        grad_feed = grad_feed + vectors_ref[k : k + 1, :] * later[pl.ds(k, rows), :]
        sums_ref[k : k + 1, :] += jnp.sum(
            grad_conv * window[pl.ds(8 - k, rows), :], axis=0, keepdims=True
        )
    sums_ref[4:5, :] += jnp.sum(grad_conv, axis=0, keepdims=True)
    sums_ref[5:6, :] += jnp.sum(pre_a, axis=0, keepdims=True)
    sums_ref[6:7, :] += jnp.sum(pre_x, axis=0, keepdims=True)
    sums_ref[7:8, :] += jnp.sum(log_rate, axis=0, keepdims=True)
    return grad_branch, grad_feed.astype(jnp.bfloat16)


def rec_backward_body(
    grad_mixed_ref, branch_ref, feed_ref, feed_before_ref, conv_ref, rate_ref, input_ref,
    state_ref, state_before_ref, vectors_ref, softness_ref, gate_a_ref, gate_x_ref,
    grad_branch_ref, grad_feed_ref, grad_a_ref, grad_x_ref, sums_ref, window, later, carry,
):
    step = pl.program_id(0)

    @pl.when(step == 0)
    def _():
        for ref in (later, carry, grad_a_ref, grad_x_ref, sums_ref):
            ref[...] = jnp.zeros_like(ref)

    keep = jnp.where(step == pl.num_programs(0) - 1, 0.0, 1.0)
    for s in range(feed_ref.shape[0]):
        before = feed_before_ref[s].astype(jnp.float32)
        grad_branch_ref[s], grad_feed_ref[s] = rec_backward_rows(
            grad_mixed_ref[s], branch_ref[s], feed_ref[s], before[before.shape[0] - 8 :] * keep, conv_ref[s],
            rate_ref[s], input_ref[s], state_ref[s], state_before_ref[s] * keep,
            vectors_ref, softness_ref, gate_a_ref, gate_x_ref, grad_a_ref, grad_x_ref, sums_ref,
            window.at[s], later.at[s], carry.at[s],
        )


def whole(shape):
    return pl.BlockSpec(shape, lambda i: (0,) * len(shape))


def rec_forward(feed, branch, vectors, softness, gate_a, gate_x):
    seqs, seq_len, channels = feed.shape
    rows = pick_rows(seq_len)
    block = pl.BlockSpec((seqs, rows, channels), lambda i: (0, i, 0))
    full = jax.ShapeDtypeStruct(feed.shape, jnp.float32)
    low = jax.ShapeDtypeStruct(feed.shape, jnp.bfloat16)
    return pl.pallas_call(
        rec_forward_body,
        grid=(seq_len // rows,),
        in_specs=[block, block]
        + [whole(v.shape) for v in (vectors, softness, gate_a, gate_x)],
        out_specs=[block] * 5,
        out_shape=[low, full, full, full, low],
        scratch_shapes=[
            pltpu.VMEM((seqs, rows + 8, channels), jnp.float32),
            pltpu.VMEM((seqs, 8, channels), jnp.float32),
        ],
        compiler_params=pltpu.CompilerParams(vmem_limit_bytes=40 << 20),
        name="rec_forward",
    )(feed, branch, vectors, softness, gate_a, gate_x)


def rec_backward(grad_mixed, branch, feed, conv, rate, gate, state, vectors, softness, gate_a, gate_x):
    seqs, seq_len, channels = feed.shape
    rows = pick_rows(seq_len)
    blocks = seq_len // rows
    block = pl.BlockSpec((seqs, rows, channels), lambda i: (0, blocks - 1 - i, 0))

    def ahead(by):
        return pl.BlockSpec(
            (seqs, by, channels),
            lambda i: (0, jnp.maximum((blocks - 1 - i) * (rows // by) - 1, 0), 0),
        )

    low = jax.ShapeDtypeStruct(feed.shape, jnp.bfloat16)
    square = jax.ShapeDtypeStruct((channels, channels), jnp.float32)
    return pl.pallas_call(
        rec_backward_body,
        grid=(blocks,),
        in_specs=[block, block, block, ahead(16), block, block, block, block, ahead(8)]
        + [whole(v.shape) for v in (vectors, softness, gate_a, gate_x)],
        out_specs=[block, block, whole((channels, channels)), whole((channels, channels)), whole((8, channels))],
        out_shape=[low, low, square, square, jax.ShapeDtypeStruct((8, channels), jnp.float32)],
        scratch_shapes=[
            pltpu.VMEM((seqs, rows + 8, channels), jnp.float32),
            pltpu.VMEM((seqs, rows + 8, channels), jnp.float32),
            pltpu.VMEM((seqs, 8, channels), jnp.float32),
        ],
        compiler_params=pltpu.CompilerParams(vmem_limit_bytes=40 << 20),
        name="rec_backward",
    )(grad_mixed, branch, feed, feed, conv, rate, gate, state, state, vectors, softness, gate_a, gate_x)


def line_place():
    return lax.axis_size("grp") // 2, lax.axis_index("grp") // 2, lax.axis_index("grp") % 2


def greet_line():
    chips, chip, core = line_place()
    barrier = pltpu.get_barrier_semaphore()

    def signal(place):
        pl.semaphore_signal(barrier, inc=1, device_id={"grp": place}, device_id_type=MESH)

    signal(chip * 2 + 1 - core)

    @pl.when(chip > 0)
    def _():
        signal(chip * 2 + core - 2)

    @pl.when(chip < chips - 1)
    def _():
        signal(chip * 2 + core + 2)

    ends = (chip == 0).astype(jnp.int32) + (chip == chips - 1).astype(jnp.int32)
    pl.semaphore_wait(barrier, 3 - ends)


def greet_axes(axes):
    barrier = pltpu.get_barrier_semaphore()
    for axis in axes:
        size = lax.axis_size(axis)
        for k in range(1, size):
            pl.semaphore_signal(
                barrier,
                inc=1,
                device_id={axis: lax.rem(lax.axis_index(axis) + k, size)},
                device_id_type=MESH,
            )
    pl.semaphore_wait(barrier, sum(lax.axis_size(axis) - 1 for axis in axes))


class Gather:
    def __init__(self, sources, outs, rows, send_sem, recv_sem, own_sem):
        self.chips, self.chip, self.core = line_place()
        self.me = self.chip * 2 + self.core
        self.sources, self.outs, self.rows = sources, outs, rows
        self.send_sem, self.recv_sem, self.own_sem = send_sem, recv_sem, own_sem

    def slot(self, p, origin):
        return self.outs[p].at[pl.ds(pl.multiple_of(origin * self.rows, self.rows), self.rows), :]

    def copy(self, p, source, origin, target, way):
        return pltpu.make_async_remote_copy(
            src_ref=source,
            dst_ref=self.slot(p, origin),
            send_sem=self.send_sem.at[way, p, origin],
            recv_sem=self.recv_sem.at[p, origin],
            device_id={"grp": target},
            device_id_type=MESH,
        )

    def to_right(self, p, source, origin):
        return self.copy(p, source, origin, self.me + 2, 0)

    def to_left(self, p, source, origin):
        return self.copy(p, source, origin, self.me - 2, 1)

    def to_partner(self, p, source, origin):
        return self.copy(p, source, origin, self.chip * 2 + 1 - self.core, 2)

    def own(self, p):
        return pltpu.make_async_copy(self.sources[p], self.slot(p, self.me), self.own_sem.at[p])

    def start(self, p):
        source = self.sources[p]

        @pl.when(self.chip < self.chips - 1)
        def _():
            self.to_right(p, source, self.me).start()

        @pl.when(self.chip > 0)
        def _():
            self.to_left(p, source, self.me).start()

        self.to_partner(p, source, self.me).start()
        self.own(p).start()

    def hop(self, p, h):
        left_origin = self.me - 2 - 2 * h
        right_origin = self.me + 2 + 2 * h

        @pl.when(self.chip - 1 - h >= 0)
        def _():
            here = self.slot(p, left_origin)
            self.to_right(p, here, left_origin).wait_recv()

            @pl.when(self.chip < self.chips - 1)
            def _():
                self.to_right(p, here, left_origin).start()

            self.to_partner(p, here, left_origin).start()

        @pl.when(self.chip + 1 + h <= self.chips - 1)
        def _():
            here = self.slot(p, right_origin)
            self.to_left(p, here, right_origin).wait_recv()

            @pl.when(self.chip > 0)
            def _():
                self.to_left(p, here, right_origin).start()

            self.to_partner(p, here, right_origin).start()

    def finish(self, p):
        for c in range(self.chips):
            origin = c * 2 + 1 - self.core
            self.to_partner(p, self.slot(p, origin), origin).wait_recv()
        self.own(p).wait()
        for c in range(self.chips):
            origin = c * 2 + self.core
            here = self.slot(p, origin)
            self.to_partner(p, here, origin).wait_send()

            @pl.when((c <= self.chip) & (self.chip < self.chips - 1))
            def _():
                self.to_right(p, here, origin).wait_send()

            @pl.when((c >= self.chip) & (self.chip > 0))
            def _():
                self.to_left(p, here, origin).wait_send()


def gather_sems(pieces):
    n = lax.axis_size("grp")
    return [
        pltpu.SemaphoreType.DMA((3, pieces, n)),
        pltpu.SemaphoreType.DMA((pieces, n)),
        pltpu.SemaphoreType.DMA((pieces,)),
    ]


class Scatter:
    def __init__(self, rows, part, out, swap_in, line_in, send_sem, recv_sem):
        self.chips, self.chip, self.core = line_place()
        self.me = self.chip * 2 + self.core
        self.rows, self.part, self.out = rows, part, out
        self.swap_in, self.line_in = swap_in, line_in
        self.send_sem, self.recv_sem = send_sem, recv_sem

    def copy(self, dest, place, way, slot, p):
        return pltpu.make_async_remote_copy(
            src_ref=self.out.at[p, slot],
            dst_ref=dest,
            send_sem=self.send_sem.at[way, p, slot],
            recv_sem=self.recv_sem.at[way, p, slot],
            device_id={"grp": place},
            device_id_type=MESH,
        )

    def swap(self, p, c):
        return self.copy(self.swap_in.at[p, c], self.chip * 2 + 1 - self.core, 0, c, p)

    def right(self, p, c):
        return self.copy(self.line_in.at[p, c], self.me + 2, 1, c, p)

    def left(self, p, c):
        slot = jnp.where(c == self.chip - 1, self.chips, c)
        return self.copy(self.line_in.at[p, slot], self.me - 2, 2, c, p)

    def from_right(self, p, c):
        slot = jnp.where(c == self.chip, self.chips, c)
        return self.copy(self.line_in.at[p, slot], self.me + 2, 2, c, p)

    def fill(self, p, s, lefts, rights, transposed, width=512):
        def rows_of(ref, core):
            at = [pl.multiple_of((c * 2 + core) * self.rows, self.rows) for c in range(self.chips)]
            return jnp.concatenate([ref[s, pl.ds(a, self.rows), :] for a in at], axis=0)

        def product(core, store):
            chosen = [rows_of(ref, core) for ref in lefts]

            @pl.loop(0, self.out.shape[-1] // width)
            def _(j):
                columns = pl.ds(pl.multiple_of(j * width, width), width)
                total = None
                for left, right in zip(chosen, rights):
                    term = matmul_nt(left, right[columns, :]) if transposed else matmul(left, right[:, columns])
                    total = term if total is None else total + term
                for c in range(self.chips):
                    store(c, columns, total[c * self.rows : (c + 1) * self.rows])

        def to_out(c, columns, value):
            self.out[p, c, :, columns] = value.astype(jnp.bfloat16)

        def to_part(c, columns, value):
            self.part[p, c, :, columns] = value

        def partners():
            product(1 - self.core, to_out)
            for c in range(self.chips):
                self.swap(p, c).start()

        def own():
            product(self.core, to_part)

        return partners, own

    def own(self, p, c):
        self.swap(p, c).wait_recv()
        return self.part[p, c] + self.swap_in[p, c].astype(jnp.float32)

    def hop(self, p, t):
        last = self.chips - 1

        def send(c, first, arrival, onward):
            self.swap(p, c).wait_send()
            total = self.own(p, c)

            @pl.when(first)
            def _():
                self.out[p, c] = total.astype(jnp.bfloat16)

            @pl.when(jnp.logical_not(first))
            def _():
                arrival(p, c).wait_recv()
                self.out[p, c] = (total + self.line_in[p, c].astype(jnp.float32)).astype(jnp.bfloat16)

            onward(p, c).start()

        @pl.when(self.chip <= t)
        def _():
            send(last - t + self.chip, self.chip == 0, self.right, self.right)

        @pl.when(last - self.chip <= t)
        def _():
            send(t - last + self.chip, self.chip == last, self.from_right, self.left)

    def result(self, p):
        chip = self.chip
        self.part[p, chip] = self.own(p, chip)

        @pl.when(chip > 0)
        def _():
            self.right(p, chip).wait_recv()
            self.part[p, chip] += self.line_in[p, chip].astype(jnp.float32)

        @pl.when(chip < self.chips - 1)
        def _():
            self.from_right(p, chip).wait_recv()
            self.part[p, chip] += self.line_in[p, self.chips].astype(jnp.float32)

        return self.part.at[p, chip]

    def finish(self, p):
        self.swap(p, self.chip).wait_send()
        for c in range(self.chips):

            @pl.when(c > self.chip)
            def _():
                self.right(p, c).wait_send()

            @pl.when(c < self.chip)
            def _():
                self.left(p, c).wait_send()


def scatter_scratch(pieces, rows, width):
    chips = lax.axis_size("grp") // 2
    return [
        pltpu.VMEM((pieces, chips, rows, width), jnp.float32),
        pltpu.VMEM((pieces, chips, rows, width), jnp.bfloat16),
        pltpu.VMEM((pieces, chips, rows, width), jnp.bfloat16),
        pltpu.VMEM((pieces, chips + 1, rows, width), jnp.bfloat16),
        pltpu.SemaphoreType.DMA((3, pieces, chips)),
        pltpu.SemaphoreType.DMA((3, pieces, chips)),
    ]


in_vmem = pl.BlockSpec(memory_space=pltpu.VMEM)
in_hbm = pl.BlockSpec(memory_space=pl.ANY)


def call(body, name, number, inputs, in_specs, outs, out_specs, scratch, us):
    return pl.pallas_call(
        body,
        in_specs=in_specs,
        out_specs=out_specs,
        out_shape=outs,
        scratch_shapes=scratch,
        name=name,
        cost_estimate=pl.CostEstimate(
            flops=us * 1000000000, bytes_accessed=us * 3000000, transcendentals=0
        ),
        compiler_params=pltpu.CompilerParams(
            collective_id=number, has_side_effects=True, vmem_limit_bytes=62 << 20
        ),
    )(*inputs)


class Exchange:
    def __init__(self, axis, source, slot, send_sem, recv_sem, steps=None, first=1):
        self.axis, self.source, self.slot, self.steps, self.first = axis, source, slot, steps, first
        self.size, self.me = lax.axis_size(axis), lax.axis_index(axis)
        self.send_sem, self.recv_sem = send_sem, recv_sem

    def copy(self, k, owner):
        peer = lax.rem(self.me + k, self.size)
        return pltpu.make_async_remote_copy(
            src_ref=self.source(peer),
            dst_ref=self.slot(owner) if self.slot else self.steps.at[k - self.first],
            send_sem=self.send_sem.at[k],
            recv_sem=self.recv_sem.at[k],
            device_id={self.axis: peer},
            device_id_type=MESH,
        )

    def own(self):
        slot = self.slot(self.me) if self.slot else self.steps.at[0]
        return pltpu.make_async_copy(self.source(self.me), slot, self.send_sem.at[0])

    def start(self):
        self.own().start()
        self.start_others()

    def start_others(self):
        for k in range(1, self.size):
            self.copy(k, self.me).start()

    def finish(self):
        self.own().wait()
        self.finish_others()

    def finish_others(self):
        for k in range(1, self.size):
            self.copy(k, lax.rem(self.me - k + self.size, self.size)).wait_recv()
        for k in range(1, self.size):
            self.copy(k, self.me).wait_send()


def sum_of(slots):
    total = slots[0]
    for k in range(1, slots.shape[0]):
        total = total + slots[k]
    return total


def block(ref, axis, parts):
    size = ref.shape[axis] // parts

    def view(k):
        at = pl.ds(pl.multiple_of(k * size, size), size)
        return ref.at[at, :] if axis == 0 else ref.at[:, at]

    return view


def weight_gathers(axes, sources, outs, send_sem, recv_sem):
    parts = lax.axis_size("seq")
    return [
        Exchange(
            "seq", lambda k, ref=source: ref, block(out, axis, parts), send_sem.at[i], recv_sem.at[i]
        )
        for i, (axis, source, out) in enumerate(zip(axes, sources, outs))
    ]


def weight_sums(axes, sources, outs, send_sem, recv_sem, first=1):
    parts = lax.axis_size("seq")
    return [
        Exchange(
            "seq", block(source, axis, parts), None, send_sem.at[i], recv_sem.at[i], out, first
        )
        for i, (axis, source, out) in enumerate(zip(axes, sources, outs))
    ]


def seq_sems(count):
    return [pltpu.SemaphoreType.DMA((count, lax.axis_size("seq")))] * 2


def gathered(block_of, axis):
    shape = list(block_of.shape)
    shape[axis] *= lax.axis_size("seq")
    return jax.ShapeDtypeStruct(shape, block_of.dtype)


def slots_of(matrix, axis, first=1):
    shape = list(matrix.shape)
    size = lax.axis_size("seq")
    shape[axis] //= size
    return jax.ShapeDtypeStruct((size - first, *shape), matrix.dtype)


weight_axes = (0, 0, 1)
mixer_axes = (1, 1, 1)


def views(ref):
    return [ref.at[s] for s in range(ref.shape[0])]


def first_body(x_ref, grad_ref, pack_ref, w0, w1, w2, later_ref, full_ref, params_ref, gains_ref, o0, o1, o2, *refs):
    small_send, small_recv, gain_send, gain_recv, weight_send, weight_recv = refs[3:]
    greet_axes(("seq", "grp"))
    seqs = x_ref.shape[0]
    gather = Gather(views(x_ref), views(full_ref), x_ref.shape[1], *refs[:3])
    weights = weight_gathers(mixer_axes, (w0, w1, w2), (o0, o1, o2), weight_send, weight_recv)
    small = Exchange("seq", lambda k: pack_ref, lambda k: params_ref.at[k], small_send, small_recv)
    small.start()
    for s in range(seqs):
        gather.start(s)
    for weight in weights:
        weight.start()
    later_ref[...] = grad_ref[...]
    small.finish()
    place = lax.axis_index("grp")
    for owner in range(small.size):
        gains_ref[place, owner] = params_ref[owner, pl.ds(pack_ref.shape[0] - 8, 8), :]
    gains = Exchange("grp", lambda k: gains_ref.at[place], lambda k: gains_ref.at[k], gain_send, gain_recv)
    gains.start_others()
    for h in range(gather.chips - 1):
        for s in range(seqs):
            gather.hop(s, h)
    gains.finish_others()
    for weight in weights:
        weight.finish()
    for s in range(seqs):
        gather.finish(s)


def gather_first(layer_in, out_grad, pack, weights):
    seqs, rows, width = layer_in.shape
    n, size = lax.axis_size("grp"), lax.axis_size("seq")
    return call(
        first_body, "gather_first", 1,
        (layer_in, out_grad, pack, *weights), [in_vmem] * 6,
        [
            jax.ShapeDtypeStruct(out_grad.shape, out_grad.dtype),
            jax.ShapeDtypeStruct((seqs, n * rows, width), jnp.bfloat16),
            jax.ShapeDtypeStruct((size,) + pack.shape, jnp.float32),
            jax.ShapeDtypeStruct((n, size, 8, 128), jnp.float32),
        ]
        + [gathered(w, axis) for w, axis in zip(weights, mixer_axes)],
        [in_vmem, in_hbm] + [in_vmem] * 2 + [in_hbm] * 3,
        gather_sems(seqs)
        + [pltpu.SemaphoreType.DMA((size,))] * 2
        + [pltpu.SemaphoreType.DMA((n,))] * 2
        + seq_sems(3),
        70,
    )


def mean_of(values):
    return jnp.mean(values, axis=-1, keepdims=True)


def sum_then_gather(scatter, gather, fills, stores, count=0, between=None, after=()):
    hops = range(1, scatter.chips - 1)
    for step in fills[0]:
        step()
    scatter.hop(0, 0)
    for p, store in enumerate(stores):
        ahead = list(fills[p + 1] if p + 1 < len(fills) else after)
        for h in hops:
            if ahead:
                ahead.pop(0)()
            scatter.hop(p, h)
            if 0 < p <= count:
                gather.hop(p - 1, h - 1)
        for step in ahead:
            step()
        if p + 1 < len(fills):
            scatter.hop(p + 1, 0)
        if between and p == 0:
            between()
        store()
        if p < count:
            gather.start(p)
        if 0 < p <= count:
            gather.hop(p - 1, gather.chips - 2)
    if count == len(stores):
        for h in range(gather.chips - 1):
            gather.hop(count - 1, h)
    for p in range(count):
        gather.finish(p)
    for p in range(len(fills)):
        scatter.finish(p)


def out_body(hidden_ref, down_w_ref, residual_ref, layer_out_ref, scatter, first):
    def fill(s):
        return scatter.fill(first + s, s, [hidden_ref], [down_w_ref], False)

    def store(s):
        layer_out_ref[s] = (residual_ref[s] + scatter.result(first + s)[...]).astype(jnp.bfloat16)

    return fill, store


def mixer_out_body(mixed_ref, out_w_ref, x_ref, gain_ref, w0, w1, w2, residual_ref, normed_ref, o0, o1, o2, low_ref, *refs):
    greet_axes(("seq", "grp"))
    seqs, rows, _ = x_ref.shape
    weights = weight_gathers(weight_axes, (w0, w1, w2), (o0, o1, o2), *refs[:2])
    for weight in weights:
        weight.start()
    gather = Gather(views(low_ref), views(normed_ref), rows, *refs[2:5])
    scatter = Scatter(rows, *refs[5:])

    def fill(s):
        return scatter.fill(s, s, [mixed_ref], [out_w_ref], False)

    def store(s):
        residual = x_ref[s].astype(jnp.float32) + scatter.result(s)[...]
        residual_ref[s] = residual
        normal = residual * lax.rsqrt(mean_of(residual * residual) + epsilon)
        low_ref[s] = (normal * gain_ref[...]).astype(jnp.bfloat16)

    sum_then_gather(
        scatter, gather, [fill(s) for s in range(seqs)], [functools.partial(store, s) for s in range(seqs)], seqs
    )
    for weight in weights:
        weight.finish()


def mixer_out(mixed, out_w, layer_in, gain, weights):
    seqs, rows, width = layer_in.shape
    full = jax.ShapeDtypeStruct((seqs, lax.axis_size("grp") * rows, width), jnp.bfloat16)
    return call(
        mixer_out_body, "mixer_out", 2,
        (mixed, out_w, layer_in, gain, *weights), [in_vmem] * 7,
        [jax.ShapeDtypeStruct(layer_in.shape, jnp.float32), full]
        + [gathered(w, axis) for w, axis in zip(weights, weight_axes)],
        [in_vmem] + [in_hbm] * 4,
        [pltpu.VMEM(layer_in.shape, jnp.bfloat16)]
        + seq_sems(3)
        + gather_sems(seqs)
        + scatter_scratch(seqs, rows, width),
        100,
    )


def mixer_forward_body(
    x_full_ref, gains_ref, branch_w_ref, rec_w_ref, out_w_ref, vectors_ref, softness_ref, gate_a_ref, gate_x_ref,
    grad_ref, w0, w1, w2,
    normed_one_ref, branch_ref, feed_ref, conv_ref, rate_ref, input_ref, state_ref, mixed_ref, residual_ref,
    normed_ref, grads_ref, o0, o1, o2, low_ref, window, carry, *refs,
):
    greet_axes(("seq", "grp"))
    seqs, seq_len, _ = x_full_ref.shape
    rows = grad_ref.shape[1]
    me = lax.axis_index("grp")
    weights = weight_gathers(weight_axes, (w0, w1, w2), (o0, o1, o2), *refs[:2])
    gather = Gather(views(low_ref) + views(grad_ref), views(normed_ref) + views(grads_ref), rows, *refs[2:5])
    scatter = Scatter(rows, *refs[5:])
    for s in range(seqs):
        gather.start(seqs + s)
    for weight in weights:
        weight.start()
    tile = pick_rows(seq_len, (256, 192, 128, 96, 64, 32, 16))
    chunk = window.shape[0] - 8
    window[...] = jnp.zeros_like(window)

    def project(s):
        @pl.loop(0, seq_len // tile)
        def _(i):
            at = pl.ds(pl.multiple_of(i * tile, tile), tile)
            inputs = x_full_ref[s, at, :].astype(jnp.float32)
            normal = inputs * lax.rsqrt(mean_of(inputs * inputs) + epsilon)
            normed = (normal * gains_ref[0]).astype(jnp.bfloat16)
            normed_one_ref[s, at, :] = normed
            branch_ref[s, at, :] = matmul_nt(normed, branch_w_ref[...])
            feed_ref[s, at, :] = matmul_nt(normed, rec_w_ref[...]).astype(jnp.bfloat16)

    def recur(s):
        window[pl.ds(0, 8), :] = jnp.zeros((8, window.shape[1]), jnp.float32)
        carry[...] = jnp.zeros_like(carry)

        @pl.loop(0, seq_len // chunk)
        def _(i):
            at = pl.ds(pl.multiple_of(i * chunk, chunk), chunk)
            conv, rate, gate, state, mixed = rec_forward_rows(
                feed_ref[s, at, :], branch_ref[s, at, :], vectors_ref, softness_ref, gate_a_ref, gate_x_ref, window, carry
            )
            conv_ref[s, at, :] = conv
            rate_ref[s, at, :] = rate
            input_ref[s, at, :] = gate
            state_ref[s, at, :] = state
            mixed_ref[s, at, :] = mixed

    def late_hop(h):
        if h < gather.chips - 1:
            for s in range(seqs):
                gather.hop(seqs + s, h)

    def steps(s):
        partners, own = scatter.fill(s, s, [mixed_ref], [out_w_ref], False)
        late = [functools.partial(late_hop, h) for h in range(gather.chips - 1)]

        def second():
            if s == 0:
                late_hop(0)
            recur(s)

        def third():
            partners()
            if s == 0:
                late_hop(1)

        def fourth():
            own()
            if s == seqs - 1:
                for hop in late[2 if seqs > 1 else 1 :]:
                    hop()

        return [functools.partial(project, s), second, third, fourth]

    def store(s):
        own = x_full_ref[s, pl.ds(pl.multiple_of(me * rows, rows), rows), :]
        residual = own.astype(jnp.float32) + scatter.result(s)[...]
        residual_ref[s] = residual
        normal = residual * lax.rsqrt(mean_of(residual * residual) + epsilon)
        low_ref[s] = (normal * gains_ref[1]).astype(jnp.bfloat16)

    sum_then_gather(
        scatter, gather, [steps(s) for s in range(seqs)], [functools.partial(store, s) for s in range(seqs)], seqs
    )
    for s in range(seqs):
        gather.finish(seqs + s)
    for weight in weights:
        weight.finish()


def mixer_forward(x_full, gains, branch_w, rec_w, out_w, vectors, softness, gate_a, gate_x, out_grad, weights):
    seqs, seq_len, width = x_full.shape
    rows, channels = out_grad.shape[1], vectors.shape[1]
    low = jax.ShapeDtypeStruct((seqs, seq_len, channels), jnp.bfloat16)
    full = jax.ShapeDtypeStruct((seqs, seq_len, channels), jnp.float32)
    outs = [x_full, full, low, low, full, full, full, low]
    outs += [jax.ShapeDtypeStruct(out_grad.shape, jnp.float32), x_full, x_full]
    outs = [jax.ShapeDtypeStruct(out.shape, out.dtype) for out in outs]
    outs += [gathered(w, axis) for w, axis in zip(weights, weight_axes)]
    return call(
        mixer_forward_body, "mixer_forward", 2,
        (x_full, gains, branch_w, rec_w, out_w, vectors, softness, gate_a, gate_x, out_grad, *weights),
        [in_vmem] * 13,
        outs, [in_vmem] * 9 + [in_hbm] * 5,
        [
            pltpu.VMEM(out_grad.shape, jnp.bfloat16),
            pltpu.VMEM((pick_rows(seq_len) + 8, channels), jnp.float32),
            pltpu.VMEM((8, channels), jnp.float32),
        ]
        + seq_sems(3)
        + gather_sems(2 * seqs)
        + scatter_scratch(seqs, rows, width),
        130,
    )


def mlp_back_body(
    with_out, gate_ref, up_ref, gate_w_ref, up_w_ref, residual_ref, grad_ref, gain_ref, w0, w1, w2, *refs
):
    if with_out:
        hidden_ref, down_w_ref = refs[:2]
        refs = refs[2:]
    grad_residual_ref, gain_grad_ref, full_ref, o0, o1, o2 = refs[:6]
    refs = refs[6:]
    if with_out:
        layer_out_ref, late_ref = refs[:2]
        refs = refs[2:]
    low_ref, *refs = refs
    greet_axes(("seq", "grp"))
    seqs, rows, _ = grad_ref.shape
    sums = weight_sums(weight_axes, (w0, w1, w2), (o0, o1, o2), *refs[:2])
    for weight in sums:
        weight.start_others()
    gather = Gather(views(low_ref), views(full_ref), rows, *refs[2:5])
    scatter = Scatter(rows, *refs[5:])
    gain_grad_ref[...] = jnp.zeros_like(gain_grad_ref)

    def fill(s):
        return scatter.fill(s, s, [gate_ref, up_ref], [gate_w_ref, up_w_ref], True)

    def store(s):
        term = scatter.result(s)[...]
        residual = residual_ref[s]
        inverse = lax.rsqrt(mean_of(residual * residual) + epsilon)
        normal = residual * inverse
        gain_grad_ref[0:1, :] += jnp.sum(term * normal, axis=0, keepdims=True)
        grad = grad_ref[s].astype(jnp.float32) + norm_back(term, normal, inverse, gain_ref[...])
        grad_residual_ref[s] = grad
        low_ref[s] = grad.astype(jnp.bfloat16)

    fills = [fill(s) for s in range(seqs)]
    stores = [functools.partial(store, s) for s in range(seqs)]
    if with_out:
        fill_out, store_out = out_body(hidden_ref, down_w_ref, residual_ref, layer_out_ref, scatter, seqs)
        fills += [fill_out(s) for s in range(seqs - 1)]
        stores += [functools.partial(store_out, s) for s in range(seqs - 1)]

    def late():
        step = 256

        @pl.loop(0, late_ref.shape[0] // step)
        def _(i):
            at = pl.ds(pl.multiple_of(i * step, step), step)
            late_ref[at, :] = matmul(hidden_ref[seqs - 1, at, :], down_w_ref[...]).astype(jnp.bfloat16)

    sum_then_gather(scatter, gather, fills, stores, seqs, after=(late,) if with_out else ())
    for weight in sums:
        weight.finish_others()


def mlp_back(grad_gate, grad_up, gate_w, up_w, residual, out_grad, gain, grads, out_inputs):
    seqs, rows, width = residual.shape
    outs = [
        jax.ShapeDtypeStruct(residual.shape, jnp.float32),
        jax.ShapeDtypeStruct((8, width), jnp.float32),
        jax.ShapeDtypeStruct((seqs, lax.axis_size("grp") * rows, width), jnp.bfloat16),
    ]
    outs += [slots_of(grad, axis) for grad, axis in zip(grads, weight_axes)]
    out_specs = [in_vmem] * 2 + [in_hbm] * 4
    if out_inputs:
        outs.append(jax.ShapeDtypeStruct((seqs - 1, rows, width), jnp.bfloat16))
        outs.append(jax.ShapeDtypeStruct((lax.axis_size("grp") * rows, width), jnp.bfloat16))
        out_specs += [in_vmem] * 2
    return call(
        functools.partial(mlp_back_body, bool(out_inputs)), "mlp_back", 3,
        (grad_gate, grad_up, gate_w, up_w, residual, out_grad, gain, *grads, *out_inputs),
        [in_vmem] * 7 + [in_hbm] * 3 + [in_vmem] * len(out_inputs),
        outs, out_specs,
        [pltpu.VMEM(residual.shape, jnp.bfloat16)]
        + seq_sems(3)
        + gather_sems(seqs)
        + scatter_scratch(seqs * 2 - 1 if out_inputs else seqs, rows, width),
        120,
    )


def last_body(
    branch_ref, feed_ref, branch_w_ref, rec_w_ref, x_ref, grad_ref, gain_ref, gain_two_ref, rec_ref,
    w0, w1, w2, *refs,
):
    grad_x_ref, rec_sum_ref, gain_sum_ref, o0, o1, o2 = refs[:6]
    refs = refs[6:]
    rec_slots, gain_local, gain_part, gain_slots, part_slots = refs[:5]
    rec_sems, gain_sems, part_sems = refs[5:7], refs[7:9], refs[9:11]
    greet_axes(("seq", "grp"))
    seqs, rows, _ = x_ref.shape
    sums = weight_sums(mixer_axes, (w0, w1, w2), (o0, o1, o2), *refs[11:13])
    scatter = Scatter(rows, *refs[13:])
    rec = Exchange("seq", lambda k: rec_ref.at[k], lambda k: rec_slots.at[k], *rec_sems)
    rec.start()
    for weight in sums:
        weight.start_others()
    gain_local[...] = jnp.zeros_like(gain_local)
    gain_local[1:2, :] = gain_two_ref[0:1, :]

    def fill(s):
        return scatter.fill(s, s, [branch_ref, feed_ref], [branch_w_ref, rec_w_ref], False)

    across = Exchange(
        "seq", block(gain_local, 1, lax.axis_size("seq")), lambda k: gain_slots.at[k], *gain_sems
    )

    def store(s):
        term = scatter.result(s)[...]
        inputs = x_ref[s].astype(jnp.float32)
        inverse = lax.rsqrt(mean_of(inputs * inputs) + epsilon)
        normal = inputs * inverse
        gain_local[0:1, :] += jnp.sum(term * normal, axis=0, keepdims=True)
        if s == seqs - 1:
            across.start()
        grad_x_ref[s] = grad_ref[s] + norm_back(term, normal, inverse, gain_ref[...])

    sum_then_gather(
        scatter, None, [fill(s) for s in range(seqs)], [functools.partial(store, s) for s in range(seqs)]
    )
    across.finish()
    gain_part[...] = sum_of(gain_slots)
    along = Exchange("grp", lambda k: gain_part, lambda k: part_slots.at[k], *part_sems)
    along.start()
    rec.finish()
    rec_sum_ref[...] = sum_of(rec_slots)
    for weight in sums:
        weight.finish_others()
    along.finish()
    gain_sum_ref[...] = sum_of(part_slots)


def last(grad_branch, grad_feed, branch_w, rec_w, layer_in, grad_residual, gain, gain_two_grad, rec_blocks, grads):
    seqs, rows, width = layer_in.shape
    size, n = lax.axis_size("seq"), lax.axis_size("grp")
    f32 = jnp.float32
    inputs = (grad_branch, grad_feed, branch_w, rec_w, layer_in, grad_residual, gain, gain_two_grad, rec_blocks)
    outs = [
        jax.ShapeDtypeStruct(layer_in.shape, f32),
        jax.ShapeDtypeStruct(rec_blocks.shape[1:], f32),
        jax.ShapeDtypeStruct((8, width // size), f32),
    ]
    outs += [slots_of(grad, axis) for grad, axis in zip(grads, mixer_axes)]
    out_specs = [in_vmem] * 3 + [in_hbm] * 3
    return call(
        last_body, "last", 4,
        inputs + tuple(grads), [in_vmem] * len(inputs) + [in_hbm] * 3,
        outs, out_specs,
        [
            pltpu.VMEM(rec_blocks.shape, f32),
            pltpu.VMEM((8, width), f32),
            pltpu.VMEM((8, width // size), f32),
            pltpu.VMEM((size, 8, width // size), f32),
            pltpu.VMEM((n, 8, width // size), f32),
        ]
        + [pltpu.SemaphoreType.DMA((size,))] * 4
        + [pltpu.SemaphoreType.DMA((n,))] * 2
        + seq_sems(3)
        + scatter_scratch(seqs, rows, width),
        80,
    )


def copies(pairs, sem):
    return [pltpu.make_async_copy(source, buffer, sem.at[i]) for i, (source, buffer) in enumerate(pairs)]


def head_windows(heads, head_dim, parts):
    part = head_dim // parts
    rows = max(-(-(k + 1) * part // 8) * 8 - k * part // 8 * 8 for k in range(parts))

    def start(h, k):
        return pl.multiple_of(h * head_dim + k * part // 8 * 8, 8)

    return rows, start


def mixer_back_body(
    heads, low_in, out_w_in, branch_in, feed_in, conv_in, rate_in, input_in, state_in, mixed_in, branch_w_in, rec_w_in,
    normed_in, vectors_ref, softness_ref, gate_a_ref, gate_x_ref, x_ref, grad_ref, gain_ref, gain_two_ref,
    grad_x_ref, squares_out_ref, sums_out_ref, gain_sum_ref, o0, o1, o2,
    low_ref, out_w_ref, branch_ref, feed_ref, conv_ref, rate_ref, input_ref, state_ref, mixed_ref, branch_w_ref,
    rec_w_ref, grad_mixed, grad_branch, grad_feed, squares, sums, window, later, carry, tiles, d0, d1, d2,
    square_slots, sum_slots_ref, gain_local, gain_part, gain_slots, part_slots, load_sem, tile_sem,
    square_send, square_recv, sum_send, sum_recv, gain_send, gain_recv, part_send, part_recv, weight_send, weight_recv,
    *refs,
):
    seqs, rows, width = x_ref.shape
    seq_len, channels = feed_ref.shape[1:]
    per_seq = (
        (low_in, low_ref), (branch_in, branch_ref), (feed_in, feed_ref), (conv_in, conv_ref), (rate_in, rate_ref),
        (input_in, input_ref), (state_in, state_ref),
    )
    pairs = [(out_w_in, out_w_ref)]
    for s in range(seqs):
        pairs += [(source.at[s], buffer.at[s]) for source, buffer in per_seq]
        if s == 0:
            pairs += [(branch_w_in, branch_w_ref), (rec_w_in, rec_w_ref)]
    pairs += [(mixed_in, mixed_ref)]
    loads = copies(pairs, load_sem)
    for load in loads:
        load.start()
    greet_axes(("seq", "grp"))
    scatter = Scatter(rows, *refs)
    parts = lax.axis_size("seq")
    for ref in (squares, sums, gain_local):
        ref[...] = jnp.zeros_like(ref)
    gain_local[1:2, :] = gain_two_ref[0:1, :]
    window_rows, start_of = head_windows(heads, channels // heads, parts)
    square_moves = [
        Exchange(
            "seq",
            lambda k, h=h: squares.at[:, pl.ds(start_of(h, k), window_rows), :],
            lambda k, h=h: square_slots.at[k, h],
            square_send.at[h],
            square_recv.at[h],
        )
        for h in range(heads)
    ]
    sum_move = Exchange("seq", lambda k: sums, lambda k: sum_slots_ref.at[k], sum_send, sum_recv)
    across = Exchange("seq", block(gain_local, 1, parts), lambda k: gain_slots.at[k], gain_send, gain_recv)
    moves = weight_sums(mixer_axes, (d0, d1, d2), (o0, o1, o2), weight_send, weight_recv, 0)
    tile_rows = pick_rows(seq_len, (256, 192, 128, 96, 64, 32, 16))
    chunk = window.shape[0] - 8

    def mix(s):
        if s == 0:
            for load in loads[: 1 + len(per_seq)]:
                load.wait()
        else:
            first = 3 + s * len(per_seq)
            for load in loads[first : first + len(per_seq)]:
                load.wait()

        @pl.loop(0, seq_len // tile_rows)
        def _(i):
            at = pl.ds(pl.multiple_of(i * tile_rows, tile_rows), tile_rows)
            grad_mixed[at, :] = matmul_nt(low_ref[s, at, :], out_w_ref[...])

    def recur(s):
        carry[...] = jnp.zeros_like(carry)
        later[...] = jnp.zeros_like(later)
        blocks = seq_len // chunk

        @pl.loop(0, blocks)
        def _(i):
            first = (blocks - 1 - i) * chunk
            at = pl.ds(pl.multiple_of(first, chunk), chunk)
            keep = jnp.where(i == blocks - 1, 0.0, 1.0)
            before8 = pl.ds(pl.multiple_of(jnp.maximum(first - 8, 0), 8), 8)
            before16 = pl.ds(pl.multiple_of(jnp.maximum(first - 16, 0), 16), 16)
            grad_branch[s, at, :], grad_feed[s, at, :] = rec_backward_rows(
                grad_mixed[at, :], branch_ref[s, at, :], feed_ref[s, at, :],
                feed_ref[s, before16, :].astype(jnp.float32)[8:] * keep, conv_ref[s, at, :], rate_ref[s, at, :],
                input_ref[s, at, :], state_ref[s, at, :], state_ref[s, before8, :] * keep,
                vectors_ref, softness_ref, gate_a_ref, gate_x_ref, squares.at[0], squares.at[1], sums,
                window, later, carry,
            )

        if s == seqs - 1:
            for move in square_moves:
                move.start()
            sum_move.start()

    def steps(s):
        partners, own = scatter.fill(s, s, [grad_branch, grad_feed], [branch_w_ref, rec_w_ref], False)

        def third():
            if s == 0:
                for load in loads[1 + len(per_seq) : 3 + len(per_seq)]:
                    load.wait()
            partners()

        def first():
            mix(s)
            if s == seqs - 1:
                out_grads()

        return [first, functools.partial(recur, s), third, own]

    def out_grads():
        loads[-1].wait()
        step = width // parts

        @pl.loop(0, parts)
        def _(k):
            at = pl.ds(pl.multiple_of(k * step, step), step)
            total = matmul_tn(mixed_ref[0], low_ref[0, :, at])
            for s in range(1, seqs):
                total = total + matmul_tn(mixed_ref[s], low_ref[s, :, at])
            d2[:, at] = total.astype(jnp.bfloat16)

        moves[2].start()

    step = tiles.shape[-1]
    count = width // parts // step

    def columns_of(i):
        peer = lax.rem(lax.axis_index("seq") + 1 + i // count, parts)
        return pl.ds(pl.multiple_of((peer * count + lax.rem(i, count)) * step, step), step)

    def tile_load(i, slot):
        return pltpu.make_async_copy(normed_in.at[:, :, columns_of(i)], tiles.at[slot], tile_sem.at[slot])

    def in_grads(part):
        if part == 0:
            tile_load(0, 0).start()

        @pl.loop(part * count, (part + 1) * count)
        def _(i):
            slot = lax.rem(i, 2)
            tile_load(i, slot).wait()

            @pl.when(i + 1 < parts * count)
            def _():
                tile_load(i + 1, 1 - slot).start()

            for to, grads in ((d0, grad_branch), (d1, grad_feed)):
                total = matmul_tn(grads[0], tiles[slot, 0])
                for s in range(1, seqs):
                    total = total + matmul_tn(grads[s], tiles[slot, s])
                to[:, columns_of(i)] = total.astype(jnp.bfloat16)

        for move in moves[:2]:
            if part < parts - 1:
                move.copy(part + 1, move.me).start()
            else:
                move.own().start()

    def grads_from(first, end):
        for part in range(first, end):
            in_grads(part)

    def store(s):
        term = scatter.result(s)[...]
        inputs = x_ref[s].astype(jnp.float32)
        inverse = lax.rsqrt(mean_of(inputs * inputs) + epsilon)
        normal = inputs * inverse
        gain_local[0:1, :] += jnp.sum(term * normal, axis=0, keepdims=True)
        if s == seqs - 1:
            across.start()
        grad_x_ref[s] = grad_ref[s] + norm_back(term, normal, inverse, gain_ref[...])

    sum_then_gather(
        scatter, None, [steps(s) for s in range(seqs)], [functools.partial(store, s) for s in range(seqs)],
        between=functools.partial(grads_from, 0, parts // 2),
        after=(functools.partial(grads_from, parts // 2, parts - 1), functools.partial(grads_from, parts - 1, parts)),
    )
    across.finish()
    gain_part[...] = sum_of(gain_slots)
    along = Exchange("grp", lambda k: gain_part, lambda k: part_slots.at[k], part_send, part_recv)
    along.start()
    for move in square_moves:
        move.finish()
    squares_out_ref[...] = sum_of(square_slots)
    sum_move.finish()
    sums_out_ref[...] = sum_of(sum_slots_ref)
    for move in moves:
        move.finish()
    along.finish()
    gain_sum_ref[...] = sum_of(part_slots)


def mixer_back(
    heads, low, out_w, branch, feed, conv, rate, gate, state, mixed, branch_w, rec_w, normed,
    vectors, softness, gate_a, gate_x, layer_in, grad_residual, gain, gain_two_grad,
):
    seqs, rows, width = layer_in.shape
    seq_len, channels = feed.shape[1:]
    size, n = lax.axis_size("seq"), lax.axis_size("grp")
    f32, bf16 = jnp.float32, jnp.bfloat16
    large = (low, out_w, branch, feed, conv, rate, gate, state, mixed, branch_w, rec_w)
    small = (vectors, softness, gate_a, gate_x, layer_in, grad_residual, gain, gain_two_grad)
    window_rows = head_windows(heads, channels // heads, size)[0]
    grads = [jax.ShapeDtypeStruct(w.shape, bf16) for w in (branch_w, rec_w, out_w)]
    squares = (heads, 2, window_rows, channels)
    part = width // size
    return call(
        functools.partial(mixer_back_body, heads), "mixer_back", 6,
        large + (normed,) + small,
        [in_hbm] * 12 + [in_vmem] * 8,
        [
            jax.ShapeDtypeStruct(layer_in.shape, f32),
            jax.ShapeDtypeStruct(squares, f32),
            jax.ShapeDtypeStruct((8, channels), f32),
            jax.ShapeDtypeStruct((8, part), f32),
        ]
        + [slots_of(grad, axis, 0) for grad, axis in zip(grads, mixer_axes)],
        [in_vmem] * 4 + [in_hbm] * 3,
        [pltpu.VMEM(v.shape, v.dtype) for v in large]
        + [
            pltpu.VMEM((seq_len, channels), f32),
            pltpu.VMEM(feed.shape, bf16),
            pltpu.VMEM(feed.shape, bf16),
            pltpu.VMEM((2, channels, channels), f32),
            pltpu.VMEM((8, channels), f32),
            pltpu.VMEM((pick_rows(seq_len) + 8, channels), f32),
            pltpu.VMEM((pick_rows(seq_len) + 8, channels), f32),
            pltpu.VMEM((8, channels), f32),
            pltpu.VMEM((2, seqs, seq_len, 256), bf16),
        ]
        + [pltpu.VMEM(grad.shape, bf16) for grad in grads]
        + [
            pltpu.VMEM((size,) + squares, f32),
            pltpu.VMEM((size, 8, channels), f32),
            pltpu.VMEM((8, width), f32),
            pltpu.VMEM((8, part), f32),
            pltpu.VMEM((size, 8, part), f32),
            pltpu.VMEM((n, 8, part), f32),
            pltpu.SemaphoreType.DMA((4 + 7 * seqs,)),
            pltpu.SemaphoreType.DMA((2,)),
        ]
        + [pltpu.SemaphoreType.DMA((heads, size))] * 2
        + [pltpu.SemaphoreType.DMA((size,))] * 4
        + [pltpu.SemaphoreType.DMA((n,))] * 2
        + seq_sems(3)
        + scatter_scratch(seqs, rows, width),
        100,
    )


def out_only_body(hidden_ref, down_w_ref, residual_ref, layer_out_ref, *scratch):
    greet_line()
    scatter = Scatter(residual_ref.shape[1], *scratch)
    fill, store = out_body(hidden_ref, down_w_ref, residual_ref, layer_out_ref, scatter, 0)
    seqs = range(residual_ref.shape[0])
    sum_then_gather(
        scatter, None, [fill(s) for s in seqs], [functools.partial(store, s) for s in seqs]
    )


def out_only(hidden, down_w, residual):
    seqs, rows, width = residual.shape
    return call(
        out_only_body, "layer_out", 5,
        (hidden, down_w, residual), [in_vmem] * 3,
        [jax.ShapeDtypeStruct(residual.shape, jnp.bfloat16)], [in_vmem],
        scatter_scratch(seqs, rows, width), 60,
    )[0]


def per_device(
    layer_in, gain_one, w_branch, w_rec, conv_w, conv_b, gate_a_w, gate_a_b, gate_x_w, gate_x_b,
    decay_logit, w_out, gain_two, mlp_gate, mlp_up, mlp_down, out_grad,
):
    seqs_here, positions, model_width = layer_in.shape
    heads_here, tap_count, part_dim = conv_w.shape
    seq_devices, grp_devices = lax.axis_size("seq"), lax.axis_size("grp")
    head_dim = part_dim * seq_devices
    channels = heads_here * head_dim
    f32 = jnp.float32

    own_params = jnp.concatenate(
        [jnp.transpose(conv_w, (0, 2, 1))]
        + [v[:, :, None] for v in (conv_b, gate_a_b, gate_x_b, decay_logit)]
        + [gate_a_w, gate_x_w],
        axis=2,
    ).astype(f32)
    own_gains = jnp.concatenate([gain_one, gain_two]).astype(f32)
    pack = jnp.concatenate(
        [padded_rows(own_params.reshape(1, -1))[0], padded_rows(own_gains.reshape(1, -1))[0]]
    )
    late_grad, x_full, params, gains, branch_w, rec_w, out_w = gather_first(
        layer_in, out_grad, pack, (w_branch.T, w_rec.T, w_out)
    )

    gains = gains.reshape(grp_devices, seq_devices, -1)[:, :, : own_gains.size]
    gains = jnp.transpose(gains.reshape(grp_devices, seq_devices, 2, -1), (2, 1, 0, 3)).reshape(2, 1, -1)
    params = params.reshape(seq_devices, -1)[:, : own_params.size]
    params = params.reshape((seq_devices,) + own_params.shape)
    params = jnp.transpose(params, (1, 0, 2, 3)).reshape(heads_here, head_dim, -1)
    vectors = params[:, :, : tap_count + 4].reshape(channels, -1).T
    at = tap_count + 4
    diag_a = head_diagonal(params[:, :, at : at + head_dim].astype(jnp.bfloat16))
    diag_x = head_diagonal(params[:, :, at + head_dim :].astype(jnp.bfloat16))
    logit = vectors[tap_count + 3 :]
    softness = jax.nn.softplus(-logit)

    short_line = seqs_here * positions * grp_devices <= 2048
    mlp_weights = (mlp_gate, mlp_up, mlp_down)
    if short_line:
        (
            normed_one, branch_pre, feed, conv, rate, gate, state, mixed, residual, normed_two, grad_output,
            gate_w, up_w, down_w,
        ) = mixer_forward(
            x_full, gains, branch_w, rec_w, out_w, vectors, softness, diag_a, diag_x, late_grad, mlp_weights
        )
        normed_one = normed_one.reshape(-1, model_width)
        grad_output = grad_output.reshape(-1, model_width)
    else:
        grad_output = jnp.concatenate(
            [lax.all_gather(late_grad[s], "grp", axis=0, tiled=True) for s in range(seqs_here)]
        )
        inputs = x_full.astype(f32)
        normal_one = inputs * lax.rsqrt(mean_of(inputs * inputs) + epsilon)
        normed_one = (normal_one * gains[0]).astype(jnp.bfloat16).reshape(-1, model_width)
        branch_pre = matmul_nt(normed_one, branch_w).reshape(seqs_here, -1, channels)
        feed = matmul_nt(normed_one, rec_w).astype(jnp.bfloat16).reshape(seqs_here, -1, channels)
        conv, rate, gate, state, mixed = rec_forward(feed, branch_pre, vectors, softness, diag_a, diag_x)
        residual, normed_two, gate_w, up_w, down_w = mixer_out(
            mixed, out_w, layer_in, gains[1], mlp_weights
        )
    mixed = mixed.reshape(-1, channels)
    normed_two = normed_two.reshape(-1, model_width)
    up_proj = matmul(normed_two, up_w)
    gate_act, gate_pull = jax.vjp(jax.nn.gelu, matmul(normed_two, gate_w))
    hidden = (gate_act * up_proj).astype(jnp.bfloat16)
    grad_hidden = matmul_nt(grad_output, down_w)
    grad_gate = gate_pull(grad_hidden * up_proj)[0].astype(jnp.bfloat16)
    grad_up = (grad_hidden * gate_act).astype(jnp.bfloat16)
    mlp_grads = low_all(
        (matmul_tn(normed_two, grad_gate), matmul_tn(normed_two, grad_up), matmul_tn(hidden, grad_output))
    )

    def by_seq(values):
        return values.reshape(seqs_here, -1, values.shape[-1])

    back_inputs = (
        by_seq(grad_gate), by_seq(grad_up), gate_w, up_w, residual, out_grad, gains[1], mlp_grads
    )
    if not short_line:
        layer_out = out_only(by_seq(hidden), down_w, residual)
        grad_residual, gain_two_grad, residual_low, *mlp_slots = mlp_back(*back_inputs, ())
    else:
        grad_residual, gain_two_grad, residual_low, *mlp_slots, layer_out, late = mlp_back(
            *back_inputs, (by_seq(hidden), down_w)
        )
        late = lax.psum_scatter(late, "grp", scatter_dimension=0, tiled=True)
        late = (residual[seqs_here - 1] + late.astype(f32)).astype(jnp.bfloat16)
        layer_out = jnp.concatenate([layer_out, late[None]])
    mlp_grads = sum_slots(mlp_grads, mlp_slots, weight_axes)
    if short_line:
        grad_x, squares, sums, gain_sum, *mixer_slots = mixer_back(
            heads_here, residual_low, out_w, branch_pre, feed, conv, rate, gate, state, by_seq(mixed), branch_w, rec_w,
            by_seq(normed_one), vectors, softness, diag_a, diag_x, layer_in, grad_residual, gains[0], gain_two_grad,
        )
        mixer_grads = [sum_all(slot) for slot in mixer_slots]
        place = lax.axis_index("seq")
        first = place * part_dim % 8
        square_parts = [
            lax.dynamic_slice_in_dim(squares[h], first, part_dim, 1)[:, :, h * head_dim : (h + 1) * head_dim]
            for h in range(heads_here)
        ]
        grad_a, grad_x_gate = (jnp.stack([part[i] for part in square_parts]) for i in range(2))
        own_sums = lax.dynamic_slice_in_dim(
            sums.reshape(at, heads_here, head_dim), place * part_dim, part_dim, 2
        )
        logit_grad = 8.0 * jax.nn.sigmoid(-decay_logit.astype(f32)) * own_sums[tap_count + 3]
        rec_outs = (
            jnp.transpose(own_sums[:tap_count], (1, 0, 2)), own_sums[tap_count], grad_a, own_sums[tap_count + 1],
            grad_x_gate, own_sums[tap_count + 2], logit_grad,
        )
        return finish(layer_out, grad_x, gain_sum, mixer_grads, rec_outs, mlp_grads)
    residual_low = residual_low.reshape(-1, model_width)
    out_weight_grad = matmul_tn(mixed, residual_low)
    grad_mixed = by_seq(matmul_nt(residual_low, out_w))
    grad_branch, grad_feed, square_a, square_x, sums = rec_backward(
        grad_mixed, branch_pre, feed, conv, rate, gate, state, vectors, softness, diag_a, diag_x
    )
    vector_grads = jnp.concatenate(
        [sums[: tap_count + 3], 8.0 * jax.nn.sigmoid(-logit) * sums[tap_count + 3 :]]
    )
    rec_grads = jnp.concatenate(
        [
            vector_grads.T.reshape(heads_here, head_dim, -1),
            diagonal_heads(square_a, heads_here),
            diagonal_heads(square_x, heads_here),
        ],
        axis=2,
    )
    rec_grads = rec_grads.reshape(heads_here, seq_devices, part_dim, -1)
    rec_blocks = padded_rows(jnp.transpose(rec_grads, (1, 0, 2, 3)))
    mixer_grads = low_all(
        (
            matmul_tn(grad_branch.reshape(-1, channels), normed_one),
            matmul_tn(grad_feed.reshape(-1, channels), normed_one),
            out_weight_grad,
        )
    )
    grad_x, rec_sum, gain_sum, *mixer_slots = last(
        grad_branch, grad_feed, branch_w, rec_w, layer_in, grad_residual, gains[0], gain_two_grad, rec_blocks,
        mixer_grads,
    )
    mixer_grads = sum_slots(mixer_grads, mixer_slots, mixer_axes)
    rec_sum = rec_sum.reshape(-1)[: own_params.size].reshape(own_params.shape)
    rec_outs = (
        jnp.transpose(rec_sum[:, :, :tap_count], (0, 2, 1)),
        rec_sum[:, :, tap_count],
        rec_sum[:, :, at : at + head_dim],
        rec_sum[:, :, tap_count + 1],
        rec_sum[:, :, at + head_dim :],
        rec_sum[:, :, tap_count + 2],
        rec_sum[:, :, tap_count + 3],
    )
    return finish(layer_out, grad_x, gain_sum, mixer_grads, rec_outs, mlp_grads)


def finish(layer_out, grad_x, gain_sum, mixer_grads, rec_outs, mlp_grads):
    part = gain_sum.shape[1] // lax.axis_size("grp")
    gain_grads = lax.dynamic_slice_in_dim(gain_sum, lax.axis_index("grp") * part, part, 1)
    return (
        layer_out, grad_x, gain_grads[0], mixer_grads[0].T, mixer_grads[1].T, *rec_outs, mixer_grads[2], gain_grads[1],
        *mlp_grads,
    )


def solution(mesh):
    placed = (
        P("seq", "grp", None),
        P(("seq", "grp")),
        P("seq", "grp"),
        P("seq", "grp"),
        P("grp", None, "seq"),
        P("grp", "seq"),
        P("grp", "seq", None),
        P("grp", "seq"),
        P("grp", "seq", None),
        P("grp", "seq"),
        P("grp", "seq"),
        P("grp", "seq"),
        P(("seq", "grp")),
        P("seq", "grp"),
        P("seq", "grp"),
        P("grp", "seq"),
        P("seq", "grp", None),
    )
    return jax.shard_map(
        per_device,
        mesh=mesh,
        in_specs=placed,
        out_specs=(
            P("seq", "grp", None),
            P("seq", "grp", None),
            P(("seq", "grp")),
            P("seq", "grp"),
            P("seq", "grp"),
            P("grp", None, "seq"),
            P("grp", "seq"),
            P("grp", "seq", None),
            P("grp", "seq"),
            P("grp", "seq", None),
            P("grp", "seq"),
            P("grp", "seq"),
            P("grp", "seq"),
            P(("seq", "grp")),
            P("seq", "grp"),
            P("seq", "grp"),
            P("grp", "seq"),
        ),
        check_vma=False,
    )
```

```python
import functools
import math

import jax
import jax.numpy as jnp
from jax import lax
from jax.experimental import pallas as pl
from jax.experimental.pallas import tpu as pltpu
from jax.sharding import PartitionSpec as P

epsilon = 1e-06
gelu_slope = math.sqrt(2.0 / math.pi)
gelu_cubic = 0.044715
MESH = pl.DeviceIdType.MESH


def matmul(left, right):
    return jnp.dot(left, right, preferred_element_type=jnp.float32)


def matmul_tn(left, right):
    return lax.dot_general(
        left, right, (((0,), (0,)), ((), ())), preferred_element_type=jnp.float32
    )


def matmul_nt(left, right):
    return lax.dot_general(
        left, right, (((1,), (1,)), ((), ())), preferred_element_type=jnp.float32
    )


def norm_back(grad_normed, normal_part, inverse, gain):
    scaled = grad_normed * gain
    return inverse * (scaled - normal_part * jnp.mean(scaled * normal_part, axis=-1, keepdims=True))


def low_all(grads):
    return tuple(grad.astype(jnp.bfloat16) for grad in grads)


def sum_slots(grads, slots, axes):
    sums = []
    for grad, slot, axis in zip(grads, slots, axes):
        size = slot.shape[1 + axis]
        own = lax.dynamic_slice_in_dim(grad, lax.axis_index("seq") * size, size, axis)
        for k in range(slot.shape[0]):
            own = own.astype(jnp.float32) + slot[k].astype(jnp.float32)
        sums.append(own)
    return sums


def sum_all(slots):
    total = slots[0].astype(jnp.float32)
    for k in range(1, slots.shape[0]):
        total = total + slots[k].astype(jnp.float32)
    return total


def padded_rows(values):
    flat = values.reshape(values.shape[0], -1)
    flat = jnp.pad(flat, ((0, 0), (0, -flat.shape[1] % 1024)))
    return flat.reshape(values.shape[0], -1, 128)


def head_diagonal(blocks):
    heads, head_dim, _ = blocks.shape
    rows = []
    for h in range(heads):
        row = [jnp.zeros((head_dim, head_dim), blocks.dtype)] * heads
        row[h] = blocks[h]
        rows.append(jnp.concatenate(row, axis=1))
    return jnp.concatenate(rows, axis=0)


def diagonal_heads(square, heads):
    head_dim = square.shape[0] // heads
    return jnp.stack(
        [
            square[h * head_dim : (h + 1) * head_dim, h * head_dim : (h + 1) * head_dim]
            for h in range(heads)
        ]
    )


def pick_rows(seq_len, choices=(128, 96, 64, 32, 16)):
    for rows in choices:
        if seq_len % rows == 0:
            return rows
    return seq_len


def gelu_parts(x):
    cubic = gelu_slope * (x + gelu_cubic * x * x * x)
    bend = jnp.tanh(cubic)
    gate = 0.5 * (1.0 + bend)
    slope = gate + 0.5 * x * (1.0 - bend * bend) * gelu_slope * (1.0 + 3.0 * gelu_cubic * x * x)
    return x * gate, slope


def minus_expm1(x):
    series = 1.0 + x * (1.0 / 9.0)
    for k in (8, 7, 6, 5, 4, 3, 2):
        series = 1.0 + x * (1.0 / k) * series
    return jnp.where(x > -0.4, -x * series, 1.0 - jnp.exp(x))


def shift_down(values, by, fill):
    rows = values.shape[0]
    if by % 8 == 0:
        return jnp.concatenate([jnp.full((by, values.shape[1]), fill), values[: rows - by]], axis=0)
    index = lax.broadcasted_iota(jnp.int32, values.shape, 0)
    return jnp.where(index >= by, pltpu.roll(values, by, 0), fill)


def shift_up(values, by, fill):
    rows = values.shape[0]
    if by % 8 == 0:
        return jnp.concatenate([values[by:], jnp.full((by, values.shape[1]), fill)], axis=0)
    index = lax.broadcasted_iota(jnp.int32, values.shape, 0)
    return jnp.where(index < rows - by, pltpu.roll(values, rows - by, 0), fill)


def scan_block(decay, drive, shift):
    by = 1
    while by < decay.shape[0]:
        drive = drive + decay * shift(drive, by, 0.0)
        decay = decay * shift(decay, by, 1.0)
        by *= 2
    return decay, drive


def decay_parts(rate, softness):
    log_decay = -8.0 * rate * softness
    return jnp.exp(log_decay), jnp.sqrt(minus_expm1(2.0 * log_decay))


def rec_forward_rows(feed, branch, vectors_ref, softness_ref, gate_a_ref, gate_x_ref, window, carry):
    rows = feed.shape[0]
    window[pl.ds(8, rows), :] = feed.astype(jnp.float32)
    conv = vectors_ref[4:5, :] + vectors_ref[0:1, :] * window[pl.ds(8, rows), :]
    for k in range(1, 4):
        conv = conv + vectors_ref[k : k + 1, :] * window[pl.ds(8 - k, rows), :]
    window[pl.ds(0, 8), :] = window[pl.ds(rows, 8), :]
    conv_low = conv.astype(jnp.bfloat16)
    rate = jax.nn.sigmoid(matmul(conv_low, gate_a_ref[...]) + vectors_ref[5:6, :])
    gate = jax.nn.sigmoid(matmul(conv_low, gate_x_ref[...]) + vectors_ref[6:7, :])
    decay, scale = decay_parts(rate, softness_ref[...])
    total, state = scan_block(decay, scale * gate * conv_low.astype(jnp.float32), shift_down)
    state = state + total * carry[0:1, :]
    carry[0:1, :] = state[rows - 1 : rows, :]
    gelu_branch = gelu_parts(branch)[0]
    mixed = (gelu_branch * state.astype(jnp.bfloat16).astype(jnp.float32)).astype(jnp.bfloat16)
    return conv_low, rate, gate, state, mixed


def rec_forward_body(
    feed_ref, branch_ref, vectors_ref, softness_ref, gate_a_ref, gate_x_ref,
    conv_ref, rate_ref, input_ref, state_ref, mixed_ref, window, carry,
):
    @pl.when(pl.program_id(0) == 0)
    def _():
        window[...] = jnp.zeros_like(window)
        carry[...] = jnp.zeros_like(carry)

    for s in range(feed_ref.shape[0]):
        conv_ref[s], rate_ref[s], input_ref[s], state_ref[s], mixed_ref[s] = rec_forward_rows(
            feed_ref[s], branch_ref[s], vectors_ref, softness_ref, gate_a_ref, gate_x_ref, window.at[s], carry.at[s]
        )


def rec_backward_rows(
    grad_mixed, branch, feed, feed_before, conv_low, rate, gate, state, state_before,
    vectors_ref, softness_ref, gate_a_ref, gate_x_ref, grad_a_ref, grad_x_ref, sums_ref, window, later, carry,
):
    rows = feed.shape[0]
    softness = softness_ref[...]
    gelu_branch, slope = gelu_parts(branch)
    state_low = state.astype(jnp.bfloat16).astype(jnp.float32)
    grad_state = (grad_mixed * gelu_branch).astype(jnp.bfloat16).astype(jnp.float32)
    grad_branch = (slope * grad_mixed * state_low).astype(jnp.bfloat16)
    decay, scale = decay_parts(rate, softness)
    total, carried = scan_block(shift_up(decay, 1, 1.0), grad_state, shift_up)
    carried = carried + total * carry[0:1, :]
    carry[0:1, :] = decay[0:1, :] * carried[0:1, :]
    index = lax.broadcasted_iota(jnp.int32, state.shape, 0)
    previous = jnp.where(index >= 1, pltpu.roll(state, 1, 0), state_before[7:8, :])
    conv = conv_low.astype(jnp.float32)
    grad_log = carried * previous * decay - carried * gate * conv * decay * decay / scale
    log_rate = grad_log * rate
    pre_a = -8.0 * softness * log_rate * (1.0 - rate)
    pre_x = carried * scale * conv * gate * (1.0 - gate)
    low_a = pre_a.astype(jnp.bfloat16)
    low_x = pre_x.astype(jnp.bfloat16)
    grad_a_ref[...] += matmul_tn(conv_low, low_a)
    grad_x_ref[...] += matmul_tn(conv_low, low_x)
    grad_conv = (
        carried * scale * gate
        + matmul_nt(low_a, gate_a_ref[...])
        + matmul_nt(low_x, gate_x_ref[...])
    )
    window[pl.ds(0, 8), :] = feed_before
    window[pl.ds(8, rows), :] = feed.astype(jnp.float32)
    later[pl.ds(rows, 8), :] = later[pl.ds(0, 8), :]
    later[pl.ds(0, rows), :] = grad_conv
    grad_feed = vectors_ref[0:1, :] * grad_conv
    sums_ref[0:1, :] += jnp.sum(grad_conv * window[pl.ds(8, rows), :], axis=0, keepdims=True)
    for k in range(1, 4):
        grad_feed = grad_feed + vectors_ref[k : k + 1, :] * later[pl.ds(k, rows), :]
        sums_ref[k : k + 1, :] += jnp.sum(
            grad_conv * window[pl.ds(8 - k, rows), :], axis=0, keepdims=True
        )
    sums_ref[4:5, :] += jnp.sum(grad_conv, axis=0, keepdims=True)
    sums_ref[5:6, :] += jnp.sum(pre_a, axis=0, keepdims=True)
    sums_ref[6:7, :] += jnp.sum(pre_x, axis=0, keepdims=True)
    sums_ref[7:8, :] += jnp.sum(log_rate, axis=0, keepdims=True)
    return grad_branch, grad_feed.astype(jnp.bfloat16)


def rec_backward_body(
    grad_mixed_ref, branch_ref, feed_ref, feed_before_ref, conv_ref, rate_ref, input_ref,
    state_ref, state_before_ref, vectors_ref, softness_ref, gate_a_ref, gate_x_ref,
    grad_branch_ref, grad_feed_ref, grad_a_ref, grad_x_ref, sums_ref, window, later, carry,
):
    step = pl.program_id(0)

    @pl.when(step == 0)
    def _():
        for ref in (later, carry, grad_a_ref, grad_x_ref, sums_ref):
            ref[...] = jnp.zeros_like(ref)

    keep = jnp.where(step == pl.num_programs(0) - 1, 0.0, 1.0)
    for s in range(feed_ref.shape[0]):
        before = feed_before_ref[s].astype(jnp.float32)
        grad_branch_ref[s], grad_feed_ref[s] = rec_backward_rows(
            grad_mixed_ref[s], branch_ref[s], feed_ref[s], before[before.shape[0] - 8 :] * keep, conv_ref[s],
            rate_ref[s], input_ref[s], state_ref[s], state_before_ref[s] * keep,
            vectors_ref, softness_ref, gate_a_ref, gate_x_ref, grad_a_ref, grad_x_ref, sums_ref,
            window.at[s], later.at[s], carry.at[s],
        )


def whole(shape):
    return pl.BlockSpec(shape, lambda i: (0,) * len(shape))


def rec_forward(feed, branch, vectors, softness, gate_a, gate_x):
    seqs, seq_len, channels = feed.shape
    rows = pick_rows(seq_len)
    block = pl.BlockSpec((seqs, rows, channels), lambda i: (0, i, 0))
    full = jax.ShapeDtypeStruct(feed.shape, jnp.float32)
    low = jax.ShapeDtypeStruct(feed.shape, jnp.bfloat16)
    return pl.pallas_call(
        rec_forward_body,
        grid=(seq_len // rows,),
        in_specs=[block, block]
        + [whole(v.shape) for v in (vectors, softness, gate_a, gate_x)],
        out_specs=[block] * 5,
        out_shape=[low, full, full, full, low],
        scratch_shapes=[
            pltpu.VMEM((seqs, rows + 8, channels), jnp.float32),
            pltpu.VMEM((seqs, 8, channels), jnp.float32),
        ],
        compiler_params=pltpu.CompilerParams(vmem_limit_bytes=40 << 20),
        name="rec_forward",
    )(feed, branch, vectors, softness, gate_a, gate_x)


def rec_backward(grad_mixed, branch, feed, conv, rate, gate, state, vectors, softness, gate_a, gate_x):
    seqs, seq_len, channels = feed.shape
    rows = pick_rows(seq_len)
    blocks = seq_len // rows
    block = pl.BlockSpec((seqs, rows, channels), lambda i: (0, blocks - 1 - i, 0))

    def ahead(by):
        return pl.BlockSpec(
            (seqs, by, channels),
            lambda i: (0, jnp.maximum((blocks - 1 - i) * (rows // by) - 1, 0), 0),
        )

    low = jax.ShapeDtypeStruct(feed.shape, jnp.bfloat16)
    square = jax.ShapeDtypeStruct((channels, channels), jnp.float32)
    return pl.pallas_call(
        rec_backward_body,
        grid=(blocks,),
        in_specs=[block, block, block, ahead(16), block, block, block, block, ahead(8)]
        + [whole(v.shape) for v in (vectors, softness, gate_a, gate_x)],
        out_specs=[block, block, whole((channels, channels)), whole((channels, channels)), whole((8, channels))],
        out_shape=[low, low, square, square, jax.ShapeDtypeStruct((8, channels), jnp.float32)],
        scratch_shapes=[
            pltpu.VMEM((seqs, rows + 8, channels), jnp.float32),
            pltpu.VMEM((seqs, rows + 8, channels), jnp.float32),
            pltpu.VMEM((seqs, 8, channels), jnp.float32),
        ],
        compiler_params=pltpu.CompilerParams(vmem_limit_bytes=40 << 20),
        name="rec_backward",
    )(grad_mixed, branch, feed, feed, conv, rate, gate, state, state, vectors, softness, gate_a, gate_x)


def line_place():
    return lax.axis_size("grp") // 2, lax.axis_index("grp") // 2, lax.axis_index("grp") % 2


def greet_line():
    chips, chip, core = line_place()
    barrier = pltpu.get_barrier_semaphore()

    def signal(place):
        pl.semaphore_signal(barrier, inc=1, device_id={"grp": place}, device_id_type=MESH)

    signal(chip * 2 + 1 - core)

    @pl.when(chip > 0)
    def _():
        signal(chip * 2 + core - 2)

    @pl.when(chip < chips - 1)
    def _():
        signal(chip * 2 + core + 2)

    ends = (chip == 0).astype(jnp.int32) + (chip == chips - 1).astype(jnp.int32)
    pl.semaphore_wait(barrier, 3 - ends)


def greet_axes(axes):
    barrier = pltpu.get_barrier_semaphore()
    for axis in axes:
        size = lax.axis_size(axis)
        for k in range(1, size):
            pl.semaphore_signal(
                barrier,
                inc=1,
                device_id={axis: lax.rem(lax.axis_index(axis) + k, size)},
                device_id_type=MESH,
            )
    pl.semaphore_wait(barrier, sum(lax.axis_size(axis) - 1 for axis in axes))


class Gather:
    def __init__(self, sources, outs, rows, send_sem, recv_sem, own_sem):
        self.chips, self.chip, self.core = line_place()
        self.me = self.chip * 2 + self.core
        self.sources, self.outs, self.rows = sources, outs, rows
        self.send_sem, self.recv_sem, self.own_sem = send_sem, recv_sem, own_sem

    def slot(self, p, origin):
        return self.outs[p].at[pl.ds(pl.multiple_of(origin * self.rows, self.rows), self.rows), :]

    def copy(self, p, source, origin, target, way):
        return pltpu.make_async_remote_copy(
            src_ref=source,
            dst_ref=self.slot(p, origin),
            send_sem=self.send_sem.at[way, p, origin],
            recv_sem=self.recv_sem.at[p, origin],
            device_id={"grp": target},
            device_id_type=MESH,
        )

    def to_right(self, p, source, origin):
        return self.copy(p, source, origin, self.me + 2, 0)

    def to_left(self, p, source, origin):
        return self.copy(p, source, origin, self.me - 2, 1)

    def to_partner(self, p, source, origin):
        return self.copy(p, source, origin, self.chip * 2 + 1 - self.core, 2)

    def own(self, p):
        return pltpu.make_async_copy(self.sources[p], self.slot(p, self.me), self.own_sem.at[p])

    def start(self, p):
        source = self.sources[p]

        @pl.when(self.chip < self.chips - 1)
        def _():
            self.to_right(p, source, self.me).start()

        @pl.when(self.chip > 0)
        def _():
            self.to_left(p, source, self.me).start()

        self.to_partner(p, source, self.me).start()
        self.own(p).start()

    def hop(self, p, h):
        left_origin = self.me - 2 - 2 * h
        right_origin = self.me + 2 + 2 * h

        @pl.when(self.chip - 1 - h >= 0)
        def _():
            here = self.slot(p, left_origin)
            self.to_right(p, here, left_origin).wait_recv()

            @pl.when(self.chip < self.chips - 1)
            def _():
                self.to_right(p, here, left_origin).start()

            self.to_partner(p, here, left_origin).start()

        @pl.when(self.chip + 1 + h <= self.chips - 1)
        def _():
            here = self.slot(p, right_origin)
            self.to_left(p, here, right_origin).wait_recv()

            @pl.when(self.chip > 0)
            def _():
                self.to_left(p, here, right_origin).start()

            self.to_partner(p, here, right_origin).start()

    def finish(self, p):
        for c in range(self.chips):
            origin = c * 2 + 1 - self.core
            self.to_partner(p, self.slot(p, origin), origin).wait_recv()
        self.own(p).wait()
        for c in range(self.chips):
            origin = c * 2 + self.core
            here = self.slot(p, origin)
            self.to_partner(p, here, origin).wait_send()

            @pl.when((c <= self.chip) & (self.chip < self.chips - 1))
            def _():
                self.to_right(p, here, origin).wait_send()

            @pl.when((c >= self.chip) & (self.chip > 0))
            def _():
                self.to_left(p, here, origin).wait_send()


def gather_sems(pieces):
    n = lax.axis_size("grp")
    return [
        pltpu.SemaphoreType.DMA((3, pieces, n)),
        pltpu.SemaphoreType.DMA((pieces, n)),
        pltpu.SemaphoreType.DMA((pieces,)),
    ]


class Scatter:
    def __init__(self, rows, part, out, swap_in, line_in, send_sem, recv_sem):
        self.chips, self.chip, self.core = line_place()
        self.me = self.chip * 2 + self.core
        self.rows, self.part, self.out = rows, part, out
        self.swap_in, self.line_in = swap_in, line_in
        self.send_sem, self.recv_sem = send_sem, recv_sem

    def copy(self, dest, place, way, slot, p):
        return pltpu.make_async_remote_copy(
            src_ref=self.out.at[p, slot],
            dst_ref=dest,
            send_sem=self.send_sem.at[way, p, slot],
            recv_sem=self.recv_sem.at[way, p, slot],
            device_id={"grp": place},
            device_id_type=MESH,
        )

    def swap(self, p, c):
        return self.copy(self.swap_in.at[p, c], self.chip * 2 + 1 - self.core, 0, c, p)

    def right(self, p, c):
        return self.copy(self.line_in.at[p, c], self.me + 2, 1, c, p)

    def left(self, p, c):
        slot = jnp.where(c == self.chip - 1, self.chips, c)
        return self.copy(self.line_in.at[p, slot], self.me - 2, 2, c, p)

    def from_right(self, p, c):
        slot = jnp.where(c == self.chip, self.chips, c)
        return self.copy(self.line_in.at[p, slot], self.me + 2, 2, c, p)

    def fill(self, p, s, lefts, rights, transposed, width=512):
        def rows_of(ref, core):
            at = [pl.multiple_of((c * 2 + core) * self.rows, self.rows) for c in range(self.chips)]
            return jnp.concatenate([ref[s, pl.ds(a, self.rows), :] for a in at], axis=0)

        def product(core, store):
            chosen = [rows_of(ref, core) for ref in lefts]

            @pl.loop(0, self.out.shape[-1] // width)
            def _(j):
                columns = pl.ds(pl.multiple_of(j * width, width), width)
                total = None
                for left, right in zip(chosen, rights):
                    term = matmul_nt(left, right[columns, :]) if transposed else matmul(left, right[:, columns])
                    total = term if total is None else total + term
                for c in range(self.chips):
                    store(c, columns, total[c * self.rows : (c + 1) * self.rows])

        def to_out(c, columns, value):
            self.out[p, c, :, columns] = value.astype(jnp.bfloat16)

        def to_part(c, columns, value):
            self.part[p, c, :, columns] = value

        def partners():
            product(1 - self.core, to_out)
            for c in range(self.chips):
                self.swap(p, c).start()

        def own():
            product(self.core, to_part)

        return partners, own

    def own(self, p, c):
        self.swap(p, c).wait_recv()
        return self.part[p, c] + self.swap_in[p, c].astype(jnp.float32)

    def hop(self, p, t):
        last = self.chips - 1

        def send(c, first, arrival, onward):
            self.swap(p, c).wait_send()
            total = self.own(p, c)

            @pl.when(first)
            def _():
                self.out[p, c] = total.astype(jnp.bfloat16)

            @pl.when(jnp.logical_not(first))
            def _():
                arrival(p, c).wait_recv()
                self.out[p, c] = (total + self.line_in[p, c].astype(jnp.float32)).astype(jnp.bfloat16)

            onward(p, c).start()

        @pl.when(self.chip <= t)
        def _():
            send(last - t + self.chip, self.chip == 0, self.right, self.right)

        @pl.when(last - self.chip <= t)
        def _():
            send(t - last + self.chip, self.chip == last, self.from_right, self.left)

    def result(self, p):
        chip = self.chip
        self.part[p, chip] = self.own(p, chip)

        @pl.when(chip > 0)
        def _():
            self.right(p, chip).wait_recv()
            self.part[p, chip] += self.line_in[p, chip].astype(jnp.float32)

        @pl.when(chip < self.chips - 1)
        def _():
            self.from_right(p, chip).wait_recv()
            self.part[p, chip] += self.line_in[p, self.chips].astype(jnp.float32)

        return self.part.at[p, chip]

    def finish(self, p):
        self.swap(p, self.chip).wait_send()
        for c in range(self.chips):

            @pl.when(c > self.chip)
            def _():
                self.right(p, c).wait_send()

            @pl.when(c < self.chip)
            def _():
                self.left(p, c).wait_send()


def scatter_scratch(pieces, rows, width):
    chips = lax.axis_size("grp") // 2
    return [
        pltpu.VMEM((pieces, chips, rows, width), jnp.float32),
        pltpu.VMEM((pieces, chips, rows, width), jnp.bfloat16),
        pltpu.VMEM((pieces, chips, rows, width), jnp.bfloat16),
        pltpu.VMEM((pieces, chips + 1, rows, width), jnp.bfloat16),
        pltpu.SemaphoreType.DMA((3, pieces, chips)),
        pltpu.SemaphoreType.DMA((3, pieces, chips)),
    ]


in_vmem = pl.BlockSpec(memory_space=pltpu.VMEM)
in_hbm = pl.BlockSpec(memory_space=pl.ANY)


def call(body, name, number, inputs, in_specs, outs, out_specs, scratch, us):
    return pl.pallas_call(
        body,
        in_specs=in_specs,
        out_specs=out_specs,
        out_shape=outs,
        scratch_shapes=scratch,
        name=name,
        cost_estimate=pl.CostEstimate(
            flops=us * 1000000000, bytes_accessed=us * 3000000, transcendentals=0
        ),
        compiler_params=pltpu.CompilerParams(
            collective_id=number, has_side_effects=True, vmem_limit_bytes=62 << 20
        ),
    )(*inputs)


class Exchange:
    def __init__(self, axis, source, slot, send_sem, recv_sem, steps=None, first=1):
        self.axis, self.source, self.slot, self.steps, self.first = axis, source, slot, steps, first
        self.size, self.me = lax.axis_size(axis), lax.axis_index(axis)
        self.send_sem, self.recv_sem = send_sem, recv_sem

    def copy(self, k, owner):
        peer = lax.rem(self.me + k, self.size)
        return pltpu.make_async_remote_copy(
            src_ref=self.source(peer),
            dst_ref=self.slot(owner) if self.slot else self.steps.at[k - self.first],
            send_sem=self.send_sem.at[k],
            recv_sem=self.recv_sem.at[k],
            device_id={self.axis: peer},
            device_id_type=MESH,
        )

    def own(self):
        slot = self.slot(self.me) if self.slot else self.steps.at[0]
        return pltpu.make_async_copy(self.source(self.me), slot, self.send_sem.at[0])

    def start(self):
        self.own().start()
        self.start_others()

    def start_others(self):
        for k in range(1, self.size):
            self.copy(k, self.me).start()

    def finish(self):
        self.own().wait()
        self.finish_others()

    def finish_others(self):
        for k in range(1, self.size):
            self.copy(k, lax.rem(self.me - k + self.size, self.size)).wait_recv()
        for k in range(1, self.size):
            self.copy(k, self.me).wait_send()


def sum_of(slots):
    total = slots[0]
    for k in range(1, slots.shape[0]):
        total = total + slots[k]
    return total


def block(ref, axis, parts):
    size = ref.shape[axis] // parts

    def view(k):
        at = pl.ds(pl.multiple_of(k * size, size), size)
        return ref.at[at, :] if axis == 0 else ref.at[:, at]

    return view


def weight_gathers(axes, sources, outs, send_sem, recv_sem):
    parts = lax.axis_size("seq")
    return [
        Exchange(
            "seq", lambda k, ref=source: ref, block(out, axis, parts), send_sem.at[i], recv_sem.at[i]
        )
        for i, (axis, source, out) in enumerate(zip(axes, sources, outs))
    ]


def weight_sums(axes, sources, outs, send_sem, recv_sem, first=1):
    parts = lax.axis_size("seq")
    return [
        Exchange(
            "seq", block(source, axis, parts), None, send_sem.at[i], recv_sem.at[i], out, first
        )
        for i, (axis, source, out) in enumerate(zip(axes, sources, outs))
    ]


def seq_sems(count):
    return [pltpu.SemaphoreType.DMA((count, lax.axis_size("seq")))] * 2


def gathered(block_of, axis):
    shape = list(block_of.shape)
    shape[axis] *= lax.axis_size("seq")
    return jax.ShapeDtypeStruct(shape, block_of.dtype)


def slots_of(matrix, axis, first=1):
    shape = list(matrix.shape)
    size = lax.axis_size("seq")
    shape[axis] //= size
    return jax.ShapeDtypeStruct((size - first, *shape), matrix.dtype)


weight_axes = (0, 0, 1)
mixer_axes = (1, 1, 1)


def copies(pairs, sem):
    return [pltpu.make_async_copy(source, buffer, sem.at[i]) for i, (source, buffer) in enumerate(pairs)]


def views(ref):
    return [ref.at[s] for s in range(ref.shape[0])]


def first_body(x_ref, grad_ref, pack_ref, w0, w1, w2, later_ref, full_ref, params_ref, gains_ref, o0, o1, o2, *refs):
    small_send, small_recv, gain_send, gain_recv, weight_send, weight_recv = refs[3:]
    greet_axes(("seq", "grp"))
    seqs = x_ref.shape[0]
    gather = Gather(views(x_ref), views(full_ref), x_ref.shape[1], *refs[:3])
    weights = weight_gathers(mixer_axes, (w0, w1, w2), (o0, o1, o2), weight_send, weight_recv)
    small = Exchange("seq", lambda k: pack_ref, lambda k: params_ref.at[k], small_send, small_recv)
    small.start()
    for s in range(seqs):
        gather.start(s)
    for weight in weights:
        weight.start()
    later_ref[...] = grad_ref[...]
    small.finish()
    place = lax.axis_index("grp")
    for owner in range(small.size):
        gains_ref[place, owner] = params_ref[owner, pl.ds(pack_ref.shape[0] - 8, 8), :]
    gains = Exchange("grp", lambda k: gains_ref.at[place], lambda k: gains_ref.at[k], gain_send, gain_recv)
    gains.start_others()
    for h in range(gather.chips - 1):
        for s in range(seqs):
            gather.hop(s, h)
    gains.finish_others()
    for weight in weights:
        weight.finish()
    for s in range(seqs):
        gather.finish(s)


def gather_first(layer_in, out_grad, pack, weights):
    seqs, rows, width = layer_in.shape
    n, size = lax.axis_size("grp"), lax.axis_size("seq")
    return call(
        first_body, "gather_first", 1,
        (layer_in, out_grad, pack, *weights), [in_vmem] * 6,
        [
            jax.ShapeDtypeStruct(out_grad.shape, out_grad.dtype),
            jax.ShapeDtypeStruct((seqs, n * rows, width), jnp.bfloat16),
            jax.ShapeDtypeStruct((size,) + pack.shape, jnp.float32),
            jax.ShapeDtypeStruct((n, size, 8, 128), jnp.float32),
        ]
        + [gathered(w, axis) for w, axis in zip(weights, mixer_axes)],
        [in_vmem, in_hbm] + [in_vmem] * 2 + [in_hbm] * 3,
        gather_sems(seqs)
        + [pltpu.SemaphoreType.DMA((size,))] * 2
        + [pltpu.SemaphoreType.DMA((n,))] * 2
        + seq_sems(3),
        70,
    )


def mean_of(values):
    return jnp.mean(values, axis=-1, keepdims=True)


def sum_then_gather(scatter, gather, fills, stores, count=0, between=None, after=()):
    hops = range(1, scatter.chips - 1)
    for step in fills[0]:
        step()
    scatter.hop(0, 0)
    for p, store in enumerate(stores):
        ahead = list(fills[p + 1] if p + 1 < len(fills) else after)
        for h in hops:
            if ahead:
                ahead.pop(0)()
            scatter.hop(p, h)
            if 0 < p <= count:
                gather.hop(p - 1, h - 1)
        for step in ahead:
            step()
        if p + 1 < len(fills):
            scatter.hop(p + 1, 0)
        if between and p == 0:
            between()
        store()
        if p < count:
            gather.start(p)
        if 0 < p <= count:
            gather.hop(p - 1, gather.chips - 2)
    if count == len(stores):
        for h in range(gather.chips - 1):
            gather.hop(count - 1, h)
    for p in range(count):
        gather.finish(p)
    for p in range(len(fills)):
        scatter.finish(p)


def out_body(hidden_ref, down_w_ref, residual_ref, layer_out_ref, scatter, first):
    def fill(s):
        return scatter.fill(first + s, s, [hidden_ref], [down_w_ref], False)

    def store(s):
        layer_out_ref[s] = (residual_ref[s] + scatter.result(first + s)[...]).astype(jnp.bfloat16)

    return fill, store


def mixer_out_body(mixed_ref, out_w_ref, x_ref, gain_ref, w0, w1, w2, residual_ref, normed_ref, o0, o1, o2, low_ref, *refs):
    greet_axes(("seq", "grp"))
    seqs, rows, _ = x_ref.shape
    weights = weight_gathers(weight_axes, (w0, w1, w2), (o0, o1, o2), *refs[:2])
    for weight in weights:
        weight.start()
    gather = Gather(views(low_ref), views(normed_ref), rows, *refs[2:5])
    scatter = Scatter(rows, *refs[5:])

    def fill(s):
        return scatter.fill(s, s, [mixed_ref], [out_w_ref], False)

    def store(s):
        residual = x_ref[s].astype(jnp.float32) + scatter.result(s)[...]
        residual_ref[s] = residual
        normal = residual * lax.rsqrt(mean_of(residual * residual) + epsilon)
        low_ref[s] = (normal * gain_ref[...]).astype(jnp.bfloat16)

    sum_then_gather(
        scatter, gather, [fill(s) for s in range(seqs)], [functools.partial(store, s) for s in range(seqs)], seqs
    )
    for weight in weights:
        weight.finish()


def mixer_out(mixed, out_w, layer_in, gain, weights):
    seqs, rows, width = layer_in.shape
    full = jax.ShapeDtypeStruct((seqs, lax.axis_size("grp") * rows, width), jnp.bfloat16)
    return call(
        mixer_out_body, "mixer_out", 2,
        (mixed, out_w, layer_in, gain, *weights), [in_vmem] * 7,
        [jax.ShapeDtypeStruct(layer_in.shape, jnp.float32), full]
        + [gathered(w, axis) for w, axis in zip(weights, weight_axes)],
        [in_vmem] + [in_hbm] * 4,
        [pltpu.VMEM(layer_in.shape, jnp.bfloat16)]
        + seq_sems(3)
        + gather_sems(seqs)
        + scatter_scratch(seqs, rows, width),
        100,
    )


def mixer_forward_body(
    x_full_in, branch_w_in, rec_w_in, out_w_in, gains_ref, vectors_ref, softness_ref, gate_a_ref, gate_x_ref,
    grad_ref, w0, w1, w2,
    residual_ref, normed_one_out, branch_out, feed_out, conv_out, rate_out, input_out, state_out, mixed_out,
    normed_ref, grads_ref, o0, o1, o2,
    x_full_ref, branch_w_ref, rec_w_ref, out_w_ref, normed_one_ref, branch_ref, feed_ref, conv_ref, rate_ref, input_ref,
    state_ref, mixed_ref, load_sem, store_sem, low_ref, window, carry, *refs,
):
    pairs = [(branch_w_in, branch_w_ref), (rec_w_in, rec_w_ref), (out_w_in, out_w_ref)]
    pairs[:0] = [(x_full_in.at[0], x_full_ref.at[0])]
    pairs += [(x_full_in.at[s], x_full_ref.at[s]) for s in range(1, x_full_ref.shape[0])]
    loads = copies(pairs, load_sem)
    for load in loads:
        load.start()
    kept = (
        (normed_one_ref, normed_one_out), (branch_ref, branch_out), (feed_ref, feed_out), (conv_ref, conv_out),
        (rate_ref, rate_out), (input_ref, input_out), (state_ref, state_out), (mixed_ref, mixed_out),
    )
    keeps = [
        copies([(buffer.at[s], out.at[s]) for buffer, out in kept], store_sem.at[s])
        for s in range(x_full_ref.shape[0])
    ]
    greet_axes(("seq", "grp"))
    seqs, seq_len, _ = x_full_ref.shape
    rows = grad_ref.shape[1]
    me = lax.axis_index("grp")
    weights = weight_gathers(weight_axes, (w0, w1, w2), (o0, o1, o2), *refs[:2])
    gather = Gather(views(low_ref) + views(grad_ref), views(normed_ref) + views(grads_ref), rows, *refs[2:5])
    scatter = Scatter(rows, *refs[5:])
    for s in range(seqs):
        gather.start(seqs + s)
    for weight in weights:
        weight.start()
    tile = pick_rows(seq_len, (256, 192, 128, 96, 64, 32, 16))
    chunk = window.shape[0] - 8
    window[...] = jnp.zeros_like(window)

    def project(s):
        for load in loads[:3] if s == 0 else loads[3 + s : 4 + s]:
            load.wait()

        @pl.loop(0, seq_len // tile)
        def _(i):
            at = pl.ds(pl.multiple_of(i * tile, tile), tile)
            inputs = x_full_ref[s, at, :].astype(jnp.float32)
            normal = inputs * lax.rsqrt(mean_of(inputs * inputs) + epsilon)
            normed = (normal * gains_ref[0]).astype(jnp.bfloat16)
            normed_one_ref[s, at, :] = normed
            branch_ref[s, at, :] = matmul_nt(normed, branch_w_ref[...])
            feed_ref[s, at, :] = matmul_nt(normed, rec_w_ref[...]).astype(jnp.bfloat16)

    def recur(s):
        window[pl.ds(0, 8), :] = jnp.zeros((8, window.shape[1]), jnp.float32)
        carry[...] = jnp.zeros_like(carry)

        @pl.loop(0, seq_len // chunk)
        def _(i):
            at = pl.ds(pl.multiple_of(i * chunk, chunk), chunk)
            conv, rate, gate, state, mixed = rec_forward_rows(
                feed_ref[s, at, :], branch_ref[s, at, :], vectors_ref, softness_ref, gate_a_ref, gate_x_ref, window, carry
            )
            conv_ref[s, at, :] = conv
            rate_ref[s, at, :] = rate
            input_ref[s, at, :] = gate
            state_ref[s, at, :] = state
            mixed_ref[s, at, :] = mixed

    def late_hop(h):
        if h < gather.chips - 1:
            for s in range(seqs):
                gather.hop(seqs + s, h)

    def steps(s):
        partners, own = scatter.fill(s, s, [mixed_ref], [out_w_ref], False)

        def first():
            if s == 1:
                late_hop(0)
            project(s)

        def second():
            recur(s)
            for keep in keeps[s]:
                keep.start()
            if s == 1:
                late_hop(1)
            if s == 0:
                loads[3].wait()

        return [first, second, partners, own]

    def last_late_hops():
        for h in range(2 if seqs > 1 else 0, gather.chips - 1):
            late_hop(h)

    def store(s):
        own = x_full_ref[s, pl.ds(pl.multiple_of(me * rows, rows), rows), :]
        residual = own.astype(jnp.float32) + scatter.result(s)[...]
        residual_ref[s] = residual
        normal = residual * lax.rsqrt(mean_of(residual * residual) + epsilon)
        low_ref[s] = (normal * gains_ref[1]).astype(jnp.bfloat16)

    sum_then_gather(
        scatter, gather, [steps(s) for s in range(seqs)], [functools.partial(store, s) for s in range(seqs)], seqs,
        after=(last_late_hops,),
    )
    for s in range(seqs):
        gather.finish(seqs + s)
        for keep in keeps[s]:
            keep.wait()
    for weight in weights:
        weight.finish()


def mixer_forward(x_full, gains, branch_w, rec_w, out_w, vectors, softness, gate_a, gate_x, out_grad, weights):
    seqs, seq_len, width = x_full.shape
    rows, channels = out_grad.shape[1], vectors.shape[1]
    low = jax.ShapeDtypeStruct((seqs, seq_len, channels), jnp.bfloat16)
    full = jax.ShapeDtypeStruct((seqs, seq_len, channels), jnp.float32)
    kept = [x_full, full, low, low, full, full, full, low]
    kept = [jax.ShapeDtypeStruct(out.shape, out.dtype) for out in kept]
    outs = [jax.ShapeDtypeStruct(out_grad.shape, jnp.float32)] + kept + [kept[0]] * 2
    outs += [gathered(w, axis) for w, axis in zip(weights, weight_axes)]
    return call(
        mixer_forward_body, "mixer_forward", 2,
        (x_full, branch_w, rec_w, out_w, gains, vectors, softness, gate_a, gate_x, out_grad, *weights),
        [in_hbm] * 4 + [in_vmem] * 9,
        outs, [in_vmem] + [in_hbm] * 13,
        [pltpu.VMEM(v.shape, v.dtype) for v in [x_full, branch_w, rec_w, out_w] + kept]
        + [
            pltpu.SemaphoreType.DMA((3 + seqs,)),
            pltpu.SemaphoreType.DMA((seqs, len(kept))),
            pltpu.VMEM(out_grad.shape, jnp.bfloat16),
            pltpu.VMEM((pick_rows(seq_len) + 8, channels), jnp.float32),
            pltpu.VMEM((8, channels), jnp.float32),
        ]
        + seq_sems(3)
        + gather_sems(2 * seqs)
        + scatter_scratch(seqs, rows, width),
        130,
    )


def mlp_back_body(
    with_out, gate_in, up_in, gate_w_in, up_w_in, residual_ref, grad_ref, gain_ref, w0, w1, w2, *refs
):
    if with_out:
        hidden_in, down_w_in = refs[:2]
        refs = refs[2:]
    grad_residual_ref, gain_grad_ref, full_ref, o0, o1, o2 = refs[:6]
    refs = refs[6:]
    if with_out:
        layer_out_ref, late_ref = refs[:2]
        refs = refs[2:]
    low_ref, load_sem, gate_ref, up_ref, gate_w_ref, up_w_ref, *refs = refs
    pairs = [(gate_in, gate_ref), (up_in, up_ref), (gate_w_in, gate_w_ref), (up_w_in, up_w_ref)]
    if with_out:
        hidden_ref, down_w_ref, *refs = refs
        pairs += [(hidden_in, hidden_ref), (down_w_in, down_w_ref)]
    loads = copies(pairs, load_sem)
    for load in loads:
        load.start()
    greet_axes(("seq", "grp"))
    seqs, rows, _ = grad_ref.shape
    sums = weight_sums(weight_axes, (w0, w1, w2), (o0, o1, o2), *refs[:2])
    for weight in sums:
        weight.start_others()
    gather = Gather(views(low_ref), views(full_ref), rows, *refs[2:5])
    scatter = Scatter(rows, *refs[5:])
    gain_grad_ref[...] = jnp.zeros_like(gain_grad_ref)

    def fill(s):
        return scatter.fill(s, s, [gate_ref, up_ref], [gate_w_ref, up_w_ref], True)

    def store(s):
        term = scatter.result(s)[...]
        residual = residual_ref[s]
        inverse = lax.rsqrt(mean_of(residual * residual) + epsilon)
        normal = residual * inverse
        gain_grad_ref[0:1, :] += jnp.sum(term * normal, axis=0, keepdims=True)
        grad = grad_ref[s].astype(jnp.float32) + norm_back(term, normal, inverse, gain_ref[...])
        grad_residual_ref[s] = grad
        low_ref[s] = grad.astype(jnp.bfloat16)

    def wait_first():
        for load in loads[:4]:
            load.wait()

    def wait_later():
        for load in loads[4:]:
            load.wait()

    fills = [fill(s) for s in range(seqs)]
    fills[0] = (wait_first, *fills[0])
    stores = [functools.partial(store, s) for s in range(seqs)]
    if with_out:
        fill_out, store_out = out_body(hidden_ref, down_w_ref, residual_ref, layer_out_ref, scatter, seqs)
        fills += [fill_out(s) for s in range(seqs - 1)]
        fills[seqs - 1] = (*fills[seqs - 1], wait_later)
        stores += [functools.partial(store_out, s) for s in range(seqs - 1)]

    def late():
        step = 256

        @pl.loop(0, late_ref.shape[0] // step)
        def _(i):
            at = pl.ds(pl.multiple_of(i * step, step), step)
            late_ref[at, :] = matmul(hidden_ref[seqs - 1, at, :], down_w_ref[...]).astype(jnp.bfloat16)

    sum_then_gather(scatter, gather, fills, stores, seqs, after=(late,) if with_out else ())
    for weight in sums:
        weight.finish_others()


def mlp_back(grad_gate, grad_up, gate_w, up_w, residual, out_grad, gain, grads, out_inputs):
    seqs, rows, width = residual.shape
    outs = [
        jax.ShapeDtypeStruct(residual.shape, jnp.float32),
        jax.ShapeDtypeStruct((8, width), jnp.float32),
        jax.ShapeDtypeStruct((seqs, lax.axis_size("grp") * rows, width), jnp.bfloat16),
    ]
    outs += [slots_of(grad, axis) for grad, axis in zip(grads, weight_axes)]
    out_specs = [in_vmem] * 2 + [in_hbm] * 4
    if out_inputs:
        outs.append(jax.ShapeDtypeStruct((seqs - 1, rows, width), jnp.bfloat16))
        outs.append(jax.ShapeDtypeStruct((lax.axis_size("grp") * rows, width), jnp.bfloat16))
        out_specs += [in_vmem] * 2
    return call(
        functools.partial(mlp_back_body, bool(out_inputs)), "mlp_back", 3,
        (grad_gate, grad_up, gate_w, up_w, residual, out_grad, gain, *grads, *out_inputs),
        [in_hbm] * 4 + [in_vmem] * 3 + [in_hbm] * (3 + len(out_inputs)),
        outs, out_specs,
        [pltpu.VMEM(residual.shape, jnp.bfloat16), pltpu.SemaphoreType.DMA((6,))]
        + [pltpu.VMEM(v.shape, v.dtype) for v in (grad_gate, grad_up, gate_w, up_w, *out_inputs)]
        + seq_sems(3)
        + gather_sems(seqs)
        + scatter_scratch(seqs * 2 - 1 if out_inputs else seqs, rows, width),
        120,
    )


def last_body(
    branch_ref, feed_ref, branch_w_ref, rec_w_ref, x_ref, grad_ref, gain_ref, gain_two_ref, rec_ref,
    w0, w1, w2, *refs,
):
    grad_x_ref, rec_sum_ref, gain_sum_ref, o0, o1, o2 = refs[:6]
    refs = refs[6:]
    rec_slots, gain_local, gain_part, gain_slots, part_slots = refs[:5]
    rec_sems, gain_sems, part_sems = refs[5:7], refs[7:9], refs[9:11]
    greet_axes(("seq", "grp"))
    seqs, rows, _ = x_ref.shape
    sums = weight_sums(mixer_axes, (w0, w1, w2), (o0, o1, o2), *refs[11:13])
    scatter = Scatter(rows, *refs[13:])
    rec = Exchange("seq", lambda k: rec_ref.at[k], lambda k: rec_slots.at[k], *rec_sems)
    rec.start()
    for weight in sums:
        weight.start_others()
    gain_local[...] = jnp.zeros_like(gain_local)
    gain_local[1:2, :] = gain_two_ref[0:1, :]

    def fill(s):
        return scatter.fill(s, s, [branch_ref, feed_ref], [branch_w_ref, rec_w_ref], False)

    across = Exchange(
        "seq", block(gain_local, 1, lax.axis_size("seq")), lambda k: gain_slots.at[k], *gain_sems
    )

    def store(s):
        term = scatter.result(s)[...]
        inputs = x_ref[s].astype(jnp.float32)
        inverse = lax.rsqrt(mean_of(inputs * inputs) + epsilon)
        normal = inputs * inverse
        gain_local[0:1, :] += jnp.sum(term * normal, axis=0, keepdims=True)
        if s == seqs - 1:
            across.start()
        grad_x_ref[s] = grad_ref[s] + norm_back(term, normal, inverse, gain_ref[...])

    sum_then_gather(
        scatter, None, [fill(s) for s in range(seqs)], [functools.partial(store, s) for s in range(seqs)]
    )
    across.finish()
    gain_part[...] = sum_of(gain_slots)
    along = Exchange("grp", lambda k: gain_part, lambda k: part_slots.at[k], *part_sems)
    along.start()
    rec.finish()
    rec_sum_ref[...] = sum_of(rec_slots)
    for weight in sums:
        weight.finish_others()
    along.finish()
    gain_sum_ref[...] = sum_of(part_slots)


def last(grad_branch, grad_feed, branch_w, rec_w, layer_in, grad_residual, gain, gain_two_grad, rec_blocks, grads):
    seqs, rows, width = layer_in.shape
    size, n = lax.axis_size("seq"), lax.axis_size("grp")
    f32 = jnp.float32
    inputs = (grad_branch, grad_feed, branch_w, rec_w, layer_in, grad_residual, gain, gain_two_grad, rec_blocks)
    outs = [
        jax.ShapeDtypeStruct(layer_in.shape, f32),
        jax.ShapeDtypeStruct(rec_blocks.shape[1:], f32),
        jax.ShapeDtypeStruct((8, width // size), f32),
    ]
    outs += [slots_of(grad, axis) for grad, axis in zip(grads, mixer_axes)]
    out_specs = [in_vmem] * 3 + [in_hbm] * 3
    return call(
        last_body, "last", 4,
        inputs + tuple(grads), [in_vmem] * len(inputs) + [in_hbm] * 3,
        outs, out_specs,
        [
            pltpu.VMEM(rec_blocks.shape, f32),
            pltpu.VMEM((8, width), f32),
            pltpu.VMEM((8, width // size), f32),
            pltpu.VMEM((size, 8, width // size), f32),
            pltpu.VMEM((n, 8, width // size), f32),
        ]
        + [pltpu.SemaphoreType.DMA((size,))] * 4
        + [pltpu.SemaphoreType.DMA((n,))] * 2
        + seq_sems(3)
        + scatter_scratch(seqs, rows, width),
        80,
    )


def head_windows(heads, head_dim, parts):
    part = head_dim // parts
    rows = max(-(-(k + 1) * part // 8) * 8 - k * part // 8 * 8 for k in range(parts))

    def start(h, k):
        return pl.multiple_of(h * head_dim + k * part // 8 * 8, 8)

    return rows, start


def mixer_back_body(
    heads, low_in, out_w_in, branch_in, feed_in, conv_in, rate_in, input_in, state_in, mixed_in, branch_w_in, rec_w_in,
    normed_in, vectors_ref, softness_ref, gate_a_ref, gate_x_ref, x_ref, grad_ref, gain_ref, gain_two_ref,
    grad_x_ref, squares_out_ref, sums_out_ref, gain_sum_ref, o0, o1, o2,
    low_ref, out_w_ref, branch_ref, feed_ref, conv_ref, rate_ref, input_ref, state_ref, mixed_ref, branch_w_ref,
    rec_w_ref, grad_mixed, grad_branch, grad_feed, squares, sums, window, later, carry, tiles, d0, d1, d2,
    square_slots, sum_slots_ref, gain_local, gain_part, gain_slots, part_slots, load_sem, tile_sem,
    square_send, square_recv, sum_send, sum_recv, gain_send, gain_recv, part_send, part_recv, weight_send, weight_recv,
    *refs,
):
    seqs, rows, width = x_ref.shape
    seq_len, channels = feed_ref.shape[1:]
    per_seq = (
        (low_in, low_ref), (branch_in, branch_ref), (feed_in, feed_ref), (conv_in, conv_ref), (rate_in, rate_ref),
        (input_in, input_ref), (state_in, state_ref),
    )
    pairs = [(out_w_in, out_w_ref)]
    for s in range(seqs):
        pairs += [(source.at[s], buffer.at[s]) for source, buffer in per_seq]
        if s == 0:
            pairs += [(branch_w_in, branch_w_ref), (rec_w_in, rec_w_ref)]
    pairs += [(mixed_in, mixed_ref)]
    loads = copies(pairs, load_sem)
    for load in loads:
        load.start()
    greet_axes(("seq", "grp"))
    scatter = Scatter(rows, *refs)
    parts = lax.axis_size("seq")
    for ref in (squares, sums, gain_local):
        ref[...] = jnp.zeros_like(ref)
    gain_local[1:2, :] = gain_two_ref[0:1, :]
    window_rows, start_of = head_windows(heads, channels // heads, parts)
    square_moves = [
        Exchange(
            "seq",
            lambda k, h=h: squares.at[:, pl.ds(start_of(h, k), window_rows), :],
            lambda k, h=h: square_slots.at[k, h],
            square_send.at[h],
            square_recv.at[h],
        )
        for h in range(heads)
    ]
    sum_move = Exchange("seq", lambda k: sums, lambda k: sum_slots_ref.at[k], sum_send, sum_recv)
    across = Exchange("seq", block(gain_local, 1, parts), lambda k: gain_slots.at[k], gain_send, gain_recv)
    moves = weight_sums(mixer_axes, (d0, d1, d2), (o0, o1, o2), weight_send, weight_recv, 0)
    tile_rows = pick_rows(seq_len, (256, 192, 128, 96, 64, 32, 16))
    chunk = window.shape[0] - 8

    def mix(s):
        if s == 0:
            for load in loads[: 1 + len(per_seq)]:
                load.wait()
        else:
            first = 3 + s * len(per_seq)
            for load in loads[first : first + len(per_seq)]:
                load.wait()

        @pl.loop(0, seq_len // tile_rows)
        def _(i):
            at = pl.ds(pl.multiple_of(i * tile_rows, tile_rows), tile_rows)
            grad_mixed[at, :] = matmul_nt(low_ref[s, at, :], out_w_ref[...])

    def recur(s):
        carry[...] = jnp.zeros_like(carry)
        later[...] = jnp.zeros_like(later)
        blocks = seq_len // chunk

        @pl.loop(0, blocks)
        def _(i):
            first = (blocks - 1 - i) * chunk
            at = pl.ds(pl.multiple_of(first, chunk), chunk)
            keep = jnp.where(i == blocks - 1, 0.0, 1.0)
            before8 = pl.ds(pl.multiple_of(jnp.maximum(first - 8, 0), 8), 8)
            before16 = pl.ds(pl.multiple_of(jnp.maximum(first - 16, 0), 16), 16)
            grad_branch[s, at, :], grad_feed[s, at, :] = rec_backward_rows(
                grad_mixed[at, :], branch_ref[s, at, :], feed_ref[s, at, :],
                feed_ref[s, before16, :].astype(jnp.float32)[8:] * keep, conv_ref[s, at, :], rate_ref[s, at, :],
                input_ref[s, at, :], state_ref[s, at, :], state_ref[s, before8, :] * keep,
                vectors_ref, softness_ref, gate_a_ref, gate_x_ref, squares.at[0], squares.at[1], sums,
                window, later, carry,
            )

        if s == seqs - 1:
            for move in square_moves:
                move.start()
            sum_move.start()

    def steps(s):
        partners, own = scatter.fill(s, s, [grad_branch, grad_feed], [branch_w_ref, rec_w_ref], False)

        def third():
            if s == 0:
                for load in loads[1 + len(per_seq) : 3 + len(per_seq)]:
                    load.wait()
            partners()

        def first():
            mix(s)
            if s == seqs - 1:
                out_grads()

        return [first, functools.partial(recur, s), third, own]

    def out_grads():
        loads[-1].wait()
        step = width // parts

        @pl.loop(0, parts)
        def _(k):
            at = pl.ds(pl.multiple_of(k * step, step), step)
            total = matmul_tn(mixed_ref[0], low_ref[0, :, at])
            for s in range(1, seqs):
                total = total + matmul_tn(mixed_ref[s], low_ref[s, :, at])
            d2[:, at] = total.astype(jnp.bfloat16)

        moves[2].start()

    step = tiles.shape[-1]
    count = width // parts // step

    def columns_of(i):
        peer = lax.rem(lax.axis_index("seq") + 1 + i // count, parts)
        return pl.ds(pl.multiple_of((peer * count + lax.rem(i, count)) * step, step), step)

    def tile_load(i, slot):
        return pltpu.make_async_copy(normed_in.at[:, :, columns_of(i)], tiles.at[slot], tile_sem.at[slot])

    def in_grads(part):
        if part == 0:
            tile_load(0, 0).start()

        @pl.loop(part * count, (part + 1) * count)
        def _(i):
            slot = lax.rem(i, 2)
            tile_load(i, slot).wait()

            @pl.when(i + 1 < parts * count)
            def _():
                tile_load(i + 1, 1 - slot).start()

            for to, grads in ((d0, grad_branch), (d1, grad_feed)):
                total = matmul_tn(grads[0], tiles[slot, 0])
                for s in range(1, seqs):
                    total = total + matmul_tn(grads[s], tiles[slot, s])
                to[:, columns_of(i)] = total.astype(jnp.bfloat16)

        for move in moves[:2]:
            if part < parts - 1:
                move.copy(part + 1, move.me).start()
            else:
                move.own().start()

    def grads_from(first, end):
        for part in range(first, end):
            in_grads(part)

    def store(s):
        term = scatter.result(s)[...]
        inputs = x_ref[s].astype(jnp.float32)
        inverse = lax.rsqrt(mean_of(inputs * inputs) + epsilon)
        normal = inputs * inverse
        gain_local[0:1, :] += jnp.sum(term * normal, axis=0, keepdims=True)
        if s == seqs - 1:
            across.start()
        grad_x_ref[s] = grad_ref[s] + norm_back(term, normal, inverse, gain_ref[...])

    sum_then_gather(
        scatter, None, [steps(s) for s in range(seqs)], [functools.partial(store, s) for s in range(seqs)],
        between=functools.partial(grads_from, 0, parts // 2),
        after=(functools.partial(grads_from, parts // 2, parts - 1), functools.partial(grads_from, parts - 1, parts)),
    )
    across.finish()
    gain_part[...] = sum_of(gain_slots)
    along = Exchange("grp", lambda k: gain_part, lambda k: part_slots.at[k], part_send, part_recv)
    along.start()
    for move in square_moves:
        move.finish()
    squares_out_ref[...] = sum_of(square_slots)
    sum_move.finish()
    sums_out_ref[...] = sum_of(sum_slots_ref)
    for move in moves:
        move.finish()
    along.finish()
    gain_sum_ref[...] = sum_of(part_slots)


def mixer_back(
    heads, low, out_w, branch, feed, conv, rate, gate, state, mixed, branch_w, rec_w, normed,
    vectors, softness, gate_a, gate_x, layer_in, grad_residual, gain, gain_two_grad,
):
    seqs, rows, width = layer_in.shape
    seq_len, channels = feed.shape[1:]
    size, n = lax.axis_size("seq"), lax.axis_size("grp")
    f32, bf16 = jnp.float32, jnp.bfloat16
    large = (low, out_w, branch, feed, conv, rate, gate, state, mixed, branch_w, rec_w)
    small = (vectors, softness, gate_a, gate_x, layer_in, grad_residual, gain, gain_two_grad)
    window_rows = head_windows(heads, channels // heads, size)[0]
    grads = [jax.ShapeDtypeStruct(w.shape, bf16) for w in (branch_w, rec_w, out_w)]
    squares = (heads, 2, window_rows, channels)
    part = width // size
    return call(
        functools.partial(mixer_back_body, heads), "mixer_back", 6,
        large + (normed,) + small,
        [in_hbm] * 12 + [in_vmem] * 8,
        [
            jax.ShapeDtypeStruct(layer_in.shape, f32),
            jax.ShapeDtypeStruct(squares, f32),
            jax.ShapeDtypeStruct((8, channels), f32),
            jax.ShapeDtypeStruct((8, part), f32),
        ]
        + [slots_of(grad, axis, 0) for grad, axis in zip(grads, mixer_axes)],
        [in_vmem] * 4 + [in_hbm] * 3,
        [pltpu.VMEM(v.shape, v.dtype) for v in large]
        + [
            pltpu.VMEM((seq_len, channels), f32),
            pltpu.VMEM(feed.shape, bf16),
            pltpu.VMEM(feed.shape, bf16),
            pltpu.VMEM((2, channels, channels), f32),
            pltpu.VMEM((8, channels), f32),
            pltpu.VMEM((pick_rows(seq_len) + 8, channels), f32),
            pltpu.VMEM((pick_rows(seq_len) + 8, channels), f32),
            pltpu.VMEM((8, channels), f32),
            pltpu.VMEM((2, seqs, seq_len, 256), bf16),
        ]
        + [pltpu.VMEM(grad.shape, bf16) for grad in grads]
        + [
            pltpu.VMEM((size,) + squares, f32),
            pltpu.VMEM((size, 8, channels), f32),
            pltpu.VMEM((8, width), f32),
            pltpu.VMEM((8, part), f32),
            pltpu.VMEM((size, 8, part), f32),
            pltpu.VMEM((n, 8, part), f32),
            pltpu.SemaphoreType.DMA((4 + 7 * seqs,)),
            pltpu.SemaphoreType.DMA((2,)),
        ]
        + [pltpu.SemaphoreType.DMA((heads, size))] * 2
        + [pltpu.SemaphoreType.DMA((size,))] * 4
        + [pltpu.SemaphoreType.DMA((n,))] * 2
        + seq_sems(3)
        + scatter_scratch(seqs, rows, width),
        100,
    )


def out_only_body(hidden_ref, down_w_ref, residual_ref, layer_out_ref, *scratch):
    greet_line()
    scatter = Scatter(residual_ref.shape[1], *scratch)
    fill, store = out_body(hidden_ref, down_w_ref, residual_ref, layer_out_ref, scatter, 0)
    seqs = range(residual_ref.shape[0])
    sum_then_gather(
        scatter, None, [fill(s) for s in seqs], [functools.partial(store, s) for s in seqs]
    )


def out_only(hidden, down_w, residual):
    seqs, rows, width = residual.shape
    return call(
        out_only_body, "layer_out", 5,
        (hidden, down_w, residual), [in_vmem] * 3,
        [jax.ShapeDtypeStruct(residual.shape, jnp.bfloat16)], [in_vmem],
        scatter_scratch(seqs, rows, width), 60,
    )[0]


def per_device(
    layer_in, gain_one, w_branch, w_rec, conv_w, conv_b, gate_a_w, gate_a_b, gate_x_w, gate_x_b,
    decay_logit, w_out, gain_two, mlp_gate, mlp_up, mlp_down, out_grad,
):
    seqs_here, positions, model_width = layer_in.shape
    heads_here, tap_count, part_dim = conv_w.shape
    seq_devices, grp_devices = lax.axis_size("seq"), lax.axis_size("grp")
    head_dim = part_dim * seq_devices
    channels = heads_here * head_dim
    f32 = jnp.float32

    own_params = jnp.concatenate(
        [jnp.transpose(conv_w, (0, 2, 1))]
        + [v[:, :, None] for v in (conv_b, gate_a_b, gate_x_b, decay_logit)]
        + [gate_a_w, gate_x_w],
        axis=2,
    ).astype(f32)
    own_gains = jnp.concatenate([gain_one, gain_two]).astype(f32)
    pack = jnp.concatenate(
        [padded_rows(own_params.reshape(1, -1))[0], padded_rows(own_gains.reshape(1, -1))[0]]
    )
    late_grad, x_full, params, gains, branch_w, rec_w, out_w = gather_first(
        layer_in, out_grad, pack, (w_branch.T, w_rec.T, w_out)
    )

    gains = gains.reshape(grp_devices, seq_devices, -1)[:, :, : own_gains.size]
    gains = jnp.transpose(gains.reshape(grp_devices, seq_devices, 2, -1), (2, 1, 0, 3)).reshape(2, 1, -1)
    params = params.reshape(seq_devices, -1)[:, : own_params.size]
    params = params.reshape((seq_devices,) + own_params.shape)
    params = jnp.transpose(params, (1, 0, 2, 3)).reshape(heads_here, head_dim, -1)
    vectors = params[:, :, : tap_count + 4].reshape(channels, -1).T
    at = tap_count + 4
    diag_a = head_diagonal(params[:, :, at : at + head_dim].astype(jnp.bfloat16))
    diag_x = head_diagonal(params[:, :, at + head_dim :].astype(jnp.bfloat16))
    logit = vectors[tap_count + 3 :]
    softness = jax.nn.softplus(-logit)

    short_line = seqs_here * positions * grp_devices <= 2048
    mlp_weights = (mlp_gate, mlp_up, mlp_down)
    if short_line:
        (
            residual, normed_one, branch_pre, feed, conv, rate, gate, state, mixed, normed_two, grad_output,
            gate_w, up_w, down_w,
        ) = mixer_forward(
            x_full, gains, branch_w, rec_w, out_w, vectors, softness, diag_a, diag_x, late_grad, mlp_weights
        )
        normed_one = normed_one.reshape(-1, model_width)
        grad_output = grad_output.reshape(-1, model_width)
    else:
        grad_output = jnp.concatenate(
            [lax.all_gather(late_grad[s], "grp", axis=0, tiled=True) for s in range(seqs_here)]
        )
        inputs = x_full.astype(f32)
        normal_one = inputs * lax.rsqrt(mean_of(inputs * inputs) + epsilon)
        normed_one = (normal_one * gains[0]).astype(jnp.bfloat16).reshape(-1, model_width)
        branch_pre = matmul_nt(normed_one, branch_w).reshape(seqs_here, -1, channels)
        feed = matmul_nt(normed_one, rec_w).astype(jnp.bfloat16).reshape(seqs_here, -1, channels)
        conv, rate, gate, state, mixed = rec_forward(feed, branch_pre, vectors, softness, diag_a, diag_x)
        residual, normed_two, gate_w, up_w, down_w = mixer_out(
            mixed, out_w, layer_in, gains[1], mlp_weights
        )
    mixed = mixed.reshape(-1, channels)
    normed_two = normed_two.reshape(-1, model_width)
    up_proj = matmul(normed_two, up_w)
    gate_act, gate_pull = jax.vjp(jax.nn.gelu, matmul(normed_two, gate_w))
    hidden = (gate_act * up_proj).astype(jnp.bfloat16)
    grad_hidden = matmul_nt(grad_output, down_w)
    grad_gate = gate_pull(grad_hidden * up_proj)[0].astype(jnp.bfloat16)
    grad_up = (grad_hidden * gate_act).astype(jnp.bfloat16)
    mlp_grads = low_all(
        (matmul_tn(normed_two, grad_gate), matmul_tn(normed_two, grad_up), matmul_tn(hidden, grad_output))
    )

    def by_seq(values):
        return values.reshape(seqs_here, -1, values.shape[-1])

    back_inputs = (
        by_seq(grad_gate), by_seq(grad_up), gate_w, up_w, residual, out_grad, gains[1], mlp_grads
    )
    if not short_line:
        layer_out = out_only(by_seq(hidden), down_w, residual)
        grad_residual, gain_two_grad, residual_low, *mlp_slots = mlp_back(*back_inputs, ())
    else:
        grad_residual, gain_two_grad, residual_low, *mlp_slots, layer_out, late = mlp_back(
            *back_inputs, (by_seq(hidden), down_w)
        )
        late = lax.psum_scatter(late, "grp", scatter_dimension=0, tiled=True)
        late = (residual[seqs_here - 1] + late.astype(f32)).astype(jnp.bfloat16)
        layer_out = jnp.concatenate([layer_out, late[None]])
    mlp_grads = sum_slots(mlp_grads, mlp_slots, weight_axes)
    if short_line:
        grad_x, squares, sums, gain_sum, *mixer_slots = mixer_back(
            heads_here, residual_low, out_w, branch_pre, feed, conv, rate, gate, state, by_seq(mixed), branch_w, rec_w,
            by_seq(normed_one), vectors, softness, diag_a, diag_x, layer_in, grad_residual, gains[0], gain_two_grad,
        )
        mixer_grads = [sum_all(slot) for slot in mixer_slots]
        place = lax.axis_index("seq")
        first = place * part_dim % 8
        square_parts = [
            lax.dynamic_slice_in_dim(squares[h], first, part_dim, 1)[:, :, h * head_dim : (h + 1) * head_dim]
            for h in range(heads_here)
        ]
        grad_a, grad_x_gate = (jnp.stack([part[i] for part in square_parts]) for i in range(2))
        own_sums = lax.dynamic_slice_in_dim(
            sums.reshape(at, heads_here, head_dim), place * part_dim, part_dim, 2
        )
        logit_grad = 8.0 * jax.nn.sigmoid(-decay_logit.astype(f32)) * own_sums[tap_count + 3]
        rec_outs = (
            jnp.transpose(own_sums[:tap_count], (1, 0, 2)), own_sums[tap_count], grad_a, own_sums[tap_count + 1],
            grad_x_gate, own_sums[tap_count + 2], logit_grad,
        )
        return finish(layer_out, grad_x, gain_sum, mixer_grads, rec_outs, mlp_grads)
    residual_low = residual_low.reshape(-1, model_width)
    out_weight_grad = matmul_tn(mixed, residual_low)
    grad_mixed = by_seq(matmul_nt(residual_low, out_w))
    grad_branch, grad_feed, square_a, square_x, sums = rec_backward(
        grad_mixed, branch_pre, feed, conv, rate, gate, state, vectors, softness, diag_a, diag_x
    )
    vector_grads = jnp.concatenate(
        [sums[: tap_count + 3], 8.0 * jax.nn.sigmoid(-logit) * sums[tap_count + 3 :]]
    )
    rec_grads = jnp.concatenate(
        [
            vector_grads.T.reshape(heads_here, head_dim, -1),
            diagonal_heads(square_a, heads_here),
            diagonal_heads(square_x, heads_here),
        ],
        axis=2,
    )
    rec_grads = rec_grads.reshape(heads_here, seq_devices, part_dim, -1)
    rec_blocks = padded_rows(jnp.transpose(rec_grads, (1, 0, 2, 3)))
    mixer_grads = low_all(
        (
            matmul_tn(grad_branch.reshape(-1, channels), normed_one),
            matmul_tn(grad_feed.reshape(-1, channels), normed_one),
            out_weight_grad,
        )
    )
    grad_x, rec_sum, gain_sum, *mixer_slots = last(
        grad_branch, grad_feed, branch_w, rec_w, layer_in, grad_residual, gains[0], gain_two_grad, rec_blocks,
        mixer_grads,
    )
    mixer_grads = sum_slots(mixer_grads, mixer_slots, mixer_axes)
    rec_sum = rec_sum.reshape(-1)[: own_params.size].reshape(own_params.shape)
    rec_outs = (
        jnp.transpose(rec_sum[:, :, :tap_count], (0, 2, 1)),
        rec_sum[:, :, tap_count],
        rec_sum[:, :, at : at + head_dim],
        rec_sum[:, :, tap_count + 1],
        rec_sum[:, :, at + head_dim :],
        rec_sum[:, :, tap_count + 2],
        rec_sum[:, :, tap_count + 3],
    )
    return finish(layer_out, grad_x, gain_sum, mixer_grads, rec_outs, mlp_grads)


def finish(layer_out, grad_x, gain_sum, mixer_grads, rec_outs, mlp_grads):
    part = gain_sum.shape[1] // lax.axis_size("grp")
    gain_grads = lax.dynamic_slice_in_dim(gain_sum, lax.axis_index("grp") * part, part, 1)
    return (
        layer_out, grad_x, gain_grads[0], mixer_grads[0].T, mixer_grads[1].T, *rec_outs, mixer_grads[2], gain_grads[1],
        *mlp_grads,
    )


def solution(mesh):
    placed = (
        P("seq", "grp", None),
        P(("seq", "grp")),
        P("seq", "grp"),
        P("seq", "grp"),
        P("grp", None, "seq"),
        P("grp", "seq"),
        P("grp", "seq", None),
        P("grp", "seq"),
        P("grp", "seq", None),
        P("grp", "seq"),
        P("grp", "seq"),
        P("grp", "seq"),
        P(("seq", "grp")),
        P("seq", "grp"),
        P("seq", "grp"),
        P("grp", "seq"),
        P("seq", "grp", None),
    )
    return jax.shard_map(
        per_device,
        mesh=mesh,
        in_specs=placed,
        out_specs=(
            P("seq", "grp", None),
            P("seq", "grp", None),
            P(("seq", "grp")),
            P("seq", "grp"),
            P("seq", "grp"),
            P("grp", None, "seq"),
            P("grp", "seq"),
            P("grp", "seq", None),
            P("grp", "seq"),
            P("grp", "seq", None),
            P("grp", "seq"),
            P("grp", "seq"),
            P("grp", "seq"),
            P(("seq", "grp")),
            P("seq", "grp"),
            P("seq", "grp"),
            P("grp", "seq"),
        ),
        check_vma=False,
    )
```

```python
import functools
import math

import jax
import jax.numpy as jnp
from jax import lax
from jax.experimental import pallas as pl
from jax.experimental.pallas import tpu as pltpu
from jax.sharding import PartitionSpec as P

epsilon = 1e-06
gelu_slope = math.sqrt(2.0 / math.pi)
gelu_cubic = 0.044715
MESH = pl.DeviceIdType.MESH


def matmul(left, right):
    return jnp.dot(left, right, preferred_element_type=jnp.float32)


def matmul_tn(left, right):
    return lax.dot_general(
        left, right, (((0,), (0,)), ((), ())), preferred_element_type=jnp.float32
    )


def matmul_nt(left, right):
    return lax.dot_general(
        left, right, (((1,), (1,)), ((), ())), preferred_element_type=jnp.float32
    )


def norm_back(grad_normed, normal_part, inverse, gain):
    scaled = grad_normed * gain
    return inverse * (scaled - normal_part * jnp.mean(scaled * normal_part, axis=-1, keepdims=True))


def low_all(grads):
    return tuple(grad.astype(jnp.bfloat16) for grad in grads)


def sum_slots(grads, slots, axes):
    sums = []
    for grad, slot, axis in zip(grads, slots, axes):
        size = slot.shape[1 + axis]
        own = lax.dynamic_slice_in_dim(grad, lax.axis_index("seq") * size, size, axis)
        for k in range(slot.shape[0]):
            own = own.astype(jnp.float32) + slot[k].astype(jnp.float32)
        sums.append(own)
    return sums


def sum_all(slots):
    total = slots[0].astype(jnp.float32)
    for k in range(1, slots.shape[0]):
        total = total + slots[k].astype(jnp.float32)
    return total


def padded_rows(values):
    flat = values.reshape(values.shape[0], -1)
    flat = jnp.pad(flat, ((0, 0), (0, -flat.shape[1] % 1024)))
    return flat.reshape(values.shape[0], -1, 128)


def head_diagonal(blocks):
    heads, head_dim, _ = blocks.shape
    rows = []
    for h in range(heads):
        row = [jnp.zeros((head_dim, head_dim), blocks.dtype)] * heads
        row[h] = blocks[h]
        rows.append(jnp.concatenate(row, axis=1))
    return jnp.concatenate(rows, axis=0)


def diagonal_heads(square, heads):
    head_dim = square.shape[0] // heads
    return jnp.stack(
        [
            square[h * head_dim : (h + 1) * head_dim, h * head_dim : (h + 1) * head_dim]
            for h in range(heads)
        ]
    )


def pick_rows(seq_len, choices=(128, 96, 64, 32, 16)):
    for rows in choices:
        if seq_len % rows == 0:
            return rows
    return seq_len


def gelu_parts(x):
    cubic = gelu_slope * (x + gelu_cubic * x * x * x)
    bend = jnp.tanh(cubic)
    gate = 0.5 * (1.0 + bend)
    slope = gate + 0.5 * x * (1.0 - bend * bend) * gelu_slope * (1.0 + 3.0 * gelu_cubic * x * x)
    return x * gate, slope


def minus_expm1(x):
    series = 1.0 + x * (1.0 / 9.0)
    for k in (8, 7, 6, 5, 4, 3, 2):
        series = 1.0 + x * (1.0 / k) * series
    return jnp.where(x > -0.4, -x * series, 1.0 - jnp.exp(x))


def shift_down(values, by, fill):
    rows = values.shape[0]
    if by % 8 == 0:
        return jnp.concatenate([jnp.full((by, values.shape[1]), fill), values[: rows - by]], axis=0)
    index = lax.broadcasted_iota(jnp.int32, values.shape, 0)
    return jnp.where(index >= by, pltpu.roll(values, by, 0), fill)


def shift_up(values, by, fill):
    rows = values.shape[0]
    if by % 8 == 0:
        return jnp.concatenate([values[by:], jnp.full((by, values.shape[1]), fill)], axis=0)
    index = lax.broadcasted_iota(jnp.int32, values.shape, 0)
    return jnp.where(index < rows - by, pltpu.roll(values, rows - by, 0), fill)


def scan_block(decay, drive, shift):
    by = 1
    while by < decay.shape[0]:
        drive = drive + decay * shift(drive, by, 0.0)
        decay = decay * shift(decay, by, 1.0)
        by *= 2
    return decay, drive


def decay_parts(rate, softness):
    log_decay = -8.0 * rate * softness
    return jnp.exp(log_decay), jnp.sqrt(minus_expm1(2.0 * log_decay))


def rec_forward_rows(feed, branch, vectors_ref, softness_ref, gate_a_ref, gate_x_ref, window, carry):
    rows = feed.shape[0]
    window[pl.ds(8, rows), :] = feed.astype(jnp.float32)
    conv = vectors_ref[4:5, :] + vectors_ref[0:1, :] * window[pl.ds(8, rows), :]
    for k in range(1, 4):
        conv = conv + vectors_ref[k : k + 1, :] * window[pl.ds(8 - k, rows), :]
    window[pl.ds(0, 8), :] = window[pl.ds(rows, 8), :]
    conv_low = conv.astype(jnp.bfloat16)
    rate = jax.nn.sigmoid(matmul(conv_low, gate_a_ref[...]) + vectors_ref[5:6, :])
    gate = jax.nn.sigmoid(matmul(conv_low, gate_x_ref[...]) + vectors_ref[6:7, :])
    decay, scale = decay_parts(rate, softness_ref[...])
    total, state = scan_block(decay, scale * gate * conv_low.astype(jnp.float32), shift_down)
    state = state + total * carry[0:1, :]
    carry[0:1, :] = state[rows - 1 : rows, :]
    gelu_branch = gelu_parts(branch)[0]
    mixed = (gelu_branch * state.astype(jnp.bfloat16).astype(jnp.float32)).astype(jnp.bfloat16)
    return conv_low, rate, gate, state, mixed


def rec_forward_body(
    feed_ref, branch_ref, vectors_ref, softness_ref, gate_a_ref, gate_x_ref,
    conv_ref, rate_ref, input_ref, state_ref, mixed_ref, window, carry,
):
    @pl.when(pl.program_id(0) == 0)
    def _():
        window[...] = jnp.zeros_like(window)
        carry[...] = jnp.zeros_like(carry)

    for s in range(feed_ref.shape[0]):
        conv_ref[s], rate_ref[s], input_ref[s], state_ref[s], mixed_ref[s] = rec_forward_rows(
            feed_ref[s], branch_ref[s], vectors_ref, softness_ref, gate_a_ref, gate_x_ref, window.at[s], carry.at[s]
        )


def rec_backward_rows(
    grad_mixed, branch, feed, feed_before, conv_low, rate, gate, state, state_before,
    vectors_ref, softness_ref, gate_a_ref, gate_x_ref, grad_a_ref, grad_x_ref, sums_ref, window, later, carry,
):
    rows = feed.shape[0]
    softness = softness_ref[...]
    gelu_branch, slope = gelu_parts(branch)
    state_low = state.astype(jnp.bfloat16).astype(jnp.float32)
    grad_state = (grad_mixed * gelu_branch).astype(jnp.bfloat16).astype(jnp.float32)
    grad_branch = (slope * grad_mixed * state_low).astype(jnp.bfloat16)
    decay, scale = decay_parts(rate, softness)
    total, carried = scan_block(shift_up(decay, 1, 1.0), grad_state, shift_up)
    carried = carried + total * carry[0:1, :]
    carry[0:1, :] = decay[0:1, :] * carried[0:1, :]
    index = lax.broadcasted_iota(jnp.int32, state.shape, 0)
    previous = jnp.where(index >= 1, pltpu.roll(state, 1, 0), state_before[7:8, :])
    conv = conv_low.astype(jnp.float32)
    grad_log = carried * previous * decay - carried * gate * conv * decay * decay / scale
    log_rate = grad_log * rate
    pre_a = -8.0 * softness * log_rate * (1.0 - rate)
    pre_x = carried * scale * conv * gate * (1.0 - gate)
    low_a = pre_a.astype(jnp.bfloat16)
    low_x = pre_x.astype(jnp.bfloat16)
    grad_a_ref[...] += matmul_tn(conv_low, low_a)
    grad_x_ref[...] += matmul_tn(conv_low, low_x)
    grad_conv = (
        carried * scale * gate
        + matmul_nt(low_a, gate_a_ref[...])
        + matmul_nt(low_x, gate_x_ref[...])
    )
    window[pl.ds(0, 8), :] = feed_before
    window[pl.ds(8, rows), :] = feed.astype(jnp.float32)
    later[pl.ds(rows, 8), :] = later[pl.ds(0, 8), :]
    later[pl.ds(0, rows), :] = grad_conv
    grad_feed = vectors_ref[0:1, :] * grad_conv
    sums_ref[0:1, :] += jnp.sum(grad_conv * window[pl.ds(8, rows), :], axis=0, keepdims=True)
    for k in range(1, 4):
        grad_feed = grad_feed + vectors_ref[k : k + 1, :] * later[pl.ds(k, rows), :]
        sums_ref[k : k + 1, :] += jnp.sum(
            grad_conv * window[pl.ds(8 - k, rows), :], axis=0, keepdims=True
        )
    sums_ref[4:5, :] += jnp.sum(grad_conv, axis=0, keepdims=True)
    sums_ref[5:6, :] += jnp.sum(pre_a, axis=0, keepdims=True)
    sums_ref[6:7, :] += jnp.sum(pre_x, axis=0, keepdims=True)
    sums_ref[7:8, :] += jnp.sum(log_rate, axis=0, keepdims=True)
    return grad_branch, grad_feed.astype(jnp.bfloat16)


def rec_backward_body(
    grad_mixed_ref, branch_ref, feed_ref, feed_before_ref, conv_ref, rate_ref, input_ref,
    state_ref, state_before_ref, vectors_ref, softness_ref, gate_a_ref, gate_x_ref,
    grad_branch_ref, grad_feed_ref, grad_a_ref, grad_x_ref, sums_ref, window, later, carry,
):
    step = pl.program_id(0)

    @pl.when(step == 0)
    def _():
        for ref in (later, carry, grad_a_ref, grad_x_ref, sums_ref):
            ref[...] = jnp.zeros_like(ref)

    keep = jnp.where(step == pl.num_programs(0) - 1, 0.0, 1.0)
    for s in range(feed_ref.shape[0]):
        before = feed_before_ref[s].astype(jnp.float32)
        grad_branch_ref[s], grad_feed_ref[s] = rec_backward_rows(
            grad_mixed_ref[s], branch_ref[s], feed_ref[s], before[before.shape[0] - 8 :] * keep, conv_ref[s],
            rate_ref[s], input_ref[s], state_ref[s], state_before_ref[s] * keep,
            vectors_ref, softness_ref, gate_a_ref, gate_x_ref, grad_a_ref, grad_x_ref, sums_ref,
            window.at[s], later.at[s], carry.at[s],
        )


def whole(shape):
    return pl.BlockSpec(shape, lambda i: (0,) * len(shape))


def rec_forward(feed, branch, vectors, softness, gate_a, gate_x):
    seqs, seq_len, channels = feed.shape
    rows = pick_rows(seq_len)
    block = pl.BlockSpec((seqs, rows, channels), lambda i: (0, i, 0))
    full = jax.ShapeDtypeStruct(feed.shape, jnp.float32)
    low = jax.ShapeDtypeStruct(feed.shape, jnp.bfloat16)
    return pl.pallas_call(
        rec_forward_body,
        grid=(seq_len // rows,),
        in_specs=[block, block]
        + [whole(v.shape) for v in (vectors, softness, gate_a, gate_x)],
        out_specs=[block] * 5,
        out_shape=[low, full, full, full, low],
        scratch_shapes=[
            pltpu.VMEM((seqs, rows + 8, channels), jnp.float32),
            pltpu.VMEM((seqs, 8, channels), jnp.float32),
        ],
        compiler_params=pltpu.CompilerParams(vmem_limit_bytes=40 << 20),
        name="rec_forward",
    )(feed, branch, vectors, softness, gate_a, gate_x)


def rec_backward(grad_mixed, branch, feed, conv, rate, gate, state, vectors, softness, gate_a, gate_x):
    seqs, seq_len, channels = feed.shape
    rows = pick_rows(seq_len)
    blocks = seq_len // rows
    block = pl.BlockSpec((seqs, rows, channels), lambda i: (0, blocks - 1 - i, 0))

    def ahead(by):
        return pl.BlockSpec(
            (seqs, by, channels),
            lambda i: (0, jnp.maximum((blocks - 1 - i) * (rows // by) - 1, 0), 0),
        )

    low = jax.ShapeDtypeStruct(feed.shape, jnp.bfloat16)
    square = jax.ShapeDtypeStruct((channels, channels), jnp.float32)
    return pl.pallas_call(
        rec_backward_body,
        grid=(blocks,),
        in_specs=[block, block, block, ahead(16), block, block, block, block, ahead(8)]
        + [whole(v.shape) for v in (vectors, softness, gate_a, gate_x)],
        out_specs=[block, block, whole((channels, channels)), whole((channels, channels)), whole((8, channels))],
        out_shape=[low, low, square, square, jax.ShapeDtypeStruct((8, channels), jnp.float32)],
        scratch_shapes=[
            pltpu.VMEM((seqs, rows + 8, channels), jnp.float32),
            pltpu.VMEM((seqs, rows + 8, channels), jnp.float32),
            pltpu.VMEM((seqs, 8, channels), jnp.float32),
        ],
        compiler_params=pltpu.CompilerParams(vmem_limit_bytes=40 << 20),
        name="rec_backward",
    )(grad_mixed, branch, feed, feed, conv, rate, gate, state, state, vectors, softness, gate_a, gate_x)


def line_place():
    return lax.axis_size("grp") // 2, lax.axis_index("grp") // 2, lax.axis_index("grp") % 2


def greet_line():
    chips, chip, core = line_place()
    barrier = pltpu.get_barrier_semaphore()

    def signal(place):
        pl.semaphore_signal(barrier, inc=1, device_id={"grp": place}, device_id_type=MESH)

    signal(chip * 2 + 1 - core)

    @pl.when(chip > 0)
    def _():
        signal(chip * 2 + core - 2)

    @pl.when(chip < chips - 1)
    def _():
        signal(chip * 2 + core + 2)

    ends = (chip == 0).astype(jnp.int32) + (chip == chips - 1).astype(jnp.int32)
    pl.semaphore_wait(barrier, 3 - ends)


def greet_axes(axes):
    barrier = pltpu.get_barrier_semaphore()
    for axis in axes:
        size = lax.axis_size(axis)
        for k in range(1, size):
            pl.semaphore_signal(
                barrier,
                inc=1,
                device_id={axis: lax.rem(lax.axis_index(axis) + k, size)},
                device_id_type=MESH,
            )
    pl.semaphore_wait(barrier, sum(lax.axis_size(axis) - 1 for axis in axes))


class Gather:
    def __init__(self, sources, outs, rows, send_sem, recv_sem, own_sem):
        self.chips, self.chip, self.core = line_place()
        self.me = self.chip * 2 + self.core
        self.sources, self.outs, self.rows = sources, outs, rows
        self.send_sem, self.recv_sem, self.own_sem = send_sem, recv_sem, own_sem

    def slot(self, p, origin):
        return self.outs[p].at[pl.ds(pl.multiple_of(origin * self.rows, self.rows), self.rows), :]

    def copy(self, p, source, origin, target, way):
        return pltpu.make_async_remote_copy(
            src_ref=source,
            dst_ref=self.slot(p, origin),
            send_sem=self.send_sem.at[way, p, origin],
            recv_sem=self.recv_sem.at[p, origin],
            device_id={"grp": target},
            device_id_type=MESH,
        )

    def to_right(self, p, source, origin):
        return self.copy(p, source, origin, self.me + 2, 0)

    def to_left(self, p, source, origin):
        return self.copy(p, source, origin, self.me - 2, 1)

    def to_partner(self, p, source, origin):
        return self.copy(p, source, origin, self.chip * 2 + 1 - self.core, 2)

    def own(self, p):
        return pltpu.make_async_copy(self.sources[p], self.slot(p, self.me), self.own_sem.at[p])

    def start(self, p):
        source = self.sources[p]

        @pl.when(self.chip < self.chips - 1)
        def _():
            self.to_right(p, source, self.me).start()

        @pl.when(self.chip > 0)
        def _():
            self.to_left(p, source, self.me).start()

        self.to_partner(p, source, self.me).start()
        self.own(p).start()

    def hop(self, p, h):
        left_origin = self.me - 2 - 2 * h
        right_origin = self.me + 2 + 2 * h

        @pl.when(self.chip - 1 - h >= 0)
        def _():
            here = self.slot(p, left_origin)
            self.to_right(p, here, left_origin).wait_recv()

            @pl.when(self.chip < self.chips - 1)
            def _():
                self.to_right(p, here, left_origin).start()

            self.to_partner(p, here, left_origin).start()

        @pl.when(self.chip + 1 + h <= self.chips - 1)
        def _():
            here = self.slot(p, right_origin)
            self.to_left(p, here, right_origin).wait_recv()

            @pl.when(self.chip > 0)
            def _():
                self.to_left(p, here, right_origin).start()

            self.to_partner(p, here, right_origin).start()

    def arrive(self, p):
        for c in range(self.chips):
            origin = c * 2 + 1 - self.core
            self.to_partner(p, self.slot(p, origin), origin).wait_recv()
        self.own(p).wait()

    def finish(self, p):
        self.arrive(p)
        self.sent(p)

    def sent(self, p):
        for c in range(self.chips):
            origin = c * 2 + self.core
            here = self.slot(p, origin)
            self.to_partner(p, here, origin).wait_send()

            @pl.when((c <= self.chip) & (self.chip < self.chips - 1))
            def _():
                self.to_right(p, here, origin).wait_send()

            @pl.when((c >= self.chip) & (self.chip > 0))
            def _():
                self.to_left(p, here, origin).wait_send()


def gather_sems(pieces):
    n = lax.axis_size("grp")
    return [
        pltpu.SemaphoreType.DMA((3, pieces, n)),
        pltpu.SemaphoreType.DMA((pieces, n)),
        pltpu.SemaphoreType.DMA((pieces,)),
    ]


class Scatter:
    def __init__(self, rows, part, out, swap_in, line_in, send_sem, recv_sem):
        self.chips, self.chip, self.core = line_place()
        self.me = self.chip * 2 + self.core
        self.rows, self.part, self.out = rows, part, out
        self.swap_in, self.line_in = swap_in, line_in
        self.send_sem, self.recv_sem = send_sem, recv_sem

    def copy(self, dest, place, way, slot, p):
        return pltpu.make_async_remote_copy(
            src_ref=self.out.at[p, slot],
            dst_ref=dest,
            send_sem=self.send_sem.at[way, p, slot],
            recv_sem=self.recv_sem.at[way, p, slot],
            device_id={"grp": place},
            device_id_type=MESH,
        )

    def swap(self, p, c):
        return self.copy(self.swap_in.at[p, c], self.chip * 2 + 1 - self.core, 0, c, p)

    def right(self, p, c):
        return self.copy(self.line_in.at[p, c], self.me + 2, 1, c, p)

    def left(self, p, c):
        slot = jnp.where(c == self.chip - 1, self.chips, c)
        return self.copy(self.line_in.at[p, slot], self.me - 2, 2, c, p)

    def from_right(self, p, c):
        slot = jnp.where(c == self.chip, self.chips, c)
        return self.copy(self.line_in.at[p, slot], self.me + 2, 2, c, p)

    def fill(self, p, s, lefts, rights, transposed, width=512):
        def rows_of(ref, core):
            at = [pl.multiple_of((c * 2 + core) * self.rows, self.rows) for c in range(self.chips)]
            return jnp.concatenate([ref[s, pl.ds(a, self.rows), :] for a in at], axis=0)

        def product(core, store):
            chosen = [rows_of(ref, core) for ref in lefts]

            @pl.loop(0, self.out.shape[-1] // width)
            def _(j):
                columns = pl.ds(pl.multiple_of(j * width, width), width)
                total = None
                for left, right in zip(chosen, rights):
                    term = matmul_nt(left, right[columns, :]) if transposed else matmul(left, right[:, columns])
                    total = term if total is None else total + term
                for c in range(self.chips):
                    store(c, columns, total[c * self.rows : (c + 1) * self.rows])

        def to_out(c, columns, value):
            self.out[p, c, :, columns] = value.astype(jnp.bfloat16)

        def to_part(c, columns, value):
            self.part[p, c, :, columns] = value

        def partners():
            product(1 - self.core, to_out)
            for c in range(self.chips):
                self.swap(p, c).start()

        def own():
            product(self.core, to_part)

        return partners, own

    def own(self, p, c):
        self.swap(p, c).wait_recv()
        return self.part[p, c] + self.swap_in[p, c].astype(jnp.float32)

    def hop(self, p, t):
        last = self.chips - 1

        def send(c, first, arrival, onward):
            self.swap(p, c).wait_send()
            total = self.own(p, c)

            @pl.when(first)
            def _():
                self.out[p, c] = total.astype(jnp.bfloat16)

            @pl.when(jnp.logical_not(first))
            def _():
                arrival(p, c).wait_recv()
                self.out[p, c] = (total + self.line_in[p, c].astype(jnp.float32)).astype(jnp.bfloat16)

            onward(p, c).start()

        @pl.when(self.chip <= t)
        def _():
            send(last - t + self.chip, self.chip == 0, self.right, self.right)

        @pl.when(last - self.chip <= t)
        def _():
            send(t - last + self.chip, self.chip == last, self.from_right, self.left)

    def result(self, p):
        chip = self.chip
        self.part[p, chip] = self.own(p, chip)

        @pl.when(chip > 0)
        def _():
            self.right(p, chip).wait_recv()
            self.part[p, chip] += self.line_in[p, chip].astype(jnp.float32)

        @pl.when(chip < self.chips - 1)
        def _():
            self.from_right(p, chip).wait_recv()
            self.part[p, chip] += self.line_in[p, self.chips].astype(jnp.float32)

        return self.part.at[p, chip]

    def finish(self, p):
        self.swap(p, self.chip).wait_send()
        for c in range(self.chips):

            @pl.when(c > self.chip)
            def _():
                self.right(p, c).wait_send()

            @pl.when(c < self.chip)
            def _():
                self.left(p, c).wait_send()


def scatter_scratch(pieces, rows, width):
    chips = lax.axis_size("grp") // 2
    return [
        pltpu.VMEM((pieces, chips, rows, width), jnp.float32),
        pltpu.VMEM((pieces, chips, rows, width), jnp.bfloat16),
        pltpu.VMEM((pieces, chips, rows, width), jnp.bfloat16),
        pltpu.VMEM((pieces, chips + 1, rows, width), jnp.bfloat16),
        pltpu.SemaphoreType.DMA((3, pieces, chips)),
        pltpu.SemaphoreType.DMA((3, pieces, chips)),
    ]


in_vmem = pl.BlockSpec(memory_space=pltpu.VMEM)
in_hbm = pl.BlockSpec(memory_space=pl.ANY)


def call(body, name, number, inputs, in_specs, outs, out_specs, scratch, us):
    return pl.pallas_call(
        body,
        in_specs=in_specs,
        out_specs=out_specs,
        out_shape=outs,
        scratch_shapes=scratch,
        name=name,
        cost_estimate=pl.CostEstimate(
            flops=us * 1000000000, bytes_accessed=us * 3000000, transcendentals=0
        ),
        compiler_params=pltpu.CompilerParams(
            collective_id=number, has_side_effects=True, vmem_limit_bytes=62 << 20
        ),
    )(*inputs)


class Exchange:
    def __init__(self, axis, source, slot, send_sem, recv_sem, steps=None, first=1):
        self.axis, self.source, self.slot, self.steps, self.first = axis, source, slot, steps, first
        self.size, self.me = lax.axis_size(axis), lax.axis_index(axis)
        self.send_sem, self.recv_sem = send_sem, recv_sem

    def copy(self, k, owner):
        peer = lax.rem(self.me + k, self.size)
        return pltpu.make_async_remote_copy(
            src_ref=self.source(peer),
            dst_ref=self.slot(owner) if self.slot else self.steps.at[k - self.first],
            send_sem=self.send_sem.at[k],
            recv_sem=self.recv_sem.at[k],
            device_id={self.axis: peer},
            device_id_type=MESH,
        )

    def own(self):
        slot = self.slot(self.me) if self.slot else self.steps.at[0]
        return pltpu.make_async_copy(self.source(self.me), slot, self.send_sem.at[0])

    def start(self):
        self.own().start()
        self.start_others()

    def start_others(self):
        for k in range(1, self.size):
            self.copy(k, self.me).start()

    def finish(self):
        self.own().wait()
        self.finish_others()

    def finish_others(self):
        for k in range(1, self.size):
            self.copy(k, lax.rem(self.me - k + self.size, self.size)).wait_recv()
        for k in range(1, self.size):
            self.copy(k, self.me).wait_send()


def sum_of(slots):
    total = slots[0]
    for k in range(1, slots.shape[0]):
        total = total + slots[k]
    return total


def block(ref, axis, parts):
    size = ref.shape[axis] // parts

    def view(k):
        at = pl.ds(pl.multiple_of(k * size, size), size)
        return ref.at[at, :] if axis == 0 else ref.at[:, at]

    return view


def weight_gathers(axes, sources, outs, send_sem, recv_sem):
    parts = lax.axis_size("seq")
    return [
        Exchange(
            "seq", lambda k, ref=source: ref, block(out, axis, parts), send_sem.at[i], recv_sem.at[i]
        )
        for i, (axis, source, out) in enumerate(zip(axes, sources, outs))
    ]


def weight_sums(axes, sources, outs, send_sem, recv_sem, first=1):
    parts = lax.axis_size("seq")
    return [
        Exchange(
            "seq", block(source, axis, parts), None, send_sem.at[i], recv_sem.at[i], out, first
        )
        for i, (axis, source, out) in enumerate(zip(axes, sources, outs))
    ]


def seq_sems(count):
    return [pltpu.SemaphoreType.DMA((count, lax.axis_size("seq")))] * 2


def gathered(block_of, axis):
    shape = list(block_of.shape)
    shape[axis] *= lax.axis_size("seq")
    return jax.ShapeDtypeStruct(shape, block_of.dtype)


def slots_of(matrix, axis, first=1):
    shape = list(matrix.shape)
    size = lax.axis_size("seq")
    shape[axis] //= size
    return jax.ShapeDtypeStruct((size - first, *shape), matrix.dtype)


weight_axes = (0, 0, 1)
mixer_axes = (1, 1, 1)


def copies(pairs, sem):
    return [pltpu.make_async_copy(source, buffer, sem.at[i]) for i, (source, buffer) in enumerate(pairs)]


def views(ref):
    return [ref.at[s] for s in range(ref.shape[0])]


def first_body(x_ref, grad_ref, pack_ref, w0, w1, w2, later_ref, full_ref, params_ref, gains_ref, o0, o1, o2, *refs):
    small_send, small_recv, gain_send, gain_recv, weight_send, weight_recv = refs[3:]
    greet_axes(("seq", "grp"))
    seqs = x_ref.shape[0]
    gather = Gather(views(x_ref), views(full_ref), x_ref.shape[1], *refs[:3])
    weights = weight_gathers(mixer_axes, (w0, w1, w2), (o0, o1, o2), weight_send, weight_recv)
    small = Exchange("seq", lambda k: pack_ref, lambda k: params_ref.at[k], small_send, small_recv)
    small.start()
    for s in range(seqs):
        gather.start(s)
    for weight in weights:
        weight.start()
    later_ref[...] = grad_ref[...]
    small.finish()
    place = lax.axis_index("grp")
    for owner in range(small.size):
        gains_ref[place, owner] = params_ref[owner, pl.ds(pack_ref.shape[0] - 8, 8), :]
    gains = Exchange("grp", lambda k: gains_ref.at[place], lambda k: gains_ref.at[k], gain_send, gain_recv)
    gains.start_others()
    for h in range(gather.chips - 1):
        for s in range(seqs):
            gather.hop(s, h)
    gains.finish_others()
    for weight in weights:
        weight.finish()
    for s in range(seqs):
        gather.finish(s)


def gather_first(layer_in, out_grad, pack, weights):
    seqs, rows, width = layer_in.shape
    n, size = lax.axis_size("grp"), lax.axis_size("seq")
    return call(
        first_body, "gather_first", 1,
        (layer_in, out_grad, pack, *weights), [in_vmem] * 6,
        [
            jax.ShapeDtypeStruct(out_grad.shape, out_grad.dtype),
            jax.ShapeDtypeStruct((seqs, n * rows, width), jnp.bfloat16),
            jax.ShapeDtypeStruct((size,) + pack.shape, jnp.float32),
            jax.ShapeDtypeStruct((n, size, 8, 128), jnp.float32),
        ]
        + [gathered(w, axis) for w, axis in zip(weights, mixer_axes)],
        [in_vmem, in_hbm] + [in_vmem] * 2 + [in_hbm] * 3,
        gather_sems(seqs)
        + [pltpu.SemaphoreType.DMA((size,))] * 2
        + [pltpu.SemaphoreType.DMA((n,))] * 2
        + seq_sems(3),
        70,
    )


def mean_of(values):
    return jnp.mean(values, axis=-1, keepdims=True)


def sum_then_gather(scatter, gather, fills, stores, count=0, between=None, after=()):
    hops = range(1, scatter.chips - 1)
    for step in fills[0]:
        step()
    scatter.hop(0, 0)
    for p, store in enumerate(stores):
        ahead = list(fills[p + 1] if p + 1 < len(fills) else after)
        for h in hops:
            if ahead:
                ahead.pop(0)()
            scatter.hop(p, h)
            if 0 < p <= count:
                gather.hop(p - 1, h - 1)
        for step in ahead:
            step()
        if p + 1 < len(fills):
            scatter.hop(p + 1, 0)
        if between and p == 0:
            between()
        store()
        if p < count:
            gather.start(p)
        if 0 < p <= count:
            gather.hop(p - 1, gather.chips - 2)
    if count == len(stores):
        for h in range(gather.chips - 1):
            gather.hop(count - 1, h)
    for p in range(count):
        gather.finish(p)
    for p in range(len(fills)):
        scatter.finish(p)


def out_body(hidden_ref, down_w_ref, residual_ref, layer_out_ref, scatter, first):
    def fill(s):
        return scatter.fill(first + s, s, [hidden_ref], [down_w_ref], False)

    def store(s):
        layer_out_ref[s] = (residual_ref[s] + scatter.result(first + s)[...]).astype(jnp.bfloat16)

    return fill, store


def mixer_out_body(mixed_ref, out_w_ref, x_ref, gain_ref, w0, w1, w2, residual_ref, normed_ref, o0, o1, o2, low_ref, *refs):
    greet_axes(("seq", "grp"))
    seqs, rows, _ = x_ref.shape
    weights = weight_gathers(weight_axes, (w0, w1, w2), (o0, o1, o2), *refs[:2])
    for weight in weights:
        weight.start()
    gather = Gather(views(low_ref), views(normed_ref), rows, *refs[2:5])
    scatter = Scatter(rows, *refs[5:])

    def fill(s):
        return scatter.fill(s, s, [mixed_ref], [out_w_ref], False)

    def store(s):
        residual = x_ref[s].astype(jnp.float32) + scatter.result(s)[...]
        residual_ref[s] = residual
        normal = residual * lax.rsqrt(mean_of(residual * residual) + epsilon)
        low_ref[s] = (normal * gain_ref[...]).astype(jnp.bfloat16)

    sum_then_gather(
        scatter, gather, [fill(s) for s in range(seqs)], [functools.partial(store, s) for s in range(seqs)], seqs
    )
    for weight in weights:
        weight.finish()


def mixer_out(mixed, out_w, layer_in, gain, weights):
    seqs, rows, width = layer_in.shape
    full = jax.ShapeDtypeStruct((seqs, lax.axis_size("grp") * rows, width), jnp.bfloat16)
    return call(
        mixer_out_body, "mixer_out", 2,
        (mixed, out_w, layer_in, gain, *weights), [in_vmem] * 7,
        [jax.ShapeDtypeStruct(layer_in.shape, jnp.float32), full]
        + [gathered(w, axis) for w, axis in zip(weights, weight_axes)],
        [in_vmem] + [in_hbm] * 4,
        [pltpu.VMEM(layer_in.shape, jnp.bfloat16)]
        + seq_sems(3)
        + gather_sems(seqs)
        + scatter_scratch(seqs, rows, width),
        100,
    )


def mixer_forward_body(
    x_ref, grad_ref, gain_pack_ref, vector_pack_ref, gate_pack_ref, v0, v1, v2, w0, w1, w2,
    residual_ref, gains_ref, vectors_ref, gate_a_ref, gate_x_ref,
    normed_one_out, branch_out, feed_out, conv_out, rate_out, input_out, state_out, mixed_out, u0, u1, u2,
    normed_ref, grads_ref, o0, o1, o2,
    normed_one_ref, branch_ref, feed_ref, conv_ref, rate_ref, input_ref, state_ref, mixed_ref,
    branch_w_ref, rec_w_ref, out_w_ref, x_full_ref, low_ref, window, carry, gates, gain_slots, vector_slots, gate_slots,
    store_sem, weight_store_sem, gain_send, gain_recv, small_send, small_recv,
    mixer_send, mixer_recv, weight_send, weight_recv, *refs,
):
    seqs, rows, width = x_ref.shape
    seq_len = x_full_ref.shape[1]
    me = lax.axis_index("grp")
    kept = (
        (normed_one_ref, normed_one_out), (branch_ref, branch_out), (feed_ref, feed_out), (conv_ref, conv_out),
        (rate_ref, rate_out), (input_ref, input_out), (state_ref, state_out), (mixed_ref, mixed_out),
    )
    keeps = [
        copies([(buffer.at[s], out.at[s]) for buffer, out in kept], store_sem.at[s]) for s in range(seqs)
    ]
    weight_keeps = copies([(branch_w_ref, u0), (rec_w_ref, u1), (out_w_ref, u2)], weight_store_sem)
    greet_axes(("seq", "grp"))
    mixer_weights = weight_gathers(
        mixer_axes, (v0, v1, v2), (branch_w_ref, rec_w_ref, out_w_ref), mixer_send, mixer_recv
    )
    weights = weight_gathers(weight_axes, (w0, w1, w2), (o0, o1, o2), weight_send, weight_recv)
    gather = Gather(
        views(low_ref) + views(grad_ref) + views(x_ref),
        views(normed_ref) + views(grads_ref) + views(x_full_ref),
        rows, *refs[:3],
    )
    scatter = Scatter(rows, *refs[3:])
    place = lax.axis_index("grp")
    small = [
        Exchange("seq", lambda k, ref=pack: ref, lambda k, ref=slots: ref.at[k], small_send.at[i], small_recv.at[i])
        for i, (pack, slots) in enumerate(
            ((gain_pack_ref, gain_slots.at[place]), (vector_pack_ref, vector_slots), (gate_pack_ref, gate_slots))
        )
    ]
    along = Exchange("grp", lambda k: gain_slots.at[place], lambda k: gain_slots.at[k], gain_send, gain_recv)
    first_x = 2 * seqs
    small[0].start()
    gather.start(first_x)
    for move in small[1:]:
        move.start()
    for weight in mixer_weights[:2]:
        weight.start()
    small[0].finish()
    along.start_others()
    last_hop = gather.chips - 2
    for h in range(gather.chips - 1):
        gather.hop(first_x, h)
        if h == max(last_hop - 1, 0):
            for s in range(1, seqs):
                gather.start(first_x + s)
    gates[...] = jnp.zeros_like(gates)
    window[...] = jnp.zeros_like(window)
    along.finish_others()
    parts = lax.axis_size("seq")
    gain_part = width // (parts * along.size)
    for k in range(parts):
        for g in range(along.size):
            at = (k * along.size + g) * gain_part
            for i in range(2):
                gains_ref[i, :, at : at + gain_part] = gain_slots[g, k, 0:1, i * gain_part : (i + 1) * gain_part]
    for move in small[1:]:
        move.finish()
    heads = gate_pack_ref.shape[0] // 2
    part, head_dim = gate_pack_ref.shape[1:]
    for k in range(parts):
        for h in range(heads):
            at = h * head_dim + k * part
            vectors_ref[:, at : at + part] = vector_slots[k, :, h * part : (h + 1) * part]
            for i in range(2):
                gates[i, at : at + part, h * head_dim : (h + 1) * head_dim] = gate_slots[k, i * heads + h]
    gate_a_ref[...] = gates[0].astype(jnp.bfloat16)
    gate_x_ref[...] = gates[1].astype(jnp.bfloat16)
    softness_ref = vectors_ref.at[pl.ds(7, 1), :]
    tile = pick_rows(seq_len // 2, (192, 128, 96, 64, 32, 16))
    chunk = window.shape[0] - 8

    def project(s, half):
        count = seq_len // tile // 2

        @pl.loop(half * count, (half + 1) * count)
        def _(i):
            at = pl.ds(pl.multiple_of(i * tile, tile), tile)
            inputs = x_full_ref[s, at, :].astype(jnp.float32)
            normal = inputs * lax.rsqrt(mean_of(inputs * inputs) + epsilon)
            normed = (normal * gains_ref[0]).astype(jnp.bfloat16)
            normed_one_ref[s, at, :] = normed
            branch_ref[s, at, :] = matmul_nt(normed, branch_w_ref[...])
            feed_ref[s, at, :] = matmul_nt(normed, rec_w_ref[...]).astype(jnp.bfloat16)

    def recur(s):
        window[pl.ds(0, 8), :] = jnp.zeros((8, window.shape[1]), jnp.float32)
        carry[...] = jnp.zeros_like(carry)

        @pl.loop(0, seq_len // chunk)
        def _(i):
            at = pl.ds(pl.multiple_of(i * chunk, chunk), chunk)
            conv, rate, gate, state, mixed = rec_forward_rows(
                feed_ref[s, at, :], branch_ref[s, at, :], vectors_ref, softness_ref, gate_a_ref, gate_x_ref, window, carry
            )
            conv_ref[s, at, :] = conv
            rate_ref[s, at, :] = rate
            input_ref[s, at, :] = gate
            state_ref[s, at, :] = state
            mixed_ref[s, at, :] = mixed

        for keep in keeps[s]:
            keep.start()

    def late_hops(first, end):
        for h in range(first, min(end, gather.chips - 1)):
            for s in range(seqs):
                gather.hop(seqs + s, h)

    def next_x(h):
        for s in range(1, seqs):
            if h <= last_hop:
                gather.hop(first_x + s, h)

    def steps(s):
        partners, own = scatter.fill(s, s, [mixed_ref], [out_w_ref], False)

        def first():
            gather.arrive(first_x + s)
            if s == 0:
                for weight in mixer_weights[:2]:
                    weight.finish()
                mixer_weights[2].start()
            project(s, 0)
            if s == 0:
                next_x(0)
            project(s, 1)
            if s == 0:
                next_x(1)
            else:
                late_hops(0, 1)

        def second():
            recur(s)
            if s == 0:
                for h in range(2, gather.chips - 1):
                    next_x(h)
                mixer_weights[2].finish()
                for weight in weights:
                    weight.start()
                for t in range(seqs):
                    gather.start(seqs + t)
                for keep in weight_keeps:
                    keep.start()
            else:
                late_hops(1, 2)

        return [first, second, partners, own]

    def store(s):
        own = x_ref[s]
        residual = own.astype(jnp.float32) + scatter.result(s)[...]
        residual_ref[s] = residual
        normal = residual * lax.rsqrt(mean_of(residual * residual) + epsilon)
        low_ref[s] = (normal * gains_ref[1]).astype(jnp.bfloat16)

    sum_then_gather(
        scatter, gather, [steps(s) for s in range(seqs)], [functools.partial(store, s) for s in range(seqs)], seqs,
        after=(lambda: None, functools.partial(late_hops, 2, gather.chips)),
    )
    for s in range(seqs):
        gather.finish(seqs + s)
        gather.sent(first_x + s)
        for keep in keeps[s]:
            keep.wait()
    for keep in weight_keeps:
        keep.wait()
    for weight in weights:
        weight.finish()


def mixer_forward(layer_in, out_grad, gain_pack, vector_pack, gate_pack, mixer_weights, weights):
    seqs, rows, width = layer_in.shape
    size, n = lax.axis_size("seq"), lax.axis_size("grp")
    seq_len, channels = n * rows, mixer_weights[0].shape[0]
    f32, bf16 = jnp.float32, jnp.bfloat16
    shape = jax.ShapeDtypeStruct
    low, full = shape((seqs, seq_len, channels), bf16), shape((seqs, seq_len, channels), f32)
    tokens = shape((seqs, seq_len, width), bf16)
    kept = [tokens, full, low, low, full, full, full, low]
    mixer_full = [gathered(w, axis) for w, axis in zip(mixer_weights, mixer_axes)]
    outs = [
        shape(layer_in.shape, f32), shape((2, 1, width), f32), shape((8, channels), f32),
        shape((channels, channels), bf16), shape((channels, channels), bf16),
    ]
    outs += kept + mixer_full + [tokens] * 2
    outs += [gathered(w, axis) for w, axis in zip(weights, weight_axes)]
    return call(
        mixer_forward_body, "mixer_forward", 7,
        (layer_in, out_grad, gain_pack, vector_pack, gate_pack, *mixer_weights, *weights),
        [in_vmem] * 11,
        outs, [in_vmem] * 5 + [in_hbm] * 16,
        [pltpu.VMEM(v.shape, v.dtype) for v in kept + mixer_full + [tokens]]
        + [
            pltpu.VMEM(layer_in.shape, bf16),
            pltpu.VMEM((pick_rows(seq_len) + 8, channels), f32),
            pltpu.VMEM((8, channels), f32),
            pltpu.VMEM((2, channels, channels), f32),
            pltpu.VMEM((n, size) + gain_pack.shape, f32),
            pltpu.VMEM((size,) + vector_pack.shape, f32),
            pltpu.VMEM((size,) + gate_pack.shape, f32),
            pltpu.SemaphoreType.DMA((seqs, len(kept))),
            pltpu.SemaphoreType.DMA((3,)),
        ]
        + [pltpu.SemaphoreType.DMA((n,))] * 2
        + seq_sems(3) * 3
        + gather_sems(3 * seqs)
        + scatter_scratch(seqs, rows, width),
        180,
    )


def mlp_back_body(
    with_out, gate_in, up_in, gate_w_in, up_w_in, residual_ref, grad_ref, gain_ref, w0, w1, w2, *refs
):
    if with_out:
        hidden_in, down_w_in = refs[:2]
        refs = refs[2:]
    grad_residual_ref, gain_grad_ref, full_ref, o0, o1, o2 = refs[:6]
    refs = refs[6:]
    if with_out:
        layer_out_ref, late_ref = refs[:2]
        refs = refs[2:]
    low_ref, load_sem, gate_ref, up_ref, gate_w_ref, up_w_ref, *refs = refs
    pairs = [(gate_in, gate_ref), (up_in, up_ref), (gate_w_in, gate_w_ref), (up_w_in, up_w_ref)]
    if with_out:
        hidden_ref, down_w_ref, *refs = refs
        pairs += [(hidden_in, hidden_ref), (down_w_in, down_w_ref)]
    loads = copies(pairs, load_sem)
    for load in loads:
        load.start()
    greet_axes(("seq", "grp"))
    seqs, rows, _ = grad_ref.shape
    sums = weight_sums(weight_axes, (w0, w1, w2), (o0, o1, o2), *refs[:2])
    for weight in sums:
        weight.start_others()
    gather = Gather(views(low_ref), views(full_ref), rows, *refs[2:5])
    scatter = Scatter(rows, *refs[5:])
    gain_grad_ref[...] = jnp.zeros_like(gain_grad_ref)

    def fill(s):
        return scatter.fill(s, s, [gate_ref, up_ref], [gate_w_ref, up_w_ref], True)

    def store(s):
        term = scatter.result(s)[...]
        residual = residual_ref[s]
        inverse = lax.rsqrt(mean_of(residual * residual) + epsilon)
        normal = residual * inverse
        gain_grad_ref[0:1, :] += jnp.sum(term * normal, axis=0, keepdims=True)
        grad = grad_ref[s].astype(jnp.float32) + norm_back(term, normal, inverse, gain_ref[...])
        grad_residual_ref[s] = grad
        low_ref[s] = grad.astype(jnp.bfloat16)

    def wait_first():
        for load in loads[:4]:
            load.wait()

    def wait_later():
        for load in loads[4:]:
            load.wait()

    fills = [fill(s) for s in range(seqs)]
    fills[0] = (wait_first, *fills[0])
    stores = [functools.partial(store, s) for s in range(seqs)]
    if with_out:
        fill_out, store_out = out_body(hidden_ref, down_w_ref, residual_ref, layer_out_ref, scatter, seqs)
        fills += [fill_out(s) for s in range(seqs - 1)]
        fills[seqs - 1] = (*fills[seqs - 1], wait_later)
        stores += [functools.partial(store_out, s) for s in range(seqs - 1)]

    def late():
        step = 256

        @pl.loop(0, late_ref.shape[0] // step)
        def _(i):
            at = pl.ds(pl.multiple_of(i * step, step), step)
            late_ref[at, :] = matmul(hidden_ref[seqs - 1, at, :], down_w_ref[...]).astype(jnp.bfloat16)

    sum_then_gather(scatter, gather, fills, stores, seqs, after=(late,) if with_out else ())
    for weight in sums:
        weight.finish_others()


def mlp_back(grad_gate, grad_up, gate_w, up_w, residual, out_grad, gain, grads, out_inputs):
    seqs, rows, width = residual.shape
    outs = [
        jax.ShapeDtypeStruct(residual.shape, jnp.float32),
        jax.ShapeDtypeStruct((8, width), jnp.float32),
        jax.ShapeDtypeStruct((seqs, lax.axis_size("grp") * rows, width), jnp.bfloat16),
    ]
    outs += [slots_of(grad, axis) for grad, axis in zip(grads, weight_axes)]
    out_specs = [in_vmem] * 2 + [in_hbm] * 4
    if out_inputs:
        outs.append(jax.ShapeDtypeStruct((seqs - 1, rows, width), jnp.bfloat16))
        outs.append(jax.ShapeDtypeStruct((lax.axis_size("grp") * rows, width), jnp.bfloat16))
        out_specs += [in_vmem] * 2
    return call(
        functools.partial(mlp_back_body, bool(out_inputs)), "mlp_back", 3,
        (grad_gate, grad_up, gate_w, up_w, residual, out_grad, gain, *grads, *out_inputs),
        [in_hbm] * 4 + [in_vmem] * 3 + [in_hbm] * (3 + len(out_inputs)),
        outs, out_specs,
        [pltpu.VMEM(residual.shape, jnp.bfloat16), pltpu.SemaphoreType.DMA((6,))]
        + [pltpu.VMEM(v.shape, v.dtype) for v in (grad_gate, grad_up, gate_w, up_w, *out_inputs)]
        + seq_sems(3)
        + gather_sems(seqs)
        + scatter_scratch(seqs * 2 - 1 if out_inputs else seqs, rows, width),
        120,
    )


def last_body(
    branch_ref, feed_ref, branch_w_ref, rec_w_ref, x_ref, grad_ref, gain_ref, gain_two_ref, rec_ref,
    w0, w1, w2, *refs,
):
    grad_x_ref, rec_sum_ref, gain_sum_ref, o0, o1, o2 = refs[:6]
    refs = refs[6:]
    rec_slots, gain_local, gain_part, gain_slots, part_slots = refs[:5]
    rec_sems, gain_sems, part_sems = refs[5:7], refs[7:9], refs[9:11]
    greet_axes(("seq", "grp"))
    seqs, rows, _ = x_ref.shape
    sums = weight_sums(mixer_axes, (w0, w1, w2), (o0, o1, o2), *refs[11:13])
    scatter = Scatter(rows, *refs[13:])
    rec = Exchange("seq", lambda k: rec_ref.at[k], lambda k: rec_slots.at[k], *rec_sems)
    rec.start()
    for weight in sums:
        weight.start_others()
    gain_local[...] = jnp.zeros_like(gain_local)
    gain_local[1:2, :] = gain_two_ref[0:1, :]

    def fill(s):
        return scatter.fill(s, s, [branch_ref, feed_ref], [branch_w_ref, rec_w_ref], False)

    across = Exchange(
        "seq", block(gain_local, 1, lax.axis_size("seq")), lambda k: gain_slots.at[k], *gain_sems
    )

    def store(s):
        term = scatter.result(s)[...]
        inputs = x_ref[s].astype(jnp.float32)
        inverse = lax.rsqrt(mean_of(inputs * inputs) + epsilon)
        normal = inputs * inverse
        gain_local[0:1, :] += jnp.sum(term * normal, axis=0, keepdims=True)
        if s == seqs - 1:
            across.start()
        grad_x_ref[s] = grad_ref[s] + norm_back(term, normal, inverse, gain_ref[...])

    sum_then_gather(
        scatter, None, [fill(s) for s in range(seqs)], [functools.partial(store, s) for s in range(seqs)]
    )
    across.finish()
    gain_part[...] = sum_of(gain_slots)
    along = Exchange("grp", lambda k: gain_part, lambda k: part_slots.at[k], *part_sems)
    along.start()
    rec.finish()
    rec_sum_ref[...] = sum_of(rec_slots)
    for weight in sums:
        weight.finish_others()
    along.finish()
    gain_sum_ref[...] = sum_of(part_slots)


def last(grad_branch, grad_feed, branch_w, rec_w, layer_in, grad_residual, gain, gain_two_grad, rec_blocks, grads):
    seqs, rows, width = layer_in.shape
    size, n = lax.axis_size("seq"), lax.axis_size("grp")
    f32 = jnp.float32
    inputs = (grad_branch, grad_feed, branch_w, rec_w, layer_in, grad_residual, gain, gain_two_grad, rec_blocks)
    outs = [
        jax.ShapeDtypeStruct(layer_in.shape, f32),
        jax.ShapeDtypeStruct(rec_blocks.shape[1:], f32),
        jax.ShapeDtypeStruct((8, width // size), f32),
    ]
    outs += [slots_of(grad, axis) for grad, axis in zip(grads, mixer_axes)]
    out_specs = [in_vmem] * 3 + [in_hbm] * 3
    return call(
        last_body, "last", 4,
        inputs + tuple(grads), [in_vmem] * len(inputs) + [in_hbm] * 3,
        outs, out_specs,
        [
            pltpu.VMEM(rec_blocks.shape, f32),
            pltpu.VMEM((8, width), f32),
            pltpu.VMEM((8, width // size), f32),
            pltpu.VMEM((size, 8, width // size), f32),
            pltpu.VMEM((n, 8, width // size), f32),
        ]
        + [pltpu.SemaphoreType.DMA((size,))] * 4
        + [pltpu.SemaphoreType.DMA((n,))] * 2
        + seq_sems(3)
        + scatter_scratch(seqs, rows, width),
        80,
    )


def head_windows(heads, head_dim, parts):
    part = head_dim // parts
    rows = max(-(-(k + 1) * part // 8) * 8 - k * part // 8 * 8 for k in range(parts))

    def start(h, k):
        return pl.multiple_of(h * head_dim + k * part // 8 * 8, 8)

    return rows, start


def mixer_back_body(
    heads, low_in, out_w_in, branch_in, feed_in, conv_in, rate_in, input_in, state_in, mixed_in, branch_w_in, rec_w_in,
    normed_in, vectors_ref, gate_a_ref, gate_x_ref, x_ref, grad_ref, gain_ref, gain_two_ref,
    grad_x_ref, squares_out_ref, sums_out_ref, gain_sum_ref, o0, o1, o2,
    low_ref, out_w_ref, branch_ref, feed_ref, conv_ref, rate_ref, input_ref, state_ref, mixed_ref, branch_w_ref,
    rec_w_ref, grad_mixed, grad_branch, grad_feed, squares, sums, window, later, carry, tiles, d0, d1, d2,
    square_slots, sum_slots_ref, gain_local, gain_part, gain_slots, part_slots, load_sem, tile_sem,
    square_send, square_recv, sum_send, sum_recv, gain_send, gain_recv, part_send, part_recv, weight_send, weight_recv,
    *refs,
):
    seqs, rows, width = x_ref.shape
    seq_len, channels = feed_ref.shape[1:]
    softness_ref = vectors_ref.at[pl.ds(7, 1), :]
    per_seq = (
        (low_in, low_ref), (branch_in, branch_ref), (feed_in, feed_ref), (conv_in, conv_ref), (rate_in, rate_ref),
        (input_in, input_ref), (state_in, state_ref),
    )
    pairs = [(out_w_in, out_w_ref)]
    for s in range(seqs):
        pairs += [(source.at[s], buffer.at[s]) for source, buffer in per_seq]
        if s == 0:
            pairs += [(branch_w_in, branch_w_ref), (rec_w_in, rec_w_ref)]
    pairs += [(mixed_in, mixed_ref)]
    loads = copies(pairs, load_sem)
    for load in loads:
        load.start()
    greet_axes(("seq", "grp"))
    scatter = Scatter(rows, *refs)
    parts = lax.axis_size("seq")
    for ref in (squares, sums, gain_local):
        ref[...] = jnp.zeros_like(ref)
    gain_local[1:2, :] = gain_two_ref[0:1, :]
    window_rows, start_of = head_windows(heads, channels // heads, parts)
    square_moves = [
        Exchange(
            "seq",
            lambda k, h=h: squares.at[:, pl.ds(start_of(h, k), window_rows), :],
            lambda k, h=h: square_slots.at[k, h],
            square_send.at[h],
            square_recv.at[h],
        )
        for h in range(heads)
    ]
    sum_move = Exchange("seq", lambda k: sums, lambda k: sum_slots_ref.at[k], sum_send, sum_recv)
    across = Exchange("seq", block(gain_local, 1, parts), lambda k: gain_slots.at[k], gain_send, gain_recv)
    moves = weight_sums(mixer_axes, (d0, d1, d2), (o0, o1, o2), weight_send, weight_recv, 0)
    tile_rows = pick_rows(seq_len, (256, 192, 128, 96, 64, 32, 16))
    chunk = window.shape[0] - 8

    def mix(s):
        if s == 0:
            for load in loads[: 1 + len(per_seq)]:
                load.wait()
        else:
            first = 3 + s * len(per_seq)
            for load in loads[first : first + len(per_seq)]:
                load.wait()

        @pl.loop(0, seq_len // tile_rows)
        def _(i):
            at = pl.ds(pl.multiple_of(i * tile_rows, tile_rows), tile_rows)
            grad_mixed[at, :] = matmul_nt(low_ref[s, at, :], out_w_ref[...])

    def recur(s):
        carry[...] = jnp.zeros_like(carry)
        later[...] = jnp.zeros_like(later)
        blocks = seq_len // chunk

        @pl.loop(0, blocks)
        def _(i):
            first = (blocks - 1 - i) * chunk
            at = pl.ds(pl.multiple_of(first, chunk), chunk)
            keep = jnp.where(i == blocks - 1, 0.0, 1.0)
            before8 = pl.ds(pl.multiple_of(jnp.maximum(first - 8, 0), 8), 8)
            before16 = pl.ds(pl.multiple_of(jnp.maximum(first - 16, 0), 16), 16)
            grad_branch[s, at, :], grad_feed[s, at, :] = rec_backward_rows(
                grad_mixed[at, :], branch_ref[s, at, :], feed_ref[s, at, :],
                feed_ref[s, before16, :].astype(jnp.float32)[8:] * keep, conv_ref[s, at, :], rate_ref[s, at, :],
                input_ref[s, at, :], state_ref[s, at, :], state_ref[s, before8, :] * keep,
                vectors_ref, softness_ref, gate_a_ref, gate_x_ref, squares.at[0], squares.at[1], sums,
                window, later, carry,
            )

        if s == seqs - 1:
            for move in square_moves:
                move.start()
            sum_move.start()

    def steps(s):
        partners, own = scatter.fill(s, s, [grad_branch, grad_feed], [branch_w_ref, rec_w_ref], False)

        def third():
            if s == 0:
                for load in loads[1 + len(per_seq) : 3 + len(per_seq)]:
                    load.wait()
            partners()

        def first():
            mix(s)
            if s == seqs - 1:
                out_grads()

        return [first, functools.partial(recur, s), third, own]

    def out_grads():
        loads[-1].wait()
        step = width // parts

        @pl.loop(0, parts)
        def _(k):
            at = pl.ds(pl.multiple_of(k * step, step), step)
            total = matmul_tn(mixed_ref[0], low_ref[0, :, at])
            for s in range(1, seqs):
                total = total + matmul_tn(mixed_ref[s], low_ref[s, :, at])
            d2[:, at] = total.astype(jnp.bfloat16)

        moves[2].start()

    step = tiles.shape[-1]
    count = width // parts // step

    def columns_of(i):
        peer = lax.rem(lax.axis_index("seq") + 1 + i // count, parts)
        return pl.ds(pl.multiple_of((peer * count + lax.rem(i, count)) * step, step), step)

    def tile_load(i, slot):
        return pltpu.make_async_copy(normed_in.at[:, :, columns_of(i)], tiles.at[slot], tile_sem.at[slot])

    def in_grads(part):
        if part == 0:
            tile_load(0, 0).start()

        @pl.loop(part * count, (part + 1) * count)
        def _(i):
            slot = lax.rem(i, 2)
            tile_load(i, slot).wait()

            @pl.when(i + 1 < parts * count)
            def _():
                tile_load(i + 1, 1 - slot).start()

            for to, grads in ((d0, grad_branch), (d1, grad_feed)):
                total = matmul_tn(grads[0], tiles[slot, 0])
                for s in range(1, seqs):
                    total = total + matmul_tn(grads[s], tiles[slot, s])
                to[:, columns_of(i)] = total.astype(jnp.bfloat16)

        for move in moves[:2]:
            if part < parts - 1:
                move.copy(part + 1, move.me).start()
            else:
                move.own().start()

    def grads_from(first, end):
        for part in range(first, end):
            in_grads(part)

    def store(s):
        term = scatter.result(s)[...]
        inputs = x_ref[s].astype(jnp.float32)
        inverse = lax.rsqrt(mean_of(inputs * inputs) + epsilon)
        normal = inputs * inverse
        gain_local[0:1, :] += jnp.sum(term * normal, axis=0, keepdims=True)
        if s == seqs - 1:
            across.start()
        grad_x_ref[s] = grad_ref[s] + norm_back(term, normal, inverse, gain_ref[...])

    sum_then_gather(
        scatter, None, [steps(s) for s in range(seqs)], [functools.partial(store, s) for s in range(seqs)],
        between=functools.partial(grads_from, 0, parts // 2),
        after=(functools.partial(grads_from, parts // 2, parts - 1), functools.partial(grads_from, parts - 1, parts)),
    )
    across.finish()
    gain_part[...] = sum_of(gain_slots)
    along = Exchange("grp", lambda k: gain_part, lambda k: part_slots.at[k], part_send, part_recv)
    along.start()
    for move in square_moves:
        move.finish()
    squares_out_ref[...] = sum_of(square_slots)
    sum_move.finish()
    sums_out_ref[...] = sum_of(sum_slots_ref)
    for move in moves:
        move.finish()
    along.finish()
    gain_sum_ref[...] = sum_of(part_slots)


def mixer_back(
    heads, low, out_w, branch, feed, conv, rate, gate, state, mixed, branch_w, rec_w, normed,
    vectors, gate_a, gate_x, layer_in, grad_residual, gain, gain_two_grad,
):
    seqs, rows, width = layer_in.shape
    seq_len, channels = feed.shape[1:]
    size, n = lax.axis_size("seq"), lax.axis_size("grp")
    f32, bf16 = jnp.float32, jnp.bfloat16
    large = (low, out_w, branch, feed, conv, rate, gate, state, mixed, branch_w, rec_w)
    small = (vectors, gate_a, gate_x, layer_in, grad_residual, gain, gain_two_grad)
    window_rows = head_windows(heads, channels // heads, size)[0]
    grads = [jax.ShapeDtypeStruct(w.shape, bf16) for w in (branch_w, rec_w, out_w)]
    squares = (heads, 2, window_rows, channels)
    part = width // size
    return call(
        functools.partial(mixer_back_body, heads), "mixer_back", 6,
        large + (normed,) + small,
        [in_hbm] * 12 + [in_vmem] * 7,
        [
            jax.ShapeDtypeStruct(layer_in.shape, f32),
            jax.ShapeDtypeStruct(squares, f32),
            jax.ShapeDtypeStruct((8, channels), f32),
            jax.ShapeDtypeStruct((8, part), f32),
        ]
        + [slots_of(grad, axis, 0) for grad, axis in zip(grads, mixer_axes)],
        [in_vmem] * 4 + [in_hbm] * 3,
        [pltpu.VMEM(v.shape, v.dtype) for v in large]
        + [
            pltpu.VMEM((seq_len, channels), f32),
            pltpu.VMEM(feed.shape, bf16),
            pltpu.VMEM(feed.shape, bf16),
            pltpu.VMEM((2, channels, channels), f32),
            pltpu.VMEM((8, channels), f32),
            pltpu.VMEM((pick_rows(seq_len) + 8, channels), f32),
            pltpu.VMEM((pick_rows(seq_len) + 8, channels), f32),
            pltpu.VMEM((8, channels), f32),
            pltpu.VMEM((2, seqs, seq_len, 256), bf16),
        ]
        + [pltpu.VMEM(grad.shape, bf16) for grad in grads]
        + [
            pltpu.VMEM((size,) + squares, f32),
            pltpu.VMEM((size, 8, channels), f32),
            pltpu.VMEM((8, width), f32),
            pltpu.VMEM((8, part), f32),
            pltpu.VMEM((size, 8, part), f32),
            pltpu.VMEM((n, 8, part), f32),
            pltpu.SemaphoreType.DMA((4 + 7 * seqs,)),
            pltpu.SemaphoreType.DMA((2,)),
        ]
        + [pltpu.SemaphoreType.DMA((heads, size))] * 2
        + [pltpu.SemaphoreType.DMA((size,))] * 4
        + [pltpu.SemaphoreType.DMA((n,))] * 2
        + seq_sems(3)
        + scatter_scratch(seqs, rows, width),
        100,
    )


def out_only_body(hidden_ref, down_w_ref, residual_ref, layer_out_ref, *scratch):
    greet_line()
    scatter = Scatter(residual_ref.shape[1], *scratch)
    fill, store = out_body(hidden_ref, down_w_ref, residual_ref, layer_out_ref, scatter, 0)
    seqs = range(residual_ref.shape[0])
    sum_then_gather(
        scatter, None, [fill(s) for s in seqs], [functools.partial(store, s) for s in seqs]
    )


def out_only(hidden, down_w, residual):
    seqs, rows, width = residual.shape
    return call(
        out_only_body, "layer_out", 5,
        (hidden, down_w, residual), [in_vmem] * 3,
        [jax.ShapeDtypeStruct(residual.shape, jnp.bfloat16)], [in_vmem],
        scatter_scratch(seqs, rows, width), 60,
    )[0]


def per_device(
    layer_in, gain_one, w_branch, w_rec, conv_w, conv_b, gate_a_w, gate_a_b, gate_x_w, gate_x_b,
    decay_logit, w_out, gain_two, mlp_gate, mlp_up, mlp_down, out_grad,
):
    seqs_here, positions, model_width = layer_in.shape
    heads_here, tap_count, part_dim = conv_w.shape
    seq_devices, grp_devices = lax.axis_size("seq"), lax.axis_size("grp")
    head_dim = part_dim * seq_devices
    channels = heads_here * head_dim
    f32 = jnp.float32

    short_line = seqs_here * positions * grp_devices <= 2048
    mixer_weights = (w_branch.T, w_rec.T, w_out)
    mlp_weights = (mlp_gate, mlp_up, mlp_down)
    at = tap_count + 4
    if short_line:
        softness = jax.nn.softplus(-decay_logit.astype(f32))
        vector_rows = [jnp.transpose(conv_w, (1, 0, 2)).reshape(tap_count, -1)]
        vector_rows += [v.reshape(1, -1) for v in (conv_b, gate_a_b, gate_x_b)]
        vector_pack = jnp.concatenate([v.astype(f32) for v in vector_rows] + [softness.reshape(1, -1)])
        vector_pack = jnp.pad(vector_pack, ((0, 0), (0, -vector_pack.shape[1] % 128)))
        gain_pack = jnp.concatenate([gain_one, gain_two]).astype(f32)[None]
        gain_pack = jnp.pad(gain_pack, ((0, 7), (0, -gain_pack.shape[1] % 128)))
        gate_pack = jnp.concatenate([gate_a_w, gate_x_w]).astype(f32)
        (
            residual, gains, vectors, diag_a, diag_x,
            normed_one, branch_pre, feed, conv, rate, gate, state, mixed, branch_w, rec_w, out_w,
            normed_two, grad_output, gate_w, up_w, down_w,
        ) = mixer_forward(layer_in, out_grad, gain_pack, vector_pack, gate_pack, mixer_weights, mlp_weights)
        normed_one = normed_one.reshape(-1, model_width)
        grad_output = grad_output.reshape(-1, model_width)
    else:
        own_params = jnp.concatenate(
            [jnp.transpose(conv_w, (0, 2, 1))]
            + [v[:, :, None] for v in (conv_b, gate_a_b, gate_x_b, decay_logit)]
            + [gate_a_w, gate_x_w],
            axis=2,
        ).astype(f32)
        own_gains = jnp.concatenate([gain_one, gain_two]).astype(f32)
        pack = jnp.concatenate(
            [padded_rows(own_params.reshape(1, -1))[0], padded_rows(own_gains.reshape(1, -1))[0]]
        )
        late_grad, x_full, params, gains, branch_w, rec_w, out_w = gather_first(
            layer_in, out_grad, pack, mixer_weights
        )

        gains = gains.reshape(grp_devices, seq_devices, -1)[:, :, : own_gains.size]
        gains = jnp.transpose(gains.reshape(grp_devices, seq_devices, 2, -1), (2, 1, 0, 3)).reshape(2, 1, -1)
        params = params.reshape(seq_devices, -1)[:, : own_params.size]
        params = params.reshape((seq_devices,) + own_params.shape)
        params = jnp.transpose(params, (1, 0, 2, 3)).reshape(heads_here, head_dim, -1)
        vectors = params[:, :, : tap_count + 4].reshape(channels, -1).T
        diag_a = head_diagonal(params[:, :, at : at + head_dim].astype(jnp.bfloat16))
        diag_x = head_diagonal(params[:, :, at + head_dim :].astype(jnp.bfloat16))
        logit = vectors[tap_count + 3 :]
        softness = jax.nn.softplus(-logit)
        grad_output = jnp.concatenate(
            [lax.all_gather(late_grad[s], "grp", axis=0, tiled=True) for s in range(seqs_here)]
        )
        inputs = x_full.astype(f32)
        normal_one = inputs * lax.rsqrt(mean_of(inputs * inputs) + epsilon)
        normed_one = (normal_one * gains[0]).astype(jnp.bfloat16).reshape(-1, model_width)
        branch_pre = matmul_nt(normed_one, branch_w).reshape(seqs_here, -1, channels)
        feed = matmul_nt(normed_one, rec_w).astype(jnp.bfloat16).reshape(seqs_here, -1, channels)
        conv, rate, gate, state, mixed = rec_forward(feed, branch_pre, vectors, softness, diag_a, diag_x)
        residual, normed_two, gate_w, up_w, down_w = mixer_out(
            mixed, out_w, layer_in, gains[1], mlp_weights
        )
    mixed = mixed.reshape(-1, channels)
    normed_two = normed_two.reshape(-1, model_width)
    up_proj = matmul(normed_two, up_w)
    gate_act, gate_pull = jax.vjp(jax.nn.gelu, matmul(normed_two, gate_w))
    hidden = (gate_act * up_proj).astype(jnp.bfloat16)
    grad_hidden = matmul_nt(grad_output, down_w)
    grad_gate = gate_pull(grad_hidden * up_proj)[0].astype(jnp.bfloat16)
    grad_up = (grad_hidden * gate_act).astype(jnp.bfloat16)
    mlp_grads = low_all(
        (matmul_tn(normed_two, grad_gate), matmul_tn(normed_two, grad_up), matmul_tn(hidden, grad_output))
    )

    def by_seq(values):
        return values.reshape(seqs_here, -1, values.shape[-1])

    back_inputs = (
        by_seq(grad_gate), by_seq(grad_up), gate_w, up_w, residual, out_grad, gains[1], mlp_grads
    )
    if not short_line:
        layer_out = out_only(by_seq(hidden), down_w, residual)
        grad_residual, gain_two_grad, residual_low, *mlp_slots = mlp_back(*back_inputs, ())
    else:
        grad_residual, gain_two_grad, residual_low, *mlp_slots, layer_out, late = mlp_back(
            *back_inputs, (by_seq(hidden), down_w)
        )
        late = lax.psum_scatter(late, "grp", scatter_dimension=0, tiled=True)
        late = (residual[seqs_here - 1] + late.astype(f32)).astype(jnp.bfloat16)
        layer_out = jnp.concatenate([layer_out, late[None]])
    mlp_grads = sum_slots(mlp_grads, mlp_slots, weight_axes)
    if short_line:
        grad_x, squares, sums, gain_sum, *mixer_slots = mixer_back(
            heads_here, residual_low, out_w, branch_pre, feed, conv, rate, gate, state, by_seq(mixed), branch_w, rec_w,
            by_seq(normed_one), vectors, diag_a, diag_x, layer_in, grad_residual, gains[0], gain_two_grad,
        )
        mixer_grads = [sum_all(slot) for slot in mixer_slots]
        place = lax.axis_index("seq")
        first = place * part_dim % 8
        square_parts = [
            lax.dynamic_slice_in_dim(squares[h], first, part_dim, 1)[:, :, h * head_dim : (h + 1) * head_dim]
            for h in range(heads_here)
        ]
        grad_a, grad_x_gate = (jnp.stack([part[i] for part in square_parts]) for i in range(2))
        own_sums = lax.dynamic_slice_in_dim(
            sums.reshape(at, heads_here, head_dim), place * part_dim, part_dim, 2
        )
        logit_grad = 8.0 * jax.nn.sigmoid(-decay_logit.astype(f32)) * own_sums[tap_count + 3]
        rec_outs = (
            jnp.transpose(own_sums[:tap_count], (1, 0, 2)), own_sums[tap_count], grad_a, own_sums[tap_count + 1],
            grad_x_gate, own_sums[tap_count + 2], logit_grad,
        )
        return finish(layer_out, grad_x, gain_sum, mixer_grads, rec_outs, mlp_grads)
    residual_low = residual_low.reshape(-1, model_width)
    out_weight_grad = matmul_tn(mixed, residual_low)
    grad_mixed = by_seq(matmul_nt(residual_low, out_w))
    grad_branch, grad_feed, square_a, square_x, sums = rec_backward(
        grad_mixed, branch_pre, feed, conv, rate, gate, state, vectors, softness, diag_a, diag_x
    )
    vector_grads = jnp.concatenate(
        [sums[: tap_count + 3], 8.0 * jax.nn.sigmoid(-logit) * sums[tap_count + 3 :]]
    )
    rec_grads = jnp.concatenate(
        [
            vector_grads.T.reshape(heads_here, head_dim, -1),
            diagonal_heads(square_a, heads_here),
            diagonal_heads(square_x, heads_here),
        ],
        axis=2,
    )
    rec_grads = rec_grads.reshape(heads_here, seq_devices, part_dim, -1)
    rec_blocks = padded_rows(jnp.transpose(rec_grads, (1, 0, 2, 3)))
    mixer_grads = low_all(
        (
            matmul_tn(grad_branch.reshape(-1, channels), normed_one),
            matmul_tn(grad_feed.reshape(-1, channels), normed_one),
            out_weight_grad,
        )
    )
    grad_x, rec_sum, gain_sum, *mixer_slots = last(
        grad_branch, grad_feed, branch_w, rec_w, layer_in, grad_residual, gains[0], gain_two_grad, rec_blocks,
        mixer_grads,
    )
    mixer_grads = sum_slots(mixer_grads, mixer_slots, mixer_axes)
    rec_sum = rec_sum.reshape(-1)[: own_params.size].reshape(own_params.shape)
    rec_outs = (
        jnp.transpose(rec_sum[:, :, :tap_count], (0, 2, 1)),
        rec_sum[:, :, tap_count],
        rec_sum[:, :, at : at + head_dim],
        rec_sum[:, :, tap_count + 1],
        rec_sum[:, :, at + head_dim :],
        rec_sum[:, :, tap_count + 2],
        rec_sum[:, :, tap_count + 3],
    )
    return finish(layer_out, grad_x, gain_sum, mixer_grads, rec_outs, mlp_grads)


def finish(layer_out, grad_x, gain_sum, mixer_grads, rec_outs, mlp_grads):
    part = gain_sum.shape[1] // lax.axis_size("grp")
    gain_grads = lax.dynamic_slice_in_dim(gain_sum, lax.axis_index("grp") * part, part, 1)
    return (
        layer_out, grad_x, gain_grads[0], mixer_grads[0].T, mixer_grads[1].T, *rec_outs, mixer_grads[2], gain_grads[1],
        *mlp_grads,
    )


def solution(mesh):
    placed = (
        P("seq", "grp", None),
        P(("seq", "grp")),
        P("seq", "grp"),
        P("seq", "grp"),
        P("grp", None, "seq"),
        P("grp", "seq"),
        P("grp", "seq", None),
        P("grp", "seq"),
        P("grp", "seq", None),
        P("grp", "seq"),
        P("grp", "seq"),
        P("grp", "seq"),
        P(("seq", "grp")),
        P("seq", "grp"),
        P("seq", "grp"),
        P("grp", "seq"),
        P("seq", "grp", None),
    )
    return jax.shard_map(
        per_device,
        mesh=mesh,
        in_specs=placed,
        out_specs=(
            P("seq", "grp", None),
            P("seq", "grp", None),
            P(("seq", "grp")),
            P("seq", "grp"),
            P("seq", "grp"),
            P("grp", None, "seq"),
            P("grp", "seq"),
            P("grp", "seq", None),
            P("grp", "seq"),
            P("grp", "seq", None),
            P("grp", "seq"),
            P("grp", "seq"),
            P("grp", "seq"),
            P(("seq", "grp")),
            P("seq", "grp"),
            P("seq", "grp"),
            P("grp", "seq"),
        ),
        check_vma=False,
    )
```

```python
import functools
import math

import jax
import jax.numpy as jnp
from jax import lax
from jax.experimental import pallas as pl
from jax.experimental.pallas import tpu as pltpu
from jax.sharding import PartitionSpec as P

epsilon = 1e-06
gelu_slope = math.sqrt(2.0 / math.pi)
gelu_cubic = 0.044715
MESH = pl.DeviceIdType.MESH


def matmul(left, right):
    return jnp.dot(left, right, preferred_element_type=jnp.float32)


def matmul_tn(left, right):
    return lax.dot_general(
        left, right, (((0,), (0,)), ((), ())), preferred_element_type=jnp.float32
    )


def matmul_nt(left, right):
    return lax.dot_general(
        left, right, (((1,), (1,)), ((), ())), preferred_element_type=jnp.float32
    )


def norm_back(grad_normed, normal_part, inverse, gain):
    scaled = grad_normed * gain
    return inverse * (scaled - normal_part * jnp.mean(scaled * normal_part, axis=-1, keepdims=True))


def low_all(grads):
    return tuple(grad.astype(jnp.bfloat16) for grad in grads)


def sum_slots(grads, slots, axes):
    sums = []
    for grad, slot, axis in zip(grads, slots, axes):
        size = slot.shape[1 + axis]
        own = lax.dynamic_slice_in_dim(grad, lax.axis_index("seq") * size, size, axis)
        for k in range(slot.shape[0]):
            own = own.astype(jnp.float32) + slot[k].astype(jnp.float32)
        sums.append(own)
    return sums


def sum_all(slots):
    total = slots[0].astype(jnp.float32)
    for k in range(1, slots.shape[0]):
        total = total + slots[k].astype(jnp.float32)
    return total


def padded_rows(values):
    flat = values.reshape(values.shape[0], -1)
    flat = jnp.pad(flat, ((0, 0), (0, -flat.shape[1] % 1024)))
    return flat.reshape(values.shape[0], -1, 128)


def head_diagonal(blocks):
    heads, head_dim, _ = blocks.shape
    rows = []
    for h in range(heads):
        row = [jnp.zeros((head_dim, head_dim), blocks.dtype)] * heads
        row[h] = blocks[h]
        rows.append(jnp.concatenate(row, axis=1))
    return jnp.concatenate(rows, axis=0)


def diagonal_heads(square, heads):
    head_dim = square.shape[0] // heads
    return jnp.stack(
        [
            square[h * head_dim : (h + 1) * head_dim, h * head_dim : (h + 1) * head_dim]
            for h in range(heads)
        ]
    )


def pick_rows(seq_len, choices=(128, 96, 64, 32, 16)):
    for rows in choices:
        if seq_len % rows == 0:
            return rows
    return seq_len


def gelu_parts(x):
    cubic = gelu_slope * (x + gelu_cubic * x * x * x)
    bend = jnp.tanh(cubic)
    gate = 0.5 * (1.0 + bend)
    slope = gate + 0.5 * x * (1.0 - bend * bend) * gelu_slope * (1.0 + 3.0 * gelu_cubic * x * x)
    return x * gate, slope


def minus_expm1(x):
    series = 1.0 + x * (1.0 / 9.0)
    for k in (8, 7, 6, 5, 4, 3, 2):
        series = 1.0 + x * (1.0 / k) * series
    return jnp.where(x > -0.4, -x * series, 1.0 - jnp.exp(x))


def shift_down(values, by, fill):
    rows = values.shape[0]
    if by % 8 == 0:
        return jnp.concatenate([jnp.full((by, values.shape[1]), fill), values[: rows - by]], axis=0)
    index = lax.broadcasted_iota(jnp.int32, values.shape, 0)
    return jnp.where(index >= by, pltpu.roll(values, by, 0), fill)


def shift_up(values, by, fill):
    rows = values.shape[0]
    if by % 8 == 0:
        return jnp.concatenate([values[by:], jnp.full((by, values.shape[1]), fill)], axis=0)
    index = lax.broadcasted_iota(jnp.int32, values.shape, 0)
    return jnp.where(index < rows - by, pltpu.roll(values, rows - by, 0), fill)


def scan_block(decay, drive, shift):
    by = 1
    while by < decay.shape[0]:
        drive = drive + decay * shift(drive, by, 0.0)
        decay = decay * shift(decay, by, 1.0)
        by *= 2
    return decay, drive


def decay_parts(rate, softness):
    log_decay = -8.0 * rate * softness
    return jnp.exp(log_decay), jnp.sqrt(minus_expm1(2.0 * log_decay))


def rec_forward_rows(feed, branch, vectors_ref, softness_ref, gate_a_ref, gate_x_ref, window, carry):
    rows = feed.shape[0]
    window[pl.ds(8, rows), :] = feed.astype(jnp.float32)
    conv = vectors_ref[4:5, :] + vectors_ref[0:1, :] * window[pl.ds(8, rows), :]
    for k in range(1, 4):
        conv = conv + vectors_ref[k : k + 1, :] * window[pl.ds(8 - k, rows), :]
    window[pl.ds(0, 8), :] = window[pl.ds(rows, 8), :]
    conv_low = conv.astype(jnp.bfloat16)
    rate = jax.nn.sigmoid(matmul(conv_low, gate_a_ref[...]) + vectors_ref[5:6, :])
    gate = jax.nn.sigmoid(matmul(conv_low, gate_x_ref[...]) + vectors_ref[6:7, :])
    decay, scale = decay_parts(rate, softness_ref[...])
    total, state = scan_block(decay, scale * gate * conv_low.astype(jnp.float32), shift_down)
    state = state + total * carry[0:1, :]
    carry[0:1, :] = state[rows - 1 : rows, :]
    gelu_branch = gelu_parts(branch)[0]
    mixed = (gelu_branch * state.astype(jnp.bfloat16).astype(jnp.float32)).astype(jnp.bfloat16)
    return conv_low, rate, gate, state, mixed


def rec_forward_body(
    feed_ref, branch_ref, vectors_ref, softness_ref, gate_a_ref, gate_x_ref,
    conv_ref, rate_ref, input_ref, state_ref, mixed_ref, window, carry,
):
    @pl.when(pl.program_id(0) == 0)
    def _():
        window[...] = jnp.zeros_like(window)
        carry[...] = jnp.zeros_like(carry)

    for s in range(feed_ref.shape[0]):
        conv_ref[s], rate_ref[s], input_ref[s], state_ref[s], mixed_ref[s] = rec_forward_rows(
            feed_ref[s], branch_ref[s], vectors_ref, softness_ref, gate_a_ref, gate_x_ref, window.at[s], carry.at[s]
        )


def rec_backward_rows(
    grad_mixed, branch, feed, feed_before, conv_low, rate, gate, state, state_before,
    vectors_ref, softness_ref, gate_a_ref, gate_x_ref, grad_a_ref, grad_x_ref, sums_ref, window, later, carry,
):
    rows = feed.shape[0]
    softness = softness_ref[...]
    gelu_branch, slope = gelu_parts(branch)
    state_low = state.astype(jnp.bfloat16).astype(jnp.float32)
    grad_state = (grad_mixed * gelu_branch).astype(jnp.bfloat16).astype(jnp.float32)
    grad_branch = (slope * grad_mixed * state_low).astype(jnp.bfloat16)
    decay, scale = decay_parts(rate, softness)
    total, carried = scan_block(shift_up(decay, 1, 1.0), grad_state, shift_up)
    carried = carried + total * carry[0:1, :]
    carry[0:1, :] = decay[0:1, :] * carried[0:1, :]
    index = lax.broadcasted_iota(jnp.int32, state.shape, 0)
    previous = jnp.where(index >= 1, pltpu.roll(state, 1, 0), state_before[7:8, :])
    conv = conv_low.astype(jnp.float32)
    grad_log = carried * previous * decay - carried * gate * conv * decay * decay / scale
    log_rate = grad_log * rate
    pre_a = -8.0 * softness * log_rate * (1.0 - rate)
    pre_x = carried * scale * conv * gate * (1.0 - gate)
    low_a = pre_a.astype(jnp.bfloat16)
    low_x = pre_x.astype(jnp.bfloat16)
    grad_a_ref[...] += matmul_tn(conv_low, low_a)
    grad_x_ref[...] += matmul_tn(conv_low, low_x)
    grad_conv = (
        carried * scale * gate
        + matmul_nt(low_a, gate_a_ref[...])
        + matmul_nt(low_x, gate_x_ref[...])
    )
    window[pl.ds(0, 8), :] = feed_before
    window[pl.ds(8, rows), :] = feed.astype(jnp.float32)
    later[pl.ds(rows, 8), :] = later[pl.ds(0, 8), :]
    later[pl.ds(0, rows), :] = grad_conv
    grad_feed = vectors_ref[0:1, :] * grad_conv
    sums_ref[0:1, :] += jnp.sum(grad_conv * window[pl.ds(8, rows), :], axis=0, keepdims=True)
    for k in range(1, 4):
        grad_feed = grad_feed + vectors_ref[k : k + 1, :] * later[pl.ds(k, rows), :]
        sums_ref[k : k + 1, :] += jnp.sum(
            grad_conv * window[pl.ds(8 - k, rows), :], axis=0, keepdims=True
        )
    sums_ref[4:5, :] += jnp.sum(grad_conv, axis=0, keepdims=True)
    sums_ref[5:6, :] += jnp.sum(pre_a, axis=0, keepdims=True)
    sums_ref[6:7, :] += jnp.sum(pre_x, axis=0, keepdims=True)
    sums_ref[7:8, :] += jnp.sum(log_rate, axis=0, keepdims=True)
    return grad_branch, grad_feed.astype(jnp.bfloat16)


def rec_backward_body(
    grad_mixed_ref, branch_ref, feed_ref, feed_before_ref, conv_ref, rate_ref, input_ref,
    state_ref, state_before_ref, vectors_ref, softness_ref, gate_a_ref, gate_x_ref,
    grad_branch_ref, grad_feed_ref, grad_a_ref, grad_x_ref, sums_ref, window, later, carry,
):
    step = pl.program_id(0)

    @pl.when(step == 0)
    def _():
        for ref in (later, carry, grad_a_ref, grad_x_ref, sums_ref):
            ref[...] = jnp.zeros_like(ref)

    keep = jnp.where(step == pl.num_programs(0) - 1, 0.0, 1.0)
    for s in range(feed_ref.shape[0]):
        before = feed_before_ref[s].astype(jnp.float32)
        grad_branch_ref[s], grad_feed_ref[s] = rec_backward_rows(
            grad_mixed_ref[s], branch_ref[s], feed_ref[s], before[before.shape[0] - 8 :] * keep, conv_ref[s],
            rate_ref[s], input_ref[s], state_ref[s], state_before_ref[s] * keep,
            vectors_ref, softness_ref, gate_a_ref, gate_x_ref, grad_a_ref, grad_x_ref, sums_ref,
            window.at[s], later.at[s], carry.at[s],
        )


def whole(shape):
    return pl.BlockSpec(shape, lambda i: (0,) * len(shape))


def rec_forward(feed, branch, vectors, softness, gate_a, gate_x):
    seqs, seq_len, channels = feed.shape
    rows = pick_rows(seq_len)
    block = pl.BlockSpec((seqs, rows, channels), lambda i: (0, i, 0))
    full = jax.ShapeDtypeStruct(feed.shape, jnp.float32)
    low = jax.ShapeDtypeStruct(feed.shape, jnp.bfloat16)
    return pl.pallas_call(
        rec_forward_body,
        grid=(seq_len // rows,),
        in_specs=[block, block]
        + [whole(v.shape) for v in (vectors, softness, gate_a, gate_x)],
        out_specs=[block] * 5,
        out_shape=[low, full, full, full, low],
        scratch_shapes=[
            pltpu.VMEM((seqs, rows + 8, channels), jnp.float32),
            pltpu.VMEM((seqs, 8, channels), jnp.float32),
        ],
        compiler_params=pltpu.CompilerParams(vmem_limit_bytes=40 << 20),
        name="rec_forward",
    )(feed, branch, vectors, softness, gate_a, gate_x)


def rec_backward(grad_mixed, branch, feed, conv, rate, gate, state, vectors, softness, gate_a, gate_x):
    seqs, seq_len, channels = feed.shape
    rows = pick_rows(seq_len)
    blocks = seq_len // rows
    block = pl.BlockSpec((seqs, rows, channels), lambda i: (0, blocks - 1 - i, 0))

    def ahead(by):
        return pl.BlockSpec(
            (seqs, by, channels),
            lambda i: (0, jnp.maximum((blocks - 1 - i) * (rows // by) - 1, 0), 0),
        )

    low = jax.ShapeDtypeStruct(feed.shape, jnp.bfloat16)
    square = jax.ShapeDtypeStruct((channels, channels), jnp.float32)
    return pl.pallas_call(
        rec_backward_body,
        grid=(blocks,),
        in_specs=[block, block, block, ahead(16), block, block, block, block, ahead(8)]
        + [whole(v.shape) for v in (vectors, softness, gate_a, gate_x)],
        out_specs=[block, block, whole((channels, channels)), whole((channels, channels)), whole((8, channels))],
        out_shape=[low, low, square, square, jax.ShapeDtypeStruct((8, channels), jnp.float32)],
        scratch_shapes=[
            pltpu.VMEM((seqs, rows + 8, channels), jnp.float32),
            pltpu.VMEM((seqs, rows + 8, channels), jnp.float32),
            pltpu.VMEM((seqs, 8, channels), jnp.float32),
        ],
        compiler_params=pltpu.CompilerParams(vmem_limit_bytes=40 << 20),
        name="rec_backward",
    )(grad_mixed, branch, feed, feed, conv, rate, gate, state, state, vectors, softness, gate_a, gate_x)


def line_place():
    return lax.axis_size("grp") // 2, lax.axis_index("grp") // 2, lax.axis_index("grp") % 2


def greet_line():
    chips, chip, core = line_place()
    barrier = pltpu.get_barrier_semaphore()

    def signal(place):
        pl.semaphore_signal(barrier, inc=1, device_id={"grp": place}, device_id_type=MESH)

    signal(chip * 2 + 1 - core)

    @pl.when(chip > 0)
    def _():
        signal(chip * 2 + core - 2)

    @pl.when(chip < chips - 1)
    def _():
        signal(chip * 2 + core + 2)

    ends = (chip == 0).astype(jnp.int32) + (chip == chips - 1).astype(jnp.int32)
    pl.semaphore_wait(barrier, 3 - ends)


def greet_axes(axes):
    barrier = pltpu.get_barrier_semaphore()
    for axis in axes:
        size = lax.axis_size(axis)
        for k in range(1, size):
            pl.semaphore_signal(
                barrier,
                inc=1,
                device_id={axis: lax.rem(lax.axis_index(axis) + k, size)},
                device_id_type=MESH,
            )
    pl.semaphore_wait(barrier, sum(lax.axis_size(axis) - 1 for axis in axes))


class Gather:
    def __init__(self, sources, outs, rows, send_sem, recv_sem, own_sem):
        self.chips, self.chip, self.core = line_place()
        self.me = self.chip * 2 + self.core
        self.sources, self.outs, self.rows = sources, outs, rows
        self.send_sem, self.recv_sem, self.own_sem = send_sem, recv_sem, own_sem

    def slot(self, p, origin):
        return self.outs[p].at[pl.ds(pl.multiple_of(origin * self.rows, self.rows), self.rows), :]

    def copy(self, p, source, origin, target, way):
        return pltpu.make_async_remote_copy(
            src_ref=source,
            dst_ref=self.slot(p, origin),
            send_sem=self.send_sem.at[way, p, origin],
            recv_sem=self.recv_sem.at[p, origin],
            device_id={"grp": target},
            device_id_type=MESH,
        )

    def to_right(self, p, source, origin):
        return self.copy(p, source, origin, self.me + 2, 0)

    def to_left(self, p, source, origin):
        return self.copy(p, source, origin, self.me - 2, 1)

    def to_partner(self, p, source, origin):
        return self.copy(p, source, origin, self.chip * 2 + 1 - self.core, 2)

    def own(self, p):
        return pltpu.make_async_copy(self.sources[p], self.slot(p, self.me), self.own_sem.at[p])

    def start(self, p):
        source = self.sources[p]

        @pl.when(self.chip < self.chips - 1)
        def _():
            self.to_right(p, source, self.me).start()

        @pl.when(self.chip > 0)
        def _():
            self.to_left(p, source, self.me).start()

        self.to_partner(p, source, self.me).start()
        self.own(p).start()

    def hop(self, p, h):
        left_origin = self.me - 2 - 2 * h
        right_origin = self.me + 2 + 2 * h

        @pl.when(self.chip - 1 - h >= 0)
        def _():
            here = self.slot(p, left_origin)
            self.to_right(p, here, left_origin).wait_recv()

            @pl.when(self.chip < self.chips - 1)
            def _():
                self.to_right(p, here, left_origin).start()

            self.to_partner(p, here, left_origin).start()

        @pl.when(self.chip + 1 + h <= self.chips - 1)
        def _():
            here = self.slot(p, right_origin)
            self.to_left(p, here, right_origin).wait_recv()

            @pl.when(self.chip > 0)
            def _():
                self.to_left(p, here, right_origin).start()

            self.to_partner(p, here, right_origin).start()

    def arrive(self, p):
        for c in range(self.chips):
            origin = c * 2 + 1 - self.core
            self.to_partner(p, self.slot(p, origin), origin).wait_recv()
        self.own(p).wait()

    def finish(self, p):
        self.arrive(p)
        self.sent(p)

    def sent(self, p):
        for c in range(self.chips):
            origin = c * 2 + self.core
            here = self.slot(p, origin)
            self.to_partner(p, here, origin).wait_send()

            @pl.when((c <= self.chip) & (self.chip < self.chips - 1))
            def _():
                self.to_right(p, here, origin).wait_send()

            @pl.when((c >= self.chip) & (self.chip > 0))
            def _():
                self.to_left(p, here, origin).wait_send()


def gather_sems(pieces):
    n = lax.axis_size("grp")
    return [
        pltpu.SemaphoreType.DMA((3, pieces, n)),
        pltpu.SemaphoreType.DMA((pieces, n)),
        pltpu.SemaphoreType.DMA((pieces,)),
    ]


class Scatter:
    def __init__(self, rows, part, out, swap_in, line_in, send_sem, recv_sem):
        self.chips, self.chip, self.core = line_place()
        self.me = self.chip * 2 + self.core
        self.rows, self.part, self.out = rows, part, out
        self.swap_in, self.line_in = swap_in, line_in
        self.send_sem, self.recv_sem = send_sem, recv_sem

    def copy(self, dest, place, way, slot, p):
        return pltpu.make_async_remote_copy(
            src_ref=self.out.at[p, slot],
            dst_ref=dest,
            send_sem=self.send_sem.at[way, p, slot],
            recv_sem=self.recv_sem.at[way, p, slot],
            device_id={"grp": place},
            device_id_type=MESH,
        )

    def swap(self, p, c):
        return self.copy(self.swap_in.at[p, c], self.chip * 2 + 1 - self.core, 0, c, p)

    def right(self, p, c):
        return self.copy(self.line_in.at[p, c], self.me + 2, 1, c, p)

    def left(self, p, c):
        slot = jnp.where(c == self.chip - 1, self.chips, c)
        return self.copy(self.line_in.at[p, slot], self.me - 2, 2, c, p)

    def from_right(self, p, c):
        slot = jnp.where(c == self.chip, self.chips, c)
        return self.copy(self.line_in.at[p, slot], self.me + 2, 2, c, p)

    def fill(self, p, s, lefts, rights, transposed, width=512):
        def rows_of(ref, core):
            at = [pl.multiple_of((c * 2 + core) * self.rows, self.rows) for c in range(self.chips)]
            return jnp.concatenate([ref[s, pl.ds(a, self.rows), :] for a in at], axis=0)

        def product(core, store):
            chosen = [rows_of(ref, core) for ref in lefts]

            @pl.loop(0, self.out.shape[-1] // width)
            def _(j):
                columns = pl.ds(pl.multiple_of(j * width, width), width)
                total = None
                for left, right in zip(chosen, rights):
                    term = matmul_nt(left, right[columns, :]) if transposed else matmul(left, right[:, columns])
                    total = term if total is None else total + term
                for c in range(self.chips):
                    store(c, columns, total[c * self.rows : (c + 1) * self.rows])

        def to_out(c, columns, value):
            self.out[p, c, :, columns] = value.astype(jnp.bfloat16)

        def to_part(c, columns, value):
            self.part[p, c, :, columns] = value

        def partners():
            product(1 - self.core, to_out)
            for c in range(self.chips):
                self.swap(p, c).start()

        def own():
            product(self.core, to_part)

        return partners, own

    def own(self, p, c):
        self.swap(p, c).wait_recv()
        return self.part[p, c] + self.swap_in[p, c].astype(jnp.float32)

    def hop(self, p, t):
        last = self.chips - 1

        def send(c, first, arrival, onward):
            self.swap(p, c).wait_send()
            total = self.own(p, c)

            @pl.when(first)
            def _():
                self.out[p, c] = total.astype(jnp.bfloat16)

            @pl.when(jnp.logical_not(first))
            def _():
                arrival(p, c).wait_recv()
                self.out[p, c] = (total + self.line_in[p, c].astype(jnp.float32)).astype(jnp.bfloat16)

            onward(p, c).start()

        @pl.when(self.chip <= t)
        def _():
            send(last - t + self.chip, self.chip == 0, self.right, self.right)

        @pl.when(last - self.chip <= t)
        def _():
            send(t - last + self.chip, self.chip == last, self.from_right, self.left)

    def result(self, p):
        chip = self.chip
        self.part[p, chip] = self.own(p, chip)

        @pl.when(chip > 0)
        def _():
            self.right(p, chip).wait_recv()
            self.part[p, chip] += self.line_in[p, chip].astype(jnp.float32)

        @pl.when(chip < self.chips - 1)
        def _():
            self.from_right(p, chip).wait_recv()
            self.part[p, chip] += self.line_in[p, self.chips].astype(jnp.float32)

        return self.part.at[p, chip]

    def finish(self, p):
        self.swap(p, self.chip).wait_send()
        for c in range(self.chips):

            @pl.when(c > self.chip)
            def _():
                self.right(p, c).wait_send()

            @pl.when(c < self.chip)
            def _():
                self.left(p, c).wait_send()


def scatter_scratch(pieces, rows, width):
    chips = lax.axis_size("grp") // 2
    return [
        pltpu.VMEM((pieces, chips, rows, width), jnp.float32),
        pltpu.VMEM((pieces, chips, rows, width), jnp.bfloat16),
        pltpu.VMEM((pieces, chips, rows, width), jnp.bfloat16),
        pltpu.VMEM((pieces, chips + 1, rows, width), jnp.bfloat16),
        pltpu.SemaphoreType.DMA((3, pieces, chips)),
        pltpu.SemaphoreType.DMA((3, pieces, chips)),
    ]


in_vmem = pl.BlockSpec(memory_space=pltpu.VMEM)
in_hbm = pl.BlockSpec(memory_space=pl.ANY)


def call(body, name, number, inputs, in_specs, outs, out_specs, scratch, us):
    return pl.pallas_call(
        body,
        in_specs=in_specs,
        out_specs=out_specs,
        out_shape=outs,
        scratch_shapes=scratch,
        name=name,
        cost_estimate=pl.CostEstimate(
            flops=us * 1000000000, bytes_accessed=us * 3000000, transcendentals=0
        ),
        compiler_params=pltpu.CompilerParams(
            collective_id=number, has_side_effects=True, vmem_limit_bytes=62 << 20
        ),
    )(*inputs)


class Exchange:
    def __init__(self, axis, source, slot, send_sem, recv_sem, steps=None, first=1):
        self.axis, self.source, self.slot, self.steps, self.first = axis, source, slot, steps, first
        self.size, self.me = lax.axis_size(axis), lax.axis_index(axis)
        self.send_sem, self.recv_sem = send_sem, recv_sem

    def copy(self, k, owner):
        peer = lax.rem(self.me + k, self.size)
        return pltpu.make_async_remote_copy(
            src_ref=self.source(peer),
            dst_ref=self.slot(owner) if self.slot else self.steps.at[k - self.first],
            send_sem=self.send_sem.at[k],
            recv_sem=self.recv_sem.at[k],
            device_id={self.axis: peer},
            device_id_type=MESH,
        )

    def own(self):
        slot = self.slot(self.me) if self.slot else self.steps.at[0]
        return pltpu.make_async_copy(self.source(self.me), slot, self.send_sem.at[0])

    def start(self):
        self.own().start()
        self.start_others()

    def start_others(self):
        for k in range(1, self.size):
            self.copy(k, self.me).start()

    def finish(self):
        self.own().wait()
        self.finish_others()

    def finish_others(self):
        for k in range(1, self.size):
            self.copy(k, lax.rem(self.me - k + self.size, self.size)).wait_recv()
        for k in range(1, self.size):
            self.copy(k, self.me).wait_send()


def sum_of(slots):
    total = slots[0]
    for k in range(1, slots.shape[0]):
        total = total + slots[k]
    return total


def block(ref, axis, parts):
    size = ref.shape[axis] // parts

    def view(k):
        at = pl.ds(pl.multiple_of(k * size, size), size)
        return ref.at[at, :] if axis == 0 else ref.at[:, at]

    return view


def weight_gathers(axes, sources, outs, send_sem, recv_sem):
    parts = lax.axis_size("seq")
    return [
        Exchange(
            "seq", lambda k, ref=source: ref, block(out, axis, parts), send_sem.at[i], recv_sem.at[i]
        )
        for i, (axis, source, out) in enumerate(zip(axes, sources, outs))
    ]


def weight_sums(axes, sources, outs, send_sem, recv_sem, first=1):
    parts = lax.axis_size("seq")
    return [
        Exchange(
            "seq", block(source, axis, parts), None, send_sem.at[i], recv_sem.at[i], out, first
        )
        for i, (axis, source, out) in enumerate(zip(axes, sources, outs))
    ]


def seq_sems(count):
    return [pltpu.SemaphoreType.DMA((count, lax.axis_size("seq")))] * 2


def gathered(block_of, axis):
    shape = list(block_of.shape)
    shape[axis] *= lax.axis_size("seq")
    return jax.ShapeDtypeStruct(shape, block_of.dtype)


def slots_of(matrix, axis, first=1):
    shape = list(matrix.shape)
    size = lax.axis_size("seq")
    shape[axis] //= size
    return jax.ShapeDtypeStruct((size - first, *shape), matrix.dtype)


weight_axes = (0, 0, 1)
mixer_axes = (1, 1, 1)


def copies(pairs, sem):
    return [pltpu.make_async_copy(source, buffer, sem.at[i]) for i, (source, buffer) in enumerate(pairs)]


def views(ref):
    return [ref.at[s] for s in range(ref.shape[0])]


def first_body(x_ref, grad_ref, pack_ref, w0, w1, w2, later_ref, full_ref, params_ref, gains_ref, o0, o1, o2, *refs):
    small_send, small_recv, gain_send, gain_recv, weight_send, weight_recv = refs[3:]
    greet_axes(("seq", "grp"))
    seqs = x_ref.shape[0]
    gather = Gather(views(x_ref), views(full_ref), x_ref.shape[1], *refs[:3])
    weights = weight_gathers(mixer_axes, (w0, w1, w2), (o0, o1, o2), weight_send, weight_recv)
    small = Exchange("seq", lambda k: pack_ref, lambda k: params_ref.at[k], small_send, small_recv)
    small.start()
    for s in range(seqs):
        gather.start(s)
    for weight in weights:
        weight.start()
    later_ref[...] = grad_ref[...]
    small.finish()
    place = lax.axis_index("grp")
    for owner in range(small.size):
        gains_ref[place, owner] = params_ref[owner, pl.ds(pack_ref.shape[0] - 8, 8), :]
    gains = Exchange("grp", lambda k: gains_ref.at[place], lambda k: gains_ref.at[k], gain_send, gain_recv)
    gains.start_others()
    for h in range(gather.chips - 1):
        for s in range(seqs):
            gather.hop(s, h)
    gains.finish_others()
    for weight in weights:
        weight.finish()
    for s in range(seqs):
        gather.finish(s)


def gather_first(layer_in, out_grad, pack, weights):
    seqs, rows, width = layer_in.shape
    n, size = lax.axis_size("grp"), lax.axis_size("seq")
    return call(
        first_body, "gather_first", 1,
        (layer_in, out_grad, pack, *weights), [in_vmem] * 6,
        [
            jax.ShapeDtypeStruct(out_grad.shape, out_grad.dtype),
            jax.ShapeDtypeStruct((seqs, n * rows, width), jnp.bfloat16),
            jax.ShapeDtypeStruct((size,) + pack.shape, jnp.float32),
            jax.ShapeDtypeStruct((n, size, 8, 128), jnp.float32),
        ]
        + [gathered(w, axis) for w, axis in zip(weights, mixer_axes)],
        [in_vmem, in_hbm] + [in_vmem] * 2 + [in_hbm] * 3,
        gather_sems(seqs)
        + [pltpu.SemaphoreType.DMA((size,))] * 2
        + [pltpu.SemaphoreType.DMA((n,))] * 2
        + seq_sems(3),
        70,
    )


def mean_of(values):
    return jnp.mean(values, axis=-1, keepdims=True)


def sum_then_gather(scatter, gather, fills, stores, count=0, between=None, after=()):
    hops = range(1, scatter.chips - 1)
    for step in fills[0]:
        step()
    scatter.hop(0, 0)
    for p, store in enumerate(stores):
        ahead = list(fills[p + 1] if p + 1 < len(fills) else after)
        for h in hops:
            if ahead:
                ahead.pop(0)()
            scatter.hop(p, h)
            if 0 < p <= count:
                gather.hop(p - 1, h - 1)
        for step in ahead:
            step()
        if p + 1 < len(fills):
            scatter.hop(p + 1, 0)
        if between and p == 0:
            between()
        store()
        if p < count:
            gather.start(p)
        if 0 < p <= count:
            gather.hop(p - 1, gather.chips - 2)
    if count == len(stores):
        for h in range(gather.chips - 1):
            gather.hop(count - 1, h)
    for p in range(count):
        gather.finish(p)
    for p in range(len(fills)):
        scatter.finish(p)


def out_body(hidden_ref, down_w_ref, residual_ref, layer_out_ref, scatter, first):
    def fill(s):
        return scatter.fill(first + s, s, [hidden_ref], [down_w_ref], False)

    def store(s):
        layer_out_ref[s] = (residual_ref[s] + scatter.result(first + s)[...]).astype(jnp.bfloat16)

    return fill, store


def mixer_out_body(mixed_ref, out_w_ref, x_ref, gain_ref, w0, w1, w2, residual_ref, normed_ref, o0, o1, o2, low_ref, *refs):
    greet_axes(("seq", "grp"))
    seqs, rows, _ = x_ref.shape
    weights = weight_gathers(weight_axes, (w0, w1, w2), (o0, o1, o2), *refs[:2])
    for weight in weights:
        weight.start()
    gather = Gather(views(low_ref), views(normed_ref), rows, *refs[2:5])
    scatter = Scatter(rows, *refs[5:])

    def fill(s):
        return scatter.fill(s, s, [mixed_ref], [out_w_ref], False)

    def store(s):
        residual = x_ref[s].astype(jnp.float32) + scatter.result(s)[...]
        residual_ref[s] = residual
        normal = residual * lax.rsqrt(mean_of(residual * residual) + epsilon)
        low_ref[s] = (normal * gain_ref[...]).astype(jnp.bfloat16)

    sum_then_gather(
        scatter, gather, [fill(s) for s in range(seqs)], [functools.partial(store, s) for s in range(seqs)], seqs
    )
    for weight in weights:
        weight.finish()


def mixer_out(mixed, out_w, layer_in, gain, weights):
    seqs, rows, width = layer_in.shape
    full = jax.ShapeDtypeStruct((seqs, lax.axis_size("grp") * rows, width), jnp.bfloat16)
    return call(
        mixer_out_body, "mixer_out", 2,
        (mixed, out_w, layer_in, gain, *weights), [in_vmem] * 7,
        [jax.ShapeDtypeStruct(layer_in.shape, jnp.float32), full]
        + [gathered(w, axis) for w, axis in zip(weights, weight_axes)],
        [in_vmem] + [in_hbm] * 4,
        [pltpu.VMEM(layer_in.shape, jnp.bfloat16)]
        + seq_sems(3)
        + gather_sems(seqs)
        + scatter_scratch(seqs, rows, width),
        100,
    )


def mixer_forward_body(
    x_ref, grad_ref, gain_pack_ref, vector_pack_ref, gate_pack_ref, v0, v1, v2, w0, w1, w2,
    residual_ref, gains_ref, vectors_ref, gate_a_ref, gate_x_ref,
    normed_one_out, branch_out, feed_out, conv_out, rate_out, input_out, state_out, mixed_out, u0, u1, u2,
    normed_ref, grads_ref, o0, o1, o2,
    normed_one_ref, branch_ref, feed_ref, conv_ref, rate_ref, input_ref, state_ref, mixed_ref,
    branch_w_ref, rec_w_ref, out_w_ref, x_full_ref, low_ref, window, carry, gates, gain_slots, vector_slots, gate_slots,
    store_sem, weight_store_sem, gain_send, gain_recv, small_send, small_recv,
    mixer_send, mixer_recv, weight_send, weight_recv, *refs,
):
    seqs, rows, width = x_ref.shape
    seq_len = x_full_ref.shape[1]
    me = lax.axis_index("grp")
    kept = (
        (normed_one_ref, normed_one_out), (branch_ref, branch_out), (feed_ref, feed_out), (conv_ref, conv_out),
        (rate_ref, rate_out), (input_ref, input_out), (state_ref, state_out), (mixed_ref, mixed_out),
    )
    keeps = [
        copies([(buffer.at[s], out.at[s]) for buffer, out in kept], store_sem.at[s]) for s in range(seqs)
    ]
    weight_keeps = copies([(branch_w_ref, u0), (rec_w_ref, u1), (out_w_ref, u2)], weight_store_sem)
    greet_axes(("seq", "grp"))
    mixer_weights = weight_gathers(
        mixer_axes, (v0, v1, v2), (branch_w_ref, rec_w_ref, out_w_ref), mixer_send, mixer_recv
    )
    weights = weight_gathers(weight_axes, (w0, w1, w2), (o0, o1, o2), weight_send, weight_recv)
    gather = Gather(
        views(low_ref) + views(grad_ref) + views(x_ref),
        views(normed_ref) + views(grads_ref) + views(x_full_ref),
        rows, *refs[:3],
    )
    scatter = Scatter(rows, *refs[3:])
    place = lax.axis_index("grp")
    small = [
        Exchange("seq", lambda k, ref=pack: ref, lambda k, ref=slots: ref.at[k], small_send.at[i], small_recv.at[i])
        for i, (pack, slots) in enumerate(
            ((gain_pack_ref, gain_slots.at[place]), (vector_pack_ref, vector_slots), (gate_pack_ref, gate_slots))
        )
    ]
    along = Exchange("grp", lambda k: gain_slots.at[place], lambda k: gain_slots.at[k], gain_send, gain_recv)
    first_x = 2 * seqs
    small[0].start()
    gather.start(first_x)
    for move in small[1:]:
        move.start()
    for weight in mixer_weights[:2]:
        weight.start()
    small[0].finish()
    along.start_others()
    last_hop = gather.chips - 2
    for h in range(gather.chips - 1):
        gather.hop(first_x, h)
        if h == max(last_hop - 1, 0):
            for s in range(1, seqs):
                gather.start(first_x + s)
    gates[...] = jnp.zeros_like(gates)
    window[...] = jnp.zeros_like(window)
    along.finish_others()
    parts = lax.axis_size("seq")
    gain_part = width // (parts * along.size)
    for k in range(parts):
        for g in range(along.size):
            at = (k * along.size + g) * gain_part
            for i in range(2):
                gains_ref[i, :, at : at + gain_part] = gain_slots[g, k, 0:1, i * gain_part : (i + 1) * gain_part]
    for move in small[1:]:
        move.finish()
    heads = gate_pack_ref.shape[0] // 2
    part, head_dim = gate_pack_ref.shape[1:]
    for k in range(parts):
        for h in range(heads):
            at = h * head_dim + k * part
            vectors_ref[:, at : at + part] = vector_slots[k, :, h * part : (h + 1) * part]
            for i in range(2):
                gates[i, at : at + part, h * head_dim : (h + 1) * head_dim] = gate_slots[k, i * heads + h]
    gate_a_ref[...] = gates[0].astype(jnp.bfloat16)
    gate_x_ref[...] = gates[1].astype(jnp.bfloat16)
    softness_ref = vectors_ref.at[pl.ds(7, 1), :]
    tile = pick_rows(seq_len // 2, (192, 128, 96, 64, 32, 16))
    chunk = window.shape[0] - 8

    def project(s, half):
        count = seq_len // tile // 2

        @pl.loop(half * count, (half + 1) * count)
        def _(i):
            at = pl.ds(pl.multiple_of(i * tile, tile), tile)
            inputs = x_full_ref[s, at, :].astype(jnp.float32)
            normal = inputs * lax.rsqrt(mean_of(inputs * inputs) + epsilon)
            normed = (normal * gains_ref[0]).astype(jnp.bfloat16)
            normed_one_ref[s, at, :] = normed
            branch_ref[s, at, :] = matmul_nt(normed, branch_w_ref[...])
            feed_ref[s, at, :] = matmul_nt(normed, rec_w_ref[...]).astype(jnp.bfloat16)

    def recur(s):
        window[pl.ds(0, 8), :] = jnp.zeros((8, window.shape[1]), jnp.float32)
        carry[...] = jnp.zeros_like(carry)

        @pl.loop(0, seq_len // chunk)
        def _(i):
            at = pl.ds(pl.multiple_of(i * chunk, chunk), chunk)
            conv, rate, gate, state, mixed = rec_forward_rows(
                feed_ref[s, at, :], branch_ref[s, at, :], vectors_ref, softness_ref, gate_a_ref, gate_x_ref, window, carry
            )
            conv_ref[s, at, :] = conv
            rate_ref[s, at, :] = rate
            input_ref[s, at, :] = gate
            state_ref[s, at, :] = state
            mixed_ref[s, at, :] = mixed

        for keep in keeps[s]:
            keep.start()

    def late_hops(first, end):
        for h in range(first, min(end, gather.chips - 1)):
            for s in range(seqs):
                gather.hop(seqs + s, h)

    def next_x(h):
        for s in range(1, seqs):
            if h <= last_hop:
                gather.hop(first_x + s, h)

    def steps(s):
        partners, own = scatter.fill(s, s, [mixed_ref], [out_w_ref], False)

        def first():
            gather.arrive(first_x + s)
            if s == 0:
                for weight in mixer_weights[:2]:
                    weight.finish()
                mixer_weights[2].start()
            project(s, 0)
            if s == 0:
                next_x(0)
            project(s, 1)
            if s == 0:
                next_x(1)
            else:
                late_hops(0, 1)

        def second():
            recur(s)
            if s == 0:
                for h in range(2, gather.chips - 1):
                    next_x(h)
                mixer_weights[2].finish()
                for weight in weights:
                    weight.start()
                for t in range(seqs):
                    gather.start(seqs + t)
                for keep in weight_keeps:
                    keep.start()
            else:
                late_hops(1, 2)

        return [first, second, partners, own]

    def store(s):
        own = x_ref[s]
        residual = own.astype(jnp.float32) + scatter.result(s)[...]
        residual_ref[s] = residual
        normal = residual * lax.rsqrt(mean_of(residual * residual) + epsilon)
        low_ref[s] = (normal * gains_ref[1]).astype(jnp.bfloat16)

    sum_then_gather(
        scatter, gather, [steps(s) for s in range(seqs)], [functools.partial(store, s) for s in range(seqs)], seqs,
        after=(lambda: None, functools.partial(late_hops, 2, gather.chips)),
    )
    for s in range(seqs):
        gather.finish(seqs + s)
        gather.sent(first_x + s)
        for keep in keeps[s]:
            keep.wait()
    for keep in weight_keeps:
        keep.wait()
    for weight in weights:
        weight.finish()


def mixer_forward(layer_in, out_grad, gain_pack, vector_pack, gate_pack, mixer_weights, weights):
    seqs, rows, width = layer_in.shape
    size, n = lax.axis_size("seq"), lax.axis_size("grp")
    seq_len, channels = n * rows, mixer_weights[0].shape[0]
    f32, bf16 = jnp.float32, jnp.bfloat16
    shape = jax.ShapeDtypeStruct
    low, full = shape((seqs, seq_len, channels), bf16), shape((seqs, seq_len, channels), f32)
    tokens = shape((seqs, seq_len, width), bf16)
    kept = [tokens, full, low, low, full, full, full, low]
    mixer_full = [gathered(w, axis) for w, axis in zip(mixer_weights, mixer_axes)]
    outs = [
        shape(layer_in.shape, f32), shape((2, 1, width), f32), shape((8, channels), f32),
        shape((channels, channels), bf16), shape((channels, channels), bf16),
    ]
    outs += kept + mixer_full + [tokens] * 2
    outs += [gathered(w, axis) for w, axis in zip(weights, weight_axes)]
    return call(
        mixer_forward_body, "mixer_forward", 7,
        (layer_in, out_grad, gain_pack, vector_pack, gate_pack, *mixer_weights, *weights),
        [in_vmem] * 11,
        outs, [in_vmem] * 5 + [in_hbm] * 16,
        [pltpu.VMEM(v.shape, v.dtype) for v in kept + mixer_full + [tokens]]
        + [
            pltpu.VMEM(layer_in.shape, bf16),
            pltpu.VMEM((pick_rows(seq_len) + 8, channels), f32),
            pltpu.VMEM((8, channels), f32),
            pltpu.VMEM((2, channels, channels), f32),
            pltpu.VMEM((n, size) + gain_pack.shape, f32),
            pltpu.VMEM((size,) + vector_pack.shape, f32),
            pltpu.VMEM((size,) + gate_pack.shape, f32),
            pltpu.SemaphoreType.DMA((seqs, len(kept))),
            pltpu.SemaphoreType.DMA((3,)),
        ]
        + [pltpu.SemaphoreType.DMA((n,))] * 2
        + seq_sems(3) * 3
        + gather_sems(3 * seqs)
        + scatter_scratch(seqs, rows, width),
        180,
    )


def mlp_back_body(
    with_out, gate_in, up_in, gate_w_in, up_w_in, residual_ref, grad_ref, gain_ref, w0, w1, w2, *refs
):
    if with_out:
        hidden_in, down_w_in = refs[:2]
        refs = refs[2:]
    grad_residual_ref, gain_grad_ref, full_ref, o0, o1, o2 = refs[:6]
    refs = refs[6:]
    if with_out:
        layer_out_ref, late_ref = refs[:2]
        refs = refs[2:]
    low_ref, load_sem, gate_ref, up_ref, gate_w_ref, up_w_ref, *refs = refs
    pairs = [(gate_in, gate_ref), (up_in, up_ref), (gate_w_in, gate_w_ref), (up_w_in, up_w_ref)]
    if with_out:
        hidden_ref, down_w_ref, tiles, made_up, made_down, tile_sem, *refs = refs
        pairs += [(hidden_in, hidden_ref), (down_w_in, down_w_ref)]
    loads = copies(pairs, load_sem)
    for load in loads:
        load.start()
    greet_axes(("seq", "grp"))
    seqs, rows, _ = grad_ref.shape
    if with_out:
        sums = weight_sums(weight_axes[:1], (w0,), (o0,), *refs[:2])
        parts, me = lax.axis_size("seq"), lax.axis_index("seq")
        moves = [
            Exchange(
                "seq", lambda k, ref=made: ref.at[lax.rem(k - me + parts, parts)], None,
                refs[0].at[i], refs[1].at[i], out, 0,
            )
            for i, made, out in ((1, made_up, o1), (2, made_down, o2))
        ]
        order = [(kind, k) for kind in range(2) for k in range(1, parts)] + [(0, 0), (1, 0)]
    else:
        sums = weight_sums(weight_axes, (w0, w1, w2), (o0, o1, o2), *refs[:2])
    for weight in sums:
        weight.start_others()
    gather = Gather(views(low_ref), views(full_ref), rows, *refs[2:5])
    scatter = Scatter(rows, *refs[5:])
    gain_grad_ref[...] = jnp.zeros_like(gain_grad_ref)

    def fill(s):
        return scatter.fill(s, s, [gate_ref, up_ref], [gate_w_ref, up_w_ref], True)

    def store(s):
        term = scatter.result(s)[...]
        residual = residual_ref[s]
        inverse = lax.rsqrt(mean_of(residual * residual) + epsilon)
        normal = residual * inverse
        gain_grad_ref[0:1, :] += jnp.sum(term * normal, axis=0, keepdims=True)
        grad = grad_ref[s].astype(jnp.float32) + norm_back(term, normal, inverse, gain_ref[...])
        grad_residual_ref[s] = grad
        low_ref[s] = grad.astype(jnp.bfloat16)

    def tile_load(i, j):
        kind, k = order[i]
        step = tiles.shape[-1]
        first = lax.rem(me + k, parts) * 2 * step + j * step
        source = (w1, w2)[kind].at[:, :, pl.ds(pl.multiple_of(first, step), step)]
        return pltpu.make_async_copy(source, tiles.at[j], tile_sem.at[j])

    def make(i):
        kind, k = order[i]
        step = tiles.shape[-1]

        @pl.loop(0, 2)
        def _(j):
            tile_load(i, j).wait()
            at = pl.ds(pl.multiple_of(j * step, step), step)
            total = None
            for s in range(seqs):
                if kind == 0:
                    term = matmul_tn(tiles[j, s], up_ref[s])
                else:
                    term = matmul_tn(hidden_ref[s], tiles[j, s])
                total = term if total is None else total + term
            if kind == 0:
                made_up[k, at, :] = total.astype(jnp.bfloat16)
            else:
                made_down[k, :, at] = total.astype(jnp.bfloat16)
            if i + 1 < len(order):
                tile_load(i + 1, j).start()

        if k:
            moves[kind].copy(k, me).start()
        else:
            moves[kind].own().start()

    def make_all(first, end):
        for i in range(first, end):
            make(i)

    def wait_first():
        for load in loads[:4]:
            load.wait()

    def wait_later():
        for load in loads[4:]:
            load.wait()

    fills = [fill(s) for s in range(seqs)]
    fills[0] = (wait_first, *fills[0])
    stores = [functools.partial(store, s) for s in range(seqs)]
    if with_out:
        fill_out, store_out = out_body(hidden_ref, down_w_ref, residual_ref, layer_out_ref, scatter, seqs)
        fills += [fill_out(s) for s in range(seqs - 1)]
        fills[seqs - 1] = (*fills[seqs - 1], wait_later)
        third = parts - 1

        def partners_then(step):
            step()
            make_all(2, third)

        def own_then(step):
            step()
            make_all(third, third + 1)

        if len(fills) > seqs:
            fills[seqs] = (
                functools.partial(partners_then, fills[seqs][0]),
                functools.partial(own_then, fills[seqs][1]),
                functools.partial(make_all, third + 1, 2 * third),
            )
        for j in range(2):
            tile_load(0, j).start()
        stores += [functools.partial(store_out, s) for s in range(seqs - 1)]

    def late():
        step = 256

        @pl.loop(0, late_ref.shape[0] // step)
        def _(i):
            at = pl.ds(pl.multiple_of(i * step, step), step)
            late_ref[at, :] = matmul(hidden_ref[seqs - 1, at, :], down_w_ref[...]).astype(jnp.bfloat16)

    def rest():
        make_all(2 * third if len(fills) > seqs else 2, len(order))

    sum_then_gather(
        scatter, gather, fills, stores, seqs,
        between=functools.partial(make_all, 0, 2) if with_out else None, after=(late, rest) if with_out else (),
    )
    for weight in sums:
        weight.finish_others()
    if with_out:
        for move in moves:
            move.finish()


def mlp_back(grad_gate, grad_up, gate_w, up_w, residual, out_grad, gain, grads, out_inputs):
    seqs, rows, width = residual.shape
    outs = [
        jax.ShapeDtypeStruct(residual.shape, jnp.float32),
        jax.ShapeDtypeStruct((8, width), jnp.float32),
        jax.ShapeDtypeStruct((seqs, lax.axis_size("grp") * rows, width), jnp.bfloat16),
    ]
    if out_inputs:
        size = lax.axis_size("seq")
        hidden_width, part = grad_gate.shape[-1], width // size
        outs.append(slots_of(grads[0], 0))
        outs.append(jax.ShapeDtypeStruct((size, part, hidden_width), jnp.bfloat16))
        outs.append(jax.ShapeDtypeStruct((size, hidden_width, part), jnp.bfloat16))
        makers = [
            pltpu.VMEM((2, *grad_gate.shape[:2], part // 2), jnp.bfloat16),
            *(pltpu.VMEM(out.shape, out.dtype) for out in outs[-2:]),
            pltpu.SemaphoreType.DMA((2,)),
        ]
    else:
        outs += [slots_of(grad, axis) for grad, axis in zip(grads, weight_axes)]
        makers = []
    out_specs = [in_vmem] * 2 + [in_hbm] * 4
    if out_inputs:
        outs.append(jax.ShapeDtypeStruct((seqs - 1, rows, width), jnp.bfloat16))
        outs.append(jax.ShapeDtypeStruct((lax.axis_size("grp") * rows, width), jnp.bfloat16))
        out_specs += [in_vmem] * 2
    return call(
        functools.partial(mlp_back_body, bool(out_inputs)), "mlp_back", 3,
        (grad_gate, grad_up, gate_w, up_w, residual, out_grad, gain, *grads, *out_inputs),
        [in_hbm] * 4 + [in_vmem] * 3 + [in_hbm] * (3 + len(out_inputs)),
        outs, out_specs,
        [pltpu.VMEM(residual.shape, jnp.bfloat16), pltpu.SemaphoreType.DMA((6,))]
        + [pltpu.VMEM(v.shape, v.dtype) for v in (grad_gate, grad_up, gate_w, up_w, *out_inputs)]
        + makers
        + seq_sems(3)
        + gather_sems(seqs)
        + scatter_scratch(seqs * 2 - 1 if out_inputs else seqs, rows, width),
        120,
    )


def last_body(
    branch_ref, feed_ref, branch_w_ref, rec_w_ref, x_ref, grad_ref, gain_ref, gain_two_ref, rec_ref,
    w0, w1, w2, *refs,
):
    grad_x_ref, rec_sum_ref, gain_sum_ref, o0, o1, o2 = refs[:6]
    refs = refs[6:]
    rec_slots, gain_local, gain_part, gain_slots, part_slots = refs[:5]
    rec_sems, gain_sems, part_sems = refs[5:7], refs[7:9], refs[9:11]
    greet_axes(("seq", "grp"))
    seqs, rows, _ = x_ref.shape
    sums = weight_sums(mixer_axes, (w0, w1, w2), (o0, o1, o2), *refs[11:13])
    scatter = Scatter(rows, *refs[13:])
    rec = Exchange("seq", lambda k: rec_ref.at[k], lambda k: rec_slots.at[k], *rec_sems)
    rec.start()
    for weight in sums:
        weight.start_others()
    gain_local[...] = jnp.zeros_like(gain_local)
    gain_local[1:2, :] = gain_two_ref[0:1, :]

    def fill(s):
        return scatter.fill(s, s, [branch_ref, feed_ref], [branch_w_ref, rec_w_ref], False)

    across = Exchange(
        "seq", block(gain_local, 1, lax.axis_size("seq")), lambda k: gain_slots.at[k], *gain_sems
    )

    def store(s):
        term = scatter.result(s)[...]
        inputs = x_ref[s].astype(jnp.float32)
        inverse = lax.rsqrt(mean_of(inputs * inputs) + epsilon)
        normal = inputs * inverse
        gain_local[0:1, :] += jnp.sum(term * normal, axis=0, keepdims=True)
        if s == seqs - 1:
            across.start()
        grad_x_ref[s] = grad_ref[s] + norm_back(term, normal, inverse, gain_ref[...])

    sum_then_gather(
        scatter, None, [fill(s) for s in range(seqs)], [functools.partial(store, s) for s in range(seqs)]
    )
    across.finish()
    gain_part[...] = sum_of(gain_slots)
    along = Exchange("grp", lambda k: gain_part, lambda k: part_slots.at[k], *part_sems)
    along.start()
    rec.finish()
    rec_sum_ref[...] = sum_of(rec_slots)
    for weight in sums:
        weight.finish_others()
    along.finish()
    gain_sum_ref[...] = sum_of(part_slots)


def last(grad_branch, grad_feed, branch_w, rec_w, layer_in, grad_residual, gain, gain_two_grad, rec_blocks, grads):
    seqs, rows, width = layer_in.shape
    size, n = lax.axis_size("seq"), lax.axis_size("grp")
    f32 = jnp.float32
    inputs = (grad_branch, grad_feed, branch_w, rec_w, layer_in, grad_residual, gain, gain_two_grad, rec_blocks)
    outs = [
        jax.ShapeDtypeStruct(layer_in.shape, f32),
        jax.ShapeDtypeStruct(rec_blocks.shape[1:], f32),
        jax.ShapeDtypeStruct((8, width // size), f32),
    ]
    outs += [slots_of(grad, axis) for grad, axis in zip(grads, mixer_axes)]
    out_specs = [in_vmem] * 3 + [in_hbm] * 3
    return call(
        last_body, "last", 4,
        inputs + tuple(grads), [in_vmem] * len(inputs) + [in_hbm] * 3,
        outs, out_specs,
        [
            pltpu.VMEM(rec_blocks.shape, f32),
            pltpu.VMEM((8, width), f32),
            pltpu.VMEM((8, width // size), f32),
            pltpu.VMEM((size, 8, width // size), f32),
            pltpu.VMEM((n, 8, width // size), f32),
        ]
        + [pltpu.SemaphoreType.DMA((size,))] * 4
        + [pltpu.SemaphoreType.DMA((n,))] * 2
        + seq_sems(3)
        + scatter_scratch(seqs, rows, width),
        80,
    )


def head_windows(heads, head_dim, parts):
    part = head_dim // parts
    rows = max(-(-(k + 1) * part // 8) * 8 - k * part // 8 * 8 for k in range(parts))

    def start(h, k):
        return pl.multiple_of(h * head_dim + k * part // 8 * 8, 8)

    return rows, start


def mixer_back_body(
    heads, low_in, out_w_in, branch_in, feed_in, conv_in, rate_in, input_in, state_in, mixed_in, branch_w_in, rec_w_in,
    normed_in, vectors_ref, gate_a_ref, gate_x_ref, x_ref, grad_ref, gain_ref, gain_two_ref,
    grad_x_ref, squares_out_ref, sums_out_ref, gain_sum_ref, o0, o1, o2,
    low_ref, out_w_ref, branch_ref, feed_ref, conv_ref, rate_ref, input_ref, state_ref, mixed_ref, branch_w_ref,
    rec_w_ref, grad_mixed, grad_branch, grad_feed, squares, sums, window, later, carry, tiles, d0, d1, d2,
    square_slots, sum_slots_ref, gain_local, gain_part, gain_slots, part_slots, load_sem, tile_sem,
    square_send, square_recv, sum_send, sum_recv, gain_send, gain_recv, part_send, part_recv, weight_send, weight_recv,
    *refs,
):
    seqs, rows, width = x_ref.shape
    seq_len, channels = feed_ref.shape[1:]
    softness_ref = vectors_ref.at[pl.ds(7, 1), :]
    per_seq = (
        (low_in, low_ref), (branch_in, branch_ref), (feed_in, feed_ref), (conv_in, conv_ref), (rate_in, rate_ref),
        (input_in, input_ref), (state_in, state_ref),
    )
    pairs = [(out_w_in, out_w_ref)]
    for s in range(seqs):
        pairs += [(source.at[s], buffer.at[s]) for source, buffer in per_seq]
        if s == 0:
            pairs += [(branch_w_in, branch_w_ref), (rec_w_in, rec_w_ref)]
    pairs += [(mixed_in, mixed_ref)]
    loads = copies(pairs, load_sem)
    for load in loads:
        load.start()
    greet_axes(("seq", "grp"))
    scatter = Scatter(rows, *refs)
    parts = lax.axis_size("seq")
    for ref in (squares, sums, gain_local):
        ref[...] = jnp.zeros_like(ref)
    gain_local[1:2, :] = gain_two_ref[0:1, :]
    window_rows, start_of = head_windows(heads, channels // heads, parts)
    square_moves = [
        Exchange(
            "seq",
            lambda k, h=h: squares.at[:, pl.ds(start_of(h, k), window_rows), :],
            lambda k, h=h: square_slots.at[k, h],
            square_send.at[h],
            square_recv.at[h],
        )
        for h in range(heads)
    ]
    sum_move = Exchange("seq", lambda k: sums, lambda k: sum_slots_ref.at[k], sum_send, sum_recv)
    across = Exchange("seq", block(gain_local, 1, parts), lambda k: gain_slots.at[k], gain_send, gain_recv)
    moves = weight_sums(mixer_axes, (d0, d1, d2), (o0, o1, o2), weight_send, weight_recv, 0)
    tile_rows = pick_rows(seq_len, (256, 192, 128, 96, 64, 32, 16))
    chunk = window.shape[0] - 8

    def mix(s):
        if s == 0:
            for load in loads[: 1 + len(per_seq)]:
                load.wait()
        else:
            first = 3 + s * len(per_seq)
            for load in loads[first : first + len(per_seq)]:
                load.wait()

        @pl.loop(0, seq_len // tile_rows)
        def _(i):
            at = pl.ds(pl.multiple_of(i * tile_rows, tile_rows), tile_rows)
            grad_mixed[at, :] = matmul_nt(low_ref[s, at, :], out_w_ref[...])

    def recur(s):
        carry[...] = jnp.zeros_like(carry)
        later[...] = jnp.zeros_like(later)
        blocks = seq_len // chunk

        @pl.loop(0, blocks)
        def _(i):
            first = (blocks - 1 - i) * chunk
            at = pl.ds(pl.multiple_of(first, chunk), chunk)
            keep = jnp.where(i == blocks - 1, 0.0, 1.0)
            before8 = pl.ds(pl.multiple_of(jnp.maximum(first - 8, 0), 8), 8)
            before16 = pl.ds(pl.multiple_of(jnp.maximum(first - 16, 0), 16), 16)
            grad_branch[s, at, :], grad_feed[s, at, :] = rec_backward_rows(
                grad_mixed[at, :], branch_ref[s, at, :], feed_ref[s, at, :],
                feed_ref[s, before16, :].astype(jnp.float32)[8:] * keep, conv_ref[s, at, :], rate_ref[s, at, :],
                input_ref[s, at, :], state_ref[s, at, :], state_ref[s, before8, :] * keep,
                vectors_ref, softness_ref, gate_a_ref, gate_x_ref, squares.at[0], squares.at[1], sums,
                window, later, carry,
            )

        if s == seqs - 1:
            for move in square_moves:
                move.start()
            sum_move.start()

    def steps(s):
        partners, own = scatter.fill(s, s, [grad_branch, grad_feed], [branch_w_ref, rec_w_ref], False)

        def third():
            if s == 0:
                for load in loads[1 + len(per_seq) : 3 + len(per_seq)]:
                    load.wait()
            partners()

        def first():
            mix(s)
            if s == seqs - 1:
                out_grads()

        return [first, functools.partial(recur, s), third, own]

    def out_grads():
        loads[-1].wait()
        step = width // parts

        @pl.loop(0, parts)
        def _(k):
            at = pl.ds(pl.multiple_of(k * step, step), step)
            total = matmul_tn(mixed_ref[0], low_ref[0, :, at])
            for s in range(1, seqs):
                total = total + matmul_tn(mixed_ref[s], low_ref[s, :, at])
            d2[:, at] = total.astype(jnp.bfloat16)

        moves[2].start()

    step = tiles.shape[-1]
    count = width // parts // step

    def columns_of(i):
        peer = lax.rem(lax.axis_index("seq") + 1 + i // count, parts)
        return pl.ds(pl.multiple_of((peer * count + lax.rem(i, count)) * step, step), step)

    def tile_load(i, slot):
        return pltpu.make_async_copy(normed_in.at[:, :, columns_of(i)], tiles.at[slot], tile_sem.at[slot])

    def in_grads(part):
        if part == 0:
            tile_load(0, 0).start()

        @pl.loop(part * count, (part + 1) * count)
        def _(i):
            slot = lax.rem(i, 2)
            tile_load(i, slot).wait()

            @pl.when(i + 1 < parts * count)
            def _():
                tile_load(i + 1, 1 - slot).start()

            for to, grads in ((d0, grad_branch), (d1, grad_feed)):
                total = matmul_tn(grads[0], tiles[slot, 0])
                for s in range(1, seqs):
                    total = total + matmul_tn(grads[s], tiles[slot, s])
                to[:, columns_of(i)] = total.astype(jnp.bfloat16)

        for move in moves[:2]:
            if part < parts - 1:
                move.copy(part + 1, move.me).start()
            else:
                move.own().start()

    def grads_from(first, end):
        for part in range(first, end):
            in_grads(part)

    def store(s):
        term = scatter.result(s)[...]
        inputs = x_ref[s].astype(jnp.float32)
        inverse = lax.rsqrt(mean_of(inputs * inputs) + epsilon)
        normal = inputs * inverse
        gain_local[0:1, :] += jnp.sum(term * normal, axis=0, keepdims=True)
        if s == seqs - 1:
            across.start()
        grad_x_ref[s] = grad_ref[s] + norm_back(term, normal, inverse, gain_ref[...])

    sum_then_gather(
        scatter, None, [steps(s) for s in range(seqs)], [functools.partial(store, s) for s in range(seqs)],
        between=functools.partial(grads_from, 0, parts // 2),
        after=(functools.partial(grads_from, parts // 2, parts - 1), functools.partial(grads_from, parts - 1, parts)),
    )
    across.finish()
    gain_part[...] = sum_of(gain_slots)
    along = Exchange("grp", lambda k: gain_part, lambda k: part_slots.at[k], part_send, part_recv)
    along.start()
    for move in square_moves:
        move.finish()
    squares_out_ref[...] = sum_of(square_slots)
    sum_move.finish()
    sums_out_ref[...] = sum_of(sum_slots_ref)
    for move in moves:
        move.finish()
    along.finish()
    gain_sum_ref[...] = sum_of(part_slots)


def mixer_back(
    heads, low, out_w, branch, feed, conv, rate, gate, state, mixed, branch_w, rec_w, normed,
    vectors, gate_a, gate_x, layer_in, grad_residual, gain, gain_two_grad,
):
    seqs, rows, width = layer_in.shape
    seq_len, channels = feed.shape[1:]
    size, n = lax.axis_size("seq"), lax.axis_size("grp")
    f32, bf16 = jnp.float32, jnp.bfloat16
    large = (low, out_w, branch, feed, conv, rate, gate, state, mixed, branch_w, rec_w)
    small = (vectors, gate_a, gate_x, layer_in, grad_residual, gain, gain_two_grad)
    window_rows = head_windows(heads, channels // heads, size)[0]
    grads = [jax.ShapeDtypeStruct(w.shape, bf16) for w in (branch_w, rec_w, out_w)]
    squares = (heads, 2, window_rows, channels)
    part = width // size
    return call(
        functools.partial(mixer_back_body, heads), "mixer_back", 6,
        large + (normed,) + small,
        [in_hbm] * 12 + [in_vmem] * 7,
        [
            jax.ShapeDtypeStruct(layer_in.shape, f32),
            jax.ShapeDtypeStruct(squares, f32),
            jax.ShapeDtypeStruct((8, channels), f32),
            jax.ShapeDtypeStruct((8, part), f32),
        ]
        + [slots_of(grad, axis, 0) for grad, axis in zip(grads, mixer_axes)],
        [in_vmem] * 4 + [in_hbm] * 3,
        [pltpu.VMEM(v.shape, v.dtype) for v in large]
        + [
            pltpu.VMEM((seq_len, channels), f32),
            pltpu.VMEM(feed.shape, bf16),
            pltpu.VMEM(feed.shape, bf16),
            pltpu.VMEM((2, channels, channels), f32),
            pltpu.VMEM((8, channels), f32),
            pltpu.VMEM((pick_rows(seq_len) + 8, channels), f32),
            pltpu.VMEM((pick_rows(seq_len) + 8, channels), f32),
            pltpu.VMEM((8, channels), f32),
            pltpu.VMEM((2, seqs, seq_len, 256), bf16),
        ]
        + [pltpu.VMEM(grad.shape, bf16) for grad in grads]
        + [
            pltpu.VMEM((size,) + squares, f32),
            pltpu.VMEM((size, 8, channels), f32),
            pltpu.VMEM((8, width), f32),
            pltpu.VMEM((8, part), f32),
            pltpu.VMEM((size, 8, part), f32),
            pltpu.VMEM((n, 8, part), f32),
            pltpu.SemaphoreType.DMA((4 + 7 * seqs,)),
            pltpu.SemaphoreType.DMA((2,)),
        ]
        + [pltpu.SemaphoreType.DMA((heads, size))] * 2
        + [pltpu.SemaphoreType.DMA((size,))] * 4
        + [pltpu.SemaphoreType.DMA((n,))] * 2
        + seq_sems(3)
        + scatter_scratch(seqs, rows, width),
        100,
    )


def out_only_body(hidden_ref, down_w_ref, residual_ref, layer_out_ref, *scratch):
    greet_line()
    scatter = Scatter(residual_ref.shape[1], *scratch)
    fill, store = out_body(hidden_ref, down_w_ref, residual_ref, layer_out_ref, scatter, 0)
    seqs = range(residual_ref.shape[0])
    sum_then_gather(
        scatter, None, [fill(s) for s in seqs], [functools.partial(store, s) for s in seqs]
    )


def out_only(hidden, down_w, residual):
    seqs, rows, width = residual.shape
    return call(
        out_only_body, "layer_out", 5,
        (hidden, down_w, residual), [in_vmem] * 3,
        [jax.ShapeDtypeStruct(residual.shape, jnp.bfloat16)], [in_vmem],
        scatter_scratch(seqs, rows, width), 60,
    )[0]


def per_device(
    layer_in, gain_one, w_branch, w_rec, conv_w, conv_b, gate_a_w, gate_a_b, gate_x_w, gate_x_b,
    decay_logit, w_out, gain_two, mlp_gate, mlp_up, mlp_down, out_grad,
):
    seqs_here, positions, model_width = layer_in.shape
    heads_here, tap_count, part_dim = conv_w.shape
    seq_devices, grp_devices = lax.axis_size("seq"), lax.axis_size("grp")
    head_dim = part_dim * seq_devices
    channels = heads_here * head_dim
    f32 = jnp.float32

    short_line = seqs_here * positions * grp_devices <= 2048 and model_width // seq_devices == 512
    mixer_weights = (w_branch.T, w_rec.T, w_out)
    mlp_weights = (mlp_gate, mlp_up, mlp_down)
    at = tap_count + 4
    if short_line:
        softness = jax.nn.softplus(-decay_logit.astype(f32))
        vector_rows = [jnp.transpose(conv_w, (1, 0, 2)).reshape(tap_count, -1)]
        vector_rows += [v.reshape(1, -1) for v in (conv_b, gate_a_b, gate_x_b)]
        vector_pack = jnp.concatenate([v.astype(f32) for v in vector_rows] + [softness.reshape(1, -1)])
        vector_pack = jnp.pad(vector_pack, ((0, 0), (0, -vector_pack.shape[1] % 128)))
        gain_pack = jnp.concatenate([gain_one, gain_two]).astype(f32)[None]
        gain_pack = jnp.pad(gain_pack, ((0, 7), (0, -gain_pack.shape[1] % 128)))
        gate_pack = jnp.concatenate([gate_a_w, gate_x_w]).astype(f32)
        (
            residual, gains, vectors, diag_a, diag_x,
            normed_one, branch_pre, feed, conv, rate, gate, state, mixed, branch_w, rec_w, out_w,
            normed_two, grad_output, gate_w, up_w, down_w,
        ) = mixer_forward(layer_in, out_grad, gain_pack, vector_pack, gate_pack, mixer_weights, mlp_weights)
        normed_one = normed_one.reshape(-1, model_width)
        grad_output = grad_output.reshape(-1, model_width)
    else:
        own_params = jnp.concatenate(
            [jnp.transpose(conv_w, (0, 2, 1))]
            + [v[:, :, None] for v in (conv_b, gate_a_b, gate_x_b, decay_logit)]
            + [gate_a_w, gate_x_w],
            axis=2,
        ).astype(f32)
        own_gains = jnp.concatenate([gain_one, gain_two]).astype(f32)
        pack = jnp.concatenate(
            [padded_rows(own_params.reshape(1, -1))[0], padded_rows(own_gains.reshape(1, -1))[0]]
        )
        late_grad, x_full, params, gains, branch_w, rec_w, out_w = gather_first(
            layer_in, out_grad, pack, mixer_weights
        )

        gains = gains.reshape(grp_devices, seq_devices, -1)[:, :, : own_gains.size]
        gains = jnp.transpose(gains.reshape(grp_devices, seq_devices, 2, -1), (2, 1, 0, 3)).reshape(2, 1, -1)
        params = params.reshape(seq_devices, -1)[:, : own_params.size]
        params = params.reshape((seq_devices,) + own_params.shape)
        params = jnp.transpose(params, (1, 0, 2, 3)).reshape(heads_here, head_dim, -1)
        vectors = params[:, :, : tap_count + 4].reshape(channels, -1).T
        diag_a = head_diagonal(params[:, :, at : at + head_dim].astype(jnp.bfloat16))
        diag_x = head_diagonal(params[:, :, at + head_dim :].astype(jnp.bfloat16))
        logit = vectors[tap_count + 3 :]
        softness = jax.nn.softplus(-logit)
        grad_output = jnp.concatenate(
            [lax.all_gather(late_grad[s], "grp", axis=0, tiled=True) for s in range(seqs_here)]
        )
        inputs = x_full.astype(f32)
        normal_one = inputs * lax.rsqrt(mean_of(inputs * inputs) + epsilon)
        normed_one = (normal_one * gains[0]).astype(jnp.bfloat16).reshape(-1, model_width)
        branch_pre = matmul_nt(normed_one, branch_w).reshape(seqs_here, -1, channels)
        feed = matmul_nt(normed_one, rec_w).astype(jnp.bfloat16).reshape(seqs_here, -1, channels)
        conv, rate, gate, state, mixed = rec_forward(feed, branch_pre, vectors, softness, diag_a, diag_x)
        residual, normed_two, gate_w, up_w, down_w = mixer_out(
            mixed, out_w, layer_in, gains[1], mlp_weights
        )
    mixed = mixed.reshape(-1, channels)
    normed_two = normed_two.reshape(-1, model_width)
    up_proj = matmul(normed_two, up_w)
    gate_act, gate_pull = jax.vjp(jax.nn.gelu, matmul(normed_two, gate_w))
    hidden = (gate_act * up_proj).astype(jnp.bfloat16)
    grad_hidden = matmul_nt(grad_output, down_w)
    grad_gate = gate_pull(grad_hidden * up_proj)[0].astype(jnp.bfloat16)
    grad_up = (grad_hidden * gate_act).astype(jnp.bfloat16)
    def by_seq(values):
        return values.reshape(seqs_here, -1, values.shape[-1])

    if short_line:
        first_grad = matmul_tn(normed_two, grad_gate).astype(jnp.bfloat16)
        mlp_grads = (first_grad, by_seq(normed_two), by_seq(grad_output))
    else:
        mlp_grads = low_all(
            (matmul_tn(normed_two, grad_gate), matmul_tn(normed_two, grad_up), matmul_tn(hidden, grad_output))
        )

    back_inputs = (
        by_seq(grad_gate), by_seq(grad_up), gate_w, up_w, residual, out_grad, gains[1], mlp_grads
    )
    if not short_line:
        layer_out = out_only(by_seq(hidden), down_w, residual)
        grad_residual, gain_two_grad, residual_low, *mlp_slots = mlp_back(*back_inputs, ())
    else:
        grad_residual, gain_two_grad, residual_low, *mlp_slots, layer_out, late = mlp_back(
            *back_inputs, (by_seq(hidden), down_w)
        )
        late = lax.psum_scatter(late, "grp", scatter_dimension=0, tiled=True)
        late = (residual[seqs_here - 1] + late.astype(f32)).astype(jnp.bfloat16)
        layer_out = jnp.concatenate([layer_out, late[None]])
    if short_line:
        mlp_grads = sum_slots(mlp_grads[:1], mlp_slots[:1], weight_axes) + [sum_all(slot) for slot in mlp_slots[1:]]
    else:
        mlp_grads = sum_slots(mlp_grads, mlp_slots, weight_axes)
    if short_line:
        grad_x, squares, sums, gain_sum, *mixer_slots = mixer_back(
            heads_here, residual_low, out_w, branch_pre, feed, conv, rate, gate, state, by_seq(mixed), branch_w, rec_w,
            by_seq(normed_one), vectors, diag_a, diag_x, layer_in, grad_residual, gains[0], gain_two_grad,
        )
        mixer_grads = [sum_all(slot) for slot in mixer_slots]
        place = lax.axis_index("seq")
        first = place * part_dim % 8
        square_parts = [
            lax.dynamic_slice_in_dim(squares[h], first, part_dim, 1)[:, :, h * head_dim : (h + 1) * head_dim]
            for h in range(heads_here)
        ]
        grad_a, grad_x_gate = (jnp.stack([part[i] for part in square_parts]) for i in range(2))
        own_sums = lax.dynamic_slice_in_dim(
            sums.reshape(at, heads_here, head_dim), place * part_dim, part_dim, 2
        )
        logit_grad = 8.0 * jax.nn.sigmoid(-decay_logit.astype(f32)) * own_sums[tap_count + 3]
        rec_outs = (
            jnp.transpose(own_sums[:tap_count], (1, 0, 2)), own_sums[tap_count], grad_a, own_sums[tap_count + 1],
            grad_x_gate, own_sums[tap_count + 2], logit_grad,
        )
        return finish(layer_out, grad_x, gain_sum, mixer_grads, rec_outs, mlp_grads)
    residual_low = residual_low.reshape(-1, model_width)
    out_weight_grad = matmul_tn(mixed, residual_low)
    grad_mixed = by_seq(matmul_nt(residual_low, out_w))
    grad_branch, grad_feed, square_a, square_x, sums = rec_backward(
        grad_mixed, branch_pre, feed, conv, rate, gate, state, vectors, softness, diag_a, diag_x
    )
    vector_grads = jnp.concatenate(
        [sums[: tap_count + 3], 8.0 * jax.nn.sigmoid(-logit) * sums[tap_count + 3 :]]
    )
    rec_grads = jnp.concatenate(
        [
            vector_grads.T.reshape(heads_here, head_dim, -1),
            diagonal_heads(square_a, heads_here),
            diagonal_heads(square_x, heads_here),
        ],
        axis=2,
    )
    rec_grads = rec_grads.reshape(heads_here, seq_devices, part_dim, -1)
    rec_blocks = padded_rows(jnp.transpose(rec_grads, (1, 0, 2, 3)))
    mixer_grads = low_all(
        (
            matmul_tn(grad_branch.reshape(-1, channels), normed_one),
            matmul_tn(grad_feed.reshape(-1, channels), normed_one),
            out_weight_grad,
        )
    )
    grad_x, rec_sum, gain_sum, *mixer_slots = last(
        grad_branch, grad_feed, branch_w, rec_w, layer_in, grad_residual, gains[0], gain_two_grad, rec_blocks,
        mixer_grads,
    )
    mixer_grads = sum_slots(mixer_grads, mixer_slots, mixer_axes)
    rec_sum = rec_sum.reshape(-1)[: own_params.size].reshape(own_params.shape)
    rec_outs = (
        jnp.transpose(rec_sum[:, :, :tap_count], (0, 2, 1)),
        rec_sum[:, :, tap_count],
        rec_sum[:, :, at : at + head_dim],
        rec_sum[:, :, tap_count + 1],
        rec_sum[:, :, at + head_dim :],
        rec_sum[:, :, tap_count + 2],
        rec_sum[:, :, tap_count + 3],
    )
    return finish(layer_out, grad_x, gain_sum, mixer_grads, rec_outs, mlp_grads)


def finish(layer_out, grad_x, gain_sum, mixer_grads, rec_outs, mlp_grads):
    part = gain_sum.shape[1] // lax.axis_size("grp")
    gain_grads = lax.dynamic_slice_in_dim(gain_sum, lax.axis_index("grp") * part, part, 1)
    return (
        layer_out, grad_x, gain_grads[0], mixer_grads[0].T, mixer_grads[1].T, *rec_outs, mixer_grads[2], gain_grads[1],
        *mlp_grads,
    )


def solution(mesh):
    placed = (
        P("seq", "grp", None),
        P(("seq", "grp")),
        P("seq", "grp"),
        P("seq", "grp"),
        P("grp", None, "seq"),
        P("grp", "seq"),
        P("grp", "seq", None),
        P("grp", "seq"),
        P("grp", "seq", None),
        P("grp", "seq"),
        P("grp", "seq"),
        P("grp", "seq"),
        P(("seq", "grp")),
        P("seq", "grp"),
        P("seq", "grp"),
        P("grp", "seq"),
        P("seq", "grp", None),
    )
    return jax.shard_map(
        per_device,
        mesh=mesh,
        in_specs=placed,
        out_specs=(
            P("seq", "grp", None),
            P("seq", "grp", None),
            P(("seq", "grp")),
            P("seq", "grp"),
            P("seq", "grp"),
            P("grp", None, "seq"),
            P("grp", "seq"),
            P("grp", "seq", None),
            P("grp", "seq"),
            P("grp", "seq", None),
            P("grp", "seq"),
            P("grp", "seq"),
            P("grp", "seq"),
            P(("seq", "grp")),
            P("seq", "grp"),
            P("seq", "grp"),
            P("grp", "seq"),
        ),
        check_vma=False,
    )
```

```python
import functools
import math

import jax
import jax.numpy as jnp
from jax import lax
from jax.experimental import pallas as pl
from jax.experimental.pallas import tpu as pltpu
from jax.sharding import PartitionSpec as P

epsilon = 1e-06
gelu_slope = math.sqrt(2.0 / math.pi)
gelu_cubic = 0.044715
MESH = pl.DeviceIdType.MESH


def matmul(left, right):
    return jnp.dot(left, right, preferred_element_type=jnp.float32)


def matmul_tn(left, right):
    return lax.dot_general(
        left, right, (((0,), (0,)), ((), ())), preferred_element_type=jnp.float32
    )


def matmul_nt(left, right):
    return lax.dot_general(
        left, right, (((1,), (1,)), ((), ())), preferred_element_type=jnp.float32
    )


def norm_back(grad_normed, normal_part, inverse, gain):
    scaled = grad_normed * gain
    return inverse * (scaled - normal_part * jnp.mean(scaled * normal_part, axis=-1, keepdims=True))


def low_all(grads):
    return tuple(grad.astype(jnp.bfloat16) for grad in grads)


def sum_slots(grads, slots, axes):
    sums = []
    for grad, slot, axis in zip(grads, slots, axes):
        size = slot.shape[1 + axis]
        own = lax.dynamic_slice_in_dim(grad, lax.axis_index("seq") * size, size, axis)
        for k in range(slot.shape[0]):
            own = own.astype(jnp.float32) + slot[k].astype(jnp.float32)
        sums.append(own)
    return sums


def sum_all(slots):
    total = slots[0].astype(jnp.float32)
    for k in range(1, slots.shape[0]):
        total = total + slots[k].astype(jnp.float32)
    return total


def padded_rows(values):
    flat = values.reshape(values.shape[0], -1)
    flat = jnp.pad(flat, ((0, 0), (0, -flat.shape[1] % 1024)))
    return flat.reshape(values.shape[0], -1, 128)


def head_diagonal(blocks):
    heads, head_dim, _ = blocks.shape
    rows = []
    for h in range(heads):
        row = [jnp.zeros((head_dim, head_dim), blocks.dtype)] * heads
        row[h] = blocks[h]
        rows.append(jnp.concatenate(row, axis=1))
    return jnp.concatenate(rows, axis=0)


def diagonal_heads(square, heads):
    head_dim = square.shape[0] // heads
    return jnp.stack(
        [
            square[h * head_dim : (h + 1) * head_dim, h * head_dim : (h + 1) * head_dim]
            for h in range(heads)
        ]
    )


def pick_rows(seq_len, choices=(128, 96, 64, 32, 16)):
    for rows in choices:
        if seq_len % rows == 0:
            return rows
    return seq_len


def gelu_parts(x):
    cubic = gelu_slope * (x + gelu_cubic * x * x * x)
    bend = jnp.tanh(cubic)
    gate = 0.5 * (1.0 + bend)
    slope = gate + 0.5 * x * (1.0 - bend * bend) * gelu_slope * (1.0 + 3.0 * gelu_cubic * x * x)
    return x * gate, slope


def minus_expm1(x):
    series = 1.0 + x * (1.0 / 9.0)
    for k in (8, 7, 6, 5, 4, 3, 2):
        series = 1.0 + x * (1.0 / k) * series
    return jnp.where(x > -0.4, -x * series, 1.0 - jnp.exp(x))


def shift_down(values, by, fill):
    rows = values.shape[0]
    if by % 8 == 0:
        return jnp.concatenate([jnp.full((by, values.shape[1]), fill), values[: rows - by]], axis=0)
    index = lax.broadcasted_iota(jnp.int32, values.shape, 0)
    return jnp.where(index >= by, pltpu.roll(values, by, 0), fill)


def shift_up(values, by, fill):
    rows = values.shape[0]
    if by % 8 == 0:
        return jnp.concatenate([values[by:], jnp.full((by, values.shape[1]), fill)], axis=0)
    index = lax.broadcasted_iota(jnp.int32, values.shape, 0)
    return jnp.where(index < rows - by, pltpu.roll(values, rows - by, 0), fill)


def scan_block(decay, drive, shift):
    by = 1
    while by < decay.shape[0]:
        drive = drive + decay * shift(drive, by, 0.0)
        decay = decay * shift(decay, by, 1.0)
        by *= 2
    return decay, drive


def decay_parts(rate, softness):
    log_decay = -8.0 * rate * softness
    return jnp.exp(log_decay), jnp.sqrt(minus_expm1(2.0 * log_decay))


def rec_forward_rows(feed, branch, vectors_ref, softness_ref, gate_a_ref, gate_x_ref, window, carry):
    rows = feed.shape[0]
    window[pl.ds(8, rows), :] = feed.astype(jnp.float32)
    conv = vectors_ref[4:5, :] + vectors_ref[0:1, :] * window[pl.ds(8, rows), :]
    for k in range(1, 4):
        conv = conv + vectors_ref[k : k + 1, :] * window[pl.ds(8 - k, rows), :]
    window[pl.ds(0, 8), :] = window[pl.ds(rows, 8), :]
    conv_low = conv.astype(jnp.bfloat16)
    rate = jax.nn.sigmoid(matmul(conv_low, gate_a_ref[...]) + vectors_ref[5:6, :])
    gate = jax.nn.sigmoid(matmul(conv_low, gate_x_ref[...]) + vectors_ref[6:7, :])
    decay, scale = decay_parts(rate, softness_ref[...])
    total, state = scan_block(decay, scale * gate * conv_low.astype(jnp.float32), shift_down)
    state = state + total * carry[0:1, :]
    carry[0:1, :] = state[rows - 1 : rows, :]
    gelu_branch = gelu_parts(branch)[0]
    mixed = (gelu_branch * state.astype(jnp.bfloat16).astype(jnp.float32)).astype(jnp.bfloat16)
    return conv_low, rate, gate, state, mixed


def rec_forward_body(
    feed_ref, branch_ref, vectors_ref, softness_ref, gate_a_ref, gate_x_ref,
    conv_ref, rate_ref, input_ref, state_ref, mixed_ref, window, carry,
):
    @pl.when(pl.program_id(0) == 0)
    def _():
        window[...] = jnp.zeros_like(window)
        carry[...] = jnp.zeros_like(carry)

    for s in range(feed_ref.shape[0]):
        conv_ref[s], rate_ref[s], input_ref[s], state_ref[s], mixed_ref[s] = rec_forward_rows(
            feed_ref[s], branch_ref[s], vectors_ref, softness_ref, gate_a_ref, gate_x_ref, window.at[s], carry.at[s]
        )


def rec_backward_rows(
    grad_mixed, branch, feed, feed_before, conv_low, rate, gate, state, state_before,
    vectors_ref, softness_ref, gate_a_ref, gate_x_ref, grad_a_ref, grad_x_ref, sums_ref, window, later, carry,
):
    rows = feed.shape[0]
    softness = softness_ref[...]
    gelu_branch, slope = gelu_parts(branch)
    state_low = state.astype(jnp.bfloat16).astype(jnp.float32)
    grad_state = (grad_mixed * gelu_branch).astype(jnp.bfloat16).astype(jnp.float32)
    grad_branch = (slope * grad_mixed * state_low).astype(jnp.bfloat16)
    decay, scale = decay_parts(rate, softness)
    total, carried = scan_block(shift_up(decay, 1, 1.0), grad_state, shift_up)
    carried = carried + total * carry[0:1, :]
    carry[0:1, :] = decay[0:1, :] * carried[0:1, :]
    index = lax.broadcasted_iota(jnp.int32, state.shape, 0)
    previous = jnp.where(index >= 1, pltpu.roll(state, 1, 0), state_before[7:8, :])
    conv = conv_low.astype(jnp.float32)
    grad_log = carried * previous * decay - carried * gate * conv * decay * decay / scale
    log_rate = grad_log * rate
    pre_a = -8.0 * softness * log_rate * (1.0 - rate)
    pre_x = carried * scale * conv * gate * (1.0 - gate)
    low_a = pre_a.astype(jnp.bfloat16)
    low_x = pre_x.astype(jnp.bfloat16)
    grad_a_ref[...] += matmul_tn(conv_low, low_a)
    grad_x_ref[...] += matmul_tn(conv_low, low_x)
    grad_conv = (
        carried * scale * gate
        + matmul_nt(low_a, gate_a_ref[...])
        + matmul_nt(low_x, gate_x_ref[...])
    )
    window[pl.ds(0, 8), :] = feed_before
    window[pl.ds(8, rows), :] = feed.astype(jnp.float32)
    later[pl.ds(rows, 8), :] = later[pl.ds(0, 8), :]
    later[pl.ds(0, rows), :] = grad_conv
    grad_feed = vectors_ref[0:1, :] * grad_conv
    sums_ref[0:1, :] += jnp.sum(grad_conv * window[pl.ds(8, rows), :], axis=0, keepdims=True)
    for k in range(1, 4):
        grad_feed = grad_feed + vectors_ref[k : k + 1, :] * later[pl.ds(k, rows), :]
        sums_ref[k : k + 1, :] += jnp.sum(
            grad_conv * window[pl.ds(8 - k, rows), :], axis=0, keepdims=True
        )
    sums_ref[4:5, :] += jnp.sum(grad_conv, axis=0, keepdims=True)
    sums_ref[5:6, :] += jnp.sum(pre_a, axis=0, keepdims=True)
    sums_ref[6:7, :] += jnp.sum(pre_x, axis=0, keepdims=True)
    sums_ref[7:8, :] += jnp.sum(log_rate, axis=0, keepdims=True)
    return grad_branch, grad_feed.astype(jnp.bfloat16)


def rec_backward_body(
    grad_mixed_ref, branch_ref, feed_ref, feed_before_ref, conv_ref, rate_ref, input_ref,
    state_ref, state_before_ref, vectors_ref, softness_ref, gate_a_ref, gate_x_ref,
    grad_branch_ref, grad_feed_ref, grad_a_ref, grad_x_ref, sums_ref, window, later, carry,
):
    step = pl.program_id(0)

    @pl.when(step == 0)
    def _():
        for ref in (later, carry, grad_a_ref, grad_x_ref, sums_ref):
            ref[...] = jnp.zeros_like(ref)

    keep = jnp.where(step == pl.num_programs(0) - 1, 0.0, 1.0)
    for s in range(feed_ref.shape[0]):
        before = feed_before_ref[s].astype(jnp.float32)
        grad_branch_ref[s], grad_feed_ref[s] = rec_backward_rows(
            grad_mixed_ref[s], branch_ref[s], feed_ref[s], before[before.shape[0] - 8 :] * keep, conv_ref[s],
            rate_ref[s], input_ref[s], state_ref[s], state_before_ref[s] * keep,
            vectors_ref, softness_ref, gate_a_ref, gate_x_ref, grad_a_ref, grad_x_ref, sums_ref,
            window.at[s], later.at[s], carry.at[s],
        )


def whole(shape):
    return pl.BlockSpec(shape, lambda i: (0,) * len(shape))


def rec_forward(feed, branch, vectors, softness, gate_a, gate_x):
    seqs, seq_len, channels = feed.shape
    rows = pick_rows(seq_len)
    block = pl.BlockSpec((seqs, rows, channels), lambda i: (0, i, 0))
    full = jax.ShapeDtypeStruct(feed.shape, jnp.float32)
    low = jax.ShapeDtypeStruct(feed.shape, jnp.bfloat16)
    return pl.pallas_call(
        rec_forward_body,
        grid=(seq_len // rows,),
        in_specs=[block, block]
        + [whole(v.shape) for v in (vectors, softness, gate_a, gate_x)],
        out_specs=[block] * 5,
        out_shape=[low, full, full, full, low],
        scratch_shapes=[
            pltpu.VMEM((seqs, rows + 8, channels), jnp.float32),
            pltpu.VMEM((seqs, 8, channels), jnp.float32),
        ],
        compiler_params=pltpu.CompilerParams(vmem_limit_bytes=40 << 20),
        name="rec_forward",
    )(feed, branch, vectors, softness, gate_a, gate_x)


def rec_backward(grad_mixed, branch, feed, conv, rate, gate, state, vectors, softness, gate_a, gate_x):
    seqs, seq_len, channels = feed.shape
    rows = pick_rows(seq_len)
    blocks = seq_len // rows
    block = pl.BlockSpec((seqs, rows, channels), lambda i: (0, blocks - 1 - i, 0))

    def ahead(by):
        return pl.BlockSpec(
            (seqs, by, channels),
            lambda i: (0, jnp.maximum((blocks - 1 - i) * (rows // by) - 1, 0), 0),
        )

    low = jax.ShapeDtypeStruct(feed.shape, jnp.bfloat16)
    square = jax.ShapeDtypeStruct((channels, channels), jnp.float32)
    return pl.pallas_call(
        rec_backward_body,
        grid=(blocks,),
        in_specs=[block, block, block, ahead(16), block, block, block, block, ahead(8)]
        + [whole(v.shape) for v in (vectors, softness, gate_a, gate_x)],
        out_specs=[block, block, whole((channels, channels)), whole((channels, channels)), whole((8, channels))],
        out_shape=[low, low, square, square, jax.ShapeDtypeStruct((8, channels), jnp.float32)],
        scratch_shapes=[
            pltpu.VMEM((seqs, rows + 8, channels), jnp.float32),
            pltpu.VMEM((seqs, rows + 8, channels), jnp.float32),
            pltpu.VMEM((seqs, 8, channels), jnp.float32),
        ],
        compiler_params=pltpu.CompilerParams(vmem_limit_bytes=40 << 20),
        name="rec_backward",
    )(grad_mixed, branch, feed, feed, conv, rate, gate, state, state, vectors, softness, gate_a, gate_x)


def line_place():
    return lax.axis_size("grp") // 2, lax.axis_index("grp") // 2, lax.axis_index("grp") % 2


def greet_line():
    chips, chip, core = line_place()
    barrier = pltpu.get_barrier_semaphore()

    def signal(place):
        pl.semaphore_signal(barrier, inc=1, device_id={"grp": place}, device_id_type=MESH)

    signal(chip * 2 + 1 - core)

    @pl.when(chip > 0)
    def _():
        signal(chip * 2 + core - 2)

    @pl.when(chip < chips - 1)
    def _():
        signal(chip * 2 + core + 2)

    ends = (chip == 0).astype(jnp.int32) + (chip == chips - 1).astype(jnp.int32)
    pl.semaphore_wait(barrier, 3 - ends)


def greet_axes(axes):
    barrier = pltpu.get_barrier_semaphore()
    for axis in axes:
        size = lax.axis_size(axis)
        for k in range(1, size):
            pl.semaphore_signal(
                barrier,
                inc=1,
                device_id={axis: lax.rem(lax.axis_index(axis) + k, size)},
                device_id_type=MESH,
            )
    pl.semaphore_wait(barrier, sum(lax.axis_size(axis) - 1 for axis in axes))


class Gather:
    def __init__(self, sources, outs, rows, send_sem, recv_sem, own_sem):
        self.chips, self.chip, self.core = line_place()
        self.me = self.chip * 2 + self.core
        self.sources, self.outs, self.rows = sources, outs, rows
        self.send_sem, self.recv_sem, self.own_sem = send_sem, recv_sem, own_sem

    def slot(self, p, origin):
        return self.outs[p].at[pl.ds(pl.multiple_of(origin * self.rows, self.rows), self.rows), :]

    def copy(self, p, source, origin, target, way):
        return pltpu.make_async_remote_copy(
            src_ref=source,
            dst_ref=self.slot(p, origin),
            send_sem=self.send_sem.at[way, p, origin],
            recv_sem=self.recv_sem.at[p, origin],
            device_id={"grp": target},
            device_id_type=MESH,
        )

    def to_right(self, p, source, origin):
        return self.copy(p, source, origin, self.me + 2, 0)

    def to_left(self, p, source, origin):
        return self.copy(p, source, origin, self.me - 2, 1)

    def to_partner(self, p, source, origin):
        return self.copy(p, source, origin, self.chip * 2 + 1 - self.core, 2)

    def own(self, p):
        return pltpu.make_async_copy(self.sources[p], self.slot(p, self.me), self.own_sem.at[p])

    def start(self, p):
        source = self.sources[p]

        @pl.when(self.chip < self.chips - 1)
        def _():
            self.to_right(p, source, self.me).start()

        @pl.when(self.chip > 0)
        def _():
            self.to_left(p, source, self.me).start()

        self.to_partner(p, source, self.me).start()
        self.own(p).start()

    def hop(self, p, h):
        left_origin = self.me - 2 - 2 * h
        right_origin = self.me + 2 + 2 * h

        @pl.when(self.chip - 1 - h >= 0)
        def _():
            here = self.slot(p, left_origin)
            self.to_right(p, here, left_origin).wait_recv()

            @pl.when(self.chip < self.chips - 1)
            def _():
                self.to_right(p, here, left_origin).start()

            self.to_partner(p, here, left_origin).start()

        @pl.when(self.chip + 1 + h <= self.chips - 1)
        def _():
            here = self.slot(p, right_origin)
            self.to_left(p, here, right_origin).wait_recv()

            @pl.when(self.chip > 0)
            def _():
                self.to_left(p, here, right_origin).start()

            self.to_partner(p, here, right_origin).start()

    def arrive(self, p):
        for c in range(self.chips):
            origin = c * 2 + 1 - self.core
            self.to_partner(p, self.slot(p, origin), origin).wait_recv()
        self.own(p).wait()

    def finish(self, p):
        self.arrive(p)
        self.sent(p)

    def sent(self, p):
        for c in range(self.chips):
            origin = c * 2 + self.core
            here = self.slot(p, origin)
            self.to_partner(p, here, origin).wait_send()

            @pl.when((c <= self.chip) & (self.chip < self.chips - 1))
            def _():
                self.to_right(p, here, origin).wait_send()

            @pl.when((c >= self.chip) & (self.chip > 0))
            def _():
                self.to_left(p, here, origin).wait_send()


def gather_sems(pieces):
    n = lax.axis_size("grp")
    return [
        pltpu.SemaphoreType.DMA((3, pieces, n)),
        pltpu.SemaphoreType.DMA((pieces, n)),
        pltpu.SemaphoreType.DMA((pieces,)),
    ]


class Scatter:
    def __init__(self, rows, part, out, swap_in, line_in, send_sem, recv_sem):
        self.chips, self.chip, self.core = line_place()
        self.me = self.chip * 2 + self.core
        self.rows, self.part, self.out = rows, part, out
        self.swap_in, self.line_in = swap_in, line_in
        self.send_sem, self.recv_sem = send_sem, recv_sem

    def copy(self, dest, place, way, slot, p):
        return pltpu.make_async_remote_copy(
            src_ref=self.out.at[p, slot],
            dst_ref=dest,
            send_sem=self.send_sem.at[way, p, slot],
            recv_sem=self.recv_sem.at[way, p, slot],
            device_id={"grp": place},
            device_id_type=MESH,
        )

    def swap(self, p, c):
        return self.copy(self.swap_in.at[p, c], self.chip * 2 + 1 - self.core, 0, c, p)

    def right(self, p, c):
        return self.copy(self.line_in.at[p, c], self.me + 2, 1, c, p)

    def left(self, p, c):
        slot = jnp.where(c == self.chip - 1, self.chips, c)
        return self.copy(self.line_in.at[p, slot], self.me - 2, 2, c, p)

    def from_right(self, p, c):
        slot = jnp.where(c == self.chip, self.chips, c)
        return self.copy(self.line_in.at[p, slot], self.me + 2, 2, c, p)

    def fill(self, p, s, lefts, rights, transposed, width=512):
        def rows_of(ref, core):
            at = [pl.multiple_of((c * 2 + core) * self.rows, self.rows) for c in range(self.chips)]
            return jnp.concatenate([ref[s, pl.ds(a, self.rows), :] for a in at], axis=0)

        def product(core, store):
            chosen = [rows_of(ref, core) for ref in lefts]

            @pl.loop(0, self.out.shape[-1] // width)
            def _(j):
                columns = pl.ds(pl.multiple_of(j * width, width), width)
                total = None
                for left, right in zip(chosen, rights):
                    term = matmul_nt(left, right[columns, :]) if transposed else matmul(left, right[:, columns])
                    total = term if total is None else total + term
                for c in range(self.chips):
                    store(c, columns, total[c * self.rows : (c + 1) * self.rows])

        def to_out(c, columns, value):
            self.out[p, c, :, columns] = value.astype(jnp.bfloat16)

        def to_part(c, columns, value):
            self.part[p, c, :, columns] = value

        def partners():
            product(1 - self.core, to_out)
            for c in range(self.chips):
                self.swap(p, c).start()

        def own():
            product(self.core, to_part)

        return partners, own

    def own(self, p, c):
        self.swap(p, c).wait_recv()
        return self.part[p, c] + self.swap_in[p, c].astype(jnp.float32)

    def hop(self, p, t):
        last = self.chips - 1

        def send(c, first, arrival, onward):
            self.swap(p, c).wait_send()
            total = self.own(p, c)

            @pl.when(first)
            def _():
                self.out[p, c] = total.astype(jnp.bfloat16)

            @pl.when(jnp.logical_not(first))
            def _():
                arrival(p, c).wait_recv()
                self.out[p, c] = (total + self.line_in[p, c].astype(jnp.float32)).astype(jnp.bfloat16)

            onward(p, c).start()

        @pl.when(self.chip <= t)
        def _():
            send(last - t + self.chip, self.chip == 0, self.right, self.right)

        @pl.when(last - self.chip <= t)
        def _():
            send(t - last + self.chip, self.chip == last, self.from_right, self.left)

    def result(self, p):
        chip = self.chip
        self.part[p, chip] = self.own(p, chip)

        @pl.when(chip > 0)
        def _():
            self.right(p, chip).wait_recv()
            self.part[p, chip] += self.line_in[p, chip].astype(jnp.float32)

        @pl.when(chip < self.chips - 1)
        def _():
            self.from_right(p, chip).wait_recv()
            self.part[p, chip] += self.line_in[p, self.chips].astype(jnp.float32)

        return self.part.at[p, chip]

    def finish(self, p):
        self.swap(p, self.chip).wait_send()
        for c in range(self.chips):

            @pl.when(c > self.chip)
            def _():
                self.right(p, c).wait_send()

            @pl.when(c < self.chip)
            def _():
                self.left(p, c).wait_send()


def scatter_scratch(pieces, rows, width):
    chips = lax.axis_size("grp") // 2
    return [
        pltpu.VMEM((pieces, chips, rows, width), jnp.float32),
        pltpu.VMEM((pieces, chips, rows, width), jnp.bfloat16),
        pltpu.VMEM((pieces, chips, rows, width), jnp.bfloat16),
        pltpu.VMEM((pieces, chips + 1, rows, width), jnp.bfloat16),
        pltpu.SemaphoreType.DMA((3, pieces, chips)),
        pltpu.SemaphoreType.DMA((3, pieces, chips)),
    ]


in_vmem = pl.BlockSpec(memory_space=pltpu.VMEM)
in_hbm = pl.BlockSpec(memory_space=pl.ANY)


def call(body, name, number, inputs, in_specs, outs, out_specs, scratch, us):
    return pl.pallas_call(
        body,
        in_specs=in_specs,
        out_specs=out_specs,
        out_shape=outs,
        scratch_shapes=scratch,
        name=name,
        cost_estimate=pl.CostEstimate(
            flops=us * 1000000000, bytes_accessed=us * 3000000, transcendentals=0
        ),
        compiler_params=pltpu.CompilerParams(
            collective_id=number, has_side_effects=True, vmem_limit_bytes=62 << 20
        ),
    )(*inputs)


class Exchange:
    def __init__(self, axis, source, slot, send_sem, recv_sem, steps=None, first=1):
        self.axis, self.source, self.slot, self.steps, self.first = axis, source, slot, steps, first
        self.size, self.me = lax.axis_size(axis), lax.axis_index(axis)
        self.send_sem, self.recv_sem = send_sem, recv_sem

    def copy(self, k, owner):
        peer = lax.rem(self.me + k, self.size)
        return pltpu.make_async_remote_copy(
            src_ref=self.source(peer),
            dst_ref=self.slot(owner) if self.slot else self.steps.at[k - self.first],
            send_sem=self.send_sem.at[k],
            recv_sem=self.recv_sem.at[k],
            device_id={self.axis: peer},
            device_id_type=MESH,
        )

    def own(self):
        slot = self.slot(self.me) if self.slot else self.steps.at[0]
        return pltpu.make_async_copy(self.source(self.me), slot, self.send_sem.at[0])

    def start(self):
        self.own().start()
        self.start_others()

    def start_others(self):
        for k in range(1, self.size):
            self.copy(k, self.me).start()

    def finish(self):
        self.own().wait()
        self.finish_others()

    def finish_others(self):
        for k in range(1, self.size):
            self.copy(k, lax.rem(self.me - k + self.size, self.size)).wait_recv()
        for k in range(1, self.size):
            self.copy(k, self.me).wait_send()


def sum_of(slots):
    total = slots[0]
    for k in range(1, slots.shape[0]):
        total = total + slots[k]
    return total


def block(ref, axis, parts):
    size = ref.shape[axis] // parts

    def view(k):
        at = pl.ds(pl.multiple_of(k * size, size), size)
        return ref.at[at, :] if axis == 0 else ref.at[:, at]

    return view


def weight_gathers(axes, sources, outs, send_sem, recv_sem):
    parts = lax.axis_size("seq")
    return [
        Exchange(
            "seq", lambda k, ref=source: ref, block(out, axis, parts), send_sem.at[i], recv_sem.at[i]
        )
        for i, (axis, source, out) in enumerate(zip(axes, sources, outs))
    ]


def weight_sums(axes, sources, outs, send_sem, recv_sem, first=1):
    parts = lax.axis_size("seq")
    return [
        Exchange(
            "seq", block(source, axis, parts), None, send_sem.at[i], recv_sem.at[i], out, first
        )
        for i, (axis, source, out) in enumerate(zip(axes, sources, outs))
    ]


def seq_sems(count):
    return [pltpu.SemaphoreType.DMA((count, lax.axis_size("seq")))] * 2


def gathered(block_of, axis):
    shape = list(block_of.shape)
    shape[axis] *= lax.axis_size("seq")
    return jax.ShapeDtypeStruct(shape, block_of.dtype)


def slots_of(matrix, axis, first=1):
    shape = list(matrix.shape)
    size = lax.axis_size("seq")
    shape[axis] //= size
    return jax.ShapeDtypeStruct((size - first, *shape), matrix.dtype)


weight_axes = (0, 0, 1)
mixer_axes = (1, 1, 1)


def copies(pairs, sem):
    return [pltpu.make_async_copy(source, buffer, sem.at[i]) for i, (source, buffer) in enumerate(pairs)]


def views(ref):
    return [ref.at[s] for s in range(ref.shape[0])]


def first_body(x_ref, grad_ref, pack_ref, w0, w1, w2, later_ref, full_ref, params_ref, gains_ref, o0, o1, o2, *refs):
    small_send, small_recv, gain_send, gain_recv, weight_send, weight_recv = refs[3:]
    greet_axes(("seq", "grp"))
    seqs = x_ref.shape[0]
    gather = Gather(views(x_ref), views(full_ref), x_ref.shape[1], *refs[:3])
    weights = weight_gathers(mixer_axes, (w0, w1, w2), (o0, o1, o2), weight_send, weight_recv)
    small = Exchange("seq", lambda k: pack_ref, lambda k: params_ref.at[k], small_send, small_recv)
    small.start()
    for s in range(seqs):
        gather.start(s)
    for weight in weights:
        weight.start()
    later_ref[...] = grad_ref[...]
    small.finish()
    place = lax.axis_index("grp")
    for owner in range(small.size):
        gains_ref[place, owner] = params_ref[owner, pl.ds(pack_ref.shape[0] - 8, 8), :]
    gains = Exchange("grp", lambda k: gains_ref.at[place], lambda k: gains_ref.at[k], gain_send, gain_recv)
    gains.start_others()
    for h in range(gather.chips - 1):
        for s in range(seqs):
            gather.hop(s, h)
    gains.finish_others()
    for weight in weights:
        weight.finish()
    for s in range(seqs):
        gather.finish(s)


def gather_first(layer_in, out_grad, pack, weights):
    seqs, rows, width = layer_in.shape
    n, size = lax.axis_size("grp"), lax.axis_size("seq")
    return call(
        first_body, "gather_first", 1,
        (layer_in, out_grad, pack, *weights), [in_vmem] * 6,
        [
            jax.ShapeDtypeStruct(out_grad.shape, out_grad.dtype),
            jax.ShapeDtypeStruct((seqs, n * rows, width), jnp.bfloat16),
            jax.ShapeDtypeStruct((size,) + pack.shape, jnp.float32),
            jax.ShapeDtypeStruct((n, size, 8, 128), jnp.float32),
        ]
        + [gathered(w, axis) for w, axis in zip(weights, mixer_axes)],
        [in_vmem, in_hbm] + [in_vmem] * 2 + [in_hbm] * 3,
        gather_sems(seqs)
        + [pltpu.SemaphoreType.DMA((size,))] * 2
        + [pltpu.SemaphoreType.DMA((n,))] * 2
        + seq_sems(3),
        70,
    )


def mean_of(values):
    return jnp.mean(values, axis=-1, keepdims=True)


def sum_then_gather(scatter, gather, fills, stores, count=0, between=None, after=()):
    hops = range(1, scatter.chips - 1)
    for step in fills[0]:
        step()
    scatter.hop(0, 0)
    for p, store in enumerate(stores):
        ahead = list(fills[p + 1] if p + 1 < len(fills) else after)
        for h in hops:
            if ahead:
                ahead.pop(0)()
            scatter.hop(p, h)
            if 0 < p <= count:
                gather.hop(p - 1, h - 1)
        for step in ahead:
            step()
        if p + 1 < len(fills):
            scatter.hop(p + 1, 0)
        if between and p == 0:
            between()
        store()
        if p < count:
            gather.start(p)
        if 0 < p <= count:
            gather.hop(p - 1, gather.chips - 2)
    if count == len(stores):
        for h in range(gather.chips - 1):
            gather.hop(count - 1, h)
    for p in range(count):
        gather.finish(p)
    for p in range(len(fills)):
        scatter.finish(p)


def out_body(hidden_ref, down_w_ref, residual_ref, layer_out_ref, scatter, first):
    def fill(s):
        return scatter.fill(first + s, s, [hidden_ref], [down_w_ref], False)

    def store(s):
        layer_out_ref[s] = (residual_ref[s] + scatter.result(first + s)[...]).astype(jnp.bfloat16)

    return fill, store


def mixer_out_body(mixed_ref, out_w_ref, x_ref, gain_ref, w0, w1, w2, residual_ref, normed_ref, o0, o1, o2, low_ref, *refs):
    greet_axes(("seq", "grp"))
    seqs, rows, _ = x_ref.shape
    weights = weight_gathers(weight_axes, (w0, w1, w2), (o0, o1, o2), *refs[:2])
    for weight in weights:
        weight.start()
    gather = Gather(views(low_ref), views(normed_ref), rows, *refs[2:5])
    scatter = Scatter(rows, *refs[5:])

    def fill(s):
        return scatter.fill(s, s, [mixed_ref], [out_w_ref], False)

    def store(s):
        residual = x_ref[s].astype(jnp.float32) + scatter.result(s)[...]
        residual_ref[s] = residual
        normal = residual * lax.rsqrt(mean_of(residual * residual) + epsilon)
        low_ref[s] = (normal * gain_ref[...]).astype(jnp.bfloat16)

    sum_then_gather(
        scatter, gather, [fill(s) for s in range(seqs)], [functools.partial(store, s) for s in range(seqs)], seqs
    )
    for weight in weights:
        weight.finish()


def mixer_out(mixed, out_w, layer_in, gain, weights):
    seqs, rows, width = layer_in.shape
    full = jax.ShapeDtypeStruct((seqs, lax.axis_size("grp") * rows, width), jnp.bfloat16)
    return call(
        mixer_out_body, "mixer_out", 2,
        (mixed, out_w, layer_in, gain, *weights), [in_vmem] * 7,
        [jax.ShapeDtypeStruct(layer_in.shape, jnp.float32), full]
        + [gathered(w, axis) for w, axis in zip(weights, weight_axes)],
        [in_vmem] + [in_hbm] * 4,
        [pltpu.VMEM(layer_in.shape, jnp.bfloat16)]
        + seq_sems(3)
        + gather_sems(seqs)
        + scatter_scratch(seqs, rows, width),
        100,
    )


def mixer_forward_body(
    x_ref, grad_ref, gain_one_ref, gain_two_ref, taps_ref, taps_bias_ref, bias_a_ref, bias_x_ref, softness_own_ref,
    weight_a_ref, weight_x_ref, v0, v1, v2, w0, w1, w2,
    residual_ref, gains_ref, vectors_ref, gate_a_ref, gate_x_ref,
    normed_one_out, branch_out, feed_out, conv_out, rate_out, input_out, state_out, mixed_out, u0, u1, u2,
    normed_ref, grads_ref, o0, o1, o2,
    normed_one_ref, branch_ref, feed_ref, conv_ref, rate_ref, input_ref, state_ref, mixed_ref,
    branch_w_ref, rec_w_ref, out_w_ref, x_full_ref, low_ref, window, carry, gates, gain_slots, vector_slots, gate_slots,
    gain_pack_ref, vector_pack_ref, gate_pack_ref,
    store_sem, weight_store_sem, gain_send, gain_recv, small_send, small_recv,
    mixer_send, mixer_recv, weight_send, weight_recv, *refs,
):
    seqs, rows, width = x_ref.shape
    seq_len = x_full_ref.shape[1]
    me = lax.axis_index("grp")
    kept = (
        (normed_one_ref, normed_one_out), (branch_ref, branch_out), (feed_ref, feed_out), (conv_ref, conv_out),
        (rate_ref, rate_out), (input_ref, input_out), (state_ref, state_out), (mixed_ref, mixed_out),
    )
    keeps = [
        copies([(buffer.at[s], out.at[s]) for buffer, out in kept], store_sem.at[s]) for s in range(seqs)
    ]
    gain_pack_ref[...] = jnp.zeros_like(gain_pack_ref)
    vector_pack_ref[...] = jnp.zeros_like(vector_pack_ref)
    gain_part = gain_one_ref.shape[1]
    gain_pack_ref[0:1, :gain_part] = gain_one_ref[...].astype(jnp.float32)
    gain_pack_ref[0:1, gain_part : 2 * gain_part] = gain_two_ref[...].astype(jnp.float32)
    heads, part, head_dim = weight_a_ref.shape
    for h in range(heads):
        columns = slice(h * part, (h + 1) * part)
        vector_pack_ref[0:4, columns] = taps_ref[h].astype(jnp.float32)
        for row, ref in enumerate((taps_bias_ref, bias_a_ref, bias_x_ref, softness_own_ref)):
            vector_pack_ref[4 + row : 5 + row, columns] = ref[...].astype(jnp.float32)[h : h + 1]
        gate_pack_ref[h] = weight_a_ref[h].astype(jnp.float32)
        gate_pack_ref[heads + h] = weight_x_ref[h].astype(jnp.float32)
    weight_keeps = copies([(branch_w_ref, u0), (rec_w_ref, u1), (out_w_ref, u2)], weight_store_sem)
    greet_axes(("seq", "grp"))
    mixer_weights = weight_gathers(
        mixer_axes, (v0, v1, v2), (branch_w_ref, rec_w_ref, out_w_ref), mixer_send, mixer_recv
    )
    weights = weight_gathers(weight_axes, (w0, w1, w2), (o0, o1, o2), weight_send, weight_recv)
    gather = Gather(
        views(low_ref) + views(grad_ref) + views(x_ref),
        views(normed_ref) + views(grads_ref) + views(x_full_ref),
        rows, *refs[:3],
    )
    scatter = Scatter(rows, *refs[3:])
    place = lax.axis_index("grp")
    small = [
        Exchange("seq", lambda k, ref=pack: ref, lambda k, ref=slots: ref.at[k], small_send.at[i], small_recv.at[i])
        for i, (pack, slots) in enumerate(
            ((gain_pack_ref, gain_slots.at[place]), (vector_pack_ref, vector_slots), (gate_pack_ref, gate_slots))
        )
    ]
    along = Exchange("grp", lambda k: gain_slots.at[place], lambda k: gain_slots.at[k], gain_send, gain_recv)
    first_x = 2 * seqs
    small[0].start()
    gather.start(first_x)
    for move in small[1:]:
        move.start()
    for weight in mixer_weights[:2]:
        weight.start()
    small[0].finish()
    along.start_others()
    last_hop = gather.chips - 2
    for h in range(gather.chips - 1):
        gather.hop(first_x, h)
        if h == max(last_hop - 1, 0):
            for s in range(1, seqs):
                gather.start(first_x + s)
    gates[...] = jnp.zeros_like(gates)
    window[...] = jnp.zeros_like(window)
    along.finish_others()
    parts = lax.axis_size("seq")
    for k in range(parts):
        for g in range(along.size):
            at = (k * along.size + g) * gain_part
            for i in range(2):
                gains_ref[i, :, at : at + gain_part] = gain_slots[g, k, 0:1, i * gain_part : (i + 1) * gain_part]
    for move in small[1:]:
        move.finish()
    for k in range(parts):
        for h in range(heads):
            at = h * head_dim + k * part
            vectors_ref[:, at : at + part] = vector_slots[k, :, h * part : (h + 1) * part]
            for i in range(2):
                gates[i, at : at + part, h * head_dim : (h + 1) * head_dim] = gate_slots[k, i * heads + h]
    gate_a_ref[...] = gates[0].astype(jnp.bfloat16)
    gate_x_ref[...] = gates[1].astype(jnp.bfloat16)
    softness_ref = vectors_ref.at[pl.ds(7, 1), :]
    tile = pick_rows(seq_len // 2, (192, 128, 96, 64, 32, 16))
    chunk = window.shape[0] - 8

    def project(s, half):
        count = seq_len // tile // 2

        @pl.loop(half * count, (half + 1) * count)
        def _(i):
            at = pl.ds(pl.multiple_of(i * tile, tile), tile)
            inputs = x_full_ref[s, at, :].astype(jnp.float32)
            normal = inputs * lax.rsqrt(mean_of(inputs * inputs) + epsilon)
            normed = (normal * gains_ref[0]).astype(jnp.bfloat16)
            normed_one_ref[s, at, :] = normed
            branch_ref[s, at, :] = matmul_nt(normed, branch_w_ref[...])
            feed_ref[s, at, :] = matmul_nt(normed, rec_w_ref[...]).astype(jnp.bfloat16)

    def recur(s):
        window[pl.ds(0, 8), :] = jnp.zeros((8, window.shape[1]), jnp.float32)
        carry[...] = jnp.zeros_like(carry)

        @pl.loop(0, seq_len // chunk)
        def _(i):
            at = pl.ds(pl.multiple_of(i * chunk, chunk), chunk)
            conv, rate, gate, state, mixed = rec_forward_rows(
                feed_ref[s, at, :], branch_ref[s, at, :], vectors_ref, softness_ref, gate_a_ref, gate_x_ref, window, carry
            )
            conv_ref[s, at, :] = conv
            rate_ref[s, at, :] = rate
            input_ref[s, at, :] = gate
            state_ref[s, at, :] = state
            mixed_ref[s, at, :] = mixed

        for keep in keeps[s]:
            keep.start()

    def late_hops(first, end):
        for h in range(first, min(end, gather.chips - 1)):
            for s in range(seqs):
                gather.hop(seqs + s, h)

    def next_x(h):
        for s in range(1, seqs):
            if h <= last_hop:
                gather.hop(first_x + s, h)

    def steps(s):
        partners, own = scatter.fill(s, s, [mixed_ref], [out_w_ref], False)

        def first():
            gather.arrive(first_x + s)
            if s == 0:
                for weight in mixer_weights[:2]:
                    weight.finish()
                mixer_weights[2].start()
            project(s, 0)
            if s == 0:
                next_x(0)
            project(s, 1)
            if s == 0:
                next_x(1)
            else:
                late_hops(0, 1)

        def second():
            recur(s)
            if s == 0:
                for h in range(2, gather.chips - 1):
                    next_x(h)
                mixer_weights[2].finish()
                for weight in weights:
                    weight.start()
                for t in range(seqs):
                    gather.start(seqs + t)
                for keep in weight_keeps:
                    keep.start()
            else:
                late_hops(1, 2)

        return [first, second, partners, own]

    def store(s):
        own = x_ref[s]
        residual = own.astype(jnp.float32) + scatter.result(s)[...]
        residual_ref[s] = residual
        normal = residual * lax.rsqrt(mean_of(residual * residual) + epsilon)
        low_ref[s] = (normal * gains_ref[1]).astype(jnp.bfloat16)

    sum_then_gather(
        scatter, gather, [steps(s) for s in range(seqs)], [functools.partial(store, s) for s in range(seqs)], seqs,
        after=(lambda: None, functools.partial(late_hops, 2, gather.chips)),
    )
    for s in range(seqs):
        gather.finish(seqs + s)
        gather.sent(first_x + s)
        for keep in keeps[s]:
            keep.wait()
    for keep in weight_keeps:
        keep.wait()
    for weight in weights:
        weight.finish()


def mixer_forward(layer_in, out_grad, small, mixer_weights, weights):
    seqs, rows, width = layer_in.shape
    size, n = lax.axis_size("seq"), lax.axis_size("grp")
    seq_len, channels = n * rows, mixer_weights[0].shape[0]
    f32, bf16 = jnp.float32, jnp.bfloat16
    shape = jax.ShapeDtypeStruct
    low, full = shape((seqs, seq_len, channels), bf16), shape((seqs, seq_len, channels), f32)
    tokens = shape((seqs, seq_len, width), bf16)
    kept = [tokens, full, low, low, full, full, full, low]
    mixer_full = [gathered(w, axis) for w, axis in zip(mixer_weights, mixer_axes)]
    heads, part, head_dim = small[-1].shape
    packs = [
        (8, -(-2 * small[0].shape[1] // 128) * 128), (8, -(-heads * part // 128) * 128), (2 * heads, part, head_dim)
    ]
    outs = [
        shape(layer_in.shape, f32), shape((2, 1, width), f32), shape((8, channels), f32),
        shape((channels, channels), bf16), shape((channels, channels), bf16),
    ]
    outs += kept + mixer_full + [tokens] * 2
    outs += [gathered(w, axis) for w, axis in zip(weights, weight_axes)]
    return call(
        mixer_forward_body, "mixer_forward", 7,
        (layer_in, out_grad, *small, *mixer_weights, *weights),
        [in_vmem] * (8 + len(small)),
        outs, [in_vmem] * 5 + [in_hbm] * 16,
        [pltpu.VMEM(v.shape, v.dtype) for v in kept + mixer_full + [tokens]]
        + [
            pltpu.VMEM(layer_in.shape, bf16),
            pltpu.VMEM((pick_rows(seq_len) + 8, channels), f32),
            pltpu.VMEM((8, channels), f32),
            pltpu.VMEM((2, channels, channels), f32),
            pltpu.VMEM((n, size) + packs[0], f32),
            pltpu.VMEM((size,) + packs[1], f32),
            pltpu.VMEM((size,) + packs[2], f32),
            *(pltpu.VMEM(pack, f32) for pack in packs),
            pltpu.SemaphoreType.DMA((seqs, len(kept))),
            pltpu.SemaphoreType.DMA((3,)),
        ]
        + [pltpu.SemaphoreType.DMA((n,))] * 2
        + seq_sems(3) * 3
        + gather_sems(3 * seqs)
        + scatter_scratch(seqs, rows, width),
        180,
    )


def mlp_back_body(
    with_out, gate_in, up_in, gate_w_in, up_w_in, residual_ref, grad_ref, gain_ref, w0, w1, w2, *refs
):
    if with_out:
        hidden_in, down_w_in = refs[:2]
        refs = refs[2:]
    grad_residual_ref, gain_grad_ref, full_ref, o0, o1, o2 = refs[:6]
    refs = refs[6:]
    if with_out:
        layer_out_ref, late_ref = refs[:2]
        refs = refs[2:]
    low_ref, load_sem, gate_ref, up_ref, gate_w_ref, up_w_ref, *refs = refs
    pairs = [(gate_in, gate_ref), (up_in, up_ref), (gate_w_in, gate_w_ref), (up_w_in, up_w_ref)]
    if with_out:
        hidden_ref, down_w_ref, tiles, made_up, made_down, tile_sem, *refs = refs
        pairs += [(hidden_in, hidden_ref), (down_w_in, down_w_ref)]
    loads = copies(pairs, load_sem)
    for load in loads:
        load.start()
    greet_axes(("seq", "grp"))
    seqs, rows, _ = grad_ref.shape
    if with_out:
        sums = weight_sums(weight_axes[:1], (w0,), (o0,), *refs[:2])
        parts, me = lax.axis_size("seq"), lax.axis_index("seq")
        moves = [
            Exchange(
                "seq", lambda k, ref=made: ref.at[lax.rem(k - me + parts, parts)], None,
                refs[0].at[i], refs[1].at[i], out, 0,
            )
            for i, made, out in ((1, made_up, o1), (2, made_down, o2))
        ]
        order = [(kind, k) for kind in range(2) for k in range(1, parts)] + [(0, 0), (1, 0)]
    else:
        sums = weight_sums(weight_axes, (w0, w1, w2), (o0, o1, o2), *refs[:2])
    for weight in sums:
        weight.start_others()
    gather = Gather(views(low_ref), views(full_ref), rows, *refs[2:5])
    scatter = Scatter(rows, *refs[5:])
    gain_grad_ref[...] = jnp.zeros_like(gain_grad_ref)

    def fill(s):
        return scatter.fill(s, s, [gate_ref, up_ref], [gate_w_ref, up_w_ref], True)

    def store(s):
        term = scatter.result(s)[...]
        residual = residual_ref[s]
        inverse = lax.rsqrt(mean_of(residual * residual) + epsilon)
        normal = residual * inverse
        gain_grad_ref[0:1, :] += jnp.sum(term * normal, axis=0, keepdims=True)
        grad = grad_ref[s].astype(jnp.float32) + norm_back(term, normal, inverse, gain_ref[...])
        grad_residual_ref[s] = grad
        low_ref[s] = grad.astype(jnp.bfloat16)

    def tile_load(i, j):
        kind, k = order[i]
        step = tiles.shape[-1]
        first = lax.rem(me + k, parts) * 2 * step + j * step
        source = (w1, w2)[kind].at[:, :, pl.ds(pl.multiple_of(first, step), step)]
        return pltpu.make_async_copy(source, tiles.at[j], tile_sem.at[j])

    def make(i):
        kind, k = order[i]
        step = tiles.shape[-1]

        @pl.loop(0, 2)
        def _(j):
            tile_load(i, j).wait()
            at = pl.ds(pl.multiple_of(j * step, step), step)
            total = None
            for s in range(seqs):
                if kind == 0:
                    term = matmul_tn(tiles[j, s], up_ref[s])
                else:
                    term = matmul_tn(hidden_ref[s], tiles[j, s])
                total = term if total is None else total + term
            if kind == 0:
                made_up[k, at, :] = total.astype(jnp.bfloat16)
            else:
                made_down[k, :, at] = total.astype(jnp.bfloat16)
            if i + 1 < len(order):
                tile_load(i + 1, j).start()

        if k:
            moves[kind].copy(k, me).start()
        else:
            moves[kind].own().start()

    def make_all(first, end):
        for i in range(first, end):
            make(i)

    def wait_first():
        for load in loads[:4]:
            load.wait()

    def wait_later():
        for load in loads[4:]:
            load.wait()

    fills = [fill(s) for s in range(seqs)]
    fills[0] = (wait_first, *fills[0])
    stores = [functools.partial(store, s) for s in range(seqs)]
    if with_out:
        fill_out, store_out = out_body(hidden_ref, down_w_ref, residual_ref, layer_out_ref, scatter, seqs)
        fills += [fill_out(s) for s in range(seqs - 1)]
        fills[seqs - 1] = (*fills[seqs - 1], wait_later)
        third = parts - 1

        def partners_then(step):
            step()
            make_all(2, third)

        def own_then(step):
            step()
            make_all(third, third + 1)

        if len(fills) > seqs:
            fills[seqs] = (
                functools.partial(partners_then, fills[seqs][0]),
                functools.partial(own_then, fills[seqs][1]),
                functools.partial(make_all, third + 1, 2 * third),
            )
        for j in range(2):
            tile_load(0, j).start()
        stores += [functools.partial(store_out, s) for s in range(seqs - 1)]

    def late():
        step = 256

        @pl.loop(0, late_ref.shape[0] // step)
        def _(i):
            at = pl.ds(pl.multiple_of(i * step, step), step)
            late_ref[at, :] = matmul(hidden_ref[seqs - 1, at, :], down_w_ref[...]).astype(jnp.bfloat16)

    def rest():
        make_all(2 * third if len(fills) > seqs else 2, len(order))

    sum_then_gather(
        scatter, gather, fills, stores, seqs,
        between=functools.partial(make_all, 0, 2) if with_out else None, after=(late, rest) if with_out else (),
    )
    for weight in sums:
        weight.finish_others()
    if with_out:
        for move in moves:
            move.finish()


def mlp_back(grad_gate, grad_up, gate_w, up_w, residual, out_grad, gain, grads, out_inputs):
    seqs, rows, width = residual.shape
    outs = [
        jax.ShapeDtypeStruct(residual.shape, jnp.float32),
        jax.ShapeDtypeStruct((8, width), jnp.float32),
        jax.ShapeDtypeStruct((seqs, lax.axis_size("grp") * rows, width), jnp.bfloat16),
    ]
    if out_inputs:
        size = lax.axis_size("seq")
        hidden_width, part = grad_gate.shape[-1], width // size
        outs.append(slots_of(grads[0], 0))
        outs.append(jax.ShapeDtypeStruct((size, part, hidden_width), jnp.bfloat16))
        outs.append(jax.ShapeDtypeStruct((size, hidden_width, part), jnp.bfloat16))
        makers = [
            pltpu.VMEM((2, *grad_gate.shape[:2], part // 2), jnp.bfloat16),
            *(pltpu.VMEM(out.shape, out.dtype) for out in outs[-2:]),
            pltpu.SemaphoreType.DMA((2,)),
        ]
    else:
        outs += [slots_of(grad, axis) for grad, axis in zip(grads, weight_axes)]
        makers = []
    out_specs = [in_vmem] * 2 + [in_hbm] * 4
    if out_inputs:
        outs.append(jax.ShapeDtypeStruct((seqs - 1, rows, width), jnp.bfloat16))
        outs.append(jax.ShapeDtypeStruct((lax.axis_size("grp") * rows, width), jnp.bfloat16))
        out_specs += [in_vmem] * 2
    return call(
        functools.partial(mlp_back_body, bool(out_inputs)), "mlp_back", 3,
        (grad_gate, grad_up, gate_w, up_w, residual, out_grad, gain, *grads, *out_inputs),
        [in_hbm] * 4 + [in_vmem] * 3 + [in_hbm] * (3 + len(out_inputs)),
        outs, out_specs,
        [pltpu.VMEM(residual.shape, jnp.bfloat16), pltpu.SemaphoreType.DMA((6,))]
        + [pltpu.VMEM(v.shape, v.dtype) for v in (grad_gate, grad_up, gate_w, up_w, *out_inputs)]
        + makers
        + seq_sems(3)
        + gather_sems(seqs)
        + scatter_scratch(seqs * 2 - 1 if out_inputs else seqs, rows, width),
        120,
    )


def last_body(
    branch_ref, feed_ref, branch_w_ref, rec_w_ref, x_ref, grad_ref, gain_ref, gain_two_ref, rec_ref,
    w0, w1, w2, *refs,
):
    grad_x_ref, rec_sum_ref, gain_sum_ref, o0, o1, o2 = refs[:6]
    refs = refs[6:]
    rec_slots, gain_local, gain_part, gain_slots, part_slots = refs[:5]
    rec_sems, gain_sems, part_sems = refs[5:7], refs[7:9], refs[9:11]
    greet_axes(("seq", "grp"))
    seqs, rows, _ = x_ref.shape
    sums = weight_sums(mixer_axes, (w0, w1, w2), (o0, o1, o2), *refs[11:13])
    scatter = Scatter(rows, *refs[13:])
    rec = Exchange("seq", lambda k: rec_ref.at[k], lambda k: rec_slots.at[k], *rec_sems)
    rec.start()
    for weight in sums:
        weight.start_others()
    gain_local[...] = jnp.zeros_like(gain_local)
    gain_local[1:2, :] = gain_two_ref[0:1, :]

    def fill(s):
        return scatter.fill(s, s, [branch_ref, feed_ref], [branch_w_ref, rec_w_ref], False)

    across = Exchange(
        "seq", block(gain_local, 1, lax.axis_size("seq")), lambda k: gain_slots.at[k], *gain_sems
    )

    def store(s):
        term = scatter.result(s)[...]
        inputs = x_ref[s].astype(jnp.float32)
        inverse = lax.rsqrt(mean_of(inputs * inputs) + epsilon)
        normal = inputs * inverse
        gain_local[0:1, :] += jnp.sum(term * normal, axis=0, keepdims=True)
        if s == seqs - 1:
            across.start()
        grad_x_ref[s] = grad_ref[s] + norm_back(term, normal, inverse, gain_ref[...])

    sum_then_gather(
        scatter, None, [fill(s) for s in range(seqs)], [functools.partial(store, s) for s in range(seqs)]
    )
    across.finish()
    gain_part[...] = sum_of(gain_slots)
    along = Exchange("grp", lambda k: gain_part, lambda k: part_slots.at[k], *part_sems)
    along.start()
    rec.finish()
    rec_sum_ref[...] = sum_of(rec_slots)
    for weight in sums:
        weight.finish_others()
    along.finish()
    gain_sum_ref[...] = sum_of(part_slots)


def last(grad_branch, grad_feed, branch_w, rec_w, layer_in, grad_residual, gain, gain_two_grad, rec_blocks, grads):
    seqs, rows, width = layer_in.shape
    size, n = lax.axis_size("seq"), lax.axis_size("grp")
    f32 = jnp.float32
    inputs = (grad_branch, grad_feed, branch_w, rec_w, layer_in, grad_residual, gain, gain_two_grad, rec_blocks)
    outs = [
        jax.ShapeDtypeStruct(layer_in.shape, f32),
        jax.ShapeDtypeStruct(rec_blocks.shape[1:], f32),
        jax.ShapeDtypeStruct((8, width // size), f32),
    ]
    outs += [slots_of(grad, axis) for grad, axis in zip(grads, mixer_axes)]
    out_specs = [in_vmem] * 3 + [in_hbm] * 3
    return call(
        last_body, "last", 4,
        inputs + tuple(grads), [in_vmem] * len(inputs) + [in_hbm] * 3,
        outs, out_specs,
        [
            pltpu.VMEM(rec_blocks.shape, f32),
            pltpu.VMEM((8, width), f32),
            pltpu.VMEM((8, width // size), f32),
            pltpu.VMEM((size, 8, width // size), f32),
            pltpu.VMEM((n, 8, width // size), f32),
        ]
        + [pltpu.SemaphoreType.DMA((size,))] * 4
        + [pltpu.SemaphoreType.DMA((n,))] * 2
        + seq_sems(3)
        + scatter_scratch(seqs, rows, width),
        80,
    )


def head_windows(heads, head_dim, parts):
    part = head_dim // parts
    rows = max(-(-(k + 1) * part // 8) * 8 - k * part // 8 * 8 for k in range(parts))

    def start(h, k):
        return pl.multiple_of(h * head_dim + k * part // 8 * 8, 8)

    return rows, start


def mixer_back_body(
    heads, low_in, out_w_in, branch_in, feed_in, conv_in, rate_in, input_in, state_in, mixed_in, branch_w_in, rec_w_in,
    normed_in, vectors_ref, gate_a_ref, gate_x_ref, x_ref, grad_ref, gain_ref, gain_two_ref,
    grad_x_ref, squares_out_ref, sums_out_ref, gain_sum_ref, o0, o1, o2,
    low_ref, out_w_ref, branch_ref, feed_ref, conv_ref, rate_ref, input_ref, state_ref, mixed_ref, branch_w_ref,
    rec_w_ref, grad_mixed, grad_branch, grad_feed, squares, sums, window, later, carry, tiles, d0, d1, d2,
    square_slots, sum_slots_ref, gain_local, gain_part, gain_slots, part_slots, load_sem, tile_sem,
    square_send, square_recv, sum_send, sum_recv, gain_send, gain_recv, part_send, part_recv, weight_send, weight_recv,
    *refs,
):
    seqs, rows, width = x_ref.shape
    seq_len, channels = feed_ref.shape[1:]
    softness_ref = vectors_ref.at[pl.ds(7, 1), :]
    per_seq = (
        (low_in, low_ref), (branch_in, branch_ref), (feed_in, feed_ref), (conv_in, conv_ref), (rate_in, rate_ref),
        (input_in, input_ref), (state_in, state_ref),
    )
    pairs = [(out_w_in, out_w_ref)]
    for s in range(seqs):
        pairs += [(source.at[s], buffer.at[s]) for source, buffer in per_seq]
        if s == 0:
            pairs += [(branch_w_in, branch_w_ref), (rec_w_in, rec_w_ref)]
    pairs += [(mixed_in, mixed_ref)]
    loads = copies(pairs, load_sem)
    for load in loads:
        load.start()
    greet_axes(("seq", "grp"))
    scatter = Scatter(rows, *refs)
    parts = lax.axis_size("seq")
    for ref in (squares, sums, gain_local):
        ref[...] = jnp.zeros_like(ref)
    gain_local[1:2, :] = gain_two_ref[0:1, :]
    window_rows, start_of = head_windows(heads, channels // heads, parts)
    square_moves = [
        Exchange(
            "seq",
            lambda k, h=h: squares.at[:, pl.ds(start_of(h, k), window_rows), :],
            lambda k, h=h: square_slots.at[k, h],
            square_send.at[h],
            square_recv.at[h],
        )
        for h in range(heads)
    ]
    sum_move = Exchange("seq", lambda k: sums, lambda k: sum_slots_ref.at[k], sum_send, sum_recv)
    across = Exchange("seq", block(gain_local, 1, parts), lambda k: gain_slots.at[k], gain_send, gain_recv)
    moves = weight_sums(mixer_axes, (d0, d1, d2), (o0, o1, o2), weight_send, weight_recv, 0)
    tile_rows = pick_rows(seq_len, (256, 192, 128, 96, 64, 32, 16))
    chunk = window.shape[0] - 8

    def mix(s):
        if s == 0:
            for load in loads[: 1 + len(per_seq)]:
                load.wait()
        else:
            first = 3 + s * len(per_seq)
            for load in loads[first : first + len(per_seq)]:
                load.wait()

        @pl.loop(0, seq_len // tile_rows)
        def _(i):
            at = pl.ds(pl.multiple_of(i * tile_rows, tile_rows), tile_rows)
            grad_mixed[at, :] = matmul_nt(low_ref[s, at, :], out_w_ref[...])

    def recur(s):
        carry[...] = jnp.zeros_like(carry)
        later[...] = jnp.zeros_like(later)
        blocks = seq_len // chunk

        @pl.loop(0, blocks)
        def _(i):
            first = (blocks - 1 - i) * chunk
            at = pl.ds(pl.multiple_of(first, chunk), chunk)
            keep = jnp.where(i == blocks - 1, 0.0, 1.0)
            before8 = pl.ds(pl.multiple_of(jnp.maximum(first - 8, 0), 8), 8)
            before16 = pl.ds(pl.multiple_of(jnp.maximum(first - 16, 0), 16), 16)
            grad_branch[s, at, :], grad_feed[s, at, :] = rec_backward_rows(
                grad_mixed[at, :], branch_ref[s, at, :], feed_ref[s, at, :],
                feed_ref[s, before16, :].astype(jnp.float32)[8:] * keep, conv_ref[s, at, :], rate_ref[s, at, :],
                input_ref[s, at, :], state_ref[s, at, :], state_ref[s, before8, :] * keep,
                vectors_ref, softness_ref, gate_a_ref, gate_x_ref, squares.at[0], squares.at[1], sums,
                window, later, carry,
            )

        if s == seqs - 1:
            for move in square_moves:
                move.start()
            sum_move.start()

    def steps(s):
        partners, own = scatter.fill(s, s, [grad_branch, grad_feed], [branch_w_ref, rec_w_ref], False)

        def third():
            if s == 0:
                for load in loads[1 + len(per_seq) : 3 + len(per_seq)]:
                    load.wait()
            partners()

        def first():
            mix(s)
            if s == seqs - 1:
                out_grads()

        return [first, functools.partial(recur, s), third, own]

    def out_grads():
        loads[-1].wait()
        step = width // parts

        @pl.loop(0, parts)
        def _(k):
            at = pl.ds(pl.multiple_of(k * step, step), step)
            total = matmul_tn(mixed_ref[0], low_ref[0, :, at])
            for s in range(1, seqs):
                total = total + matmul_tn(mixed_ref[s], low_ref[s, :, at])
            d2[:, at] = total.astype(jnp.bfloat16)

        moves[2].start()

    step = tiles.shape[-1]
    count = width // parts // step

    def columns_of(i):
        peer = lax.rem(lax.axis_index("seq") + 1 + i // count, parts)
        return pl.ds(pl.multiple_of((peer * count + lax.rem(i, count)) * step, step), step)

    def tile_load(i, slot):
        return pltpu.make_async_copy(normed_in.at[:, :, columns_of(i)], tiles.at[slot], tile_sem.at[slot])

    def in_grads(part):
        if part == 0:
            tile_load(0, 0).start()

        @pl.loop(part * count, (part + 1) * count)
        def _(i):
            slot = lax.rem(i, 2)
            tile_load(i, slot).wait()

            @pl.when(i + 1 < parts * count)
            def _():
                tile_load(i + 1, 1 - slot).start()

            for to, grads in ((d0, grad_branch), (d1, grad_feed)):
                total = matmul_tn(grads[0], tiles[slot, 0])
                for s in range(1, seqs):
                    total = total + matmul_tn(grads[s], tiles[slot, s])
                to[:, columns_of(i)] = total.astype(jnp.bfloat16)

        for move in moves[:2]:
            if part < parts - 1:
                move.copy(part + 1, move.me).start()
            else:
                move.own().start()

    def grads_from(first, end):
        for part in range(first, end):
            in_grads(part)

    def store(s):
        term = scatter.result(s)[...]
        inputs = x_ref[s].astype(jnp.float32)
        inverse = lax.rsqrt(mean_of(inputs * inputs) + epsilon)
        normal = inputs * inverse
        gain_local[0:1, :] += jnp.sum(term * normal, axis=0, keepdims=True)
        if s == seqs - 1:
            across.start()
        grad_x_ref[s] = grad_ref[s] + norm_back(term, normal, inverse, gain_ref[...])

    sum_then_gather(
        scatter, None, [steps(s) for s in range(seqs)], [functools.partial(store, s) for s in range(seqs)],
        between=functools.partial(grads_from, 0, parts // 2),
        after=(functools.partial(grads_from, parts // 2, parts - 1), functools.partial(grads_from, parts - 1, parts)),
    )
    across.finish()
    gain_part[...] = sum_of(gain_slots)
    along = Exchange("grp", lambda k: gain_part, lambda k: part_slots.at[k], part_send, part_recv)
    along.start()
    for move in square_moves:
        move.finish()
    squares_out_ref[...] = sum_of(square_slots)
    sum_move.finish()
    sums_out_ref[...] = sum_of(sum_slots_ref)
    for move in moves:
        move.finish()
    along.finish()
    gain_sum_ref[...] = sum_of(part_slots)


def mixer_back(
    heads, low, out_w, branch, feed, conv, rate, gate, state, mixed, branch_w, rec_w, normed,
    vectors, gate_a, gate_x, layer_in, grad_residual, gain, gain_two_grad,
):
    seqs, rows, width = layer_in.shape
    seq_len, channels = feed.shape[1:]
    size, n = lax.axis_size("seq"), lax.axis_size("grp")
    f32, bf16 = jnp.float32, jnp.bfloat16
    large = (low, out_w, branch, feed, conv, rate, gate, state, mixed, branch_w, rec_w)
    small = (vectors, gate_a, gate_x, layer_in, grad_residual, gain, gain_two_grad)
    window_rows = head_windows(heads, channels // heads, size)[0]
    grads = [jax.ShapeDtypeStruct(w.shape, bf16) for w in (branch_w, rec_w, out_w)]
    squares = (heads, 2, window_rows, channels)
    part = width // size
    return call(
        functools.partial(mixer_back_body, heads), "mixer_back", 6,
        large + (normed,) + small,
        [in_hbm] * 12 + [in_vmem] * 7,
        [
            jax.ShapeDtypeStruct(layer_in.shape, f32),
            jax.ShapeDtypeStruct(squares, f32),
            jax.ShapeDtypeStruct((8, channels), f32),
            jax.ShapeDtypeStruct((8, part), f32),
        ]
        + [slots_of(grad, axis, 0) for grad, axis in zip(grads, mixer_axes)],
        [in_vmem] * 4 + [in_hbm] * 3,
        [pltpu.VMEM(v.shape, v.dtype) for v in large]
        + [
            pltpu.VMEM((seq_len, channels), f32),
            pltpu.VMEM(feed.shape, bf16),
            pltpu.VMEM(feed.shape, bf16),
            pltpu.VMEM((2, channels, channels), f32),
            pltpu.VMEM((8, channels), f32),
            pltpu.VMEM((pick_rows(seq_len) + 8, channels), f32),
            pltpu.VMEM((pick_rows(seq_len) + 8, channels), f32),
            pltpu.VMEM((8, channels), f32),
            pltpu.VMEM((2, seqs, seq_len, 256), bf16),
        ]
        + [pltpu.VMEM(grad.shape, bf16) for grad in grads]
        + [
            pltpu.VMEM((size,) + squares, f32),
            pltpu.VMEM((size, 8, channels), f32),
            pltpu.VMEM((8, width), f32),
            pltpu.VMEM((8, part), f32),
            pltpu.VMEM((size, 8, part), f32),
            pltpu.VMEM((n, 8, part), f32),
            pltpu.SemaphoreType.DMA((4 + 7 * seqs,)),
            pltpu.SemaphoreType.DMA((2,)),
        ]
        + [pltpu.SemaphoreType.DMA((heads, size))] * 2
        + [pltpu.SemaphoreType.DMA((size,))] * 4
        + [pltpu.SemaphoreType.DMA((n,))] * 2
        + seq_sems(3)
        + scatter_scratch(seqs, rows, width),
        100,
    )


def out_only_body(hidden_ref, down_w_ref, residual_ref, layer_out_ref, *scratch):
    greet_line()
    scatter = Scatter(residual_ref.shape[1], *scratch)
    fill, store = out_body(hidden_ref, down_w_ref, residual_ref, layer_out_ref, scatter, 0)
    seqs = range(residual_ref.shape[0])
    sum_then_gather(
        scatter, None, [fill(s) for s in seqs], [functools.partial(store, s) for s in seqs]
    )


def out_only(hidden, down_w, residual):
    seqs, rows, width = residual.shape
    return call(
        out_only_body, "layer_out", 5,
        (hidden, down_w, residual), [in_vmem] * 3,
        [jax.ShapeDtypeStruct(residual.shape, jnp.bfloat16)], [in_vmem],
        scatter_scratch(seqs, rows, width), 60,
    )[0]


def per_device(
    layer_in, gain_one, w_branch, w_rec, conv_w, conv_b, gate_a_w, gate_a_b, gate_x_w, gate_x_b,
    decay_logit, w_out, gain_two, mlp_gate, mlp_up, mlp_down, out_grad,
):
    seqs_here, positions, model_width = layer_in.shape
    heads_here, tap_count, part_dim = conv_w.shape
    seq_devices, grp_devices = lax.axis_size("seq"), lax.axis_size("grp")
    head_dim = part_dim * seq_devices
    channels = heads_here * head_dim
    f32 = jnp.float32

    short_line = seqs_here * positions * grp_devices <= 2048 and model_width // seq_devices == 512
    mixer_weights = (w_branch.T, w_rec.T, w_out)
    mlp_weights = (mlp_gate, mlp_up, mlp_down)
    at = tap_count + 4
    if short_line:
        softness = jax.nn.softplus(-decay_logit.astype(f32))
        small = (
            gain_one[None], gain_two[None], conv_w, conv_b, gate_a_b, gate_x_b, softness, gate_a_w, gate_x_w
        )
        (
            residual, gains, vectors, diag_a, diag_x,
            normed_one, branch_pre, feed, conv, rate, gate, state, mixed, branch_w, rec_w, out_w,
            normed_two, grad_output, gate_w, up_w, down_w,
        ) = mixer_forward(layer_in, out_grad, small, mixer_weights, mlp_weights)
        normed_one = normed_one.reshape(-1, model_width)
        grad_output = grad_output.reshape(-1, model_width)
    else:
        own_params = jnp.concatenate(
            [jnp.transpose(conv_w, (0, 2, 1))]
            + [v[:, :, None] for v in (conv_b, gate_a_b, gate_x_b, decay_logit)]
            + [gate_a_w, gate_x_w],
            axis=2,
        ).astype(f32)
        own_gains = jnp.concatenate([gain_one, gain_two]).astype(f32)
        pack = jnp.concatenate(
            [padded_rows(own_params.reshape(1, -1))[0], padded_rows(own_gains.reshape(1, -1))[0]]
        )
        late_grad, x_full, params, gains, branch_w, rec_w, out_w = gather_first(
            layer_in, out_grad, pack, mixer_weights
        )

        gains = gains.reshape(grp_devices, seq_devices, -1)[:, :, : own_gains.size]
        gains = jnp.transpose(gains.reshape(grp_devices, seq_devices, 2, -1), (2, 1, 0, 3)).reshape(2, 1, -1)
        params = params.reshape(seq_devices, -1)[:, : own_params.size]
        params = params.reshape((seq_devices,) + own_params.shape)
        params = jnp.transpose(params, (1, 0, 2, 3)).reshape(heads_here, head_dim, -1)
        vectors = params[:, :, : tap_count + 4].reshape(channels, -1).T
        diag_a = head_diagonal(params[:, :, at : at + head_dim].astype(jnp.bfloat16))
        diag_x = head_diagonal(params[:, :, at + head_dim :].astype(jnp.bfloat16))
        logit = vectors[tap_count + 3 :]
        softness = jax.nn.softplus(-logit)
        grad_output = jnp.concatenate(
            [lax.all_gather(late_grad[s], "grp", axis=0, tiled=True) for s in range(seqs_here)]
        )
        inputs = x_full.astype(f32)
        normal_one = inputs * lax.rsqrt(mean_of(inputs * inputs) + epsilon)
        normed_one = (normal_one * gains[0]).astype(jnp.bfloat16).reshape(-1, model_width)
        branch_pre = matmul_nt(normed_one, branch_w).reshape(seqs_here, -1, channels)
        feed = matmul_nt(normed_one, rec_w).astype(jnp.bfloat16).reshape(seqs_here, -1, channels)
        conv, rate, gate, state, mixed = rec_forward(feed, branch_pre, vectors, softness, diag_a, diag_x)
        residual, normed_two, gate_w, up_w, down_w = mixer_out(
            mixed, out_w, layer_in, gains[1], mlp_weights
        )
    mixed = mixed.reshape(-1, channels)
    normed_two = normed_two.reshape(-1, model_width)
    up_proj = matmul(normed_two, up_w)
    gate_act, gate_pull = jax.vjp(jax.nn.gelu, matmul(normed_two, gate_w))
    hidden = (gate_act * up_proj).astype(jnp.bfloat16)
    grad_hidden = matmul_nt(grad_output, down_w)
    grad_gate = gate_pull(grad_hidden * up_proj)[0].astype(jnp.bfloat16)
    grad_up = (grad_hidden * gate_act).astype(jnp.bfloat16)
    def by_seq(values):
        return values.reshape(seqs_here, -1, values.shape[-1])

    if short_line:
        first_grad = matmul_tn(normed_two, grad_gate).astype(jnp.bfloat16)
        mlp_grads = (first_grad, by_seq(normed_two), by_seq(grad_output))
    else:
        mlp_grads = low_all(
            (matmul_tn(normed_two, grad_gate), matmul_tn(normed_two, grad_up), matmul_tn(hidden, grad_output))
        )

    back_inputs = (
        by_seq(grad_gate), by_seq(grad_up), gate_w, up_w, residual, out_grad, gains[1], mlp_grads
    )
    if not short_line:
        layer_out = out_only(by_seq(hidden), down_w, residual)
        grad_residual, gain_two_grad, residual_low, *mlp_slots = mlp_back(*back_inputs, ())
    else:
        grad_residual, gain_two_grad, residual_low, *mlp_slots, layer_out, late = mlp_back(
            *back_inputs, (by_seq(hidden), down_w)
        )
        late = lax.psum_scatter(late, "grp", scatter_dimension=0, tiled=True)
        late = (residual[seqs_here - 1] + late.astype(f32)).astype(jnp.bfloat16)
        layer_out = jnp.concatenate([layer_out, late[None]])
    if short_line:
        mlp_grads = sum_slots(mlp_grads[:1], mlp_slots[:1], weight_axes) + [sum_all(slot) for slot in mlp_slots[1:]]
    else:
        mlp_grads = sum_slots(mlp_grads, mlp_slots, weight_axes)
    if short_line:
        grad_x, squares, sums, gain_sum, *mixer_slots = mixer_back(
            heads_here, residual_low, out_w, branch_pre, feed, conv, rate, gate, state, by_seq(mixed), branch_w, rec_w,
            by_seq(normed_one), vectors, diag_a, diag_x, layer_in, grad_residual, gains[0], gain_two_grad,
        )
        mixer_grads = [sum_all(slot) for slot in mixer_slots]
        place = lax.axis_index("seq")
        first = place * part_dim % 8
        square_parts = [
            lax.dynamic_slice_in_dim(squares[h], first, part_dim, 1)[:, :, h * head_dim : (h + 1) * head_dim]
            for h in range(heads_here)
        ]
        grad_a, grad_x_gate = (jnp.stack([part[i] for part in square_parts]) for i in range(2))
        own_sums = lax.dynamic_slice_in_dim(
            sums.reshape(at, heads_here, head_dim), place * part_dim, part_dim, 2
        )
        logit_grad = 8.0 * jax.nn.sigmoid(-decay_logit.astype(f32)) * own_sums[tap_count + 3]
        rec_outs = (
            jnp.transpose(own_sums[:tap_count], (1, 0, 2)), own_sums[tap_count], grad_a, own_sums[tap_count + 1],
            grad_x_gate, own_sums[tap_count + 2], logit_grad,
        )
        return finish(layer_out, grad_x, gain_sum, mixer_grads, rec_outs, mlp_grads)
    residual_low = residual_low.reshape(-1, model_width)
    out_weight_grad = matmul_tn(mixed, residual_low)
    grad_mixed = by_seq(matmul_nt(residual_low, out_w))
    grad_branch, grad_feed, square_a, square_x, sums = rec_backward(
        grad_mixed, branch_pre, feed, conv, rate, gate, state, vectors, softness, diag_a, diag_x
    )
    vector_grads = jnp.concatenate(
        [sums[: tap_count + 3], 8.0 * jax.nn.sigmoid(-logit) * sums[tap_count + 3 :]]
    )
    rec_grads = jnp.concatenate(
        [
            vector_grads.T.reshape(heads_here, head_dim, -1),
            diagonal_heads(square_a, heads_here),
            diagonal_heads(square_x, heads_here),
        ],
        axis=2,
    )
    rec_grads = rec_grads.reshape(heads_here, seq_devices, part_dim, -1)
    rec_blocks = padded_rows(jnp.transpose(rec_grads, (1, 0, 2, 3)))
    mixer_grads = low_all(
        (
            matmul_tn(grad_branch.reshape(-1, channels), normed_one),
            matmul_tn(grad_feed.reshape(-1, channels), normed_one),
            out_weight_grad,
        )
    )
    grad_x, rec_sum, gain_sum, *mixer_slots = last(
        grad_branch, grad_feed, branch_w, rec_w, layer_in, grad_residual, gains[0], gain_two_grad, rec_blocks,
        mixer_grads,
    )
    mixer_grads = sum_slots(mixer_grads, mixer_slots, mixer_axes)
    rec_sum = rec_sum.reshape(-1)[: own_params.size].reshape(own_params.shape)
    rec_outs = (
        jnp.transpose(rec_sum[:, :, :tap_count], (0, 2, 1)),
        rec_sum[:, :, tap_count],
        rec_sum[:, :, at : at + head_dim],
        rec_sum[:, :, tap_count + 1],
        rec_sum[:, :, at + head_dim :],
        rec_sum[:, :, tap_count + 2],
        rec_sum[:, :, tap_count + 3],
    )
    return finish(layer_out, grad_x, gain_sum, mixer_grads, rec_outs, mlp_grads)


def finish(layer_out, grad_x, gain_sum, mixer_grads, rec_outs, mlp_grads):
    part = gain_sum.shape[1] // lax.axis_size("grp")
    gain_grads = lax.dynamic_slice_in_dim(gain_sum, lax.axis_index("grp") * part, part, 1)
    return (
        layer_out, grad_x, gain_grads[0], mixer_grads[0].T, mixer_grads[1].T, *rec_outs, mixer_grads[2], gain_grads[1],
        *mlp_grads,
    )


def solution(mesh):
    placed = (
        P("seq", "grp", None),
        P(("seq", "grp")),
        P("seq", "grp"),
        P("seq", "grp"),
        P("grp", None, "seq"),
        P("grp", "seq"),
        P("grp", "seq", None),
        P("grp", "seq"),
        P("grp", "seq", None),
        P("grp", "seq"),
        P("grp", "seq"),
        P("grp", "seq"),
        P(("seq", "grp")),
        P("seq", "grp"),
        P("seq", "grp"),
        P("grp", "seq"),
        P("seq", "grp", None),
    )
    return jax.shard_map(
        per_device,
        mesh=mesh,
        in_specs=placed,
        out_specs=(
            P("seq", "grp", None),
            P("seq", "grp", None),
            P(("seq", "grp")),
            P("seq", "grp"),
            P("seq", "grp"),
            P("grp", None, "seq"),
            P("grp", "seq"),
            P("grp", "seq", None),
            P("grp", "seq"),
            P("grp", "seq", None),
            P("grp", "seq"),
            P("grp", "seq"),
            P("grp", "seq"),
            P(("seq", "grp")),
            P("seq", "grp"),
            P("seq", "grp"),
            P("grp", "seq"),
        ),
        check_vma=False,
    )
```

```python
import functools
import math

import jax
import jax.numpy as jnp
from jax import lax
from jax.experimental import pallas as pl
from jax.experimental.pallas import tpu as pltpu
from jax.sharding import PartitionSpec as P

epsilon = 1e-06
gelu_slope = math.sqrt(2.0 / math.pi)
gelu_cubic = 0.044715
MESH = pl.DeviceIdType.MESH


def matmul(left, right):
    return jnp.dot(left, right, preferred_element_type=jnp.float32)


def matmul_tn(left, right):
    return lax.dot_general(
        left, right, (((0,), (0,)), ((), ())), preferred_element_type=jnp.float32
    )


def matmul_nt(left, right):
    return lax.dot_general(
        left, right, (((1,), (1,)), ((), ())), preferred_element_type=jnp.float32
    )


def norm_back(grad_normed, normal_part, inverse, gain):
    scaled = grad_normed * gain
    return inverse * (scaled - normal_part * jnp.mean(scaled * normal_part, axis=-1, keepdims=True))


def low_all(grads):
    return tuple(grad.astype(jnp.bfloat16) for grad in grads)


def sum_slots(grads, slots, axes):
    sums = []
    for grad, slot, axis in zip(grads, slots, axes):
        size = slot.shape[1 + axis]
        own = lax.dynamic_slice_in_dim(grad, lax.axis_index("seq") * size, size, axis)
        for k in range(slot.shape[0]):
            own = own.astype(jnp.float32) + slot[k].astype(jnp.float32)
        sums.append(own)
    return sums


def sum_all(slots):
    total = slots[0].astype(jnp.float32)
    for k in range(1, slots.shape[0]):
        total = total + slots[k].astype(jnp.float32)
    return total


def padded_rows(values):
    flat = values.reshape(values.shape[0], -1)
    flat = jnp.pad(flat, ((0, 0), (0, -flat.shape[1] % 1024)))
    return flat.reshape(values.shape[0], -1, 128)


def head_diagonal(blocks):
    heads, head_dim, _ = blocks.shape
    rows = []
    for h in range(heads):
        row = [jnp.zeros((head_dim, head_dim), blocks.dtype)] * heads
        row[h] = blocks[h]
        rows.append(jnp.concatenate(row, axis=1))
    return jnp.concatenate(rows, axis=0)


def diagonal_heads(square, heads):
    head_dim = square.shape[0] // heads
    return jnp.stack(
        [
            square[h * head_dim : (h + 1) * head_dim, h * head_dim : (h + 1) * head_dim]
            for h in range(heads)
        ]
    )


def pick_rows(seq_len, choices=(192, 128, 96, 64, 32, 16)):
    for rows in choices:
        if seq_len % rows == 0:
            return rows
    return seq_len


def gelu_parts(x):
    cubic = gelu_slope * (x + gelu_cubic * x * x * x)
    bend = jnp.tanh(cubic)
    gate = 0.5 * (1.0 + bend)
    slope = gate + 0.5 * x * (1.0 - bend * bend) * gelu_slope * (1.0 + 3.0 * gelu_cubic * x * x)
    return x * gate, slope


def minus_expm1(x):
    series = 1.0 + x * (1.0 / 9.0)
    for k in (8, 7, 6, 5, 4, 3, 2):
        series = 1.0 + x * (1.0 / k) * series
    return jnp.where(x > -0.4, -x * series, 1.0 - jnp.exp(x))


def shift_down(values, by, fill):
    rows = values.shape[0]
    if by % 8 == 0:
        return jnp.concatenate([jnp.full((by, values.shape[1]), fill), values[: rows - by]], axis=0)
    index = lax.broadcasted_iota(jnp.int32, values.shape, 0)
    return jnp.where(index >= by, pltpu.roll(values, by, 0), fill)


def shift_up(values, by, fill):
    rows = values.shape[0]
    if by % 8 == 0:
        return jnp.concatenate([values[by:], jnp.full((by, values.shape[1]), fill)], axis=0)
    index = lax.broadcasted_iota(jnp.int32, values.shape, 0)
    return jnp.where(index < rows - by, pltpu.roll(values, rows - by, 0), fill)


def scan_block(decay, drive, shift):
    by = 1
    while by < decay.shape[0]:
        drive = drive + decay * shift(drive, by, 0.0)
        decay = decay * shift(decay, by, 1.0)
        by *= 2
    return decay, drive


def decay_parts(rate, softness):
    log_decay = -8.0 * rate * softness
    return jnp.exp(log_decay), jnp.sqrt(minus_expm1(2.0 * log_decay))


def rec_forward_rows(feed, branch, vectors_ref, softness_ref, gate_a_ref, gate_x_ref, window, carry):
    rows = feed.shape[0]
    window[pl.ds(8, rows), :] = feed.astype(jnp.float32)
    conv = vectors_ref[4:5, :] + vectors_ref[0:1, :] * window[pl.ds(8, rows), :]
    for k in range(1, 4):
        conv = conv + vectors_ref[k : k + 1, :] * window[pl.ds(8 - k, rows), :]
    window[pl.ds(0, 8), :] = window[pl.ds(rows, 8), :]
    conv_low = conv.astype(jnp.bfloat16)
    rate = jax.nn.sigmoid(matmul(conv_low, gate_a_ref[...]) + vectors_ref[5:6, :])
    gate = jax.nn.sigmoid(matmul(conv_low, gate_x_ref[...]) + vectors_ref[6:7, :])
    decay, scale = decay_parts(rate, softness_ref[...])
    total, state = scan_block(decay, scale * gate * conv_low.astype(jnp.float32), shift_down)
    state = state + total * carry[0:1, :]
    carry[0:1, :] = state[rows - 1 : rows, :]
    gelu_branch = gelu_parts(branch)[0]
    mixed = (gelu_branch * state.astype(jnp.bfloat16).astype(jnp.float32)).astype(jnp.bfloat16)
    return conv_low, rate, gate, state, mixed


def rec_forward_body(
    feed_ref, branch_ref, vectors_ref, softness_ref, gate_a_ref, gate_x_ref,
    conv_ref, rate_ref, input_ref, state_ref, mixed_ref, window, carry,
):
    @pl.when(pl.program_id(0) == 0)
    def _():
        window[...] = jnp.zeros_like(window)
        carry[...] = jnp.zeros_like(carry)

    for s in range(feed_ref.shape[0]):
        conv_ref[s], rate_ref[s], input_ref[s], state_ref[s], mixed_ref[s] = rec_forward_rows(
            feed_ref[s], branch_ref[s], vectors_ref, softness_ref, gate_a_ref, gate_x_ref, window.at[s], carry.at[s]
        )


def rec_backward_rows(
    grad_mixed, branch, feed, feed_before, conv_low, rate, gate, state, state_before,
    vectors_ref, softness_ref, gate_a_ref, gate_x_ref, grad_a_ref, grad_x_ref, sums_ref, window, later, carry,
):
    rows = feed.shape[0]
    softness = softness_ref[...]
    gelu_branch, slope = gelu_parts(branch)
    state_low = state.astype(jnp.bfloat16).astype(jnp.float32)
    grad_state = (grad_mixed * gelu_branch).astype(jnp.bfloat16).astype(jnp.float32)
    grad_branch = (slope * grad_mixed * state_low).astype(jnp.bfloat16)
    decay, scale = decay_parts(rate, softness)
    total, carried = scan_block(shift_up(decay, 1, 1.0), grad_state, shift_up)
    carried = carried + total * carry[0:1, :]
    carry[0:1, :] = decay[0:1, :] * carried[0:1, :]
    index = lax.broadcasted_iota(jnp.int32, state.shape, 0)
    previous = jnp.where(index >= 1, pltpu.roll(state, 1, 0), state_before[7:8, :])
    conv = conv_low.astype(jnp.float32)
    grad_log = carried * previous * decay - carried * gate * conv * decay * decay / scale
    log_rate = grad_log * rate
    pre_a = -8.0 * softness * log_rate * (1.0 - rate)
    pre_x = carried * scale * conv * gate * (1.0 - gate)
    low_a = pre_a.astype(jnp.bfloat16)
    low_x = pre_x.astype(jnp.bfloat16)
    grad_a_ref[...] += matmul_tn(conv_low, low_a)
    grad_x_ref[...] += matmul_tn(conv_low, low_x)
    grad_conv = (
        carried * scale * gate
        + matmul_nt(low_a, gate_a_ref[...])
        + matmul_nt(low_x, gate_x_ref[...])
    )
    window[pl.ds(0, 8), :] = feed_before
    window[pl.ds(8, rows), :] = feed.astype(jnp.float32)
    later[pl.ds(rows, 8), :] = later[pl.ds(0, 8), :]
    later[pl.ds(0, rows), :] = grad_conv
    grad_feed = vectors_ref[0:1, :] * grad_conv
    sums_ref[0:1, :] += jnp.sum(grad_conv * window[pl.ds(8, rows), :], axis=0, keepdims=True)
    for k in range(1, 4):
        grad_feed = grad_feed + vectors_ref[k : k + 1, :] * later[pl.ds(k, rows), :]
        sums_ref[k : k + 1, :] += jnp.sum(
            grad_conv * window[pl.ds(8 - k, rows), :], axis=0, keepdims=True
        )
    sums_ref[4:5, :] += jnp.sum(grad_conv, axis=0, keepdims=True)
    sums_ref[5:6, :] += jnp.sum(pre_a, axis=0, keepdims=True)
    sums_ref[6:7, :] += jnp.sum(pre_x, axis=0, keepdims=True)
    sums_ref[7:8, :] += jnp.sum(log_rate, axis=0, keepdims=True)
    return grad_branch, grad_feed.astype(jnp.bfloat16)


def rec_backward_body(
    grad_mixed_ref, branch_ref, feed_ref, feed_before_ref, conv_ref, rate_ref, input_ref,
    state_ref, state_before_ref, vectors_ref, softness_ref, gate_a_ref, gate_x_ref,
    grad_branch_ref, grad_feed_ref, grad_a_ref, grad_x_ref, sums_ref, window, later, carry,
):
    step = pl.program_id(0)

    @pl.when(step == 0)
    def _():
        for ref in (later, carry, grad_a_ref, grad_x_ref, sums_ref):
            ref[...] = jnp.zeros_like(ref)

    keep = jnp.where(step == pl.num_programs(0) - 1, 0.0, 1.0)
    for s in range(feed_ref.shape[0]):
        before = feed_before_ref[s].astype(jnp.float32)
        grad_branch_ref[s], grad_feed_ref[s] = rec_backward_rows(
            grad_mixed_ref[s], branch_ref[s], feed_ref[s], before[before.shape[0] - 8 :] * keep, conv_ref[s],
            rate_ref[s], input_ref[s], state_ref[s], state_before_ref[s] * keep,
            vectors_ref, softness_ref, gate_a_ref, gate_x_ref, grad_a_ref, grad_x_ref, sums_ref,
            window.at[s], later.at[s], carry.at[s],
        )


def whole(shape):
    return pl.BlockSpec(shape, lambda i: (0,) * len(shape))


def rec_forward(feed, branch, vectors, softness, gate_a, gate_x):
    seqs, seq_len, channels = feed.shape
    rows = pick_rows(seq_len)
    block = pl.BlockSpec((seqs, rows, channels), lambda i: (0, i, 0))
    full = jax.ShapeDtypeStruct(feed.shape, jnp.float32)
    low = jax.ShapeDtypeStruct(feed.shape, jnp.bfloat16)
    return pl.pallas_call(
        rec_forward_body,
        grid=(seq_len // rows,),
        in_specs=[block, block]
        + [whole(v.shape) for v in (vectors, softness, gate_a, gate_x)],
        out_specs=[block] * 5,
        out_shape=[low, full, full, full, low],
        scratch_shapes=[
            pltpu.VMEM((seqs, rows + 8, channels), jnp.float32),
            pltpu.VMEM((seqs, 8, channels), jnp.float32),
        ],
        compiler_params=pltpu.CompilerParams(vmem_limit_bytes=40 << 20),
        name="rec_forward",
    )(feed, branch, vectors, softness, gate_a, gate_x)


def rec_backward(grad_mixed, branch, feed, conv, rate, gate, state, vectors, softness, gate_a, gate_x):
    seqs, seq_len, channels = feed.shape
    rows = pick_rows(seq_len)
    blocks = seq_len // rows
    block = pl.BlockSpec((seqs, rows, channels), lambda i: (0, blocks - 1 - i, 0))

    def ahead(by):
        return pl.BlockSpec(
            (seqs, by, channels),
            lambda i: (0, jnp.maximum((blocks - 1 - i) * (rows // by) - 1, 0), 0),
        )

    low = jax.ShapeDtypeStruct(feed.shape, jnp.bfloat16)
    square = jax.ShapeDtypeStruct((channels, channels), jnp.float32)
    return pl.pallas_call(
        rec_backward_body,
        grid=(blocks,),
        in_specs=[block, block, block, ahead(16), block, block, block, block, ahead(8)]
        + [whole(v.shape) for v in (vectors, softness, gate_a, gate_x)],
        out_specs=[block, block, whole((channels, channels)), whole((channels, channels)), whole((8, channels))],
        out_shape=[low, low, square, square, jax.ShapeDtypeStruct((8, channels), jnp.float32)],
        scratch_shapes=[
            pltpu.VMEM((seqs, rows + 8, channels), jnp.float32),
            pltpu.VMEM((seqs, rows + 8, channels), jnp.float32),
            pltpu.VMEM((seqs, 8, channels), jnp.float32),
        ],
        compiler_params=pltpu.CompilerParams(vmem_limit_bytes=40 << 20),
        name="rec_backward",
    )(grad_mixed, branch, feed, feed, conv, rate, gate, state, state, vectors, softness, gate_a, gate_x)


def line_place():
    return lax.axis_size("grp") // 2, lax.axis_index("grp") // 2, lax.axis_index("grp") % 2


def greet_line():
    chips, chip, core = line_place()
    barrier = pltpu.get_barrier_semaphore()

    def signal(place):
        pl.semaphore_signal(barrier, inc=1, device_id={"grp": place}, device_id_type=MESH)

    signal(chip * 2 + 1 - core)

    @pl.when(chip > 0)
    def _():
        signal(chip * 2 + core - 2)

    @pl.when(chip < chips - 1)
    def _():
        signal(chip * 2 + core + 2)

    ends = (chip == 0).astype(jnp.int32) + (chip == chips - 1).astype(jnp.int32)
    pl.semaphore_wait(barrier, 3 - ends)


def greet_axes(axes):
    barrier = pltpu.get_barrier_semaphore()
    for axis in axes:
        size = lax.axis_size(axis)
        for k in range(1, size):
            pl.semaphore_signal(
                barrier,
                inc=1,
                device_id={axis: lax.rem(lax.axis_index(axis) + k, size)},
                device_id_type=MESH,
            )
    pl.semaphore_wait(barrier, sum(lax.axis_size(axis) - 1 for axis in axes))


class Gather:
    def __init__(self, sources, outs, rows, send_sem, recv_sem, own_sem):
        self.chips, self.chip, self.core = line_place()
        self.me = self.chip * 2 + self.core
        self.sources, self.outs, self.rows = sources, outs, rows
        self.send_sem, self.recv_sem, self.own_sem = send_sem, recv_sem, own_sem

    def slot(self, p, origin):
        return self.outs[p].at[pl.ds(pl.multiple_of(origin * self.rows, self.rows), self.rows), :]

    def copy(self, p, source, origin, target, way):
        return pltpu.make_async_remote_copy(
            src_ref=source,
            dst_ref=self.slot(p, origin),
            send_sem=self.send_sem.at[way, p, origin],
            recv_sem=self.recv_sem.at[p, origin],
            device_id={"grp": target},
            device_id_type=MESH,
        )

    def to_right(self, p, source, origin):
        return self.copy(p, source, origin, self.me + 2, 0)

    def to_left(self, p, source, origin):
        return self.copy(p, source, origin, self.me - 2, 1)

    def to_partner(self, p, source, origin):
        return self.copy(p, source, origin, self.chip * 2 + 1 - self.core, 2)

    def own(self, p):
        return pltpu.make_async_copy(self.sources[p], self.slot(p, self.me), self.own_sem.at[p])

    def start(self, p):
        source = self.sources[p]

        @pl.when(self.chip < self.chips - 1)
        def _():
            self.to_right(p, source, self.me).start()

        @pl.when(self.chip > 0)
        def _():
            self.to_left(p, source, self.me).start()

        self.to_partner(p, source, self.me).start()
        self.own(p).start()

    def hop(self, p, h):
        left_origin = self.me - 2 - 2 * h
        right_origin = self.me + 2 + 2 * h

        @pl.when(self.chip - 1 - h >= 0)
        def _():
            here = self.slot(p, left_origin)
            self.to_right(p, here, left_origin).wait_recv()

            @pl.when(self.chip < self.chips - 1)
            def _():
                self.to_right(p, here, left_origin).start()

            self.to_partner(p, here, left_origin).start()

        @pl.when(self.chip + 1 + h <= self.chips - 1)
        def _():
            here = self.slot(p, right_origin)
            self.to_left(p, here, right_origin).wait_recv()

            @pl.when(self.chip > 0)
            def _():
                self.to_left(p, here, right_origin).start()

            self.to_partner(p, here, right_origin).start()

    def arrive(self, p):
        for c in range(self.chips):
            origin = c * 2 + 1 - self.core
            self.to_partner(p, self.slot(p, origin), origin).wait_recv()
        self.own(p).wait()

    def finish(self, p):
        self.arrive(p)
        self.sent(p)

    def sent(self, p):
        for c in range(self.chips):
            origin = c * 2 + self.core
            here = self.slot(p, origin)
            self.to_partner(p, here, origin).wait_send()

            @pl.when((c <= self.chip) & (self.chip < self.chips - 1))
            def _():
                self.to_right(p, here, origin).wait_send()

            @pl.when((c >= self.chip) & (self.chip > 0))
            def _():
                self.to_left(p, here, origin).wait_send()


def gather_sems(pieces):
    n = lax.axis_size("grp")
    return [
        pltpu.SemaphoreType.DMA((3, pieces, n)),
        pltpu.SemaphoreType.DMA((pieces, n)),
        pltpu.SemaphoreType.DMA((pieces,)),
    ]


class Scatter:
    def __init__(self, rows, part, out, swap_in, line_in, send_sem, recv_sem):
        self.chips, self.chip, self.core = line_place()
        self.me = self.chip * 2 + self.core
        self.rows, self.part, self.out = rows, part, out
        self.swap_in, self.line_in = swap_in, line_in
        self.send_sem, self.recv_sem = send_sem, recv_sem

    def copy(self, dest, place, way, slot, p):
        return pltpu.make_async_remote_copy(
            src_ref=self.out.at[p, slot],
            dst_ref=dest,
            send_sem=self.send_sem.at[way, p, slot],
            recv_sem=self.recv_sem.at[way, p, slot],
            device_id={"grp": place},
            device_id_type=MESH,
        )

    def swap(self, p, c):
        return self.copy(self.swap_in.at[p, c], self.chip * 2 + 1 - self.core, 0, c, p)

    def right(self, p, c):
        return self.copy(self.line_in.at[p, c], self.me + 2, 1, c, p)

    def left(self, p, c):
        slot = jnp.where(c == self.chip - 1, self.chips, c)
        return self.copy(self.line_in.at[p, slot], self.me - 2, 2, c, p)

    def from_right(self, p, c):
        slot = jnp.where(c == self.chip, self.chips, c)
        return self.copy(self.line_in.at[p, slot], self.me + 2, 2, c, p)

    def fill(self, p, s, lefts, rights, transposed, width=512):
        def rows_of(ref, core):
            at = [pl.multiple_of((c * 2 + core) * self.rows, self.rows) for c in range(self.chips)]
            return jnp.concatenate([ref[s, pl.ds(a, self.rows), :] for a in at], axis=0)

        def product(core, store):
            chosen = [rows_of(ref, core) for ref in lefts]

            @pl.loop(0, self.out.shape[-1] // width)
            def _(j):
                columns = pl.ds(pl.multiple_of(j * width, width), width)
                total = None
                for left, right in zip(chosen, rights):
                    term = matmul_nt(left, right[columns, :]) if transposed else matmul(left, right[:, columns])
                    total = term if total is None else total + term
                for c in range(self.chips):
                    store(c, columns, total[c * self.rows : (c + 1) * self.rows])

        def to_out(c, columns, value):
            self.out[p, c, :, columns] = value.astype(jnp.bfloat16)

        def to_part(c, columns, value):
            self.part[p, c, :, columns] = value

        def partners():
            product(1 - self.core, to_out)
            for c in range(self.chips):
                self.swap(p, c).start()

        def own():
            product(self.core, to_part)

        return partners, own

    def own(self, p, c):
        self.swap(p, c).wait_recv()
        return self.part[p, c] + self.swap_in[p, c].astype(jnp.float32)

    def hop(self, p, t):
        last = self.chips - 1

        def send(c, first, arrival, onward):
            self.swap(p, c).wait_send()
            total = self.own(p, c)

            @pl.when(first)
            def _():
                self.out[p, c] = total.astype(jnp.bfloat16)

            @pl.when(jnp.logical_not(first))
            def _():
                arrival(p, c).wait_recv()
                self.out[p, c] = (total + self.line_in[p, c].astype(jnp.float32)).astype(jnp.bfloat16)

            onward(p, c).start()

        @pl.when(self.chip <= t)
        def _():
            send(last - t + self.chip, self.chip == 0, self.right, self.right)

        @pl.when(last - self.chip <= t)
        def _():
            send(t - last + self.chip, self.chip == last, self.from_right, self.left)

    def result(self, p):
        chip = self.chip
        self.part[p, chip] = self.own(p, chip)

        @pl.when(chip > 0)
        def _():
            self.right(p, chip).wait_recv()
            self.part[p, chip] += self.line_in[p, chip].astype(jnp.float32)

        @pl.when(chip < self.chips - 1)
        def _():
            self.from_right(p, chip).wait_recv()
            self.part[p, chip] += self.line_in[p, self.chips].astype(jnp.float32)

        return self.part.at[p, chip]

    def finish(self, p):
        self.swap(p, self.chip).wait_send()
        for c in range(self.chips):

            @pl.when(c > self.chip)
            def _():
                self.right(p, c).wait_send()

            @pl.when(c < self.chip)
            def _():
                self.left(p, c).wait_send()


def scatter_scratch(pieces, rows, width):
    chips = lax.axis_size("grp") // 2
    return [
        pltpu.VMEM((pieces, chips, rows, width), jnp.float32),
        pltpu.VMEM((pieces, chips, rows, width), jnp.bfloat16),
        pltpu.VMEM((pieces, chips, rows, width), jnp.bfloat16),
        pltpu.VMEM((pieces, chips + 1, rows, width), jnp.bfloat16),
        pltpu.SemaphoreType.DMA((3, pieces, chips)),
        pltpu.SemaphoreType.DMA((3, pieces, chips)),
    ]


in_vmem = pl.BlockSpec(memory_space=pltpu.VMEM)
in_hbm = pl.BlockSpec(memory_space=pl.ANY)


def call(body, name, number, inputs, in_specs, outs, out_specs, scratch, us):
    return pl.pallas_call(
        body,
        in_specs=in_specs,
        out_specs=out_specs,
        out_shape=outs,
        scratch_shapes=scratch,
        name=name,
        cost_estimate=pl.CostEstimate(
            flops=us * 1000000000, bytes_accessed=us * 3000000, transcendentals=0
        ),
        compiler_params=pltpu.CompilerParams(
            collective_id=number, has_side_effects=True, vmem_limit_bytes=62 << 20
        ),
    )(*inputs)


class Exchange:
    def __init__(self, axis, source, slot, send_sem, recv_sem, steps=None, first=1):
        self.axis, self.source, self.slot, self.steps, self.first = axis, source, slot, steps, first
        self.size, self.me = lax.axis_size(axis), lax.axis_index(axis)
        self.send_sem, self.recv_sem = send_sem, recv_sem

    def copy(self, k, owner):
        peer = lax.rem(self.me + k, self.size)
        return pltpu.make_async_remote_copy(
            src_ref=self.source(peer),
            dst_ref=self.slot(owner) if self.slot else self.steps.at[k - self.first],
            send_sem=self.send_sem.at[k],
            recv_sem=self.recv_sem.at[k],
            device_id={self.axis: peer},
            device_id_type=MESH,
        )

    def own(self):
        slot = self.slot(self.me) if self.slot else self.steps.at[0]
        return pltpu.make_async_copy(self.source(self.me), slot, self.send_sem.at[0])

    def start(self):
        self.own().start()
        self.start_others()

    def start_others(self):
        for k in range(1, self.size):
            self.copy(k, self.me).start()

    def finish(self):
        self.own().wait()
        self.finish_others()

    def finish_others(self):
        for k in range(1, self.size):
            self.copy(k, lax.rem(self.me - k + self.size, self.size)).wait_recv()
        for k in range(1, self.size):
            self.copy(k, self.me).wait_send()


def sum_of(slots):
    total = slots[0]
    for k in range(1, slots.shape[0]):
        total = total + slots[k]
    return total


def block(ref, axis, parts):
    size = ref.shape[axis] // parts

    def view(k):
        at = pl.ds(pl.multiple_of(k * size, size), size)
        return ref.at[at, :] if axis == 0 else ref.at[:, at]

    return view


def weight_gathers(axes, sources, outs, send_sem, recv_sem):
    parts = lax.axis_size("seq")
    return [
        Exchange(
            "seq", lambda k, ref=source: ref, block(out, axis, parts), send_sem.at[i], recv_sem.at[i]
        )
        for i, (axis, source, out) in enumerate(zip(axes, sources, outs))
    ]


def weight_sums(axes, sources, outs, send_sem, recv_sem, first=1):
    parts = lax.axis_size("seq")
    return [
        Exchange(
            "seq", block(source, axis, parts), None, send_sem.at[i], recv_sem.at[i], out, first
        )
        for i, (axis, source, out) in enumerate(zip(axes, sources, outs))
    ]


def seq_sems(count):
    return [pltpu.SemaphoreType.DMA((count, lax.axis_size("seq")))] * 2


def gathered(block_of, axis):
    shape = list(block_of.shape)
    shape[axis] *= lax.axis_size("seq")
    return jax.ShapeDtypeStruct(shape, block_of.dtype)


def slots_of(matrix, axis, first=1):
    shape = list(matrix.shape)
    size = lax.axis_size("seq")
    shape[axis] //= size
    return jax.ShapeDtypeStruct((size - first, *shape), matrix.dtype)


weight_axes = (0, 0, 1)
mixer_axes = (1, 1, 1)


def copies(pairs, sem):
    return [pltpu.make_async_copy(source, buffer, sem.at[i]) for i, (source, buffer) in enumerate(pairs)]


def views(ref):
    return [ref.at[s] for s in range(ref.shape[0])]


def first_body(x_ref, grad_ref, pack_ref, w0, w1, w2, later_ref, full_ref, params_ref, gains_ref, o0, o1, o2, *refs):
    small_send, small_recv, gain_send, gain_recv, weight_send, weight_recv = refs[3:]
    greet_axes(("seq", "grp"))
    seqs = x_ref.shape[0]
    gather = Gather(views(x_ref), views(full_ref), x_ref.shape[1], *refs[:3])
    weights = weight_gathers(mixer_axes, (w0, w1, w2), (o0, o1, o2), weight_send, weight_recv)
    small = Exchange("seq", lambda k: pack_ref, lambda k: params_ref.at[k], small_send, small_recv)
    small.start()
    for s in range(seqs):
        gather.start(s)
    for weight in weights:
        weight.start()
    later_ref[...] = grad_ref[...]
    small.finish()
    place = lax.axis_index("grp")
    for owner in range(small.size):
        gains_ref[place, owner] = params_ref[owner, pl.ds(pack_ref.shape[0] - 8, 8), :]
    gains = Exchange("grp", lambda k: gains_ref.at[place], lambda k: gains_ref.at[k], gain_send, gain_recv)
    gains.start_others()
    for h in range(gather.chips - 1):
        for s in range(seqs):
            gather.hop(s, h)
    gains.finish_others()
    for weight in weights:
        weight.finish()
    for s in range(seqs):
        gather.finish(s)


def gather_first(layer_in, out_grad, pack, weights):
    seqs, rows, width = layer_in.shape
    n, size = lax.axis_size("grp"), lax.axis_size("seq")
    return call(
        first_body, "gather_first", 1,
        (layer_in, out_grad, pack, *weights), [in_vmem] * 6,
        [
            jax.ShapeDtypeStruct(out_grad.shape, out_grad.dtype),
            jax.ShapeDtypeStruct((seqs, n * rows, width), jnp.bfloat16),
            jax.ShapeDtypeStruct((size,) + pack.shape, jnp.float32),
            jax.ShapeDtypeStruct((n, size, 8, 128), jnp.float32),
        ]
        + [gathered(w, axis) for w, axis in zip(weights, mixer_axes)],
        [in_vmem, in_hbm] + [in_vmem] * 2 + [in_hbm] * 3,
        gather_sems(seqs)
        + [pltpu.SemaphoreType.DMA((size,))] * 2
        + [pltpu.SemaphoreType.DMA((n,))] * 2
        + seq_sems(3),
        70,
    )


def mean_of(values):
    return jnp.mean(values, axis=-1, keepdims=True)


def sum_then_gather(scatter, gather, fills, stores, count=0, between=None, after=()):
    hops = range(1, scatter.chips - 1)
    for step in fills[0]:
        step()
    scatter.hop(0, 0)
    for p, store in enumerate(stores):
        ahead = list(fills[p + 1] if p + 1 < len(fills) else after)
        for h in hops:
            if ahead:
                ahead.pop(0)()
            scatter.hop(p, h)
            if 0 < p <= count:
                gather.hop(p - 1, h - 1)
        for step in ahead:
            step()
        if p + 1 < len(fills):
            scatter.hop(p + 1, 0)
        if between and p == 0:
            between()
        store()
        if p < count:
            gather.start(p)
        if 0 < p <= count:
            gather.hop(p - 1, gather.chips - 2)
    if count == len(stores):
        for h in range(gather.chips - 1):
            gather.hop(count - 1, h)
    for p in range(count):
        gather.finish(p)
    for p in range(len(fills)):
        scatter.finish(p)


def out_body(hidden_ref, down_w_ref, residual_ref, layer_out_ref, scatter, first):
    def fill(s):
        return scatter.fill(first + s, s, [hidden_ref], [down_w_ref], False)

    def store(s):
        layer_out_ref[s] = (residual_ref[s] + scatter.result(first + s)[...]).astype(jnp.bfloat16)

    return fill, store


def mixer_out_body(mixed_ref, out_w_ref, x_ref, gain_ref, w0, w1, w2, residual_ref, normed_ref, o0, o1, o2, low_ref, *refs):
    greet_axes(("seq", "grp"))
    seqs, rows, _ = x_ref.shape
    weights = weight_gathers(weight_axes, (w0, w1, w2), (o0, o1, o2), *refs[:2])
    for weight in weights:
        weight.start()
    gather = Gather(views(low_ref), views(normed_ref), rows, *refs[2:5])
    scatter = Scatter(rows, *refs[5:])

    def fill(s):
        return scatter.fill(s, s, [mixed_ref], [out_w_ref], False)

    def store(s):
        residual = x_ref[s].astype(jnp.float32) + scatter.result(s)[...]
        residual_ref[s] = residual
        normal = residual * lax.rsqrt(mean_of(residual * residual) + epsilon)
        low_ref[s] = (normal * gain_ref[...]).astype(jnp.bfloat16)

    sum_then_gather(
        scatter, gather, [fill(s) for s in range(seqs)], [functools.partial(store, s) for s in range(seqs)], seqs
    )
    for weight in weights:
        weight.finish()


def mixer_out(mixed, out_w, layer_in, gain, weights):
    seqs, rows, width = layer_in.shape
    full = jax.ShapeDtypeStruct((seqs, lax.axis_size("grp") * rows, width), jnp.bfloat16)
    return call(
        mixer_out_body, "mixer_out", 2,
        (mixed, out_w, layer_in, gain, *weights), [in_vmem] * 7,
        [jax.ShapeDtypeStruct(layer_in.shape, jnp.float32), full]
        + [gathered(w, axis) for w, axis in zip(weights, weight_axes)],
        [in_vmem] + [in_hbm] * 4,
        [pltpu.VMEM(layer_in.shape, jnp.bfloat16)]
        + seq_sems(3)
        + gather_sems(seqs)
        + scatter_scratch(seqs, rows, width),
        100,
    )


def mixer_forward_body(
    x_ref, grad_ref, gain_one_ref, gain_two_ref, taps_ref, taps_bias_ref, bias_a_ref, bias_x_ref, softness_own_ref,
    weight_a_ref, weight_x_ref, v0, v1, v2, w0, w1, w2,
    residual_ref, gains_ref, vectors_ref, gate_a_ref, gate_x_ref,
    normed_one_out, branch_out, feed_out, conv_out, rate_out, input_out, state_out, mixed_out, u0, u1, u2,
    normed_ref, grads_ref, o0, o1, o2,
    normed_one_ref, branch_ref, feed_ref, conv_ref, rate_ref, input_ref, state_ref, mixed_ref,
    branch_w_ref, rec_w_ref, out_w_ref, x_full_ref, low_ref, window, carry, gates, gain_slots, vector_slots, gate_slots,
    gain_pack_ref, vector_pack_ref, gate_pack_ref,
    store_sem, weight_store_sem, gain_send, gain_recv, small_send, small_recv,
    mixer_send, mixer_recv, weight_send, weight_recv, *refs,
):
    seqs, rows, width = x_ref.shape
    seq_len = x_full_ref.shape[1]
    me = lax.axis_index("grp")
    kept = (
        (normed_one_ref, normed_one_out), (branch_ref, branch_out), (feed_ref, feed_out), (conv_ref, conv_out),
        (rate_ref, rate_out), (input_ref, input_out), (state_ref, state_out), (mixed_ref, mixed_out),
    )
    keeps = [
        copies([(buffer.at[s], out.at[s]) for buffer, out in kept], store_sem.at[s]) for s in range(seqs)
    ]
    gain_pack_ref[...] = jnp.zeros_like(gain_pack_ref)
    vector_pack_ref[...] = jnp.zeros_like(vector_pack_ref)
    gain_part = gain_one_ref.shape[1]
    gain_pack_ref[0:1, :gain_part] = gain_one_ref[...].astype(jnp.float32)
    gain_pack_ref[0:1, gain_part : 2 * gain_part] = gain_two_ref[...].astype(jnp.float32)
    heads, part, head_dim = weight_a_ref.shape
    for h in range(heads):
        columns = slice(h * part, (h + 1) * part)
        vector_pack_ref[0:4, columns] = taps_ref[h].astype(jnp.float32)
        for row, ref in enumerate((taps_bias_ref, bias_a_ref, bias_x_ref, softness_own_ref)):
            vector_pack_ref[4 + row : 5 + row, columns] = ref[...].astype(jnp.float32)[h : h + 1]
        gate_pack_ref[h] = weight_a_ref[h].astype(jnp.float32)
        gate_pack_ref[heads + h] = weight_x_ref[h].astype(jnp.float32)
    weight_keeps = copies([(branch_w_ref, u0), (rec_w_ref, u1), (out_w_ref, u2)], weight_store_sem)
    greet_axes(("seq", "grp"))
    mixer_weights = weight_gathers(
        mixer_axes, (v0, v1, v2), (branch_w_ref, rec_w_ref, out_w_ref), mixer_send, mixer_recv
    )
    weights = weight_gathers(weight_axes, (w0, w1, w2), (o0, o1, o2), weight_send, weight_recv)
    gather = Gather(
        views(low_ref) + views(grad_ref) + views(x_ref),
        views(normed_ref) + views(grads_ref) + views(x_full_ref),
        rows, *refs[:3],
    )
    scatter = Scatter(rows, *refs[3:])
    place = lax.axis_index("grp")
    small = [
        Exchange("seq", lambda k, ref=pack: ref, lambda k, ref=slots: ref.at[k], small_send.at[i], small_recv.at[i])
        for i, (pack, slots) in enumerate(
            ((gain_pack_ref, gain_slots.at[place]), (vector_pack_ref, vector_slots), (gate_pack_ref, gate_slots))
        )
    ]
    along = Exchange("grp", lambda k: gain_slots.at[place], lambda k: gain_slots.at[k], gain_send, gain_recv)
    first_x = 2 * seqs
    small[0].start()
    gather.start(first_x)
    for move in small[1:]:
        move.start()
    for weight in mixer_weights[:2]:
        weight.start()
    small[0].finish()
    along.start_others()
    last_hop = gather.chips - 2
    for h in range(gather.chips - 1):
        gather.hop(first_x, h)
        if h == max(last_hop - 1, 0):
            for s in range(1, seqs):
                gather.start(first_x + s)
    gates[...] = jnp.zeros_like(gates)
    window[...] = jnp.zeros_like(window)
    along.finish_others()
    parts = lax.axis_size("seq")
    for k in range(parts):
        for g in range(along.size):
            at = (k * along.size + g) * gain_part
            for i in range(2):
                gains_ref[i, :, at : at + gain_part] = gain_slots[g, k, 0:1, i * gain_part : (i + 1) * gain_part]
    for move in small[1:]:
        move.finish()
    for k in range(parts):
        for h in range(heads):
            at = h * head_dim + k * part
            vectors_ref[:, at : at + part] = vector_slots[k, :, h * part : (h + 1) * part]
            for i in range(2):
                gates[i, at : at + part, h * head_dim : (h + 1) * head_dim] = gate_slots[k, i * heads + h]
    gate_a_ref[...] = gates[0].astype(jnp.bfloat16)
    gate_x_ref[...] = gates[1].astype(jnp.bfloat16)
    softness_ref = vectors_ref.at[pl.ds(7, 1), :]
    tile = pick_rows(seq_len // 2, (192, 128, 96, 64, 32, 16))
    chunk = window.shape[0] - 8

    def project(s, half):
        count = seq_len // tile // 2

        @pl.loop(half * count, (half + 1) * count)
        def _(i):
            at = pl.ds(pl.multiple_of(i * tile, tile), tile)
            inputs = x_full_ref[s, at, :].astype(jnp.float32)
            normal = inputs * lax.rsqrt(mean_of(inputs * inputs) + epsilon)
            normed = (normal * gains_ref[0]).astype(jnp.bfloat16)
            normed_one_ref[s, at, :] = normed
            branch_ref[s, at, :] = matmul_nt(normed, branch_w_ref[...])
            feed_ref[s, at, :] = matmul_nt(normed, rec_w_ref[...]).astype(jnp.bfloat16)

    def recur(s):
        window[pl.ds(0, 8), :] = jnp.zeros((8, window.shape[1]), jnp.float32)
        carry[...] = jnp.zeros_like(carry)

        @pl.loop(0, seq_len // chunk)
        def _(i):
            at = pl.ds(pl.multiple_of(i * chunk, chunk), chunk)
            conv, rate, gate, state, mixed = rec_forward_rows(
                feed_ref[s, at, :], branch_ref[s, at, :], vectors_ref, softness_ref, gate_a_ref, gate_x_ref, window, carry
            )
            conv_ref[s, at, :] = conv
            rate_ref[s, at, :] = rate
            input_ref[s, at, :] = gate
            state_ref[s, at, :] = state
            mixed_ref[s, at, :] = mixed

        for keep in keeps[s]:
            keep.start()

    def late_hops(first, end):
        for h in range(first, min(end, gather.chips - 1)):
            for s in range(seqs):
                gather.hop(seqs + s, h)

    def next_x(h):
        for s in range(1, seqs):
            if h <= last_hop:
                gather.hop(first_x + s, h)

    def steps(s):
        partners, own = scatter.fill(s, s, [mixed_ref], [out_w_ref], False)

        def first():
            gather.arrive(first_x + s)
            if s == 0:
                for weight in mixer_weights[:2]:
                    weight.finish()
                mixer_weights[2].start()
            project(s, 0)
            if s == 0:
                next_x(0)
            project(s, 1)
            if s == 0:
                next_x(1)
            else:
                late_hops(0, 1)

        def second():
            recur(s)
            if s == 0:
                for h in range(2, gather.chips - 1):
                    next_x(h)
                mixer_weights[2].finish()
                for weight in weights:
                    weight.start()
                for t in range(seqs):
                    gather.start(seqs + t)
                for keep in weight_keeps:
                    keep.start()
            else:
                late_hops(1, 2)

        return [first, second, partners, own]

    def store(s):
        own = x_ref[s]
        residual = own.astype(jnp.float32) + scatter.result(s)[...]
        residual_ref[s] = residual
        normal = residual * lax.rsqrt(mean_of(residual * residual) + epsilon)
        low_ref[s] = (normal * gains_ref[1]).astype(jnp.bfloat16)

    sum_then_gather(
        scatter, gather, [steps(s) for s in range(seqs)], [functools.partial(store, s) for s in range(seqs)], seqs,
        after=(lambda: None, functools.partial(late_hops, 2, gather.chips)),
    )
    for s in range(seqs):
        gather.finish(seqs + s)
        gather.sent(first_x + s)
        for keep in keeps[s]:
            keep.wait()
    for keep in weight_keeps:
        keep.wait()
    for weight in weights:
        weight.finish()


def mixer_forward(layer_in, out_grad, small, mixer_weights, weights):
    seqs, rows, width = layer_in.shape
    size, n = lax.axis_size("seq"), lax.axis_size("grp")
    seq_len, channels = n * rows, mixer_weights[0].shape[0]
    f32, bf16 = jnp.float32, jnp.bfloat16
    shape = jax.ShapeDtypeStruct
    low, full = shape((seqs, seq_len, channels), bf16), shape((seqs, seq_len, channels), f32)
    tokens = shape((seqs, seq_len, width), bf16)
    kept = [tokens, full, low, low, full, full, full, low]
    mixer_full = [gathered(w, axis) for w, axis in zip(mixer_weights, mixer_axes)]
    heads, part, head_dim = small[-1].shape
    packs = [
        (8, -(-2 * small[0].shape[1] // 128) * 128), (8, -(-heads * part // 128) * 128), (2 * heads, part, head_dim)
    ]
    outs = [
        shape(layer_in.shape, f32), shape((2, 1, width), f32), shape((8, channels), f32),
        shape((channels, channels), bf16), shape((channels, channels), bf16),
    ]
    outs += kept + mixer_full + [tokens] * 2
    outs += [gathered(w, axis) for w, axis in zip(weights, weight_axes)]
    return call(
        mixer_forward_body, "mixer_forward", 7,
        (layer_in, out_grad, *small, *mixer_weights, *weights),
        [in_vmem] * (8 + len(small)),
        outs, [in_vmem] * 5 + [in_hbm] * 16,
        [pltpu.VMEM(v.shape, v.dtype) for v in kept + mixer_full + [tokens]]
        + [
            pltpu.VMEM(layer_in.shape, bf16),
            pltpu.VMEM((pick_rows(seq_len) + 8, channels), f32),
            pltpu.VMEM((8, channels), f32),
            pltpu.VMEM((2, channels, channels), f32),
            pltpu.VMEM((n, size) + packs[0], f32),
            pltpu.VMEM((size,) + packs[1], f32),
            pltpu.VMEM((size,) + packs[2], f32),
            *(pltpu.VMEM(pack, f32) for pack in packs),
            pltpu.SemaphoreType.DMA((seqs, len(kept))),
            pltpu.SemaphoreType.DMA((3,)),
        ]
        + [pltpu.SemaphoreType.DMA((n,))] * 2
        + seq_sems(3) * 3
        + gather_sems(3 * seqs)
        + scatter_scratch(seqs, rows, width),
        180,
    )


def mlp_back_body(
    with_out, gate_in, up_in, gate_w_in, up_w_in, residual_ref, grad_ref, gain_ref, w0, w1, w2, *refs
):
    if with_out:
        hidden_in, down_w_in = refs[:2]
        refs = refs[2:]
    grad_residual_ref, gain_grad_ref, full_ref, o0, o1, o2 = refs[:6]
    refs = refs[6:]
    if with_out:
        layer_out_ref, late_ref = refs[:2]
        refs = refs[2:]
    low_ref, load_sem, gate_ref, up_ref, gate_w_ref, up_w_ref, *refs = refs
    pairs = [(gate_in, gate_ref), (up_in, up_ref), (gate_w_in, gate_w_ref), (up_w_in, up_w_ref)]
    if with_out:
        hidden_ref, down_w_ref, tiles, made_up, made_down, tile_sem, *refs = refs
        pairs += [(hidden_in, hidden_ref), (down_w_in, down_w_ref)]
    loads = copies(pairs, load_sem)
    for load in loads:
        load.start()
    greet_axes(("seq", "grp"))
    seqs, rows, _ = grad_ref.shape
    if with_out:
        sums = weight_sums(weight_axes[:1], (w0,), (o0,), *refs[:2])
        parts, me = lax.axis_size("seq"), lax.axis_index("seq")
        moves = [
            Exchange(
                "seq", lambda k, ref=made: ref.at[lax.rem(k - me + parts, parts)], None,
                refs[0].at[i], refs[1].at[i], out, 0,
            )
            for i, made, out in ((1, made_up, o1), (2, made_down, o2))
        ]
        order = [(kind, k) for kind in range(2) for k in range(1, parts)] + [(0, 0), (1, 0)]
    else:
        sums = weight_sums(weight_axes, (w0, w1, w2), (o0, o1, o2), *refs[:2])
    for weight in sums:
        weight.start_others()
    gather = Gather(views(low_ref), views(full_ref), rows, *refs[2:5])
    scatter = Scatter(rows, *refs[5:])
    gain_grad_ref[...] = jnp.zeros_like(gain_grad_ref)

    def fill(s):
        return scatter.fill(s, s, [gate_ref, up_ref], [gate_w_ref, up_w_ref], True)

    def store(s):
        term = scatter.result(s)[...]
        residual = residual_ref[s]
        inverse = lax.rsqrt(mean_of(residual * residual) + epsilon)
        normal = residual * inverse
        gain_grad_ref[0:1, :] += jnp.sum(term * normal, axis=0, keepdims=True)
        grad = grad_ref[s].astype(jnp.float32) + norm_back(term, normal, inverse, gain_ref[...])
        grad_residual_ref[s] = grad
        low_ref[s] = grad.astype(jnp.bfloat16)

    def tile_load(i, j):
        kind, k = order[i]
        step = tiles.shape[-1]
        first = lax.rem(me + k, parts) * 2 * step + j * step
        source = (w1, w2)[kind].at[:, :, pl.ds(pl.multiple_of(first, step), step)]
        return pltpu.make_async_copy(source, tiles.at[j], tile_sem.at[j])

    def make(i):
        kind, k = order[i]
        step = tiles.shape[-1]

        @pl.loop(0, 2)
        def _(j):
            tile_load(i, j).wait()
            at = pl.ds(pl.multiple_of(j * step, step), step)
            total = None
            for s in range(seqs):
                if kind == 0:
                    term = matmul_tn(tiles[j, s], up_ref[s])
                else:
                    term = matmul_tn(hidden_ref[s], tiles[j, s])
                total = term if total is None else total + term
            if kind == 0:
                made_up[k, at, :] = total.astype(jnp.bfloat16)
            else:
                made_down[k, :, at] = total.astype(jnp.bfloat16)
            if i + 1 < len(order):
                tile_load(i + 1, j).start()

        if k:
            moves[kind].copy(k, me).start()
        else:
            moves[kind].own().start()

    def make_all(first, end):
        for i in range(first, end):
            make(i)

    def wait_first():
        for load in loads[:4]:
            load.wait()

    def wait_later():
        for load in loads[4:]:
            load.wait()

    fills = [fill(s) for s in range(seqs)]
    fills[0] = (wait_first, *fills[0])
    stores = [functools.partial(store, s) for s in range(seqs)]
    if with_out:
        fill_out, store_out = out_body(hidden_ref, down_w_ref, residual_ref, layer_out_ref, scatter, seqs)
        fills += [fill_out(s) for s in range(seqs - 1)]
        fills[seqs - 1] = (*fills[seqs - 1], wait_later)
        third = parts - 1

        def partners_then(step):
            step()
            make_all(2, third)

        def own_then(step):
            step()
            make_all(third, third + 1)

        if len(fills) > seqs:
            fills[seqs] = (
                functools.partial(partners_then, fills[seqs][0]),
                functools.partial(own_then, fills[seqs][1]),
                functools.partial(make_all, third + 1, 2 * third),
            )
        for j in range(2):
            tile_load(0, j).start()
        stores += [functools.partial(store_out, s) for s in range(seqs - 1)]

    def late():
        step = 256

        @pl.loop(0, late_ref.shape[0] // step)
        def _(i):
            at = pl.ds(pl.multiple_of(i * step, step), step)
            late_ref[at, :] = matmul(hidden_ref[seqs - 1, at, :], down_w_ref[...]).astype(jnp.bfloat16)

    def rest():
        make_all(2 * third if len(fills) > seqs else 2, len(order))

    sum_then_gather(
        scatter, gather, fills, stores, seqs,
        between=functools.partial(make_all, 0, 2) if with_out else None, after=(late, rest) if with_out else (),
    )
    for weight in sums:
        weight.finish_others()
    if with_out:
        for move in moves:
            move.finish()


def mlp_back(grad_gate, grad_up, gate_w, up_w, residual, out_grad, gain, grads, out_inputs):
    seqs, rows, width = residual.shape
    outs = [
        jax.ShapeDtypeStruct(residual.shape, jnp.float32),
        jax.ShapeDtypeStruct((8, width), jnp.float32),
        jax.ShapeDtypeStruct((seqs, lax.axis_size("grp") * rows, width), jnp.bfloat16),
    ]
    if out_inputs:
        size = lax.axis_size("seq")
        hidden_width, part = grad_gate.shape[-1], width // size
        outs.append(slots_of(grads[0], 0))
        outs.append(jax.ShapeDtypeStruct((size, part, hidden_width), jnp.bfloat16))
        outs.append(jax.ShapeDtypeStruct((size, hidden_width, part), jnp.bfloat16))
        makers = [
            pltpu.VMEM((2, *grad_gate.shape[:2], part // 2), jnp.bfloat16),
            *(pltpu.VMEM(out.shape, out.dtype) for out in outs[-2:]),
            pltpu.SemaphoreType.DMA((2,)),
        ]
    else:
        outs += [slots_of(grad, axis) for grad, axis in zip(grads, weight_axes)]
        makers = []
    out_specs = [in_vmem] * 2 + [in_hbm] * 4
    if out_inputs:
        outs.append(jax.ShapeDtypeStruct((seqs - 1, rows, width), jnp.bfloat16))
        outs.append(jax.ShapeDtypeStruct((lax.axis_size("grp") * rows, width), jnp.bfloat16))
        out_specs += [in_vmem] * 2
    return call(
        functools.partial(mlp_back_body, bool(out_inputs)), "mlp_back", 3,
        (grad_gate, grad_up, gate_w, up_w, residual, out_grad, gain, *grads, *out_inputs),
        [in_hbm] * 4 + [in_vmem] * 3 + [in_hbm] * (3 + len(out_inputs)),
        outs, out_specs,
        [pltpu.VMEM(residual.shape, jnp.bfloat16), pltpu.SemaphoreType.DMA((6,))]
        + [pltpu.VMEM(v.shape, v.dtype) for v in (grad_gate, grad_up, gate_w, up_w, *out_inputs)]
        + makers
        + seq_sems(3)
        + gather_sems(seqs)
        + scatter_scratch(seqs * 2 - 1 if out_inputs else seqs, rows, width),
        120,
    )


def last_body(
    branch_ref, feed_ref, branch_w_ref, rec_w_ref, x_ref, grad_ref, gain_ref, gain_two_ref, rec_ref,
    w0, w1, w2, *refs,
):
    grad_x_ref, rec_sum_ref, gain_sum_ref, o0, o1, o2 = refs[:6]
    refs = refs[6:]
    rec_slots, gain_local, gain_part, gain_slots, part_slots = refs[:5]
    rec_sems, gain_sems, part_sems = refs[5:7], refs[7:9], refs[9:11]
    greet_axes(("seq", "grp"))
    seqs, rows, _ = x_ref.shape
    sums = weight_sums(mixer_axes, (w0, w1, w2), (o0, o1, o2), *refs[11:13])
    scatter = Scatter(rows, *refs[13:])
    rec = Exchange("seq", lambda k: rec_ref.at[k], lambda k: rec_slots.at[k], *rec_sems)
    rec.start()
    for weight in sums:
        weight.start_others()
    gain_local[...] = jnp.zeros_like(gain_local)
    gain_local[1:2, :] = gain_two_ref[0:1, :]

    def fill(s):
        return scatter.fill(s, s, [branch_ref, feed_ref], [branch_w_ref, rec_w_ref], False)

    across = Exchange(
        "seq", block(gain_local, 1, lax.axis_size("seq")), lambda k: gain_slots.at[k], *gain_sems
    )

    def store(s):
        term = scatter.result(s)[...]
        inputs = x_ref[s].astype(jnp.float32)
        inverse = lax.rsqrt(mean_of(inputs * inputs) + epsilon)
        normal = inputs * inverse
        gain_local[0:1, :] += jnp.sum(term * normal, axis=0, keepdims=True)
        if s == seqs - 1:
            across.start()
        grad_x_ref[s] = grad_ref[s] + norm_back(term, normal, inverse, gain_ref[...])

    sum_then_gather(
        scatter, None, [fill(s) for s in range(seqs)], [functools.partial(store, s) for s in range(seqs)]
    )
    across.finish()
    gain_part[...] = sum_of(gain_slots)
    along = Exchange("grp", lambda k: gain_part, lambda k: part_slots.at[k], *part_sems)
    along.start()
    rec.finish()
    rec_sum_ref[...] = sum_of(rec_slots)
    for weight in sums:
        weight.finish_others()
    along.finish()
    gain_sum_ref[...] = sum_of(part_slots)


def last(grad_branch, grad_feed, branch_w, rec_w, layer_in, grad_residual, gain, gain_two_grad, rec_blocks, grads):
    seqs, rows, width = layer_in.shape
    size, n = lax.axis_size("seq"), lax.axis_size("grp")
    f32 = jnp.float32
    inputs = (grad_branch, grad_feed, branch_w, rec_w, layer_in, grad_residual, gain, gain_two_grad, rec_blocks)
    outs = [
        jax.ShapeDtypeStruct(layer_in.shape, f32),
        jax.ShapeDtypeStruct(rec_blocks.shape[1:], f32),
        jax.ShapeDtypeStruct((8, width // size), f32),
    ]
    outs += [slots_of(grad, axis) for grad, axis in zip(grads, mixer_axes)]
    out_specs = [in_vmem] * 3 + [in_hbm] * 3
    return call(
        last_body, "last", 4,
        inputs + tuple(grads), [in_vmem] * len(inputs) + [in_hbm] * 3,
        outs, out_specs,
        [
            pltpu.VMEM(rec_blocks.shape, f32),
            pltpu.VMEM((8, width), f32),
            pltpu.VMEM((8, width // size), f32),
            pltpu.VMEM((size, 8, width // size), f32),
            pltpu.VMEM((n, 8, width // size), f32),
        ]
        + [pltpu.SemaphoreType.DMA((size,))] * 4
        + [pltpu.SemaphoreType.DMA((n,))] * 2
        + seq_sems(3)
        + scatter_scratch(seqs, rows, width),
        80,
    )


def head_windows(heads, head_dim, parts):
    part = head_dim // parts
    rows = max(-(-(k + 1) * part // 8) * 8 - k * part // 8 * 8 for k in range(parts))

    def start(h, k):
        return pl.multiple_of(h * head_dim + k * part // 8 * 8, 8)

    return rows, start


def mixer_back_body(
    heads, low_in, out_w_in, branch_in, feed_in, conv_in, rate_in, input_in, state_in, mixed_in, branch_w_in, rec_w_in,
    normed_in, vectors_ref, gate_a_ref, gate_x_ref, x_ref, grad_ref, gain_ref, gain_two_ref,
    grad_x_ref, squares_out_ref, sums_out_ref, gain_sum_ref, o0, o1, o2,
    low_ref, out_w_ref, branch_ref, feed_ref, conv_ref, rate_ref, input_ref, state_ref, mixed_ref, branch_w_ref,
    rec_w_ref, grad_mixed, grad_branch, grad_feed, squares, sums, window, later, carry, tiles, d0, d1, d2,
    square_slots, sum_slots_ref, gain_local, gain_part, gain_slots, part_slots, load_sem, tile_sem,
    square_send, square_recv, sum_send, sum_recv, gain_send, gain_recv, part_send, part_recv, weight_send, weight_recv,
    *refs,
):
    seqs, rows, width = x_ref.shape
    seq_len, channels = feed_ref.shape[1:]
    softness_ref = vectors_ref.at[pl.ds(7, 1), :]
    per_seq = (
        (low_in, low_ref), (branch_in, branch_ref), (feed_in, feed_ref), (conv_in, conv_ref), (rate_in, rate_ref),
        (input_in, input_ref), (state_in, state_ref),
    )
    pairs = [(out_w_in, out_w_ref)]
    for s in range(seqs):
        pairs += [(source.at[s], buffer.at[s]) for source, buffer in per_seq]
        if s == 0:
            pairs += [(branch_w_in, branch_w_ref), (rec_w_in, rec_w_ref)]
    pairs += [(mixed_in, mixed_ref)]
    loads = copies(pairs, load_sem)
    for load in loads:
        load.start()
    greet_axes(("seq", "grp"))
    scatter = Scatter(rows, *refs)
    parts = lax.axis_size("seq")
    for ref in (squares, sums, gain_local):
        ref[...] = jnp.zeros_like(ref)
    gain_local[1:2, :] = gain_two_ref[0:1, :]
    window_rows, start_of = head_windows(heads, channels // heads, parts)
    square_moves = [
        Exchange(
            "seq",
            lambda k, h=h: squares.at[:, pl.ds(start_of(h, k), window_rows), :],
            lambda k, h=h: square_slots.at[k, h],
            square_send.at[h],
            square_recv.at[h],
        )
        for h in range(heads)
    ]
    sum_move = Exchange("seq", lambda k: sums, lambda k: sum_slots_ref.at[k], sum_send, sum_recv)
    across = Exchange("seq", block(gain_local, 1, parts), lambda k: gain_slots.at[k], gain_send, gain_recv)
    moves = weight_sums(mixer_axes, (d0, d1, d2), (o0, o1, o2), weight_send, weight_recv, 0)
    tile_rows = pick_rows(seq_len, (256, 192, 128, 96, 64, 32, 16))
    chunk = window.shape[0] - 8

    def mix(s):
        if s == 0:
            for load in loads[: 1 + len(per_seq)]:
                load.wait()
        else:
            first = 3 + s * len(per_seq)
            for load in loads[first : first + len(per_seq)]:
                load.wait()

        @pl.loop(0, seq_len // tile_rows)
        def _(i):
            at = pl.ds(pl.multiple_of(i * tile_rows, tile_rows), tile_rows)
            grad_mixed[at, :] = matmul_nt(low_ref[s, at, :], out_w_ref[...])

    def recur(s):
        carry[...] = jnp.zeros_like(carry)
        later[...] = jnp.zeros_like(later)
        blocks = seq_len // chunk

        @pl.loop(0, blocks)
        def _(i):
            first = (blocks - 1 - i) * chunk
            at = pl.ds(pl.multiple_of(first, chunk), chunk)
            keep = jnp.where(i == blocks - 1, 0.0, 1.0)
            before8 = pl.ds(pl.multiple_of(jnp.maximum(first - 8, 0), 8), 8)
            before16 = pl.ds(pl.multiple_of(jnp.maximum(first - 16, 0), 16), 16)
            grad_branch[s, at, :], grad_feed[s, at, :] = rec_backward_rows(
                grad_mixed[at, :], branch_ref[s, at, :], feed_ref[s, at, :],
                feed_ref[s, before16, :].astype(jnp.float32)[8:] * keep, conv_ref[s, at, :], rate_ref[s, at, :],
                input_ref[s, at, :], state_ref[s, at, :], state_ref[s, before8, :] * keep,
                vectors_ref, softness_ref, gate_a_ref, gate_x_ref, squares.at[0], squares.at[1], sums,
                window, later, carry,
            )

        if s == seqs - 1:
            for move in square_moves:
                move.start()
            sum_move.start()

    def steps(s):
        partners, own = scatter.fill(s, s, [grad_branch, grad_feed], [branch_w_ref, rec_w_ref], False)

        def third():
            if s == 0:
                for load in loads[1 + len(per_seq) : 3 + len(per_seq)]:
                    load.wait()
            partners()

        def first():
            mix(s)
            if s == seqs - 1:
                out_grads()

        return [first, functools.partial(recur, s), third, own]

    def out_grads():
        loads[-1].wait()
        step = width // parts

        @pl.loop(0, parts)
        def _(k):
            at = pl.ds(pl.multiple_of(k * step, step), step)
            total = matmul_tn(mixed_ref[0], low_ref[0, :, at])
            for s in range(1, seqs):
                total = total + matmul_tn(mixed_ref[s], low_ref[s, :, at])
            d2[:, at] = total.astype(jnp.bfloat16)

        moves[2].start()

    step = tiles.shape[-1]
    count = width // parts // step

    def columns_of(i):
        peer = lax.rem(lax.axis_index("seq") + 1 + i // count, parts)
        return pl.ds(pl.multiple_of((peer * count + lax.rem(i, count)) * step, step), step)

    def tile_load(i, slot):
        return pltpu.make_async_copy(normed_in.at[:, :, columns_of(i)], tiles.at[slot], tile_sem.at[slot])

    def in_grads(part):
        if part == 0:
            tile_load(0, 0).start()

        @pl.loop(part * count, (part + 1) * count)
        def _(i):
            slot = lax.rem(i, 2)
            tile_load(i, slot).wait()

            @pl.when(i + 1 < parts * count)
            def _():
                tile_load(i + 1, 1 - slot).start()

            for to, grads in ((d0, grad_branch), (d1, grad_feed)):
                total = matmul_tn(grads[0], tiles[slot, 0])
                for s in range(1, seqs):
                    total = total + matmul_tn(grads[s], tiles[slot, s])
                to[:, columns_of(i)] = total.astype(jnp.bfloat16)

        for move in moves[:2]:
            if part < parts - 1:
                move.copy(part + 1, move.me).start()
            else:
                move.own().start()

    def grads_from(first, end):
        for part in range(first, end):
            in_grads(part)

    def store(s):
        term = scatter.result(s)[...]
        inputs = x_ref[s].astype(jnp.float32)
        inverse = lax.rsqrt(mean_of(inputs * inputs) + epsilon)
        normal = inputs * inverse
        gain_local[0:1, :] += jnp.sum(term * normal, axis=0, keepdims=True)
        if s == seqs - 1:
            across.start()
        grad_x_ref[s] = grad_ref[s] + norm_back(term, normal, inverse, gain_ref[...])

    sum_then_gather(
        scatter, None, [steps(s) for s in range(seqs)], [functools.partial(store, s) for s in range(seqs)],
        between=functools.partial(grads_from, 0, parts // 2),
        after=(functools.partial(grads_from, parts // 2, parts - 1), functools.partial(grads_from, parts - 1, parts)),
    )
    across.finish()
    gain_part[...] = sum_of(gain_slots)
    along = Exchange("grp", lambda k: gain_part, lambda k: part_slots.at[k], part_send, part_recv)
    along.start()
    for move in square_moves:
        move.finish()
    squares_out_ref[...] = sum_of(square_slots)
    sum_move.finish()
    sums_out_ref[...] = sum_of(sum_slots_ref)
    for move in moves:
        move.finish()
    along.finish()
    gain_sum_ref[...] = sum_of(part_slots)


def mixer_back(
    heads, low, out_w, branch, feed, conv, rate, gate, state, mixed, branch_w, rec_w, normed,
    vectors, gate_a, gate_x, layer_in, grad_residual, gain, gain_two_grad,
):
    seqs, rows, width = layer_in.shape
    seq_len, channels = feed.shape[1:]
    size, n = lax.axis_size("seq"), lax.axis_size("grp")
    f32, bf16 = jnp.float32, jnp.bfloat16
    large = (low, out_w, branch, feed, conv, rate, gate, state, mixed, branch_w, rec_w)
    small = (vectors, gate_a, gate_x, layer_in, grad_residual, gain, gain_two_grad)
    window_rows = head_windows(heads, channels // heads, size)[0]
    grads = [jax.ShapeDtypeStruct(w.shape, bf16) for w in (branch_w, rec_w, out_w)]
    squares = (heads, 2, window_rows, channels)
    part = width // size
    return call(
        functools.partial(mixer_back_body, heads), "mixer_back", 6,
        large + (normed,) + small,
        [in_hbm] * 12 + [in_vmem] * 7,
        [
            jax.ShapeDtypeStruct(layer_in.shape, f32),
            jax.ShapeDtypeStruct(squares, f32),
            jax.ShapeDtypeStruct((8, channels), f32),
            jax.ShapeDtypeStruct((8, part), f32),
        ]
        + [slots_of(grad, axis, 0) for grad, axis in zip(grads, mixer_axes)],
        [in_vmem] * 4 + [in_hbm] * 3,
        [pltpu.VMEM(v.shape, v.dtype) for v in large]
        + [
            pltpu.VMEM((seq_len, channels), f32),
            pltpu.VMEM(feed.shape, bf16),
            pltpu.VMEM(feed.shape, bf16),
            pltpu.VMEM((2, channels, channels), f32),
            pltpu.VMEM((8, channels), f32),
            pltpu.VMEM((pick_rows(seq_len) + 8, channels), f32),
            pltpu.VMEM((pick_rows(seq_len) + 8, channels), f32),
            pltpu.VMEM((8, channels), f32),
            pltpu.VMEM((2, seqs, seq_len, 256), bf16),
        ]
        + [pltpu.VMEM(grad.shape, bf16) for grad in grads]
        + [
            pltpu.VMEM((size,) + squares, f32),
            pltpu.VMEM((size, 8, channels), f32),
            pltpu.VMEM((8, width), f32),
            pltpu.VMEM((8, part), f32),
            pltpu.VMEM((size, 8, part), f32),
            pltpu.VMEM((n, 8, part), f32),
            pltpu.SemaphoreType.DMA((4 + 7 * seqs,)),
            pltpu.SemaphoreType.DMA((2,)),
        ]
        + [pltpu.SemaphoreType.DMA((heads, size))] * 2
        + [pltpu.SemaphoreType.DMA((size,))] * 4
        + [pltpu.SemaphoreType.DMA((n,))] * 2
        + seq_sems(3)
        + scatter_scratch(seqs, rows, width),
        100,
    )


def out_only_body(hidden_ref, down_w_ref, residual_ref, layer_out_ref, *scratch):
    greet_line()
    scatter = Scatter(residual_ref.shape[1], *scratch)
    fill, store = out_body(hidden_ref, down_w_ref, residual_ref, layer_out_ref, scatter, 0)
    seqs = range(residual_ref.shape[0])
    sum_then_gather(
        scatter, None, [fill(s) for s in seqs], [functools.partial(store, s) for s in seqs]
    )


def out_only(hidden, down_w, residual):
    seqs, rows, width = residual.shape
    return call(
        out_only_body, "layer_out", 5,
        (hidden, down_w, residual), [in_vmem] * 3,
        [jax.ShapeDtypeStruct(residual.shape, jnp.bfloat16)], [in_vmem],
        scatter_scratch(seqs, rows, width), 60,
    )[0]


def per_device(
    layer_in, gain_one, w_branch, w_rec, conv_w, conv_b, gate_a_w, gate_a_b, gate_x_w, gate_x_b,
    decay_logit, w_out, gain_two, mlp_gate, mlp_up, mlp_down, out_grad,
):
    seqs_here, positions, model_width = layer_in.shape
    heads_here, tap_count, part_dim = conv_w.shape
    seq_devices, grp_devices = lax.axis_size("seq"), lax.axis_size("grp")
    head_dim = part_dim * seq_devices
    channels = heads_here * head_dim
    f32 = jnp.float32

    short_line = seqs_here * positions * grp_devices <= 2048 and model_width // seq_devices == 512
    mixer_weights = (w_branch.T, w_rec.T, w_out)
    mlp_weights = (mlp_gate, mlp_up, mlp_down)
    at = tap_count + 4
    if short_line:
        softness = jax.nn.softplus(-decay_logit.astype(f32))
        small = (
            gain_one[None], gain_two[None], conv_w, conv_b, gate_a_b, gate_x_b, softness, gate_a_w, gate_x_w
        )
        (
            residual, gains, vectors, diag_a, diag_x,
            normed_one, branch_pre, feed, conv, rate, gate, state, mixed, branch_w, rec_w, out_w,
            normed_two, grad_output, gate_w, up_w, down_w,
        ) = mixer_forward(layer_in, out_grad, small, mixer_weights, mlp_weights)
        normed_one = normed_one.reshape(-1, model_width)
        grad_output = grad_output.reshape(-1, model_width)
    else:
        own_params = jnp.concatenate(
            [jnp.transpose(conv_w, (0, 2, 1))]
            + [v[:, :, None] for v in (conv_b, gate_a_b, gate_x_b, decay_logit)]
            + [gate_a_w, gate_x_w],
            axis=2,
        ).astype(f32)
        own_gains = jnp.concatenate([gain_one, gain_two]).astype(f32)
        pack = jnp.concatenate(
            [padded_rows(own_params.reshape(1, -1))[0], padded_rows(own_gains.reshape(1, -1))[0]]
        )
        late_grad, x_full, params, gains, branch_w, rec_w, out_w = gather_first(
            layer_in, out_grad, pack, mixer_weights
        )

        gains = gains.reshape(grp_devices, seq_devices, -1)[:, :, : own_gains.size]
        gains = jnp.transpose(gains.reshape(grp_devices, seq_devices, 2, -1), (2, 1, 0, 3)).reshape(2, 1, -1)
        params = params.reshape(seq_devices, -1)[:, : own_params.size]
        params = params.reshape((seq_devices,) + own_params.shape)
        params = jnp.transpose(params, (1, 0, 2, 3)).reshape(heads_here, head_dim, -1)
        vectors = params[:, :, : tap_count + 4].reshape(channels, -1).T
        diag_a = head_diagonal(params[:, :, at : at + head_dim].astype(jnp.bfloat16))
        diag_x = head_diagonal(params[:, :, at + head_dim :].astype(jnp.bfloat16))
        logit = vectors[tap_count + 3 :]
        softness = jax.nn.softplus(-logit)
        grad_output = jnp.concatenate(
            [lax.all_gather(late_grad[s], "grp", axis=0, tiled=True) for s in range(seqs_here)]
        )
        inputs = x_full.astype(f32)
        normal_one = inputs * lax.rsqrt(mean_of(inputs * inputs) + epsilon)
        normed_one = (normal_one * gains[0]).astype(jnp.bfloat16).reshape(-1, model_width)
        branch_pre = matmul_nt(normed_one, branch_w).reshape(seqs_here, -1, channels)
        feed = matmul_nt(normed_one, rec_w).astype(jnp.bfloat16).reshape(seqs_here, -1, channels)
        conv, rate, gate, state, mixed = rec_forward(feed, branch_pre, vectors, softness, diag_a, diag_x)
        residual, normed_two, gate_w, up_w, down_w = mixer_out(
            mixed, out_w, layer_in, gains[1], mlp_weights
        )
    mixed = mixed.reshape(-1, channels)
    normed_two = normed_two.reshape(-1, model_width)
    up_proj = matmul(normed_two, up_w)
    gate_act, gate_pull = jax.vjp(jax.nn.gelu, matmul(normed_two, gate_w))
    hidden = (gate_act * up_proj).astype(jnp.bfloat16)
    grad_hidden = matmul_nt(grad_output, down_w)
    grad_gate = gate_pull(grad_hidden * up_proj)[0].astype(jnp.bfloat16)
    grad_up = (grad_hidden * gate_act).astype(jnp.bfloat16)
    def by_seq(values):
        return values.reshape(seqs_here, -1, values.shape[-1])

    if short_line:
        first_grad = matmul_tn(normed_two, grad_gate).astype(jnp.bfloat16)
        mlp_grads = (first_grad, by_seq(normed_two), by_seq(grad_output))
    else:
        mlp_grads = low_all(
            (matmul_tn(normed_two, grad_gate), matmul_tn(normed_two, grad_up), matmul_tn(hidden, grad_output))
        )

    back_inputs = (
        by_seq(grad_gate), by_seq(grad_up), gate_w, up_w, residual, out_grad, gains[1], mlp_grads
    )
    if not short_line:
        layer_out = out_only(by_seq(hidden), down_w, residual)
        grad_residual, gain_two_grad, residual_low, *mlp_slots = mlp_back(*back_inputs, ())
    else:
        grad_residual, gain_two_grad, residual_low, *mlp_slots, layer_out, late = mlp_back(
            *back_inputs, (by_seq(hidden), down_w)
        )
        late = lax.psum_scatter(late, "grp", scatter_dimension=0, tiled=True)
        late = (residual[seqs_here - 1] + late.astype(f32)).astype(jnp.bfloat16)
        layer_out = jnp.concatenate([layer_out, late[None]])
    if short_line:
        mlp_grads = sum_slots(mlp_grads[:1], mlp_slots[:1], weight_axes) + [sum_all(slot) for slot in mlp_slots[1:]]
    else:
        mlp_grads = sum_slots(mlp_grads, mlp_slots, weight_axes)
    if short_line:
        grad_x, squares, sums, gain_sum, *mixer_slots = mixer_back(
            heads_here, residual_low, out_w, branch_pre, feed, conv, rate, gate, state, by_seq(mixed), branch_w, rec_w,
            by_seq(normed_one), vectors, diag_a, diag_x, layer_in, grad_residual, gains[0], gain_two_grad,
        )
        mixer_grads = [sum_all(slot) for slot in mixer_slots]
        place = lax.axis_index("seq")
        first = place * part_dim % 8
        square_parts = [
            lax.dynamic_slice_in_dim(squares[h], first, part_dim, 1)[:, :, h * head_dim : (h + 1) * head_dim]
            for h in range(heads_here)
        ]
        grad_a, grad_x_gate = (jnp.stack([part[i] for part in square_parts]) for i in range(2))
        own_sums = lax.dynamic_slice_in_dim(
            sums.reshape(at, heads_here, head_dim), place * part_dim, part_dim, 2
        )
        logit_grad = 8.0 * jax.nn.sigmoid(-decay_logit.astype(f32)) * own_sums[tap_count + 3]
        rec_outs = (
            jnp.transpose(own_sums[:tap_count], (1, 0, 2)), own_sums[tap_count], grad_a, own_sums[tap_count + 1],
            grad_x_gate, own_sums[tap_count + 2], logit_grad,
        )
        return finish(layer_out, grad_x, gain_sum, mixer_grads, rec_outs, mlp_grads)
    residual_low = residual_low.reshape(-1, model_width)
    out_weight_grad = matmul_tn(mixed, residual_low)
    grad_mixed = by_seq(matmul_nt(residual_low, out_w))
    grad_branch, grad_feed, square_a, square_x, sums = rec_backward(
        grad_mixed, branch_pre, feed, conv, rate, gate, state, vectors, softness, diag_a, diag_x
    )
    vector_grads = jnp.concatenate(
        [sums[: tap_count + 3], 8.0 * jax.nn.sigmoid(-logit) * sums[tap_count + 3 :]]
    )
    rec_grads = jnp.concatenate(
        [
            vector_grads.T.reshape(heads_here, head_dim, -1),
            diagonal_heads(square_a, heads_here),
            diagonal_heads(square_x, heads_here),
        ],
        axis=2,
    )
    rec_grads = rec_grads.reshape(heads_here, seq_devices, part_dim, -1)
    rec_blocks = padded_rows(jnp.transpose(rec_grads, (1, 0, 2, 3)))
    mixer_grads = low_all(
        (
            matmul_tn(grad_branch.reshape(-1, channels), normed_one),
            matmul_tn(grad_feed.reshape(-1, channels), normed_one),
            out_weight_grad,
        )
    )
    grad_x, rec_sum, gain_sum, *mixer_slots = last(
        grad_branch, grad_feed, branch_w, rec_w, layer_in, grad_residual, gains[0], gain_two_grad, rec_blocks,
        mixer_grads,
    )
    mixer_grads = sum_slots(mixer_grads, mixer_slots, mixer_axes)
    rec_sum = rec_sum.reshape(-1)[: own_params.size].reshape(own_params.shape)
    rec_outs = (
        jnp.transpose(rec_sum[:, :, :tap_count], (0, 2, 1)),
        rec_sum[:, :, tap_count],
        rec_sum[:, :, at : at + head_dim],
        rec_sum[:, :, tap_count + 1],
        rec_sum[:, :, at + head_dim :],
        rec_sum[:, :, tap_count + 2],
        rec_sum[:, :, tap_count + 3],
    )
    return finish(layer_out, grad_x, gain_sum, mixer_grads, rec_outs, mlp_grads)


def finish(layer_out, grad_x, gain_sum, mixer_grads, rec_outs, mlp_grads):
    part = gain_sum.shape[1] // lax.axis_size("grp")
    gain_grads = lax.dynamic_slice_in_dim(gain_sum, lax.axis_index("grp") * part, part, 1)
    return (
        layer_out, grad_x, gain_grads[0], mixer_grads[0].T, mixer_grads[1].T, *rec_outs, mixer_grads[2], gain_grads[1],
        *mlp_grads,
    )


def solution(mesh):
    placed = (
        P("seq", "grp", None),
        P(("seq", "grp")),
        P("seq", "grp"),
        P("seq", "grp"),
        P("grp", None, "seq"),
        P("grp", "seq"),
        P("grp", "seq", None),
        P("grp", "seq"),
        P("grp", "seq", None),
        P("grp", "seq"),
        P("grp", "seq"),
        P("grp", "seq"),
        P(("seq", "grp")),
        P("seq", "grp"),
        P("seq", "grp"),
        P("grp", "seq"),
        P("seq", "grp", None),
    )
    return jax.shard_map(
        per_device,
        mesh=mesh,
        in_specs=placed,
        out_specs=(
            P("seq", "grp", None),
            P("seq", "grp", None),
            P(("seq", "grp")),
            P("seq", "grp"),
            P("seq", "grp"),
            P("grp", None, "seq"),
            P("grp", "seq"),
            P("grp", "seq", None),
            P("grp", "seq"),
            P("grp", "seq", None),
            P("grp", "seq"),
            P("grp", "seq"),
            P("grp", "seq"),
            P(("seq", "grp")),
            P("seq", "grp"),
            P("seq", "grp"),
            P("grp", "seq"),
        ),
        check_vma=False,
    )
```
